32 devices in a mesh: leaf: 4 (over y, core), blk: 8 (over z, x).
Axes of the slice: x: 2, y: 2, z: 4, core: 2. Of those that a mesh axis runs over, the one named last changes fastest.
Arguments:
- ln_rate: float32 [16384], P(('leaf', 'blk')), may hold values from -1 to 0.5
- log_state: float32 [16384], P(('leaf', 'blk')), may hold values from -1 to 1
- sigma: float32 [16384], P(('leaf', 'blk')), may hold values from 40 to 120
- fric_a: float32 [16384], P(('leaf', 'blk')), may hold values from 0.005 to 0.015
- fric_b: float32 [16384], P(('leaf', 'blk')), may hold values from 0.006 to 0.02
- slip_dist: float32 [16384], P(('leaf', 'blk')), may hold values from 1 to 4
- leaf_of_elem: int32 [16384], P(('leaf', 'blk')), may hold values from 0 to 16383, as said below
- near_blocks: bfloat16 [96, 512, 512], P(('leaf', 'blk')), may hold values from -0.25 to 0.25
- near_col: int32 [96], P(('leaf', 'blk')), may hold values from 0 to 7, as said below
- near_count: int32 [32], P(('leaf', 'blk')), may hold values from 1 to 3, as said below
- far_u: bfloat16 [128, 16, 512], P(('leaf', 'blk')), may hold values from -0.75 to 0.75
- far_v: bfloat16 [128, 16, 512], P(('leaf', 'blk')), may hold values from -0.25 to 0.25
- far_col: int32 [128], P(('leaf', 'blk')), may hold values from 0 to 7
- far_rank: int32 [128], P(('leaf', 'blk')), may hold values from 4 to 16, as said below
- coarse_u: bfloat16 [4, 16, 16384], P(None, None, ('leaf', 'blk')), may hold values from -0.75 to 0.75
- coarse_v: bfloat16 [4, 16, 16384], P(None, None, ('leaf', 'blk')), may hold values from -0.09375 to 0.09375
Outputs:
- ln_rate_next: float32 [16384], P(('leaf', 'blk'))
- log_state_next: float32 [16384], P(('leaf', 'blk'))
The draws below stay inside these ranges and needn't reach their ends.
Inputs may be any that keep to these rules, and one draw needn't show every extreme that they name: `leaf_of_elem`: A bijection; an element's leaf-order row lies in the group of the element's own device, and the rows owned by one device take exactly 64 elements from each device of that group. `near_col`: within two blocks of the slot's row block; equal to it in a device's first 1 slots. Slots of a device from position near_count on hold no block. In every group some device has all 3 slots live. `far_rank`: every device has a block of rank 16.
All inputs are finite; a program needn't handle non-finite values.
Results may differ from the reference program's by a relative error of at most 0.00076.
Values may be sent and summed in bfloat16 or wider, within the bound.
No kernel may reach another device: no remote copies, remote signals or barrier semaphores. Data moves between devices by JAX's collectives and lax.ppermute only.
A program may use at most 64 MiB of HBM per device.

```python
import math
import jax
import jax.numpy as jnp
from jax import lax

LEAF = 512
RANK = 16
FAR_CAP = 4
BLK_DEV = 1
GROUPS = 4
MEMBERS = 8
ELEM_DEV = 512
PER_PEER = 64
GROUP_BLOCKS = 8
GROUP_ROWS = 4096
ELEMS = 16384
NEAR_DEV = 3
FAR_DEV = 4
DEVICES = 32


def draw_near_col(key, part):
    key = jax.random.fold_in(key, 41)
    devices_all = GROUPS * MEMBERS
    member = jnp.arange(devices_all, dtype=jnp.int32) % MEMBERS
    slot_index = jnp.arange(NEAR_DEV, dtype=jnp.int32)
    rows_all = member[:, None] * BLK_DEV + (slot_index % BLK_DEV)[None, :]
    step_pick = jax.random.randint(key, (devices_all, NEAR_DEV), 0, 4, dtype=jnp.int32)
    offsets = jnp.array([-2, -1, 1, 2], dtype=jnp.int32)[step_pick]
    cols_drawn = jnp.clip(rows_all + offsets, 0, GROUP_BLOCKS - 1)
    is_diagonal = (slot_index < BLK_DEV)[None, :]
    return jnp.where(is_diagonal, rows_all, cols_drawn).reshape(-1)


def draw_near_count(key, part):
    key = jax.random.fold_in(key, 3)
    key_base, key_full = jax.random.split(key)
    devices_all = GROUPS * MEMBERS
    device_index = jnp.arange(devices_all, dtype=jnp.int32)
    counts = jax.random.randint(key_base, (devices_all,), BLK_DEV, NEAR_DEV + 1, dtype=jnp.int32)
    chosen = jax.random.randint(key_full, (GROUPS,), 0, MEMBERS, dtype=jnp.int32)
    full_device = device_index % MEMBERS == chosen[device_index // MEMBERS]
    return jnp.where(full_device, NEAR_DEV, counts)


def draw_far_rank(key, part):
    key = jax.random.fold_in(key, 5)
    key_base, key_full = jax.random.split(key)
    devices_all = GROUPS * MEMBERS
    lowest = max(1, RANK // 4)
    ranks = jax.random.randint(key_base, (devices_all, FAR_DEV), lowest, RANK + 1, dtype=jnp.int32)
    chosen = jax.random.randint(key_full, (devices_all, 1), 0, FAR_DEV, dtype=jnp.int32)
    full_slot = jnp.arange(FAR_DEV, dtype=jnp.int32)[None, :] == chosen
    return jnp.where(full_slot, RANK, ranks).reshape(-1)


def draw_leaf_of_elem(key, part):
    key = jax.random.fold_in(key, 7)
    key_send, key_mix = jax.random.split(key)
    devices_all = GROUPS * MEMBERS
    shuffle = jax.vmap(lambda single: jax.random.permutation(single, ELEM_DEV))
    local = shuffle(jax.random.split(key_send, devices_all)).astype(jnp.int32)
    offsets = (jnp.arange(devices_all, dtype=jnp.int32) * ELEM_DEV)[:, None]
    owned = (local + offsets).reshape(GROUPS, MEMBERS, MEMBERS, PER_PEER)
    arriving = jnp.transpose(owned, (0, 2, 1, 3)).reshape(devices_all, ELEM_DEV)
    mixing = shuffle(jax.random.split(key_mix, devices_all)).astype(jnp.int32)
    elem_of_leaf = jnp.take_along_axis(arriving, mixing, axis=1).reshape(-1)
    return jnp.zeros((ELEMS,), jnp.int32).at[elem_of_leaf].set(jnp.arange(ELEMS, dtype=jnp.int32))


def set_ends(drawn, stream_key, low, top_value):
    longest = drawn.shape.index(max(drawn.shape))
    spots = []
    for shift in (0, 1):
        where = [jax.random.randint(jax.random.fold_in(stream_key, axis), (), 0, length) for axis, length in enumerate(drawn.shape)]
        where[longest] = (where[longest] + shift) % drawn.shape[longest]
        spots.append(tuple(where))
    return drawn.at[spots[0]].set(low).at[spots[1]].set(top_value)


def levels(own_key, dims, cuts, low, largest):
    def one(dim, shards_of):
        heights = jax.random.uniform(jax.random.fold_in(jax.random.fold_in(own_key, 6), dim), (shards_of,), jnp.float32, low / len(cuts), largest / len(cuts))
        return jnp.repeat(jnp.exp(heights), dims[dim] // shards_of).reshape((-1,) + (1,) * (len(dims) - dim - 1))

    loudness = one(*cuts[0])
    for cut in cuts[1:]:
        loudness = loudness * one(*cut)
    return loudness


def normal_values(key, shape, width, limit, cuts=(), kind=jnp.bfloat16):
    factor_of = levels(key, shape, cuts, -0.22, 0.18) if cuts else 1.0
    entries = jax.random.normal(key, shape, jnp.float32) * width * factor_of
    return jnp.minimum(jnp.maximum(entries, -limit), limit).astype(kind)


def setup_inputs(seed: int = 0) -> dict:
    streams_of = jax.random.split(jax.random.key(seed), 17)
    ln_rate = jnp.clip(-1.0 + 1.5 * jax.random.uniform(streams_of[0], (ELEMS,), jnp.float32) ** levels(streams_of[0], (ELEMS,), ((0, 32),), -0.2, 0.2), -1.0, 0.5)
    log_state = jnp.clip(jax.random.uniform(streams_of[1], (ELEMS,), jnp.float32, -1.0, 1.0) * levels(streams_of[1], (ELEMS,), ((0, 32),), -0.4, 0.0), -1.0, 1.0)
    sigma = jnp.clip(jnp.exp(math.log(120.0) - 1.0986123 * jax.random.uniform(streams_of[2], (ELEMS,), jnp.float32) ** levels(streams_of[2], (ELEMS,), ((0, 32),), -0.2, 0.2)), 40.0, 120.0)
    fric_a = jnp.clip(jnp.exp(math.log(0.015) - 1.0986123 * jax.random.uniform(streams_of[3], (ELEMS,), jnp.float32) ** levels(streams_of[3], (ELEMS,), ((0, 32),), -0.2, 0.2)), 0.005, 0.015)
    fric_b = jnp.clip(jnp.exp(math.log(0.02) - 1.2039728 * jax.random.uniform(streams_of[4], (ELEMS,), jnp.float32) ** levels(streams_of[4], (ELEMS,), ((0, 32),), -0.2, 0.2)), 0.006, 0.02)
    slip_dist = jnp.clip(jnp.exp(math.log(4.0) - 1.3862944 * jax.random.uniform(streams_of[5], (ELEMS,), jnp.float32) ** levels(streams_of[5], (ELEMS,), ((0, 32),), -0.2, 0.2)), 1.0, 4.0)
    leaf_of_elem = draw_leaf_of_elem(jax.random.fold_in(streams_of[16], 71), 0)
    near_blocks = normal_values(streams_of[7], (DEVICES * NEAR_DEV, LEAF, LEAF), LEAF ** -0.5, 0.25, ((0, 32),))
    near_col = draw_near_col(jax.random.fold_in(streams_of[16], 71), 0)
    near_count = draw_near_count(jax.random.fold_in(streams_of[16], 71), 0)
    far_u = normal_values(streams_of[10], (DEVICES * FAR_DEV, RANK, LEAF), (RANK * FAR_CAP) ** -0.5, 0.75, ((0, 32),))
    far_v = normal_values(streams_of[11], (DEVICES * FAR_DEV, RANK, LEAF), LEAF ** -0.5, 0.25, ((0, 32),))
    far_col = set_ends(jax.random.randint(streams_of[12], (DEVICES * FAR_DEV,), 0, GROUP_BLOCKS), jax.random.fold_in(streams_of[12], 1), 0, GROUP_BLOCKS - 1).astype(jnp.int32)
    far_rank = draw_far_rank(jax.random.fold_in(streams_of[16], 71), 0)
    coarse_u = normal_values(streams_of[14], (GROUPS, RANK, ELEMS), (RANK * GROUPS) ** -0.5, 0.75, ((2, 32),))
    coarse_v = normal_values(streams_of[15], (GROUPS, RANK, ELEMS), GROUP_ROWS ** -0.5, 0.09375, ((2, 32),))
    return {"ln_rate": ln_rate, "log_state": log_state, "sigma": sigma, "fric_a": fric_a, "fric_b": fric_b, "slip_dist": slip_dist, "leaf_of_elem": leaf_of_elem, "near_blocks": near_blocks, "near_col": near_col, "near_count": near_count, "far_u": far_u, "far_v": far_v, "far_col": far_col, "far_rank": far_rank, "coarse_u": coarse_u, "coarse_v": coarse_v}


DAMPING = 0.5
PLATE_RATE = 1.0
TIME_STEP = 0.2


def near_field(blocks, near_blocks, near_col, near_count):
    devices_all = GROUPS * MEMBERS
    slot_index = jnp.arange(devices_all * NEAR_DEV, dtype=jnp.int32)
    slot_owner = slot_index // NEAR_DEV
    slot_group = slot_owner // MEMBERS
    live_slots = (slot_index % NEAR_DEV) < near_count[slot_owner]
    target = slot_owner * BLK_DEV + (slot_index % NEAR_DEV) % BLK_DEV
    source = slot_group * GROUP_BLOCKS + near_col
    vectors = blocks[source].reshape(devices_all, NEAR_DEV, LEAF)
    matrices = near_blocks.reshape(devices_all, NEAR_DEV, LEAF, LEAF)

    def apply_one(pieces):
        return jnp.einsum("sij,sj->si", pieces[0].astype(jnp.float32), pieces[1].astype(jnp.float32))

    products = lax.map(apply_one, (matrices, vectors)).reshape(devices_all * NEAR_DEV, LEAF)
    products = jnp.where(live_slots[:, None], products, 0.0)
    return jax.ops.segment_sum(products, target, num_segments=devices_all * BLK_DEV)


def far_field(blocks, far_u, far_v, far_col, far_rank):
    devices_all = GROUPS * MEMBERS
    slot_index = jnp.arange(devices_all * FAR_DEV, dtype=jnp.int32)
    slot_owner = slot_index // FAR_DEV
    source = (slot_owner // MEMBERS) * GROUP_BLOCKS + far_col
    target = slot_owner * BLK_DEV + (slot_index % FAR_DEV) // FAR_CAP
    project = jnp.einsum("srj,sj->sr", far_v.astype(jnp.float32), blocks[source].astype(jnp.float32))
    kept_ranks = jnp.arange(RANK, dtype=jnp.int32)[None, :] < far_rank[:, None]
    project = jnp.where(kept_ranks, project, 0.0).astype(jnp.bfloat16)
    values = jnp.einsum("sr,srj->sj", project.astype(jnp.float32), far_u.astype(jnp.float32))
    return jax.ops.segment_sum(values, target, num_segments=devices_all * BLK_DEV)


def coarse_field(leaf_deficit, coarse_u, coarse_v):
    grouped = leaf_deficit.reshape(GROUPS, GROUP_ROWS).astype(jnp.float32)

    def coef_one(basis):
        return jnp.einsum("rhq,hq->hr", basis.astype(jnp.float32).reshape(RANK, GROUPS, GROUP_ROWS), grouped)

    coefficients = lax.map(coef_one, coarse_v)
    same = jnp.arange(GROUPS)[:, None] == jnp.arange(GROUPS)[None, :]
    coefficients = jnp.where(same[:, :, None], 0.0, coefficients).astype(jnp.bfloat16)
    row_bases = coarse_u.reshape(GROUPS, RANK, GROUPS, GROUP_ROWS)

    def term_one(group_index):
        basis = lax.dynamic_index_in_dim(row_bases, group_index, axis=2, keepdims=False)
        weights = lax.dynamic_index_in_dim(coefficients, group_index, axis=0, keepdims=False)
        return jnp.einsum("hrp,hr->p", basis.astype(jnp.float32), weights.astype(jnp.float32))

    return lax.map(term_one, jnp.arange(GROUPS, dtype=jnp.int32)).reshape(-1)


def derivatives(ln_now, state_now, sigma, fric_a, fric_b, slip_dist, leaf_of_elem, fields):
    near_blocks, near_col, near_count, far_u, far_v, far_col, far_rank, coarse_u, coarse_v = fields
    velocity = jnp.exp(ln_now)
    deficit = (PLATE_RATE - velocity).astype(jnp.bfloat16)
    leaf_deficit = jnp.zeros((ELEMS,), jnp.bfloat16).at[leaf_of_elem].set(deficit)
    blocks = leaf_deficit.reshape(GROUPS * MEMBERS * BLK_DEV, LEAF)
    local_part = near_field(blocks, near_blocks, near_col, near_count)
    local_part = local_part + far_field(blocks, far_u, far_v, far_col, far_rank)
    load_rate = local_part.reshape(-1) + coarse_field(leaf_deficit, coarse_u, coarse_v)
    stress_rate = load_rate[leaf_of_elem]
    state_rate = (jnp.exp(-state_now) - velocity) / slip_dist
    log_rate = (stress_rate - sigma * fric_b * state_rate) / (sigma * fric_a + DAMPING * velocity)
    return log_rate, state_rate


def reference(ln_rate, log_state, sigma, fric_a, fric_b, slip_dist, leaf_of_elem, near_blocks, near_col, near_count, far_u, far_v, far_col, far_rank, coarse_u, coarse_v):
    fields = (near_blocks, near_col, near_count, far_u, far_v, far_col, far_rank, coarse_u, coarse_v)
    first_ln, first_state = derivatives(ln_rate, log_state, sigma, fric_a, fric_b, slip_dist, leaf_of_elem, fields)
    second_ln, second_state = derivatives(ln_rate + TIME_STEP * first_ln, log_state + TIME_STEP * first_state, sigma, fric_a, fric_b, slip_dist, leaf_of_elem, fields)
    ln_rate_next = ln_rate + 0.5 * TIME_STEP * (first_ln + second_ln)
    log_state_next = log_state + 0.5 * TIME_STEP * (first_state + second_state)
    return ln_rate_next, log_state_next
```

```python
import functools

import jax
import jax.numpy as jnp
from jax import lax
from jax.experimental import pallas as pl
from jax.experimental.pallas import tpu as pltpu
from jax.sharding import PartitionSpec as P

DAMPING = 0.5
PLATE_RATE = 1.0
TIME_STEP = 0.2

NN = (((1,), (0,)), ((), ()))
NT = (((1,), (1,)), ((), ()))
VMEM = pltpu.VMEM
SMEM = pltpu.SMEM


def dot(left, right, dims):
    return lax.dot_general(left, right, dims, preferred_element_type=jnp.float32)


def selection(index_row, count):
    rows = lax.broadcasted_iota(jnp.int32, (count, index_row.shape[1]), 0)
    return jnp.where(rows == index_row, 1.0, 0.0).astype(jnp.bfloat16)


def select_columns(values, matrix, dims):
    high = values.astype(jnp.bfloat16).astype(jnp.float32)
    rest = values - high
    middle = rest.astype(jnp.bfloat16).astype(jnp.float32)
    parts = jnp.concatenate([high, middle, rest - middle], axis=0).astype(jnp.bfloat16)
    moved = dot(parts, matrix, dims)
    return moved[0:8] + moved[8:16] + moved[16:24]


def sort_kernel(members, index_ref, u_ref, phi_ref, sigma_ref, a_ref, b_ref, dist_ref, leaf_ref, sent_ref, slot_ref):
    elem_count = u_ref.shape[1]
    peer_rows = elem_count // members
    local = leaf_ref[...] - index_ref[0] * (members * elem_count)
    target = local // elem_count
    target_row = local - target * elem_count
    onehot = selection(target, members)
    before = lax.broadcasted_iota(jnp.int32, (elem_count, elem_count), 0)
    after = lax.broadcasted_iota(jnp.int32, (elem_count, elem_count), 1)
    earlier = dot(onehot, jnp.where(before < after, 1.0, 0.0).astype(jnp.bfloat16), NN)
    rank = jnp.sum(earlier * onehot.astype(jnp.float32), axis=0, keepdims=True)
    slot = target * peer_rows + rank.astype(jnp.int32)
    slot_ref[...] = slot
    sigma = sigma_ref[...]
    rows = [
        u_ref[...],
        phi_ref[...],
        sigma * a_ref[...],
        sigma * b_ref[...],
        dist_ref[...],
        target_row.astype(jnp.float32),
    ]
    pad = jnp.zeros((8 - len(rows), elem_count), jnp.float32)
    sent = select_columns(jnp.concatenate(rows + [pad], axis=0), selection(slot, elem_count), NT)
    for peer in range(members):
        sent_ref[peer] = sent[:, peer * peer_rows:(peer + 1) * peer_rows]


def outgoing(deficit, coarse_v_ref, out_ref):
    elem_count = deficit.shape[1]
    pieces = elem_count // 128
    wide = jnp.broadcast_to(deficit, (8, elem_count))
    partial = dot(wide.astype(jnp.bfloat16), coarse_v_ref[...], NT)
    out_ref[...] = jnp.zeros(out_ref.shape, jnp.float32)
    for piece in range(pieces):
        out_ref[piece:piece + 1, :] = deficit[:, piece * 128:(piece + 1) * 128]
    width = partial.shape[1]
    for piece in range(pl.cdiv(width, 128)):
        span = min(128, width - piece * 128)
        out_ref[pieces + piece:pieces + piece + 1, 0:span] = partial[0:1, piece * 128:piece * 128 + span]


def place_kernel(members, got_ref, coarse_v_ref, state_ref, rows_ref, out_ref, flat_ref):
    peer_rows = got_ref.shape[2]
    elem_count = members * peer_rows
    for peer in range(members):
        flat_ref[:, peer * peer_rows:(peer + 1) * peer_rows] = got_ref[peer]
    flat = flat_ref[...]
    rows = flat[5:6].astype(jnp.int32)
    rows_ref[...] = rows
    state = select_columns(flat, selection(rows, elem_count), NT)
    state_ref[...] = state
    deficit = (PLATE_RATE - jnp.exp(state[0:1])).astype(jnp.bfloat16).astype(jnp.float32)
    outgoing(deficit, coarse_v_ref, out_ref)


def coef_kernel(groups, rank, pieces, index_ref, got_ref, coef_ref):
    total = jnp.sum(got_ref[...], axis=0)
    coef_ref[...] = jnp.zeros(coef_ref.shape, jnp.float32)
    per_row = 128 // rank
    for group in range(groups):
        row, place = pieces + group // per_row, (group % per_row) * rank
        keep = jnp.where(index_ref[0] == group, 0.0, 1.0)
        coef_ref[group, 0:1, 0:rank] = total[row:row + 1, place:place + rank] * keep


def inside_kernel(
    got_ref, near_ref, far_u_ref, far_v_ref, near_col_ref, near_count_ref, far_col_ref, far_rank_ref, out_ref, flat_ref
):
    members = got_ref.shape[0]
    near_slots, leaf_size = near_ref.shape[0], near_ref.shape[2]
    far_slots, rank = far_col_ref.shape[0], far_u_ref.shape[0] // far_col_ref.shape[0]
    for piece in range(leaf_size // 128):
        flat_ref[:, piece * 128:(piece + 1) * 128] = got_ref[:, piece, :]
    deficits = flat_ref[...]
    block = lax.broadcasted_iota(jnp.int32, (members, leaf_size), 0)
    total = jnp.zeros((members, leaf_size), jnp.float32)
    for slot in range(near_slots):
        column = jnp.where(slot < near_count_ref[0], near_col_ref[slot], -1)
        source = jnp.where(block == column, deficits, 0.0).astype(jnp.bfloat16)
        total = total + dot(source, near_ref[slot], NT)
    project = dot(deficits.astype(jnp.bfloat16), far_v_ref[...], NT)
    block = lax.broadcasted_iota(jnp.int32, project.shape, 0)
    lane = lax.broadcasted_iota(jnp.int32, project.shape, 1)
    column = jnp.full(project.shape, -1, jnp.int32)
    for slot in range(far_slots):
        low = slot * rank
        mine = (lane >= low) & (lane < low + far_rank_ref[slot])
        column = jnp.where(mine, far_col_ref[slot], column)
    project = jnp.sum(jnp.where(block == column, project, 0.0), axis=0, keepdims=True)
    project = jnp.broadcast_to(project, (8, project.shape[1])).astype(jnp.bfloat16)
    far = dot(project, far_u_ref[...], NN)
    out_ref[...] = jnp.sum(total, axis=0, keepdims=True) + far[0:1]


def rates(load, ln_now, state_now, sa, sb, dist):
    velocity = jnp.exp(ln_now)
    state_rate = (jnp.exp(-state_now) - velocity) / dist
    log_rate = (load - sb * state_rate) / (sa + DAMPING * velocity)
    return log_rate, state_rate


def coarse_rows(coef_ref, coarse_u_ref):
    groups, leaf_size = coef_ref.shape[0], coarse_u_ref.shape[1]
    rank = coarse_u_ref.shape[0] // groups
    total = jnp.zeros((8, leaf_size), jnp.float32)
    for group in range(groups):
        weights = coef_ref[group][:, 0:rank].astype(jnp.bfloat16)
        total = total + dot(weights, coarse_u_ref[group * rank:(group + 1) * rank, :], NN)
    return total[0:1]


def first_kernel(state_ref, inside_ref, coef_ref, coarse_u_ref, coarse_v_ref, next_ref, out_ref):
    state = state_ref[...]
    load = inside_ref[...] + coarse_rows(coef_ref, coarse_u_ref)
    u, phi, sa, sb, dist = (state[i:i + 1] for i in range(5))
    k1u, k1p = rates(load, u, phi, sa, sb, dist)
    u2 = u + TIME_STEP * k1u
    phi2 = phi + TIME_STEP * k1p
    deficit = (PLATE_RATE - jnp.exp(u2)).astype(jnp.bfloat16).astype(jnp.float32)
    outgoing(deficit, coarse_v_ref, out_ref)
    next_ref[...] = jnp.concatenate([u2, phi2, k1u, k1p, jnp.zeros((4, u.shape[1]), jnp.float32)], axis=0)


def second_kernel(state_ref, next_ref, rows_ref, inside_ref, coef_ref, coarse_u_ref, sent_ref):
    state = state_ref[...]
    later = next_ref[...]
    load = inside_ref[...] + coarse_rows(coef_ref, coarse_u_ref)
    u, phi, sa, sb, dist = (state[i:i + 1] for i in range(5))
    u2, phi2, k1u, k1p = (later[i:i + 1] for i in range(4))
    k2u, k2p = rates(load, u2, phi2, sa, sb, dist)
    u = u + 0.5 * TIME_STEP * (k1u + k2u)
    phi = phi + 0.5 * TIME_STEP * (k1p + k2p)
    elem_count = u.shape[1]
    values = jnp.concatenate([u, phi, jnp.zeros((6, elem_count), jnp.float32)], axis=0)
    sent = select_columns(values, selection(rows_ref[...], elem_count), NN)
    members = sent_ref.shape[0]
    peer_rows = elem_count // members
    for peer in range(members):
        sent_ref[peer] = sent[:, peer * peer_rows:(peer + 1) * peer_rows]


def unsort_kernel(got_ref, slot_ref, u_ref, phi_ref, flat_ref):
    members, _, peer_rows = got_ref.shape
    for peer in range(members):
        flat_ref[:, peer * peer_rows:(peer + 1) * peer_rows] = got_ref[peer]
    out = select_columns(flat_ref[...], selection(slot_ref[...], members * peer_rows), NN)
    u_ref[...] = out[0:1]
    phi_ref[...] = out[1:2]


def call(kernel, outs, *args, scalars=(), scratch=(), flops=1000, moved=1000):
    specs = [
        pl.BlockSpec(memory_space=SMEM if i in scalars else VMEM) for i in range(len(args))
    ]
    return pl.pallas_call(
        kernel,
        out_shape=outs,
        in_specs=specs,
        out_specs=jax.tree.map(lambda _: pl.BlockSpec(memory_space=VMEM), outs),
        scratch_shapes=list(scratch),
        cost_estimate=pl.CostEstimate(flops=flops, bytes_accessed=moved, transcendentals=0),
        compiler_params=pltpu.CompilerParams(vmem_limit_bytes=32 * 1024 * 1024),
    )(*args)


def shape(*dims, dtype=jnp.float32):
    return jax.ShapeDtypeStruct(dims, dtype)


def body(
    ln_rate,
    log_state,
    sigma,
    fric_a,
    fric_b,
    slip_dist,
    leaf_of_elem,
    near_blocks,
    near_col,
    near_count,
    far_u,
    far_v,
    far_col,
    far_rank,
    coarse_u,
    coarse_v,
):
    members = lax.axis_size("blk")
    group_index = lax.axis_index("leaf").astype(jnp.int32).reshape(1)
    elems = ln_rate.shape[0]
    leaf_size = near_blocks.shape[1]
    groups, rank = coarse_v.shape[0], coarse_v.shape[1]
    peer_rows = elems // members
    pieces = elems // 128
    out_rows = pl.cdiv(pieces + pl.cdiv(groups * rank, 128), 8) * 8
    far_u = far_u.reshape(-1, leaf_size)
    far_v = far_v.reshape(-1, leaf_size)
    coarse_u = coarse_u.reshape(-1, elems)
    coarse_v = coarse_v.reshape(-1, elems)

    def swap(value, axis):
        return lax.all_to_all(value, axis, split_axis=0, concat_axis=0, tiled=True)

    def flat(value):
        return value.reshape(1, elems)

    sent, slot = call(
        functools.partial(sort_kernel, members),
        (shape(members, 8, peer_rows), shape(1, elems, dtype=jnp.int32)),
        group_index, flat(ln_rate), flat(log_state), flat(sigma), flat(fric_a), flat(fric_b),
        flat(slip_dist), flat(leaf_of_elem), scalars=(0,),
    )
    got = swap(sent, "blk")
    state, rows, out = call(
        functools.partial(place_kernel, members),
        (shape(8, elems), shape(1, elems, dtype=jnp.int32), shape(out_rows, 128)),
        got, coarse_v, scratch=[VMEM((8, elems), jnp.float32)],
    )

    def section(out):
        everyone = swap(jnp.broadcast_to(out[None], (members,) + out.shape), "blk")
        coef = call(
            functools.partial(coef_kernel, groups, rank, pieces),
            shape(groups, 8, 128), group_index, everyone, scalars=(0,),
        )
        coef = swap(coef, "leaf")
        inside = call(
            inside_kernel, shape(1, elems),
            everyone, near_blocks, far_u, far_v, near_col, near_count, far_col, far_rank,
            scalars=(4, 5, 6, 7), scratch=[VMEM((members, leaf_size), jnp.float32)],
            flops=2 * members * near_blocks.size, moved=2 * near_blocks.size,
        )
        return coef, inside

    coef, inside = section(out)
    later, out = call(
        first_kernel, (shape(8, elems), shape(out_rows, 128)), state, inside, coef, coarse_u, coarse_v
    )
    coef, inside = section(out)
    sent = call(
        second_kernel, shape(members, 8, peer_rows), state, later, rows, inside, coef, coarse_u
    )
    got = swap(sent, "blk")
    u, phi = call(
        unsort_kernel, (shape(1, elems), shape(1, elems)),
        got, slot, scratch=[VMEM((8, elems), jnp.float32)],
    )
    return u.reshape(elems), phi.reshape(elems)


def solution(mesh):
    each = P(("leaf", "blk"))
    blocks = P(("leaf", "blk"), None, None)
    last = P(None, None, ("leaf", "blk"))
    in_specs = (each,) * 7 + (blocks, each, each, blocks, blocks, each, each, last, last)
    return jax.shard_map(body, mesh=mesh, in_specs=in_specs, out_specs=(each, each), check_vma=False)
```

```python
import functools

import jax
import jax.numpy as jnp
from jax import lax
from jax.experimental import pallas as pl
from jax.experimental.pallas import tpu as pltpu
from jax.sharding import PartitionSpec as P

DAMPING = 0.5
PLATE_RATE = 1.0
TIME_STEP = 0.2

NN = (((1,), (0,)), ((), ()))
NT = (((1,), (1,)), ((), ()))
VMEM = pltpu.VMEM
SMEM = pltpu.SMEM


def dot(left, right, dims):
    return lax.dot_general(left, right, dims, preferred_element_type=jnp.float32)


def selection(index_row, count):
    rows = lax.broadcasted_iota(jnp.int32, (count, index_row.shape[1]), 0)
    return jnp.where(rows == index_row, 1.0, 0.0).astype(jnp.bfloat16)


def select_columns(values, matrix, dims):
    high = values.astype(jnp.bfloat16).astype(jnp.float32)
    rest = values - high
    middle = rest.astype(jnp.bfloat16).astype(jnp.float32)
    parts = jnp.concatenate([high, middle, rest - middle], axis=0).astype(jnp.bfloat16)
    moved = dot(parts, matrix, dims)
    return moved[0:8] + moved[8:16] + moved[16:24]


def sort_kernel(members, index_ref, near_count, *refs):
    elem_refs, weight_refs, scalar_refs = refs[:7], refs[7:12], refs[12:15]
    sent_ref, slot_ref, near_mask_ref, far_mask_ref = refs[15:19]
    weight_outs = refs[19:24]
    elem_bufs, scalar_bufs, sems = refs[24:31], refs[31:34], refs[34]
    sources = elem_refs + scalar_refs + weight_refs
    targets = elem_bufs + scalar_bufs + weight_outs
    copies = [
        pltpu.make_async_copy(source, target, sems.at[i])
        for i, (source, target) in enumerate(zip(sources, targets))
    ]
    for copy in copies:
        copy.start()
    elem_count = elem_bufs[0].shape[1]
    peer_rows = elem_count // members
    before = lax.broadcasted_iota(jnp.int32, (elem_count, elem_count), 0)
    after = lax.broadcasted_iota(jnp.int32, (elem_count, elem_count), 1)
    triangle = jnp.where(before < after, 1.0, 0.0).astype(jnp.bfloat16)
    for copy in copies[:7]:
        copy.wait()
    u, phi, sigma, fric_a, fric_b, dist, leaf = (buf[...] for buf in elem_bufs)
    local = leaf - index_ref[0] * (members * elem_count)
    target = local // elem_count
    target_row = local - target * elem_count
    onehot = selection(target, members)
    earlier = dot(onehot, triangle, NN)
    rank = jnp.sum(earlier * onehot.astype(jnp.float32), axis=0, keepdims=True)
    slot = target * peer_rows + rank.astype(jnp.int32)
    slot_ref[...] = slot
    rows = [u, phi, sigma * fric_a, sigma * fric_b, dist, target_row.astype(jnp.float32)]
    pad = jnp.zeros((8 - len(rows), elem_count), jnp.float32)
    sent = select_columns(jnp.concatenate(rows + [pad], axis=0), selection(slot, elem_count), NT)
    for peer in range(members):
        sent_ref[peer, :, 0:peer_rows] = sent[:, peer * peer_rows:(peer + 1) * peer_rows]
    for copy in copies[7:]:
        copy.wait()
    near_col, far_col, far_rank = scalar_bufs
    near_slots = near_mask_ref.shape[0]
    far_slots = far_col.shape[0]
    far_width = far_mask_ref.shape[1] // far_slots

    def owner(dims):
        shift = lax.broadcasted_iota(jnp.int32, dims, 0)
        block = index_ref[1] - shift
        return jnp.where(block < 0, block + members, block)

    block = owner(near_mask_ref.shape[1:])
    for number in range(near_slots):
        column = jnp.where(number < near_count[0], near_col[number], -1)
        near_mask_ref[number] = jnp.where(block == column, 1.0, 0.0)
    block = owner(far_mask_ref.shape)
    lane = lax.broadcasted_iota(jnp.int32, far_mask_ref.shape, 1)
    column = jnp.full(far_mask_ref.shape, -1, jnp.int32)
    for number in range(far_slots):
        low = number * far_width
        mine = (lane >= low) & (lane < low + far_rank[number])
        column = jnp.where(mine, far_col[number], column)
    far_mask_ref[...] = jnp.where(block == column, 1.0, 0.0)


def outgoing(deficit, coarse_v_ref, out_ref):
    elem_count = deficit.shape[1]
    pieces = elem_count // 128
    wide = jnp.broadcast_to(deficit, (8, elem_count))
    partial = dot(wide.astype(jnp.bfloat16), coarse_v_ref[...], NT)
    out_ref[...] = jnp.zeros(out_ref.shape, jnp.float32)
    for piece in range(pieces):
        out_ref[piece:piece + 1, :] = deficit[:, piece * 128:(piece + 1) * 128]
    width = partial.shape[1]
    for piece in range(pl.cdiv(width, 128)):
        span = min(128, width - piece * 128)
        out_ref[pieces + piece:pieces + piece + 1, 0:span] = partial[0:1, piece * 128:piece * 128 + span]


def place_kernel(members, got_ref, coarse_v_ref, state_ref, rows_ref, out_ref, flat_ref):
    elem_count = state_ref.shape[1]
    peer_rows = elem_count // members
    for peer in range(members):
        flat_ref[:, peer * peer_rows:(peer + 1) * peer_rows] = got_ref[peer, :, 0:peer_rows]
    flat = flat_ref[...]
    rows = flat[5:6].astype(jnp.int32)
    rows_ref[...] = rows
    state = select_columns(flat, selection(rows, elem_count), NT)
    state_ref[...] = state
    deficit = (PLATE_RATE - jnp.exp(state[0:1])).astype(jnp.bfloat16).astype(jnp.float32)
    outgoing(deficit, coarse_v_ref, out_ref)


def coef_kernel(pieces, *refs):
    out_ref = refs[-1]
    total = refs[0][...]
    for ref in refs[1:-1]:
        total = total + ref[...]
    out_ref[...] = total


def inside_kernel(members, *refs):
    got_refs = refs[:members]
    near_ref, far_u_ref, far_v_ref, near_mask_ref, far_mask_ref, out_ref, flat_ref = refs[members:]
    leaf_size = near_ref.shape[2]
    for member in range(members):
        for piece in range(leaf_size // 128):
            span = slice(piece * 128, (piece + 1) * 128)
            flat_ref[member:member + 1, span] = got_refs[member][piece:piece + 1, :]
    deficits = flat_ref[...]
    total = jnp.zeros((members, leaf_size), jnp.float32)
    for slot in range(near_ref.shape[0]):
        source = (deficits * near_mask_ref[slot]).astype(jnp.bfloat16)
        total = total + dot(source, near_ref[slot], NT)
    project = dot(deficits.astype(jnp.bfloat16), far_v_ref[...], NT) * far_mask_ref[...]
    project = jnp.sum(project, axis=0, keepdims=True)
    project = jnp.broadcast_to(project, (8, project.shape[1])).astype(jnp.bfloat16)
    far = dot(project, far_u_ref[...], NN)
    out_ref[...] = jnp.sum(total, axis=0, keepdims=True) + far[0:1]


def rates(load, ln_now, state_now, sa, sb, dist):
    velocity = jnp.exp(ln_now)
    state_rate = (jnp.exp(-state_now) - velocity) / dist
    log_rate = (load - sb * state_rate) / (sa + DAMPING * velocity)
    return log_rate, state_rate


def coarse_rows(index_ref, coef_refs, pieces, coarse_u_ref):
    groups = len(coef_refs) + 1
    width, leaf_size = coarse_u_ref.shape
    rank = width // groups
    lane = lax.broadcasted_iota(jnp.int32, (1, width), 1)
    low = index_ref[0] * rank
    mine = (lane >= low) & (lane < low + rank)
    weights = jnp.zeros((1, width), jnp.float32)
    for shift in range(1, groups):
        got = coef_refs[shift - 1]
        count = pl.cdiv(width, 128)
        row = jnp.concatenate([got[pieces + i:pieces + i + 1, :] for i in range(count)], axis=1)
        row = jnp.where(mine, row[:, 0:width], 0.0)
        twice = jnp.concatenate([row, row], axis=1)
        weights = weights + twice[:, shift * rank:shift * rank + width]
    weights = jnp.broadcast_to(weights, (8, width)).astype(jnp.bfloat16)
    return dot(weights, coarse_u_ref[...], NN)[0:1]


def first_kernel(pieces, index_ref, state_ref, inside_ref, coarse_u_ref, coarse_v_ref, *refs):
    coef_refs, next_ref, out_ref = refs[:-2], refs[-2], refs[-1]
    state = state_ref[...]
    load = inside_ref[...] + coarse_rows(index_ref, coef_refs, pieces, coarse_u_ref)
    u, phi, sa, sb, dist = (state[i:i + 1] for i in range(5))
    k1u, k1p = rates(load, u, phi, sa, sb, dist)
    u2 = u + TIME_STEP * k1u
    phi2 = phi + TIME_STEP * k1p
    deficit = (PLATE_RATE - jnp.exp(u2)).astype(jnp.bfloat16).astype(jnp.float32)
    outgoing(deficit, coarse_v_ref, out_ref)
    next_ref[...] = jnp.concatenate([u2, phi2, k1u, k1p, jnp.zeros((4, u.shape[1]), jnp.float32)], axis=0)


def second_kernel(pieces, index_ref, state_ref, next_ref, rows_ref, inside_ref, coarse_u_ref, *refs):
    coef_refs, sent_ref = refs[:-1], refs[-1]
    state = state_ref[...]
    later = next_ref[...]
    load = inside_ref[...] + coarse_rows(index_ref, coef_refs, pieces, coarse_u_ref)
    u, phi, sa, sb, dist = (state[i:i + 1] for i in range(5))
    u2, phi2, k1u, k1p = (later[i:i + 1] for i in range(4))
    k2u, k2p = rates(load, u2, phi2, sa, sb, dist)
    u = u + 0.5 * TIME_STEP * (k1u + k2u)
    phi = phi + 0.5 * TIME_STEP * (k1p + k2p)
    elem_count = u.shape[1]
    values = jnp.concatenate([u, phi, jnp.zeros((6, elem_count), jnp.float32)], axis=0)
    sent = select_columns(values, selection(rows_ref[...], elem_count), NN)
    members = sent_ref.shape[0]
    peer_rows = elem_count // members
    for peer in range(members):
        sent_ref[peer, :, 0:peer_rows] = sent[:, peer * peer_rows:(peer + 1) * peer_rows]


def unsort_kernel(got_ref, slot_ref, u_ref, phi_ref, flat_ref):
    members, elem_count = got_ref.shape[0], u_ref.shape[1]
    peer_rows = elem_count // members
    for peer in range(members):
        flat_ref[:, peer * peer_rows:(peer + 1) * peer_rows] = got_ref[peer, :, 0:peer_rows]
    out = select_columns(flat_ref[...], selection(slot_ref[...], elem_count), NN)
    u_ref[...] = out[0:1]
    phi_ref[...] = out[1:2]


def call(kernel, outs, *args, scalars=(), far=(), scratch=(), flops=1000, moved=1000):
    spaces = [SMEM if i in scalars else pl.ANY if i in far else VMEM for i in range(len(args))]
    return pl.pallas_call(
        kernel,
        out_shape=outs,
        in_specs=[pl.BlockSpec(memory_space=space) for space in spaces],
        out_specs=jax.tree.map(lambda _: pl.BlockSpec(memory_space=VMEM), outs),
        scratch_shapes=list(scratch),
        cost_estimate=pl.CostEstimate(flops=flops, bytes_accessed=moved, transcendentals=0),
        compiler_params=pltpu.CompilerParams(vmem_limit_bytes=32 * 1024 * 1024),
    )(*[pltpu.with_memory_space_constraint(v, pltpu.HBM) if i in far else v for i, v in enumerate(args)])


def shape(*dims, dtype=jnp.float32):
    return jax.ShapeDtypeStruct(dims, dtype)


def body(
    ln_rate,
    log_state,
    sigma,
    fric_a,
    fric_b,
    slip_dist,
    leaf_of_elem,
    near_blocks,
    near_col,
    near_count,
    far_u,
    far_v,
    far_col,
    far_rank,
    coarse_u,
    coarse_v,
):
    members = lax.axis_size("blk")
    place = jnp.stack([lax.axis_index("leaf"), lax.axis_index("blk")]).astype(jnp.int32)
    elems = ln_rate.shape[0]
    leaf_size = near_blocks.shape[1]
    groups, rank = coarse_v.shape[0], coarse_v.shape[1]
    pieces = elems // 128
    out_rows = pl.cdiv(pieces + pl.cdiv(groups * rank, 128), 8) * 8

    def swap(value):
        return lax.all_to_all(value, "blk", split_axis=0, concat_axis=0, tiled=True)

    def shifted(value, axis):
        count = lax.axis_size(axis)
        moved = [
            lax.ppermute(value, axis, [(i, (i + shift) % count) for i in range(count)])
            for shift in range(1, count)
        ]
        return [value] + moved

    elem_args = [
        value.reshape(1, elems)
        for value in (ln_rate, log_state, sigma, fric_a, fric_b, slip_dist, leaf_of_elem)
    ]
    weights = [near_blocks] + [
        value.reshape(-1, value.shape[2]) for value in (far_u, far_v, coarse_u, coarse_v)
    ]
    scalar_args = [near_col, far_col, far_rank]
    whole = [shape(*value.shape, dtype=value.dtype) for value in weights]
    sent, slot, near_mask, far_mask, near, far_u, far_v, coarse_u, coarse_v = call(
        functools.partial(sort_kernel, members),
        (
            shape(members, 8, 128),
            shape(1, elems, dtype=jnp.int32),
            shape(near_blocks.shape[0], members, leaf_size),
            shape(members, far_u.shape[0] * far_u.shape[1]),
            *whole,
        ),
        place, near_count, *elem_args, *weights, *scalar_args, scalars=(0, 1), far=range(2, 17),
        scratch=[VMEM(value.shape, value.dtype) for value in elem_args]
        + [SMEM(value.shape, value.dtype) for value in scalar_args]
        + [pltpu.SemaphoreType.DMA((15,))],
    )
    got = swap(sent)
    state, rows, out = call(
        functools.partial(place_kernel, members),
        (shape(8, elems), shape(1, elems, dtype=jnp.int32), shape(out_rows, 128)),
        got, coarse_v, scratch=[VMEM((8, elems), jnp.float32)],
    )

    def section(out):
        everyone = shifted(out, "blk")
        total = call(functools.partial(coef_kernel, pieces), shape(out_rows, 128), *everyone)
        coefs = shifted(total, "leaf")[1:]
        inside = call(
            functools.partial(inside_kernel, members), shape(1, elems),
            *everyone, near, far_u, far_v, near_mask, far_mask,
            scratch=[VMEM((members, leaf_size), jnp.float32)],
            flops=2 * members * near.size, moved=2 * near.size,
        )
        return coefs, inside

    coefs, inside = section(out)
    later, out = call(
        functools.partial(first_kernel, pieces), (shape(8, elems), shape(out_rows, 128)),
        place, state, inside, coarse_u, coarse_v, *coefs, scalars=(0,),
    )
    coefs, inside = section(out)
    sent = call(
        functools.partial(second_kernel, pieces), shape(members, 8, 128),
        place, state, later, rows, inside, coarse_u, *coefs, scalars=(0,),
    )
    u, phi = call(
        unsort_kernel, (shape(1, elems), shape(1, elems)),
        swap(sent), slot, scratch=[VMEM((8, elems), jnp.float32)],
    )
    return u.reshape(elems), phi.reshape(elems)


def solution(mesh):
    each = P(("leaf", "blk"))
    blocks = P(("leaf", "blk"), None, None)
    last = P(None, None, ("leaf", "blk"))
    in_specs = (each,) * 7 + (blocks, each, each, blocks, blocks, each, each, last, last)
    return jax.shard_map(body, mesh=mesh, in_specs=in_specs, out_specs=(each, each), check_vma=False)
```

```python
import functools

import jax
import jax.numpy as jnp
from jax import lax
from jax.experimental import pallas as pl
from jax.experimental.pallas import tpu as pltpu
from jax.sharding import PartitionSpec as P

DAMPING = 0.5
PLATE_RATE = 1.0
TIME_STEP = 0.2

NN = (((1,), (0,)), ((), ()))
NT = (((1,), (1,)), ((), ()))
VMEM = pltpu.VMEM
SMEM = pltpu.SMEM


def dot(left, right, dims):
    return lax.dot_general(left, right, dims, preferred_element_type=jnp.float32)


def selection(index_row, count):
    rows = lax.broadcasted_iota(jnp.int32, (count, index_row.shape[1]), 0)
    return jnp.where(rows == index_row, 1.0, 0.0).astype(jnp.bfloat16)


def select_columns(values, matrix, dims):
    high = values.astype(jnp.bfloat16).astype(jnp.float32)
    rest = values - high
    middle = rest.astype(jnp.bfloat16).astype(jnp.float32)
    parts = jnp.concatenate([high, middle, rest - middle], axis=0).astype(jnp.bfloat16)
    moved = dot(parts, matrix, dims)
    return moved[0:8] + moved[8:16] + moved[16:24]


def merged(held, came, width, bit):
    block = lax.broadcasted_iota(jnp.int32, held.shape, 1) // width
    return jnp.where((block >> bit) & 1 == 1, came, held)


def merge_kernel(width, bit, held_ref, came_ref, out_ref):
    out_ref[...] = merged(held_ref[...], came_ref[...], width, bit)


def stack_kernel(held_ref, came_ref, out_ref):
    count = held_ref.shape[0]
    out_ref[0:count, :] = held_ref[...]
    out_ref[count:2 * count, :] = came_ref[...]


def start_copies(sources, targets, sems):
    copies = [
        pltpu.make_async_copy(source, target, sems.at[i])
        for i, (source, target) in enumerate(zip(sources, targets))
    ]
    for copy in copies:
        copy.start()
    return copies


def sort_kernel(members, index_ref, *refs):
    elem_refs, sent_ref, slot_ref, bufs, sems = refs[:7], refs[7], refs[8], refs[9:16], refs[16]
    copies = start_copies(elem_refs, bufs, sems)
    elem_count = bufs[0].shape[1]
    peer_rows = elem_count // members
    before = lax.broadcasted_iota(jnp.int32, (elem_count, elem_count), 0)
    after = lax.broadcasted_iota(jnp.int32, (elem_count, elem_count), 1)
    triangle = jnp.where(before < after, 1.0, 0.0).astype(jnp.bfloat16)
    for copy in copies:
        copy.wait()
    u, phi, sigma, fric_a, fric_b, dist, leaf = (buf[...] for buf in bufs)
    local = leaf - index_ref[0] * (members * elem_count)
    target = local // elem_count
    target_row = local - target * elem_count
    onehot = selection(target, members)
    earlier = dot(onehot, triangle, NN)
    rank = jnp.sum(earlier * onehot.astype(jnp.float32), axis=0, keepdims=True)
    slot = (target ^ index_ref[1]) * peer_rows + rank.astype(jnp.int32)
    slot_ref[...] = slot
    rows = [u, phi, sigma * fric_a, sigma * fric_b, dist, target_row.astype(jnp.float32)]
    pad = jnp.zeros((8 - len(rows), elem_count), jnp.float32)
    values = jnp.concatenate(rows + [pad], axis=0)
    sent_ref[...] = select_columns(values, selection(slot, elem_count), NT)


def load_kernel(members, index_ref, near_count, *refs):
    near_ref, far_u_ref, far_v_ref, coarse_u_ref, coarse_v_ref = refs[:5]
    scalar_refs, outs, scalar_bufs, sems = refs[5:8], refs[8:15], refs[15:18], refs[18]
    near_mask_ref, far_mask_ref, near_out, far_u_out, far_v_out, coarse_u_out, coarse_v_out = outs
    groups, rank = coarse_u_ref.shape[0], coarse_u_ref.shape[1]
    sources = [*scalar_refs, near_ref, far_u_ref, far_v_ref]
    targets = [*scalar_bufs, near_out, far_u_out, far_v_out]
    for shift in range(groups):
        group = index_ref[0] ^ shift
        span = pl.ds(shift * rank, rank)
        sources += [coarse_u_ref.at[group], coarse_v_ref.at[group]]
        targets += [coarse_u_out.at[span, :], coarse_v_out.at[span, :]]
    copies = start_copies(sources, targets, sems)
    for copy in copies[:3]:
        copy.wait()
    near_col, far_col, far_rank = scalar_bufs
    far_slots = far_col.shape[0]
    far_width = far_mask_ref.shape[1] // far_slots
    block = lax.broadcasted_iota(jnp.int32, near_mask_ref.shape[1:], 0) ^ index_ref[1]
    for number in range(near_mask_ref.shape[0]):
        column = jnp.where(number < near_count[0], near_col[number], -1)
        near_mask_ref[number] = jnp.where(block == column, 1.0, 0.0)
    block = lax.broadcasted_iota(jnp.int32, far_mask_ref.shape, 0) ^ index_ref[1]
    lane = lax.broadcasted_iota(jnp.int32, far_mask_ref.shape, 1)
    column = jnp.full(far_mask_ref.shape, -1, jnp.int32)
    for number in range(far_slots):
        low = number * far_width
        mine = (lane >= low) & (lane < low + far_rank[number])
        column = jnp.where(mine, far_col[number], column)
    far_mask_ref[...] = jnp.where(block == column, 1.0, 0.0)
    for copy in copies[3:]:
        copy.wait()


def outgoing(deficit, coarse_v_ref, out_ref):
    elem_count = deficit.shape[1]
    wide = jnp.broadcast_to(deficit, (8, elem_count)).astype(jnp.bfloat16)
    partial = dot(wide, coarse_v_ref[...], NT)[0:1]
    width = partial.shape[1]
    out_ref[:, 0:elem_count] = deficit
    if elem_count + width < out_ref.shape[1]:
        out_ref[:, elem_count + width:] = jnp.zeros((1, out_ref.shape[1] - elem_count - width), jnp.float32)
    out_ref[:, elem_count:elem_count + width] = partial


def place_kernel(members, bit, held_ref, came_ref, coarse_v_ref, state_ref, rows_ref, out_ref):
    elem_count = held_ref.shape[1]
    flat = merged(held_ref[...], came_ref[...], elem_count // members, bit)
    rows = flat[5:6].astype(jnp.int32)
    rows_ref[...] = rows
    state = select_columns(flat, selection(rows, elem_count), NT)
    state_ref[...] = state
    deficit = (PLATE_RATE - jnp.exp(state[0:1])).astype(jnp.bfloat16).astype(jnp.float32)
    outgoing(deficit, coarse_v_ref, out_ref)


def gather_kernel(held_ref, came_ref, all_ref, total_ref):
    stack_kernel(held_ref, came_ref, all_ref)
    low = all_ref.shape[1] - total_ref.shape[1]
    total_ref[...] = jnp.sum(all_ref[:, low:], axis=0, keepdims=True)


def inside_kernel(all_ref, near_ref, far_u_ref, far_v_ref, near_mask_ref, far_mask_ref, out_ref):
    leaf_size = near_ref.shape[2]
    deficits = all_ref[:, 0:leaf_size]
    total = jnp.zeros(deficits.shape, jnp.float32)
    for slot in range(near_ref.shape[0]):
        source = (deficits * near_mask_ref[slot]).astype(jnp.bfloat16)
        total = total + dot(source, near_ref[slot], NT)
    project = dot(deficits.astype(jnp.bfloat16), far_v_ref[...], NT) * far_mask_ref[...]
    project = jnp.sum(project, axis=0, keepdims=True)
    project = jnp.broadcast_to(project, (8, project.shape[1])).astype(jnp.bfloat16)
    far = dot(project, far_u_ref[...], NN)
    out_ref[...] = jnp.sum(total, axis=0, keepdims=True) + far[0:1]


def rates(load, ln_now, state_now, sa, sb, dist):
    velocity = jnp.exp(ln_now)
    state_rate = (jnp.exp(-state_now) - velocity) / dist
    log_rate = (load - sb * state_rate) / (sa + DAMPING * velocity)
    return log_rate, state_rate


def coarse_rows(rank, bit, held_ref, came_ref, coarse_u_ref):
    width = coarse_u_ref.shape[0]
    weights = merged(held_ref[...], came_ref[...], rank, bit)[:, 0:width]
    lane = lax.broadcasted_iota(jnp.int32, weights.shape, 1)
    weights = jnp.where(lane >= rank, weights, 0.0)
    weights = jnp.broadcast_to(weights, (8, width)).astype(jnp.bfloat16)
    return dot(weights, coarse_u_ref[...], NN)[0:1]


def first_kernel(rank, bit, state_ref, inside_ref, held_ref, came_ref, coarse_u_ref, coarse_v_ref, next_ref, out_ref):
    state = state_ref[...]
    load = inside_ref[...] + coarse_rows(rank, bit, held_ref, came_ref, coarse_u_ref)
    u, phi, sa, sb, dist = (state[i:i + 1] for i in range(5))
    k1u, k1p = rates(load, u, phi, sa, sb, dist)
    u2 = u + TIME_STEP * k1u
    phi2 = phi + TIME_STEP * k1p
    deficit = (PLATE_RATE - jnp.exp(u2)).astype(jnp.bfloat16).astype(jnp.float32)
    outgoing(deficit, coarse_v_ref, out_ref)
    next_ref[...] = jnp.concatenate([u2, phi2, k1u, k1p, jnp.zeros((4, u.shape[1]), jnp.float32)], axis=0)


def second_kernel(rank, bit, state_ref, next_ref, rows_ref, inside_ref, held_ref, came_ref, coarse_u_ref, sent_ref):
    state = state_ref[...]
    later = next_ref[...]
    load = inside_ref[...] + coarse_rows(rank, bit, held_ref, came_ref, coarse_u_ref)
    u, phi, sa, sb, dist = (state[i:i + 1] for i in range(5))
    u2, phi2, k1u, k1p = (later[i:i + 1] for i in range(4))
    k2u, k2p = rates(load, u2, phi2, sa, sb, dist)
    u = u + 0.5 * TIME_STEP * (k1u + k2u)
    phi = phi + 0.5 * TIME_STEP * (k1p + k2p)
    elem_count = u.shape[1]
    values = jnp.concatenate([u, phi, jnp.zeros((6, elem_count), jnp.float32)], axis=0)
    sent_ref[...] = select_columns(values, selection(rows_ref[...], elem_count), NN)[0:2]


def unsort_kernel(members, bit, held_ref, came_ref, slot_ref, u_ref, phi_ref):
    elem_count = held_ref.shape[1]
    flat = merged(held_ref[...], came_ref[...], elem_count // members, bit)
    flat = jnp.concatenate([flat, jnp.zeros((6, elem_count), jnp.float32)], axis=0)
    out = select_columns(flat, selection(slot_ref[...], elem_count), NN)
    u_ref[...] = out[0:1]
    phi_ref[...] = out[1:2]


def call(kernel, outs, *args, scalars=(), far=(), scratch=(), flops=1000, moved=1000):
    spaces = [SMEM if i in scalars else pl.ANY if i in far else VMEM for i in range(len(args))]
    args = [
        pltpu.with_memory_space_constraint(arg, pltpu.HBM) if i in far else arg
        for i, arg in enumerate(args)
    ]
    return pl.pallas_call(
        kernel,
        out_shape=outs,
        in_specs=[pl.BlockSpec(memory_space=space) for space in spaces],
        out_specs=jax.tree.map(lambda _: pl.BlockSpec(memory_space=VMEM), outs),
        scratch_shapes=list(scratch),
        cost_estimate=pl.CostEstimate(flops=flops, bytes_accessed=moved, transcendentals=0),
        compiler_params=pltpu.CompilerParams(vmem_limit_bytes=32 * 1024 * 1024),
    )(*args)


def shape(*dims, dtype=jnp.float32):
    return jax.ShapeDtypeStruct(dims, dtype)


def body(
    ln_rate,
    log_state,
    sigma,
    fric_a,
    fric_b,
    slip_dist,
    leaf_of_elem,
    near_blocks,
    near_col,
    near_count,
    far_u,
    far_v,
    far_col,
    far_rank,
    coarse_u,
    coarse_v,
):
    members = lax.axis_size("blk")
    place = jnp.stack([lax.axis_index("leaf"), lax.axis_index("blk")]).astype(jnp.int32)
    elems = ln_rate.shape[0]
    leaf_size = near_blocks.shape[1]
    groups, rank = coarse_v.shape[0], coarse_v.shape[1]
    width = pl.cdiv(groups * rank, 128) * 128
    block_bits = range(members.bit_length() - 1)
    group_bits = range(groups.bit_length() - 1)

    def partner(value, axis, bit):
        count = lax.axis_size(axis)
        return lax.ppermute(value, axis, [(i, i ^ (1 << bit)) for i in range(count)])

    def trade(value, axis, bits, lanes):
        for bit in bits[:-1]:
            came = partner(value, axis, bit)
            value = call(
                functools.partial(merge_kernel, lanes, bit), shape(*value.shape), value, came
            )
        return value, partner(value, axis, bits[-1])

    elem_args = [
        value.reshape(1, elems)
        for value in (ln_rate, log_state, sigma, fric_a, fric_b, slip_dist, leaf_of_elem)
    ]
    sent, slot = call(
        functools.partial(sort_kernel, members),
        (shape(8, elems), shape(1, elems, dtype=jnp.int32)),
        place, *elem_args, scalars=(0,), far=range(1, 8),
        scratch=[VMEM(value.shape, value.dtype) for value in elem_args]
        + [pltpu.SemaphoreType.DMA((7,))],
    )
    weights = [
        near_blocks, far_u.reshape(-1, leaf_size), far_v.reshape(-1, leaf_size), coarse_u, coarse_v
    ]
    scalar_args = [near_col, far_col, far_rank]
    far_rows = weights[1].shape[0]
    near_mask, far_mask, near, far_u, far_v, coarse_u, coarse_v = call(
        functools.partial(load_kernel, members),
        (
            shape(near_blocks.shape[0], members, leaf_size),
            shape(members, far_rows),
            shape(*near_blocks.shape, dtype=jnp.bfloat16),
            shape(far_rows, leaf_size, dtype=jnp.bfloat16),
            shape(far_rows, leaf_size, dtype=jnp.bfloat16),
            shape(groups * rank, elems, dtype=jnp.bfloat16),
            shape(groups * rank, elems, dtype=jnp.bfloat16),
        ),
        place, near_count, *weights, *scalar_args, scalars=(0, 1), far=range(2, 10),
        scratch=[SMEM(value.shape, value.dtype) for value in scalar_args]
        + [pltpu.SemaphoreType.DMA((6 + 2 * groups,))],
        flops=2 * near_blocks.size, moved=2 * near_blocks.size * 2,
    )
    held, came = trade(sent, "blk", block_bits, elems // members)
    state, rows, out = call(
        functools.partial(place_kernel, members, block_bits[-1]),
        (shape(8, elems), shape(1, elems, dtype=jnp.int32), shape(1, elems + width)),
        held, came, coarse_v,
    )

    def section(out):
        for bit in block_bits[:-1]:
            out = call(
                stack_kernel, shape(2 * out.shape[0], out.shape[1]), out, partner(out, "blk", bit)
            )
        everyone, total = call(
            gather_kernel, (shape(members, elems + width), shape(1, width)),
            out, partner(out, "blk", block_bits[-1]),
        )
        coefs = trade(total, "leaf", group_bits, rank)
        inside = call(
            inside_kernel, shape(1, elems), everyone, near, far_u, far_v, near_mask, far_mask,
            flops=2 * members * near.size, moved=2 * near.size,
        )
        return coefs, inside

    coefs, inside = section(out)
    later, out = call(
        functools.partial(first_kernel, rank, group_bits[-1]),
        (shape(8, elems), shape(1, elems + width)),
        state, inside, *coefs, coarse_u, coarse_v,
    )
    coefs, inside = section(out)
    sent = call(
        functools.partial(second_kernel, rank, group_bits[-1]), shape(2, elems),
        state, later, rows, inside, *coefs, coarse_u,
    )
    held, came = trade(sent, "blk", block_bits, elems // members)
    u, phi = call(
        functools.partial(unsort_kernel, members, block_bits[-1]),
        (shape(1, elems), shape(1, elems)),
        held, came, slot,
    )
    return u.reshape(elems), phi.reshape(elems)


def solution(mesh):
    each = P(("leaf", "blk"))
    blocks = P(("leaf", "blk"), None, None)
    last = P(None, None, ("leaf", "blk"))
    in_specs = (each,) * 7 + (blocks, each, each, blocks, blocks, each, each, last, last)
    return jax.shard_map(body, mesh=mesh, in_specs=in_specs, out_specs=(each, each), check_vma=False)
```

```python
import functools

import jax
import jax.numpy as jnp
from jax import lax
from jax.experimental import pallas as pl
from jax.experimental.pallas import tpu as pltpu
from jax.sharding import PartitionSpec as P

DAMPING = 0.5
PLATE_RATE = 1.0
TIME_STEP = 0.2

NN = (((1,), (0,)), ((), ()))
NT = (((1,), (1,)), ((), ()))
VMEM = pltpu.VMEM
SMEM = pltpu.SMEM


def dot(left, right, dims):
    return lax.dot_general(left, right, dims, preferred_element_type=jnp.float32)


def selection(index_row, count):
    rows = lax.broadcasted_iota(jnp.int32, (count, index_row.shape[1]), 0)
    return jnp.where(rows == index_row, 1.0, 0.0).astype(jnp.bfloat16)


def select_columns(values, matrix, dims):
    high = values.astype(jnp.bfloat16).astype(jnp.float32)
    rest = values - high
    middle = rest.astype(jnp.bfloat16).astype(jnp.float32)
    parts = jnp.concatenate([high, middle, rest - middle], axis=0).astype(jnp.bfloat16)
    moved = dot(parts, matrix, dims)
    return moved[0:8] + moved[8:16] + moved[16:24]


def spread(flat, sent_ref):
    members = sent_ref.shape[0]
    peer_rows = flat.shape[1] // members
    for peer in range(members):
        sent_ref[peer, :, 0:peer_rows] = flat[:, peer * peer_rows:(peer + 1) * peer_rows]


def flattened(got_ref, elem_count):
    members = got_ref.shape[0]
    peer_rows = elem_count // members
    return jnp.concatenate([got_ref[peer, :, 0:peer_rows] for peer in range(members)], axis=1)


def start_copies(sources, targets, sems):
    copies = [
        pltpu.make_async_copy(source, target, sems.at[i])
        for i, (source, target) in enumerate(zip(sources, targets))
    ]
    for copy in copies:
        copy.start()
    return copies


def sort_kernel(members, index_ref, *refs):
    elem_refs, sent_ref, slot_ref, bufs, sems = refs[:7], refs[7], refs[8], refs[9:16], refs[16]
    copies = start_copies(elem_refs, bufs, sems)
    elem_count = bufs[0].shape[1]
    peer_rows = elem_count // members
    before = lax.broadcasted_iota(jnp.int32, (elem_count, elem_count), 0)
    after = lax.broadcasted_iota(jnp.int32, (elem_count, elem_count), 1)
    triangle = jnp.where(before < after, 1.0, 0.0).astype(jnp.bfloat16)
    for copy in copies:
        copy.wait()
    u, phi, sigma, fric_a, fric_b, dist, leaf = (buf[...] for buf in bufs)
    local = leaf - index_ref[0] * (members * elem_count)
    target = local // elem_count
    target_row = local - target * elem_count
    onehot = selection(target, members)
    earlier = dot(onehot, triangle, NN)
    rank = jnp.sum(earlier * onehot.astype(jnp.float32), axis=0, keepdims=True)
    slot = target * peer_rows + rank.astype(jnp.int32)
    slot_ref[...] = slot
    rows = [u, phi, sigma * fric_a, sigma * fric_b, dist, target_row.astype(jnp.float32)]
    pad = jnp.zeros((8 - len(rows), elem_count), jnp.float32)
    values = jnp.concatenate(rows + [pad], axis=0)
    spread(select_columns(values, selection(slot, elem_count), NT), sent_ref)


def load_kernel(index_ref, near_count, *refs):
    near_ref, far_u_ref, far_v_ref, coarse_u_ref, coarse_v_ref = refs[:5]
    scalar_refs, outs, scalar_bufs, sems = refs[5:8], refs[8:15], refs[15:18], refs[18]
    near_mask_ref, far_mask_ref, near_out, far_u_out, far_v_out, coarse_u_out, coarse_v_out = outs
    groups, rank = coarse_u_ref.shape[0], coarse_u_ref.shape[1]
    sources = [*scalar_refs, near_ref, far_u_ref, far_v_ref]
    targets = [*scalar_bufs, near_out, far_u_out, far_v_out]
    for shift in range(groups):
        group = index_ref[0] ^ shift
        span = pl.ds(shift * rank, rank)
        sources += [coarse_u_ref.at[group], coarse_v_ref.at[group]]
        targets += [coarse_u_out.at[span, :], coarse_v_out.at[span, :]]
    copies = start_copies(sources, targets, sems)
    for copy in copies[:3]:
        copy.wait()
    near_col, far_col, far_rank = scalar_bufs
    far_slots = far_col.shape[0]
    far_width = far_mask_ref.shape[1] // far_slots
    block = lax.broadcasted_iota(jnp.int32, near_mask_ref.shape[1:], 0)
    for number in range(near_mask_ref.shape[0]):
        column = jnp.where(number < near_count[0], near_col[number], -1)
        near_mask_ref[number] = jnp.where(block == column, 1.0, 0.0)
    block = lax.broadcasted_iota(jnp.int32, far_mask_ref.shape, 0)
    lane = lax.broadcasted_iota(jnp.int32, far_mask_ref.shape, 1)
    column = jnp.full(far_mask_ref.shape, -1, jnp.int32)
    for number in range(far_slots):
        low = number * far_width
        mine = (lane >= low) & (lane < low + far_rank[number])
        column = jnp.where(mine, far_col[number], column)
    far_mask_ref[...] = jnp.where(block == column, 1.0, 0.0)
    for copy in copies[3:]:
        copy.wait()


def outgoing(deficit, coarse_v_ref, out_ref):
    elem_count = deficit.shape[1]
    wide = jnp.broadcast_to(deficit, (8, elem_count)).astype(jnp.bfloat16)
    partial = dot(wide, coarse_v_ref[...], NT)[0:1]
    pieces = [deficit, partial]
    rest = out_ref.shape[2] - elem_count - partial.shape[1]
    if rest:
        pieces.append(jnp.zeros((1, rest), jnp.float32))
    out_ref[...] = jnp.broadcast_to(jnp.concatenate(pieces, axis=1)[None], out_ref.shape)


def place_kernel(got_ref, coarse_v_ref, state_ref, rows_ref, out_ref):
    elem_count = state_ref.shape[1]
    flat = flattened(got_ref, elem_count)
    rows = flat[5:6].astype(jnp.int32)
    rows_ref[...] = rows
    state = select_columns(flat, selection(rows, elem_count), NT)
    state_ref[...] = state
    deficit = (PLATE_RATE - jnp.exp(state[0:1])).astype(jnp.bfloat16).astype(jnp.float32)
    outgoing(deficit, coarse_v_ref, out_ref)


def load_rows(
    index_ref, all_ref, near_ref, far_u_ref, far_v_ref, near_mask_ref, far_mask_ref, coarse_u_ref, groups
):
    members, leaf_size = near_mask_ref.shape[1], near_ref.shape[2]
    coarse_width = coarse_u_ref.shape[0]
    rank = coarse_width // groups
    mine = index_ref[0]
    deficits = all_ref[pl.ds(mine * members, members), 0, 0:leaf_size]
    total = jnp.zeros(deficits.shape, jnp.float32)
    for slot in range(near_ref.shape[0]):
        source = (deficits * near_mask_ref[slot]).astype(jnp.bfloat16)
        total = total + dot(source, near_ref[slot], NT)
    project = dot(deficits.astype(jnp.bfloat16), far_v_ref[...], NT) * far_mask_ref[...]
    project = jnp.sum(project, axis=0, keepdims=True)
    project = jnp.broadcast_to(project, (8, project.shape[1])).astype(jnp.bfloat16)
    far = dot(project, far_u_ref[...], NN)
    lane = lax.broadcasted_iota(jnp.int32, (members, coarse_width), 1)
    weights = jnp.zeros((members, coarse_width), jnp.float32)
    for shift in range(1, groups):
        start = (mine ^ shift) * members
        part = all_ref[pl.ds(start, members), 0, leaf_size:leaf_size + coarse_width]
        weights = jnp.where(lane // rank == shift, part, weights)
    weights = jnp.sum(weights, axis=0, keepdims=True)
    weights = jnp.broadcast_to(weights, (8, coarse_width)).astype(jnp.bfloat16)
    coarse = dot(weights, coarse_u_ref[...], NN)
    return jnp.sum(total, axis=0, keepdims=True) + far[0:1] + coarse[0:1]


def rates(load, ln_now, state_now, sa, sb, dist):
    velocity = jnp.exp(ln_now)
    state_rate = (jnp.exp(-state_now) - velocity) / dist
    log_rate = (load - sb * state_rate) / (sa + DAMPING * velocity)
    return log_rate, state_rate


def first_kernel(groups, index_ref, state_ref, coarse_v_ref, *refs):
    field_refs, next_ref, out_ref = refs[:-2], refs[-2], refs[-1]
    state = state_ref[...]
    load = load_rows(index_ref, *field_refs, groups)
    u, phi, sa, sb, dist = (state[i:i + 1] for i in range(5))
    k1u, k1p = rates(load, u, phi, sa, sb, dist)
    u2 = u + TIME_STEP * k1u
    phi2 = phi + TIME_STEP * k1p
    deficit = (PLATE_RATE - jnp.exp(u2)).astype(jnp.bfloat16).astype(jnp.float32)
    outgoing(deficit, coarse_v_ref, out_ref)
    next_ref[...] = jnp.concatenate([u2, phi2, k1u, k1p, jnp.zeros((4, u.shape[1]), jnp.float32)], axis=0)


def second_kernel(groups, index_ref, state_ref, next_ref, rows_ref, *refs):
    field_refs, sent_ref = refs[:-1], refs[-1]
    state = state_ref[...]
    later = next_ref[...]
    load = load_rows(index_ref, *field_refs, groups)
    u, phi, sa, sb, dist = (state[i:i + 1] for i in range(5))
    u2, phi2, k1u, k1p = (later[i:i + 1] for i in range(4))
    k2u, k2p = rates(load, u2, phi2, sa, sb, dist)
    u = u + 0.5 * TIME_STEP * (k1u + k2u)
    phi = phi + 0.5 * TIME_STEP * (k1p + k2p)
    elem_count = u.shape[1]
    values = jnp.concatenate([u, phi, jnp.zeros((6, elem_count), jnp.float32)], axis=0)
    spread(select_columns(values, selection(rows_ref[...], elem_count), NN)[0:2], sent_ref)


def unsort_kernel(got_ref, slot_ref, u_ref, phi_ref):
    elem_count = slot_ref.shape[1]
    flat = flattened(got_ref, elem_count)
    flat = jnp.concatenate([flat, jnp.zeros((6, elem_count), jnp.float32)], axis=0)
    out = select_columns(flat, selection(slot_ref[...], elem_count), NN)
    u_ref[...] = out[0:1]
    phi_ref[...] = out[1:2]


def call(kernel, outs, *args, scalars=(), far=(), scratch=(), flops=1000, moved=1000):
    spaces = [SMEM if i in scalars else pl.ANY if i in far else VMEM for i in range(len(args))]
    args = [
        pltpu.with_memory_space_constraint(arg, pltpu.HBM) if i in far else arg
        for i, arg in enumerate(args)
    ]
    return pl.pallas_call(
        kernel,
        out_shape=outs,
        in_specs=[pl.BlockSpec(memory_space=space) for space in spaces],
        out_specs=jax.tree.map(lambda _: pl.BlockSpec(memory_space=VMEM), outs),
        scratch_shapes=list(scratch),
        cost_estimate=pl.CostEstimate(flops=flops, bytes_accessed=moved, transcendentals=0),
        compiler_params=pltpu.CompilerParams(vmem_limit_bytes=32 * 1024 * 1024),
    )(*args)


def shape(*dims, dtype=jnp.float32):
    return jax.ShapeDtypeStruct(dims, dtype)


def body(
    ln_rate,
    log_state,
    sigma,
    fric_a,
    fric_b,
    slip_dist,
    leaf_of_elem,
    near_blocks,
    near_col,
    near_count,
    far_u,
    far_v,
    far_col,
    far_rank,
    coarse_u,
    coarse_v,
):
    members = lax.axis_size("blk")
    place = jnp.stack([lax.axis_index("leaf"), lax.axis_index("blk")]).astype(jnp.int32)
    elems = ln_rate.shape[0]
    leaf_size = near_blocks.shape[1]
    groups, rank = coarse_v.shape[0], coarse_v.shape[1]
    width = pl.cdiv(groups * rank, 128) * 128
    devices = groups * members

    def swap(value, axes):
        return lax.all_to_all(value, axes, split_axis=0, concat_axis=0, tiled=True)

    elem_args = [
        value.reshape(1, elems)
        for value in (ln_rate, log_state, sigma, fric_a, fric_b, slip_dist, leaf_of_elem)
    ]
    sent, slot = call(
        functools.partial(sort_kernel, members),
        (shape(members, 8, 128), shape(1, elems, dtype=jnp.int32)),
        place, *elem_args, scalars=(0,), far=range(1, 8),
        scratch=[VMEM(value.shape, value.dtype) for value in elem_args]
        + [pltpu.SemaphoreType.DMA((7,))],
    )
    weights = [
        near_blocks, far_u.reshape(-1, leaf_size), far_v.reshape(-1, leaf_size), coarse_u, coarse_v
    ]
    scalar_args = [near_col, far_col, far_rank]
    far_rows = weights[1].shape[0]
    near_mask, far_mask, near, far_u, far_v, coarse_u, coarse_v = call(
        load_kernel,
        (
            shape(near_blocks.shape[0], members, leaf_size),
            shape(members, far_rows),
            shape(*near_blocks.shape, dtype=jnp.bfloat16),
            shape(far_rows, leaf_size, dtype=jnp.bfloat16),
            shape(far_rows, leaf_size, dtype=jnp.bfloat16),
            shape(groups * rank, elems, dtype=jnp.bfloat16),
            shape(groups * rank, elems, dtype=jnp.bfloat16),
        ),
        place, near_count, *weights, *scalar_args, scalars=(0, 1), far=range(2, 10),
        scratch=[SMEM(value.shape, value.dtype) for value in scalar_args]
        + [pltpu.SemaphoreType.DMA((6 + 2 * groups,))],
        flops=2 * near_blocks.size, moved=2 * near_blocks.size * 2,
    )
    state, rows, out = call(
        place_kernel,
        (shape(8, elems), shape(1, elems, dtype=jnp.int32), shape(devices, 1, elems + width)),
        swap(sent, "blk"), coarse_v,
    )
    fields = near, far_u, far_v, near_mask, far_mask, coarse_u

    def share(out):
        return swap(out, ("leaf", "blk"))

    later, out = call(
        functools.partial(first_kernel, groups), (shape(8, elems), shape(devices, 1, elems + width)),
        place, state, coarse_v, share(out), *fields, scalars=(0,),
    )
    sent = call(
        functools.partial(second_kernel, groups), shape(members, 2, 128),
        place, state, later, rows, share(out), *fields, scalars=(0,),
    )
    u, phi = call(
        unsort_kernel, (shape(1, elems), shape(1, elems)), swap(sent, "blk"), slot
    )
    return u.reshape(elems), phi.reshape(elems)


def solution(mesh):
    each = P(("leaf", "blk"))
    blocks = P(("leaf", "blk"), None, None)
    last = P(None, None, ("leaf", "blk"))
    in_specs = (each,) * 7 + (blocks, each, each, blocks, blocks, each, each, last, last)
    return jax.shard_map(body, mesh=mesh, in_specs=in_specs, out_specs=(each, each), check_vma=False)
```

```python
import functools

import jax
import jax.numpy as jnp
from jax import lax
from jax.experimental import pallas as pl
from jax.experimental.pallas import tpu as pltpu
from jax.sharding import PartitionSpec as P

DAMPING = 0.5
PLATE_RATE = 1.0
TIME_STEP = 0.2

NN = (((1,), (0,)), ((), ()))
NT = (((1,), (1,)), ((), ()))
VMEM = pltpu.VMEM
SMEM = pltpu.SMEM


def dot(left, right, dims):
    return lax.dot_general(left, right, dims, preferred_element_type=jnp.float32)


def selection(index_row, count):
    rows = lax.broadcasted_iota(jnp.int32, (count, index_row.shape[1]), 0)
    return jnp.where(rows == index_row, 1.0, 0.0).astype(jnp.bfloat16)


def select_columns(values, matrix, dims):
    high = values.astype(jnp.bfloat16).astype(jnp.float32)
    rest = values - high
    middle = rest.astype(jnp.bfloat16).astype(jnp.float32)
    parts = jnp.concatenate([high, middle, rest - middle], axis=0).astype(jnp.bfloat16)
    moved = dot(parts, matrix, dims)
    return moved[0:8] + moved[8:16] + moved[16:24]


def spread(flat, sent_ref):
    members = sent_ref.shape[0]
    peer_rows = flat.shape[1] // members
    for peer in range(members):
        sent_ref[peer, :, 0:peer_rows] = flat[:, peer * peer_rows:(peer + 1) * peer_rows]


def flattened(got_ref, elem_count):
    members = got_ref.shape[0]
    peer_rows = elem_count // members
    return jnp.concatenate([got_ref[peer, :, 0:peer_rows] for peer in range(members)], axis=1)


def start_copies(sources, targets, sems):
    copies = [
        pltpu.make_async_copy(source, target, sems.at[i])
        for i, (source, target) in enumerate(zip(sources, targets))
    ]
    for copy in copies:
        copy.start()
    return copies


def sort_kernel(members, near_count, *refs):
    elem_refs, scalar_refs, weight_refs = refs[:7], refs[7:10], refs[10:15]
    sent_ref, order_ref, near_mask_ref, far_mask_ref = refs[15:19]
    weight_outs, elem_bufs, scalar_bufs, sems = refs[19:24], refs[24:31], refs[31:34], refs[34]
    mine = lax.axis_index("leaf")
    coarse_u_ref, coarse_v_ref = weight_refs[3:]
    coarse_u_out, coarse_v_out = weight_outs[3:]
    groups, rank = coarse_u_ref.shape[0], coarse_u_ref.shape[1]
    sources = [*elem_refs, *scalar_refs, *weight_refs[:3]]
    targets = [*elem_bufs, *scalar_bufs, *weight_outs[:3]]
    for shift in range(groups):
        group = mine ^ shift
        span = pl.ds(shift * rank, rank)
        sources += [coarse_u_ref.at[group], coarse_v_ref.at[group]]
        targets += [coarse_u_out.at[span, :], coarse_v_out.at[span, :]]
    copies = start_copies(sources, targets, sems)

    elem_count = elem_bufs[0].shape[1]
    peer_rows = elem_count // members
    before = lax.broadcasted_iota(jnp.int32, (elem_count, elem_count), 0)
    after = lax.broadcasted_iota(jnp.int32, (elem_count, elem_count), 1)
    triangle = jnp.where(before < after, 1.0, 0.0).astype(jnp.bfloat16)
    copies[0].wait()
    local = elem_bufs[0][...] - mine * (members * elem_count)
    target = local // elem_count
    target_row = local - target * elem_count
    onehot = selection(target, members)
    earlier = dot(onehot, triangle, NN)
    rank_within = jnp.sum(earlier * onehot.astype(jnp.float32), axis=0, keepdims=True)
    slot = target * peer_rows + rank_within.astype(jnp.int32)
    order = selection(slot, elem_count)
    order_ref[...] = order
    for copy in copies[1:7]:
        copy.wait()
    u, phi, sigma, fric_a, fric_b, dist = (buf[...] for buf in elem_bufs[1:])
    rows = [u, phi, sigma * fric_a, sigma * fric_b, dist, target_row.astype(jnp.float32)]
    pad = jnp.zeros((8 - len(rows), elem_count), jnp.float32)
    spread(select_columns(jnp.concatenate(rows + [pad], axis=0), order, NT), sent_ref)

    for copy in copies[7:10]:
        copy.wait()
    near_col, far_col, far_rank = scalar_bufs
    far_slots = far_col.shape[0]
    far_width = far_mask_ref.shape[1] // far_slots
    block = lax.broadcasted_iota(jnp.int32, near_mask_ref.shape[1:], 0)
    for number in range(near_mask_ref.shape[0]):
        column = jnp.where(number < near_count[0], near_col[number], -1)
        near_mask_ref[number] = jnp.where(block == column, 1.0, 0.0)
    block = lax.broadcasted_iota(jnp.int32, far_mask_ref.shape, 0)
    lane = lax.broadcasted_iota(jnp.int32, far_mask_ref.shape, 1)
    column = jnp.full(far_mask_ref.shape, -1, jnp.int32)
    for number in range(far_slots):
        low = number * far_width
        kept = (lane >= low) & (lane < low + far_rank[number])
        column = jnp.where(kept, far_col[number], column)
    far_mask_ref[...] = jnp.where(block == column, 1.0, 0.0)
    for copy in copies[10:]:
        copy.wait()


def outgoing(deficit, coarse_v_ref, out_ref):
    elem_count = deficit.shape[1]
    wide = jnp.broadcast_to(deficit, (8, elem_count)).astype(jnp.bfloat16)
    partial = dot(wide, coarse_v_ref[...], NT)[0:1]
    pieces = [deficit, partial]
    rest = out_ref.shape[2] - elem_count - partial.shape[1]
    if rest:
        pieces.append(jnp.zeros((1, rest), jnp.float32))
    out_ref[...] = jnp.broadcast_to(jnp.concatenate(pieces, axis=1)[None], out_ref.shape)


def place_kernel(got_ref, coarse_v_ref, state_ref, order_ref, out_ref):
    elem_count = state_ref.shape[1]
    flat = flattened(got_ref, elem_count)
    order = selection(flat[5:6].astype(jnp.int32), elem_count)
    order_ref[...] = order
    state = select_columns(flat, order, NT)
    state_ref[...] = state
    deficit = (PLATE_RATE - jnp.exp(state[0:1])).astype(jnp.bfloat16).astype(jnp.float32)
    outgoing(deficit, coarse_v_ref, out_ref)


def load_rows(
    all_ref, near_ref, far_u_ref, far_v_ref, near_mask_ref, far_mask_ref, coarse_u_ref, groups
):
    members, leaf_size = near_mask_ref.shape[1], near_ref.shape[2]
    coarse_width = coarse_u_ref.shape[0]
    rank = coarse_width // groups
    mine = lax.axis_index("leaf")
    deficits = all_ref[pl.ds(mine * members, members), 0, 0:leaf_size]
    total = jnp.zeros(deficits.shape, jnp.float32)
    for slot in range(near_ref.shape[0]):
        source = (deficits * near_mask_ref[slot]).astype(jnp.bfloat16)
        total = total + dot(source, near_ref[slot], NT)
    project = dot(deficits.astype(jnp.bfloat16), far_v_ref[...], NT) * far_mask_ref[...]
    project = jnp.sum(project, axis=0, keepdims=True)
    project = jnp.broadcast_to(project, (8, project.shape[1])).astype(jnp.bfloat16)
    far = dot(project, far_u_ref[...], NN)
    lane = lax.broadcasted_iota(jnp.int32, (members, coarse_width), 1)
    weights = jnp.zeros((members, coarse_width), jnp.float32)
    for shift in range(1, groups):
        start = (mine ^ shift) * members
        part = all_ref[pl.ds(start, members), 0, leaf_size:leaf_size + coarse_width]
        weights = jnp.where(lane // rank == shift, part, weights)
    weights = jnp.sum(weights, axis=0, keepdims=True)
    weights = jnp.broadcast_to(weights, (8, coarse_width)).astype(jnp.bfloat16)
    coarse = dot(weights, coarse_u_ref[...], NN)
    return jnp.sum(total, axis=0, keepdims=True) + far[0:1] + coarse[0:1]


def rates(load, ln_now, state_now, sa, sb, dist):
    velocity = jnp.exp(ln_now)
    state_rate = (jnp.exp(-state_now) - velocity) / dist
    log_rate = (load - sb * state_rate) / (sa + DAMPING * velocity)
    return log_rate, state_rate


def first_kernel(groups, state_ref, coarse_v_ref, *refs):
    field_refs, next_ref, out_ref = refs[:-2], refs[-2], refs[-1]
    state = state_ref[...]
    load = load_rows(*field_refs, groups)
    u, phi, sa, sb, dist = (state[i:i + 1] for i in range(5))
    k1u, k1p = rates(load, u, phi, sa, sb, dist)
    u2 = u + TIME_STEP * k1u
    phi2 = phi + TIME_STEP * k1p
    deficit = (PLATE_RATE - jnp.exp(u2)).astype(jnp.bfloat16).astype(jnp.float32)
    outgoing(deficit, coarse_v_ref, out_ref)
    next_ref[...] = jnp.concatenate([u2, phi2, k1u, k1p, jnp.zeros((4, u.shape[1]), jnp.float32)], axis=0)


def second_kernel(groups, state_ref, next_ref, order_ref, *refs):
    field_refs, sent_ref = refs[:-1], refs[-1]
    state = state_ref[...]
    later = next_ref[...]
    load = load_rows(*field_refs, groups)
    u, phi, sa, sb, dist = (state[i:i + 1] for i in range(5))
    u2, phi2, k1u, k1p = (later[i:i + 1] for i in range(4))
    k2u, k2p = rates(load, u2, phi2, sa, sb, dist)
    u = u + 0.5 * TIME_STEP * (k1u + k2u)
    phi = phi + 0.5 * TIME_STEP * (k1p + k2p)
    elem_count = u.shape[1]
    values = jnp.concatenate([u, phi, jnp.zeros((6, elem_count), jnp.float32)], axis=0)
    spread(select_columns(values, order_ref[...], NN)[0:2], sent_ref)


def unsort_kernel(got_ref, order_ref, u_ref, phi_ref):
    elem_count = order_ref.shape[1]
    flat = flattened(got_ref, elem_count)
    flat = jnp.concatenate([flat, jnp.zeros((6, elem_count), jnp.float32)], axis=0)
    out = select_columns(flat, order_ref[...], NN)
    u_ref[...] = out[0:1]
    phi_ref[...] = out[1:2]


def call(kernel, outs, *args, scalars=(), far=(), scratch=(), flops=1000, moved=1000):
    spaces = [SMEM if i in scalars else pl.ANY if i in far else VMEM for i in range(len(args))]
    args = [
        pltpu.with_memory_space_constraint(arg, pltpu.HBM) if i in far else arg
        for i, arg in enumerate(args)
    ]
    return pl.pallas_call(
        kernel,
        out_shape=outs,
        in_specs=[pl.BlockSpec(memory_space=space) for space in spaces],
        out_specs=jax.tree.map(lambda _: pl.BlockSpec(memory_space=VMEM), outs),
        scratch_shapes=list(scratch),
        cost_estimate=pl.CostEstimate(flops=flops, bytes_accessed=moved, transcendentals=0),
        compiler_params=pltpu.CompilerParams(vmem_limit_bytes=32 * 1024 * 1024),
    )(*args)


def shape(*dims, dtype=jnp.float32):
    return jax.ShapeDtypeStruct(dims, dtype)


def body(
    ln_rate,
    log_state,
    sigma,
    fric_a,
    fric_b,
    slip_dist,
    leaf_of_elem,
    near_blocks,
    near_col,
    near_count,
    far_u,
    far_v,
    far_col,
    far_rank,
    coarse_u,
    coarse_v,
):
    members = lax.axis_size("blk")
    elems = ln_rate.shape[0]
    leaf_size = near_blocks.shape[1]
    groups, rank = coarse_v.shape[0], coarse_v.shape[1]
    width = pl.cdiv(groups * rank, 128) * 128
    devices = groups * members

    def swap(value, axes):
        return lax.all_to_all(value, axes, split_axis=0, concat_axis=0, tiled=True)

    elem_args = [
        value.reshape(1, elems)
        for value in (leaf_of_elem, ln_rate, log_state, sigma, fric_a, fric_b, slip_dist)
    ]
    scalar_args = [near_col, far_col, far_rank]
    weights = [
        near_blocks, far_u.reshape(-1, leaf_size), far_v.reshape(-1, leaf_size), coarse_u, coarse_v
    ]
    far_rows = weights[1].shape[0]
    bases = [near_blocks.shape] + [(far_rows, leaf_size)] * 2 + [(groups * rank, elems)] * 2
    sent, elem_order, near_mask, far_mask, near, far_u, far_v, coarse_u, coarse_v = call(
        functools.partial(sort_kernel, members),
        (
            shape(members, 8, 128),
            shape(elems, elems, dtype=jnp.bfloat16),
            shape(near_blocks.shape[0], members, leaf_size),
            shape(members, far_rows),
            *[shape(*dims, dtype=jnp.bfloat16) for dims in bases],
        ),
        near_count, *elem_args, *scalar_args, *weights, scalars=(0,), far=range(1, 16),
        scratch=[VMEM(value.shape, value.dtype) for value in elem_args]
        + [SMEM(value.shape, value.dtype) for value in scalar_args]
        + [pltpu.SemaphoreType.DMA((13 + 2 * groups,))],
    )
    state, leaf_order, out = call(
        place_kernel,
        (
            shape(8, elems),
            shape(elems, elems, dtype=jnp.bfloat16),
            shape(devices, 1, elems + width),
        ),
        swap(sent, "blk"), coarse_v,
    )
    fields = near, far_u, far_v, near_mask, far_mask, coarse_u

    def share(out):
        return swap(out, ("leaf", "blk"))

    later, out = call(
        functools.partial(first_kernel, groups), (shape(8, elems), shape(devices, 1, elems + width)),
        state, coarse_v, share(out), *fields,
    )
    sent = call(
        functools.partial(second_kernel, groups), shape(members, 2, 128),
        state, later, leaf_order, share(out), *fields,
    )
    u, phi = call(
        unsort_kernel, (shape(1, elems), shape(1, elems)), swap(sent, "blk"), elem_order
    )
    return u.reshape(elems), phi.reshape(elems)


def solution(mesh):
    each = P(("leaf", "blk"))
    blocks = P(("leaf", "blk"), None, None)
    last = P(None, None, ("leaf", "blk"))
    in_specs = (each,) * 7 + (blocks, each, each, blocks, blocks, each, each, last, last)
    return jax.shard_map(body, mesh=mesh, in_specs=in_specs, out_specs=(each, each), check_vma=False)
```

```python
import functools

import jax
import jax.numpy as jnp
from jax import lax
from jax.experimental import pallas as pl
from jax.experimental.pallas import tpu as pltpu
from jax.sharding import PartitionSpec as P

DAMPING = 0.5
PLATE_RATE = 1.0
TIME_STEP = 0.2

NN = (((1,), (0,)), ((), ()))
NT = (((1,), (1,)), ((), ()))
VMEM = pltpu.VMEM
SMEM = pltpu.SMEM

LANES = 128


def dot(left, right, dims):
    return lax.dot_general(left, right, dims, preferred_element_type=jnp.float32)


def low_matrix(index_row):
    rows = lax.broadcasted_iota(jnp.int32, (LANES, index_row.shape[1]), 0)
    return jnp.where(rows == (index_row & (LANES - 1)), 1.0, 0.0).astype(jnp.bfloat16)


def three_parts(values):
    high = values.astype(jnp.bfloat16).astype(jnp.float32)
    rest = values - high
    middle = rest.astype(jnp.bfloat16).astype(jnp.float32)
    return jnp.concatenate([high, middle, rest - middle], axis=0)


def joined(parts):
    count = parts.shape[0] // 3
    return parts[0:count] + parts[count:2 * count] + parts[2 * count:]


def scattered(values, index_row):
    parts = three_parts(values)
    count = parts.shape[0]
    high = index_row // LANES
    pieces = values.shape[1] // LANES
    left = jnp.concatenate([jnp.where(high == piece, parts, 0.0) for piece in range(pieces)], axis=0)
    moved = dot(left.astype(jnp.bfloat16), low_matrix(index_row), NT)
    return jnp.concatenate(
        [joined(moved[piece * count:(piece + 1) * count]) for piece in range(pieces)], axis=1
    )


def gathered(values, index_row):
    parts = three_parts(values)
    count = parts.shape[0]
    high = index_row // LANES
    pieces = values.shape[1] // LANES
    left = jnp.concatenate(
        [parts[:, piece * LANES:(piece + 1) * LANES] for piece in range(pieces)], axis=0
    )
    moved = dot(left.astype(jnp.bfloat16), low_matrix(index_row), NN)
    total = jnp.zeros((count, index_row.shape[1]), jnp.float32)
    for piece in range(pieces):
        total = jnp.where(high == piece, moved[piece * count:(piece + 1) * count], total)
    return joined(total)


def padded(rows, count):
    missing = count - len(rows)
    if missing:
        rows = rows + [jnp.zeros((missing, rows[0].shape[1]), jnp.float32)]
    return jnp.concatenate(rows, axis=0)


def as_lines(row):
    return jnp.concatenate(
        [row[:, i * LANES:(i + 1) * LANES] for i in range(row.shape[1] // LANES)], axis=0
    )


def peer_lanes(ref, first, members, rows, elem_count):
    width = elem_count // members
    return jnp.concatenate([ref[first + peer, 0:rows, 0:width] for peer in range(members)], axis=1)


def start_copies(sources, targets, sems):
    copies = [
        pltpu.make_async_copy(source, target, sems.at[i])
        for i, (source, target) in enumerate(zip(sources, targets))
    ]
    for copy in copies:
        copy.start()
    return copies


def sort_kernel(members, near_count, *refs):
    elem_refs, scalar_refs, weight_refs = refs[:7], refs[7:10], refs[10:14]
    sent_ref, slot_ref, slot_row_ref, near_mask_ref, far_mask_ref = refs[14:19]
    weight_outs, elem_bufs, scalar_bufs, sems = refs[19:23], refs[23:30], refs[30:33], refs[33]
    copies = start_copies(
        [*elem_refs, *scalar_refs, *weight_refs], [*elem_bufs, *scalar_bufs, *weight_outs], sems
    )
    mine = lax.axis_index("leaf")
    elem_count = elem_bufs[0].shape[1]
    peer_rows = elem_count // members
    pieces = elem_count // LANES
    before = lax.broadcasted_iota(jnp.int32, (LANES, LANES), 0)
    after = lax.broadcasted_iota(jnp.int32, (LANES, LANES), 1)
    triangle = jnp.where(before < after, 1.0, 0.0).astype(jnp.bfloat16)
    copies[0].wait()
    local = elem_bufs[0][...] - mine * (members * elem_count)
    target = local // elem_count
    target_row = local - target * elem_count
    peers = lax.broadcasted_iota(jnp.int32, (members, elem_count), 0)
    onehot = jnp.where(peers == target, 1.0, 0.0)
    lines = [onehot[:, i * LANES:(i + 1) * LANES] for i in range(pieces)]
    inside = dot(jnp.concatenate(lines, axis=0).astype(jnp.bfloat16), triangle, NN)
    passed = jnp.zeros((members, 1), jnp.float32)
    ranks = []
    for i, line in enumerate(lines):
        earlier = inside[i * members:(i + 1) * members] + passed
        ranks.append(jnp.sum(earlier * line, axis=0, keepdims=True))
        passed = passed + jnp.sum(line, axis=1, keepdims=True)
    slot = target * peer_rows + jnp.concatenate(ranks, axis=1).astype(jnp.int32)
    slot_ref[...] = slot
    for copy in copies[1:7]:
        copy.wait()
    u, phi, sigma, fric_a, fric_b, dist = (buf[...] for buf in elem_bufs[1:])
    deficit = (PLATE_RATE - jnp.exp(u)).astype(jnp.bfloat16).astype(jnp.float32)
    rows = [u, phi, sigma * fric_a, sigma * fric_b, dist, target_row.astype(jnp.float32), deficit]
    values = scattered(padded(rows, 8), slot)
    slot_row_ref[...] = values[5:6].astype(jnp.int32)
    everyone = jnp.concatenate([as_lines(values[6:7]), as_lines(values[5:6])], axis=0)
    for peer in range(members):
        sent_ref[peer, 0:8, 0:peer_rows] = values[:, peer * peer_rows:(peer + 1) * peer_rows]
        sent_ref[peer, 8:8 + 2 * pieces, :] = everyone

    for copy in copies[7:10]:
        copy.wait()
    near_col, far_col, far_rank = scalar_bufs
    far_slots = far_col.shape[0]
    far_width = far_mask_ref.shape[1] // far_slots
    block = lax.broadcasted_iota(jnp.int32, near_mask_ref.shape[1:], 0)
    for number in range(near_mask_ref.shape[0]):
        column = jnp.where(number < near_count[0], near_col[number], -1)
        near_mask_ref[number] = jnp.where(block == column, 1.0, 0.0)
    block = lax.broadcasted_iota(jnp.int32, far_mask_ref.shape, 0)
    lane = lax.broadcasted_iota(jnp.int32, far_mask_ref.shape, 1)
    column = jnp.full(far_mask_ref.shape, -1, jnp.int32)
    for number in range(far_slots):
        low = number * far_width
        kept = (lane >= low) & (lane < low + far_rank[number])
        column = jnp.where(kept, far_col[number], column)
    far_mask_ref[...] = jnp.where(block == column, 1.0, 0.0)
    for copy in copies[10:]:
        copy.wait()


def partial_row(deficit, coarse_v_ref):
    wide = jnp.broadcast_to(deficit, (8, deficit.shape[1])).astype(jnp.bfloat16)
    partial = dot(wide, coarse_v_ref[...], NT)[0:1]
    rest = -partial.shape[1] % LANES
    if rest:
        partial = jnp.concatenate([partial, jnp.zeros((1, rest), jnp.float32)], axis=1)
    return partial


def inside_rows(deficits, near_ref, far_u_ref, far_v_ref, near_mask_ref, far_mask_ref):
    total = jnp.zeros(deficits.shape, jnp.float32)
    for slot in range(near_ref.shape[0]):
        source = (deficits * near_mask_ref[slot]).astype(jnp.bfloat16)
        total = total + dot(source, near_ref[slot], NT)
    project = dot(deficits.astype(jnp.bfloat16), far_v_ref[...], NT) * far_mask_ref[...]
    project = jnp.sum(project, axis=0, keepdims=True)
    project = jnp.broadcast_to(project, (8, project.shape[1])).astype(jnp.bfloat16)
    far = dot(project, far_u_ref[...], NN)
    return jnp.sum(total, axis=0, keepdims=True) + far[0:1]


def coefficients(sums, rank):
    groups, width = len(sums), sums[0].shape[1]
    mine = lax.axis_index("leaf")
    table = padded(sums, -(-groups // 8) * 8)
    lane = lax.broadcasted_iota(jnp.int32, table.shape, 1) // rank
    row = lax.broadcasted_iota(jnp.int32, table.shape, 0)
    table = jnp.where(lane == mine, table, 0.0).astype(jnp.bfloat16)
    across = lax.broadcasted_iota(jnp.int32, (width, width), 0) % rank
    down = lax.broadcasted_iota(jnp.int32, (width, width), 1) % rank
    spread = dot(table, jnp.where(across == down, 1.0, 0.0).astype(jnp.bfloat16), NN)
    kept = (lane == row) & (row != mine)
    return jnp.sum(jnp.where(kept, spread, 0.0), axis=0, keepdims=True)


def coarse_all(weights, members, bases_ref):
    width = weights.shape[1]
    tiled = jnp.concatenate([weights] * members, axis=1)
    lane = lax.broadcasted_iota(jnp.int32, (members, members * width), 1) // width
    row = lax.broadcasted_iota(jnp.int32, (members, members * width), 0)
    left = jnp.where(lane == row, tiled, 0.0).astype(jnp.bfloat16)
    return dot(left, bases_ref[...], NN)


def place_kernel(got_ref, coarse_v_ref, *refs):
    field_refs, state_ref, rows_ref, out_ref, lines_ref = refs[:5], refs[5], refs[6], refs[7], refs[8]
    members = got_ref.shape[0]
    elem_count = state_ref.shape[1]
    pieces = elem_count // LANES
    peer_rows = elem_count // members
    per_line = LANES // peer_rows
    line_block = lax.broadcasted_iota(jnp.int32, (per_line * pieces, LANES), 0) // pieces
    line_piece = lax.broadcasted_iota(jnp.int32, (per_line * pieces, LANES), 0) % pieces
    lane_block = lax.broadcasted_iota(jnp.int32, (per_line * pieces, LANES), 1) // peer_rows
    own_lane = line_block == lane_block
    for line in range(pieces):
        left, right = [], []
        for peer in range(members):
            value = got_ref[peer, 8 + line:9 + line, :]
            row = got_ref[peer, 8 + pieces + line:9 + pieces + line, :].astype(jnp.int32)
            left.append(jnp.where(own_lane & (line_piece == row // LANES), value, 0.0))
            right.append(low_matrix(row))
        left = jnp.concatenate(left, axis=1).astype(jnp.bfloat16)
        count = per_line * pieces
        lines_ref[line * count:(line + 1) * count, :] = dot(left, jnp.concatenate(right, axis=1), NT)
    deficits = jnp.concatenate(
        [lines_ref[pl.ds(piece, members, stride=pieces), :] for piece in range(pieces)], axis=1
    )
    inside = inside_rows(deficits, *field_refs)

    flat = peer_lanes(got_ref, 0, members, 8, elem_count)
    rows = flat[5:6].astype(jnp.int32)
    rows_ref[...] = rows
    state = scattered(flat, rows)
    u, phi, sa, sb, dist = (state[i:i + 1] for i in range(5))
    velocity = jnp.exp(u)
    k1p = (jnp.exp(-phi) - velocity) / dist
    inverse = 1.0 / (sa + DAMPING * velocity)
    u2 = u + TIME_STEP * ((inside - sb * k1p) * inverse)
    factor = TIME_STEP * inverse
    state_ref[...] = jnp.concatenate([u, phi, sa, sb, dist, k1p, u2, factor], axis=0)
    sent = jnp.concatenate([u2, factor, partial_row(state[6:7], coarse_v_ref)], axis=1)
    out_ref[...] = jnp.broadcast_to(sent[None], out_ref.shape)


def second_kernel(
    groups, state_ref, rows_ref, all_ref, bases_ref, coarse_v_ref, *refs
):
    field_refs, sent_ref, bases_out, sem = refs[:5], refs[5], refs[6], refs[7]
    copy = pltpu.make_async_copy(bases_ref, bases_out, sem.at[0])
    copy.start()
    members, elem_count = refs[3].shape[1], state_ref.shape[1]
    width = coarse_v_ref.shape[0]
    mine, me = lax.axis_index("leaf"), lax.axis_index("blk")
    sums = [
        jnp.sum(
            all_ref[group * members:(group + 1) * members, 0, 2 * elem_count:2 * elem_count + width],
            axis=0, keepdims=True,
        )
        for group in range(groups)
    ]
    weights = coefficients(sums, width // groups)
    own = all_ref[pl.ds(mine * members, members), 0, 0:2 * elem_count]
    copy.wait()
    coarse = coarse_all(weights, members, bases_out)
    u2_all = own[:, 0:elem_count] + own[:, elem_count:] * coarse
    deficits = (PLATE_RATE - jnp.exp(u2_all)).astype(jnp.bfloat16).astype(jnp.float32)
    inside = inside_rows(deficits, *field_refs)

    state = state_ref[...]
    u, phi, sa, sb, dist, k1p = (state[i:i + 1] for i in range(6))
    here = lax.broadcasted_iota(jnp.int32, u2_all.shape, 0) == me
    u2 = jnp.sum(jnp.where(here, u2_all, 0.0), axis=0, keepdims=True)
    deficit = jnp.sum(jnp.where(here, deficits, 0.0), axis=0, keepdims=True)
    phi2 = phi + TIME_STEP * k1p
    velocity = jnp.exp(u2)
    k2p = (jnp.exp(-phi2) - velocity) / dist
    inverse = 0.5 * TIME_STEP / (sa + DAMPING * velocity)
    u_next = 0.5 * (u + u2) + (inside - sb * k2p) * inverse
    phi_next = phi + 0.5 * TIME_STEP * (k1p + k2p)
    sent = gathered(padded([u_next, inverse, phi_next], 8), rows_ref[...])
    partial = as_lines(partial_row(deficit, coarse_v_ref))
    peer_rows = elem_count // members
    for device in range(groups * members):
        peer = device % members
        sent_ref[device, 0:3, 0:peer_rows] = sent[0:3, peer * peer_rows:(peer + 1) * peer_rows]
        sent_ref[device, 3:3 + partial.shape[0], :] = partial


def finish_kernel(groups, width, got_ref, bases_ref, slot_ref, slot_row_ref, u_ref, phi_ref, *scratch):
    if scratch:
        copy = pltpu.make_async_copy(bases_ref, scratch[0], scratch[1].at[0])
        copy.start()
        copy.wait()
        bases_ref = scratch[0]
    elem_count = slot_ref.shape[1]
    members = got_ref.shape[0] // groups
    sums = []
    for group in range(groups):
        total = jnp.sum(got_ref[group * members:(group + 1) * members], axis=0)
        lines = [total[3 + i:4 + i, :] for i in range(pl.cdiv(width, LANES))]
        sums.append(jnp.concatenate(lines, axis=1)[:, 0:width])
    coarse = coarse_all(coefficients(sums, width // groups), members, bases_ref)
    row = slot_row_ref[...]
    block = lax.broadcasted_iota(jnp.int32, (members, elem_count), 0)
    lane_block = lax.broadcasted_iota(jnp.int32, (members, elem_count), 1) // (elem_count // members)
    rows = gathered(coarse, row)
    found = jnp.sum(jnp.where(block == lane_block, rows, 0.0), axis=0, keepdims=True)
    first = lax.axis_index("leaf") * members
    flat = peer_lanes(got_ref, first, members, 3, elem_count)
    u_next = flat[0:1] + flat[1:2] * found
    out = gathered(padded([u_next, flat[2:3]], 8), slot_ref[...])
    u_ref[...] = out[0:1]
    phi_ref[...] = out[1:2]


def call(kernel, outs, *args, scalars=(), far=(), scratch=(), flops=1000, moved=1000):
    spaces = [SMEM if i in scalars else pl.ANY if i in far else VMEM for i in range(len(args))]
    args = [
        pltpu.with_memory_space_constraint(arg, pltpu.HBM) if i in far else arg
        for i, arg in enumerate(args)
    ]
    return pl.pallas_call(
        kernel,
        out_shape=outs,
        in_specs=[pl.BlockSpec(memory_space=space) for space in spaces],
        out_specs=jax.tree.map(lambda _: pl.BlockSpec(memory_space=VMEM), outs),
        scratch_shapes=list(scratch),
        cost_estimate=pl.CostEstimate(flops=flops, bytes_accessed=moved, transcendentals=0),
        compiler_params=pltpu.CompilerParams(vmem_limit_bytes=32 * 1024 * 1024),
    )(*args)


def shape(*dims, dtype=jnp.float32):
    return jax.ShapeDtypeStruct(dims, dtype)


def body(
    ln_rate,
    log_state,
    sigma,
    fric_a,
    fric_b,
    slip_dist,
    leaf_of_elem,
    near_blocks,
    near_col,
    near_count,
    far_u,
    far_v,
    far_col,
    far_rank,
    coarse_u,
    coarse_v,
):
    members = lax.axis_size("blk")
    elems = ln_rate.shape[0]
    leaf_size = near_blocks.shape[1]
    groups, rank = coarse_v.shape[0], coarse_v.shape[1]
    devices = groups * members
    width = groups * rank
    lines = pl.cdiv(width, LANES)
    sent_rows = 1 << (2 + lines).bit_length()
    integer = jnp.int32

    def swap(value, axes):
        return lax.all_to_all(value, axes, split_axis=0, concat_axis=0, tiled=True)

    bases = lax.all_gather(coarse_u.reshape(width, elems), "blk", axis=0, tiled=True)
    elem_args = [
        value.reshape(1, elems)
        for value in (leaf_of_elem, ln_rate, log_state, sigma, fric_a, fric_b, slip_dist)
    ]
    scalar_args = [near_col, far_col, far_rank]
    weights = [
        near_blocks, far_u.reshape(-1, leaf_size), far_v.reshape(-1, leaf_size),
        coarse_v.reshape(width, elems),
    ]
    far_rows = weights[1].shape[0]
    sent, slot, slot_row, near_mask, far_mask, near, far_u, far_v, coarse_v = call(
        functools.partial(sort_kernel, members),
        (
            shape(members, 8 + 2 * (elems // LANES), LANES),
            shape(1, elems, dtype=integer),
            shape(1, elems, dtype=integer),
            shape(near_blocks.shape[0], members, leaf_size),
            shape(members, far_rows),
            *[shape(*value.shape, dtype=jnp.bfloat16) for value in weights],
        ),
        near_count, *elem_args, *scalar_args, *weights, scalars=(0,), far=range(1, 15),
        scratch=[VMEM(value.shape, value.dtype) for value in elem_args]
        + [SMEM(value.shape, value.dtype) for value in scalar_args]
        + [pltpu.SemaphoreType.DMA((14,))],
    )
    fields = near, far_u, far_v, near_mask, far_mask
    state, rows, out = call(
        place_kernel,
        (
            shape(8, elems),
            shape(1, elems, dtype=integer),
            shape(devices, 1, 2 * elems + lines * LANES),
        ),
        swap(sent, "blk"), coarse_v, *fields,
        scratch=[VMEM((members * (elems // LANES), LANES), jnp.float32)],
    )
    held = members * width * elems <= 1 << 21
    place = shape(members * width, elems, dtype=jnp.bfloat16)
    buffer = [VMEM(place.shape, place.dtype)]
    signal = [pltpu.SemaphoreType.DMA((1,))]
    outs = call(
        functools.partial(second_kernel, groups),
        (shape(devices, sent_rows, LANES),) + (place,) * held,
        state, rows, swap(out, ("leaf", "blk")), bases, coarse_v, *fields, far=(3,),
        scratch=signal if held else buffer + signal,
    )
    u, phi = call(
        functools.partial(finish_kernel, groups, width), (shape(1, elems), shape(1, elems)),
        swap(outs[0], ("leaf", "blk")), outs[1] if held else bases, slot, slot_row,
        far=() if held else (1,), scratch=() if held else buffer + signal,
    )
    return u.reshape(elems), phi.reshape(elems)


def solution(mesh):
    each = P(("leaf", "blk"))
    blocks = P(("leaf", "blk"), None, None)
    last = P(None, None, ("leaf", "blk"))
    in_specs = (each,) * 7 + (blocks, each, each, blocks, blocks, each, each, last, last)
    return jax.shard_map(body, mesh=mesh, in_specs=in_specs, out_specs=(each, each), check_vma=False)
```

```python
import functools

import jax
import jax.numpy as jnp
from jax import lax
from jax.experimental import pallas as pl
from jax.experimental.pallas import tpu as pltpu
from jax.sharding import PartitionSpec as P

DAMPING = 0.5
PLATE_RATE = 1.0
TIME_STEP = 0.2

NN = (((1,), (0,)), ((), ()))
NT = (((1,), (1,)), ((), ()))
VMEM = pltpu.VMEM
SMEM = pltpu.SMEM

LANES = 128


def dot(left, right, dims):
    return lax.dot_general(left, right, dims, preferred_element_type=jnp.float32)


def low_matrix(index_row):
    rows = lax.broadcasted_iota(jnp.int32, (LANES, index_row.shape[1]), 0)
    return jnp.where(rows == (index_row & (LANES - 1)), 1.0, 0.0).astype(jnp.bfloat16)


def three_parts(values):
    high = values.astype(jnp.bfloat16).astype(jnp.float32)
    rest = values - high
    middle = rest.astype(jnp.bfloat16).astype(jnp.float32)
    return jnp.concatenate([high, middle, rest - middle], axis=0)


def joined(parts):
    count = parts.shape[0] // 3
    return parts[0:count] + parts[count:2 * count] + parts[2 * count:]


def scattered(values, index_row):
    parts = three_parts(values)
    count = parts.shape[0]
    high = index_row // LANES
    pieces = values.shape[1] // LANES
    left = jnp.concatenate([jnp.where(high == piece, parts, 0.0) for piece in range(pieces)], axis=0)
    moved = dot(left.astype(jnp.bfloat16), low_matrix(index_row), NT)
    return jnp.concatenate(
        [joined(moved[piece * count:(piece + 1) * count]) for piece in range(pieces)], axis=1
    )


def gathered(values, index_row):
    parts = three_parts(values)
    count = parts.shape[0]
    high = index_row // LANES
    pieces = values.shape[1] // LANES
    left = jnp.concatenate(
        [parts[:, piece * LANES:(piece + 1) * LANES] for piece in range(pieces)], axis=0
    )
    moved = dot(left.astype(jnp.bfloat16), low_matrix(index_row), NN)
    total = jnp.zeros((count, index_row.shape[1]), jnp.float32)
    for piece in range(pieces):
        total = jnp.where(high == piece, moved[piece * count:(piece + 1) * count], total)
    return joined(total)


def padded(rows, count):
    missing = count - len(rows)
    if missing:
        rows = rows + [jnp.zeros((missing, rows[0].shape[1]), jnp.float32)]
    return jnp.concatenate(rows, axis=0)


def as_lines(row):
    return jnp.concatenate(
        [row[:, i * LANES:(i + 1) * LANES] for i in range(row.shape[1] // LANES)], axis=0
    )


def peer_lanes(ref, first, members, rows, elem_count):
    width = elem_count // members
    return jnp.concatenate([ref[first + peer, 0:rows, 0:width] for peer in range(members)], axis=1)


def start_copies(sources, targets, sems):
    copies = [
        pltpu.make_async_copy(source, target, sems.at[i])
        for i, (source, target) in enumerate(zip(sources, targets))
    ]
    for copy in copies:
        copy.start()
    return copies


def sort_kernel(members, *refs):
    elem_refs, scalar_refs, weight_refs = refs[:7], refs[7:10], refs[10:14]
    sent_ref, slot_ref, slot_row_ref, near_mask_ref, far_mask_ref = refs[14:19]
    weight_outs, elem_bufs, scalar_bufs, sems = refs[19:23], refs[23:30], refs[30:33], refs[33]
    copies = start_copies(
        [*elem_refs, *scalar_refs, *weight_refs], [*elem_bufs, *scalar_bufs, *weight_outs], sems
    )
    mine = lax.axis_index("leaf")
    elem_count = elem_bufs[0].shape[1]
    peer_rows = elem_count // members
    pieces = elem_count // LANES
    before = lax.broadcasted_iota(jnp.int32, (LANES, LANES), 0)
    after = lax.broadcasted_iota(jnp.int32, (LANES, LANES), 1)
    triangle = jnp.where(before < after, 1.0, 0.0).astype(jnp.bfloat16)
    copies[0].wait()
    local = elem_bufs[0][...] - mine * (members * elem_count)
    target = local // elem_count
    target_row = local - target * elem_count
    peers = lax.broadcasted_iota(jnp.int32, (members, elem_count), 0)
    onehot = jnp.where(peers == target, 1.0, 0.0)
    lines = [onehot[:, i * LANES:(i + 1) * LANES] for i in range(pieces)]
    inside = dot(jnp.concatenate(lines, axis=0).astype(jnp.bfloat16), triangle, NN)
    passed = jnp.zeros((members, 1), jnp.float32)
    ranks = []
    for i, line in enumerate(lines):
        earlier = inside[i * members:(i + 1) * members] + passed
        ranks.append(jnp.sum(earlier * line, axis=0, keepdims=True))
        passed = passed + jnp.sum(line, axis=1, keepdims=True)
    slot = target * peer_rows + jnp.concatenate(ranks, axis=1).astype(jnp.int32)
    slot_ref[...] = slot
    for copy in copies[1:7]:
        copy.wait()
    u, phi, sigma, fric_a, fric_b, dist = (buf[...] for buf in elem_bufs[1:])
    deficit = (PLATE_RATE - jnp.exp(u)).astype(jnp.bfloat16).astype(jnp.float32)
    rows = [u, phi, sigma * fric_a, sigma * fric_b, dist, target_row.astype(jnp.float32), deficit]
    values = scattered(padded(rows, 8), slot)
    slot_row_ref[...] = values[5:6].astype(jnp.int32)
    everyone = jnp.concatenate([as_lines(values[6:7]), as_lines(values[5:6])], axis=0)
    for peer in range(members):
        sent_ref[peer, 0:8, 0:peer_rows] = values[:, peer * peer_rows:(peer + 1) * peer_rows]
        sent_ref[peer, 8:8 + 2 * pieces, :] = everyone

    for copy in copies[7:10]:
        copy.wait()
    near_col, far_col, far_rank = scalar_bufs
    far_slots = far_col.shape[0]
    far_width = far_mask_ref.shape[1] // far_slots
    block = lax.broadcasted_iota(jnp.int32, near_mask_ref.shape[1:], 0)
    for number in range(near_mask_ref.shape[0]):
        near_mask_ref[number] = jnp.where(block == near_col[number], 1.0, 0.0)
    block = lax.broadcasted_iota(jnp.int32, far_mask_ref.shape, 0)
    lane = lax.broadcasted_iota(jnp.int32, far_mask_ref.shape, 1)
    column = jnp.full(far_mask_ref.shape, -1, jnp.int32)
    for number in range(far_slots):
        low = number * far_width
        kept = (lane >= low) & (lane < low + far_rank[number])
        column = jnp.where(kept, far_col[number], column)
    far_mask_ref[...] = jnp.where(block == column, 1.0, 0.0)
    for copy in copies[10:]:
        copy.wait()


def partial_row(deficit, coarse_v_ref):
    wide = jnp.broadcast_to(deficit, (8, deficit.shape[1])).astype(jnp.bfloat16)
    partial = dot(wide, coarse_v_ref[...], NT)[0:1]
    rest = -partial.shape[1] % LANES
    if rest:
        partial = jnp.concatenate([partial, jnp.zeros((1, rest), jnp.float32)], axis=1)
    return partial


def inside_rows(deficits, near_count, near_ref, far_u_ref, far_v_ref, near_mask_ref, far_mask_ref):
    total = jnp.zeros(deficits.shape, jnp.float32)
    for slot in range(near_ref.shape[0]):
        live = jnp.where(slot < near_count[0], 1.0, 0.0)
        source = (deficits * (near_mask_ref[slot] * live)).astype(jnp.bfloat16)
        total = total + dot(source, near_ref[slot], NT)
    project = dot(deficits.astype(jnp.bfloat16), far_v_ref[...], NT) * far_mask_ref[...]
    project = jnp.sum(project, axis=0, keepdims=True)
    project = jnp.broadcast_to(project, (8, project.shape[1])).astype(jnp.bfloat16)
    far = dot(project, far_u_ref[...], NN)
    return jnp.sum(total, axis=0, keepdims=True) + far[0:1]


def coefficients(sums, rank):
    groups, width = len(sums), sums[0].shape[1]
    mine = lax.axis_index("leaf")
    table = padded(sums, -(-groups // 8) * 8)
    lane = lax.broadcasted_iota(jnp.int32, table.shape, 1) // rank
    row = lax.broadcasted_iota(jnp.int32, table.shape, 0)
    table = jnp.where(lane == mine, table, 0.0).astype(jnp.bfloat16)
    across = lax.broadcasted_iota(jnp.int32, (width, width), 0) % rank
    down = lax.broadcasted_iota(jnp.int32, (width, width), 1) % rank
    spread = dot(table, jnp.where(across == down, 1.0, 0.0).astype(jnp.bfloat16), NN)
    kept = (lane == row) & (row != mine)
    return jnp.sum(jnp.where(kept, spread, 0.0), axis=0, keepdims=True)


def coarse_all(weights, members, bases_refs):
    width = weights.shape[1]
    half = members // 2
    tiled = jnp.concatenate([weights] * half, axis=1)
    place = lax.broadcasted_iota(jnp.int32, (members, half * width), 1) // width
    row = lax.broadcasted_iota(jnp.int32, (members, half * width), 0) ^ lax.axis_index("blk")
    bits = members.bit_length() - 1
    total = jnp.zeros((members, bases_refs[0].shape[1]), jnp.float32)
    for number, ref in enumerate(bases_refs):
        source = jnp.full(place.shape, number, jnp.int32)
        for bit in range(bits - 1):
            source = source | (((place >> bit) & 1) << (bits - 1 - bit))
        left = jnp.where(source == row, tiled, 0.0).astype(jnp.bfloat16)
        total = total + dot(left, ref[...], NN)
    return total


def stack_kernel(held_ref, came_ref, *refs):
    out_ref = refs[-1]
    count = held_ref.shape[0]
    out_ref[0:count, :] = held_ref[...]
    out_ref[count:2 * count, :] = came_ref[...]


def place_kernel(got_ref, coarse_v_ref, *refs):
    field_refs, state_ref, rows_ref, out_ref, lines_ref = refs[:6], refs[6], refs[7], refs[8], refs[9]
    members = got_ref.shape[0]
    elem_count = state_ref.shape[1]
    pieces = elem_count // LANES
    peer_rows = elem_count // members
    per_line = LANES // peer_rows
    line_block = lax.broadcasted_iota(jnp.int32, (per_line * pieces, LANES), 0) // pieces
    line_piece = lax.broadcasted_iota(jnp.int32, (per_line * pieces, LANES), 0) % pieces
    lane_block = lax.broadcasted_iota(jnp.int32, (per_line * pieces, LANES), 1) // peer_rows
    own_lane = line_block == lane_block
    for line in range(pieces):
        left, right = [], []
        for peer in range(members):
            value = got_ref[peer, 8 + line:9 + line, :]
            row = got_ref[peer, 8 + pieces + line:9 + pieces + line, :].astype(jnp.int32)
            left.append(jnp.where(own_lane & (line_piece == row // LANES), value, 0.0))
            right.append(low_matrix(row))
        left = jnp.concatenate(left, axis=1).astype(jnp.bfloat16)
        count = per_line * pieces
        lines_ref[line * count:(line + 1) * count, :] = dot(left, jnp.concatenate(right, axis=1), NT)
    deficits = jnp.concatenate(
        [lines_ref[pl.ds(piece, members, stride=pieces), :] for piece in range(pieces)], axis=1
    )
    inside = inside_rows(deficits, *field_refs)

    flat = peer_lanes(got_ref, 0, members, 8, elem_count)
    rows = flat[5:6].astype(jnp.int32)
    rows_ref[...] = rows
    state = scattered(flat, rows)
    u, phi, sa, sb, dist = (state[i:i + 1] for i in range(5))
    velocity = jnp.exp(u)
    k1p = (jnp.exp(-phi) - velocity) / dist
    inverse = 1.0 / (sa + DAMPING * velocity)
    u2 = u + TIME_STEP * ((inside - sb * k1p) * inverse)
    factor = TIME_STEP * inverse
    state_ref[...] = jnp.concatenate([u, phi, sa, sb, dist, k1p, u2, factor], axis=0)
    sent = jnp.concatenate([u2, factor, partial_row(state[6:7], coarse_v_ref)], axis=1)
    out_ref[...] = jnp.broadcast_to(sent[None], out_ref.shape)


def second_kernel(groups, state_ref, rows_ref, all_ref, held_ref, came_ref, coarse_v_ref, *refs):
    field_refs, sent_ref = refs[:6], refs[6]
    members, elem_count = refs[4].shape[1], state_ref.shape[1]
    width = coarse_v_ref.shape[0]
    mine, me = lax.axis_index("leaf"), lax.axis_index("blk")
    sums = [
        jnp.sum(
            all_ref[group * members:(group + 1) * members, 0, 2 * elem_count:2 * elem_count + width],
            axis=0, keepdims=True,
        )
        for group in range(groups)
    ]
    weights = coefficients(sums, width // groups)
    own = all_ref[pl.ds(mine * members, members), 0, 0:2 * elem_count]
    coarse = coarse_all(weights, members, (held_ref, came_ref))
    u2_all = own[:, 0:elem_count] + own[:, elem_count:] * coarse
    deficits = (PLATE_RATE - jnp.exp(u2_all)).astype(jnp.bfloat16).astype(jnp.float32)
    inside = inside_rows(deficits, *field_refs)

    state = state_ref[...]
    u, phi, sa, sb, dist, k1p = (state[i:i + 1] for i in range(6))
    here = lax.broadcasted_iota(jnp.int32, u2_all.shape, 0) == me
    u2 = jnp.sum(jnp.where(here, u2_all, 0.0), axis=0, keepdims=True)
    deficit = jnp.sum(jnp.where(here, deficits, 0.0), axis=0, keepdims=True)
    phi2 = phi + TIME_STEP * k1p
    velocity = jnp.exp(u2)
    k2p = (jnp.exp(-phi2) - velocity) / dist
    inverse = 0.5 * TIME_STEP / (sa + DAMPING * velocity)
    u_next = 0.5 * (u + u2) + (inside - sb * k2p) * inverse
    phi_next = phi + 0.5 * TIME_STEP * (k1p + k2p)
    sent = gathered(padded([u_next, inverse, phi_next], 8), rows_ref[...])
    partial = as_lines(partial_row(deficit, coarse_v_ref))
    peer_rows = elem_count // members
    for device in range(groups * members):
        peer = device % members
        sent_ref[device, 0:3, 0:peer_rows] = sent[0:3, peer * peer_rows:(peer + 1) * peer_rows]
        sent_ref[device, 3:3 + partial.shape[0], :] = partial


def finish_kernel(
    groups, width, got_ref, held_ref, came_ref, slot_ref, slot_row_ref, u_ref, phi_ref
):
    elem_count = slot_ref.shape[1]
    members = got_ref.shape[0] // groups
    sums = []
    for group in range(groups):
        total = jnp.sum(got_ref[group * members:(group + 1) * members], axis=0)
        lines = [total[3 + i:4 + i, :] for i in range(pl.cdiv(width, LANES))]
        sums.append(jnp.concatenate(lines, axis=1)[:, 0:width])
    coarse = coarse_all(coefficients(sums, width // groups), members, (held_ref, came_ref))
    row = slot_row_ref[...]
    block = lax.broadcasted_iota(jnp.int32, (members, elem_count), 0)
    lane_block = lax.broadcasted_iota(jnp.int32, (members, elem_count), 1) // (elem_count // members)
    rows = gathered(coarse, row)
    found = jnp.sum(jnp.where(block == lane_block, rows, 0.0), axis=0, keepdims=True)
    first = lax.axis_index("leaf") * members
    flat = peer_lanes(got_ref, first, members, 3, elem_count)
    u_next = flat[0:1] + flat[1:2] * found
    out = gathered(padded([u_next, flat[2:3]], 8), slot_ref[...])
    u_ref[...] = out[0:1]
    phi_ref[...] = out[1:2]


def call(kernel, outs, *args, scalars=(), far=(), scratch=(), flops=1000, moved=1000):
    spaces = [SMEM if i in scalars else pl.ANY if i in far else VMEM for i in range(len(args))]
    args = [
        pltpu.with_memory_space_constraint(arg, pltpu.HBM) if i in far else arg
        for i, arg in enumerate(args)
    ]
    return pl.pallas_call(
        kernel,
        out_shape=outs,
        in_specs=[pl.BlockSpec(memory_space=space) for space in spaces],
        out_specs=jax.tree.map(lambda _: pl.BlockSpec(memory_space=VMEM), outs),
        scratch_shapes=list(scratch),
        cost_estimate=pl.CostEstimate(flops=flops, bytes_accessed=moved, transcendentals=0),
        compiler_params=pltpu.CompilerParams(vmem_limit_bytes=32 * 1024 * 1024),
    )(*args)


def shape(*dims, dtype=jnp.float32):
    return jax.ShapeDtypeStruct(dims, dtype)


def body(
    ln_rate,
    log_state,
    sigma,
    fric_a,
    fric_b,
    slip_dist,
    leaf_of_elem,
    near_blocks,
    near_col,
    near_count,
    far_u,
    far_v,
    far_col,
    far_rank,
    coarse_u,
    coarse_v,
):
    members = lax.axis_size("blk")
    elems = ln_rate.shape[0]
    leaf_size = near_blocks.shape[1]
    groups, rank = coarse_v.shape[0], coarse_v.shape[1]
    devices = groups * members
    width = groups * rank
    lines = pl.cdiv(width, LANES)
    sent_rows = 1 << (2 + lines).bit_length()
    integer = jnp.int32

    def swap(value, axes):
        return lax.all_to_all(value, axes, split_axis=0, concat_axis=0, tiled=True)

    def partner(value, bit):
        return lax.ppermute(value, "blk", [(i, i ^ (1 << bit)) for i in range(members)])

    elem_args = [
        value.reshape(1, elems)
        for value in (leaf_of_elem, ln_rate, log_state, sigma, fric_a, fric_b, slip_dist)
    ]
    scalar_args = [near_col, far_col, far_rank]
    weights = [
        near_blocks, far_u.reshape(-1, leaf_size), far_v.reshape(-1, leaf_size),
        coarse_v.reshape(width, elems),
    ]
    far_rows = weights[1].shape[0]
    sent, slot, slot_row, near_mask, far_mask, near, far_u, far_v, coarse_v = call(
        functools.partial(sort_kernel, members),
        (
            shape(members, 8 + 2 * (elems // LANES), LANES),
            shape(1, elems, dtype=integer),
            shape(1, elems, dtype=integer),
            shape(near_blocks.shape[0], members, leaf_size),
            shape(members, far_rows),
            *[shape(*value.shape, dtype=jnp.bfloat16) for value in weights],
        ),
        *elem_args, *scalar_args, *weights, far=range(14),
        scratch=[VMEM(value.shape, value.dtype) for value in elem_args]
        + [SMEM(value.shape, value.dtype) for value in scalar_args]
        + [pltpu.SemaphoreType.DMA((14,))],
    )
    bases = coarse_u.reshape(width, elems)
    for bit in range(members.bit_length() - 2, 0, -1):
        came = partner(bases, bit)
        stacked = shape(2 * bases.shape[0], elems, dtype=jnp.bfloat16)
        bases = call(stack_kernel, stacked, bases, came, slot, flops=2**26, moved=2**22)
    bases = bases, partner(bases, 0)
    fields = near_count, near, far_u, far_v, near_mask, far_mask
    state, rows, out = call(
        place_kernel,
        (
            shape(8, elems),
            shape(1, elems, dtype=integer),
            shape(devices, 1, 2 * elems + lines * LANES),
        ),
        swap(sent, "blk"), coarse_v, *fields, scalars=(2,),
        scratch=[VMEM((members * (elems // LANES), LANES), jnp.float32)],
    )
    sent = call(
        functools.partial(second_kernel, groups), shape(devices, sent_rows, LANES),
        state, rows, swap(out, ("leaf", "blk")), *bases, coarse_v, *fields, scalars=(6,),
    )
    u, phi = call(
        functools.partial(finish_kernel, groups, width), (shape(1, elems), shape(1, elems)),
        swap(sent, ("leaf", "blk")), *bases, slot, slot_row,
    )
    return u.reshape(elems), phi.reshape(elems)


def solution(mesh):
    each = P(("leaf", "blk"))
    blocks = P(("leaf", "blk"), None, None)
    last = P(None, None, ("leaf", "blk"))
    in_specs = (each,) * 7 + (blocks, each, each, blocks, blocks, each, each, last, last)
    return jax.shard_map(body, mesh=mesh, in_specs=in_specs, out_specs=(each, each), check_vma=False)
```

```python
import functools

import jax
import jax.numpy as jnp
from jax import lax
from jax.experimental import pallas as pl
from jax.experimental.pallas import tpu as pltpu
from jax.sharding import PartitionSpec as P

DAMPING = 0.5
PLATE_RATE = 1.0
TIME_STEP = 0.2

NN = (((1,), (0,)), ((), ()))
NT = (((1,), (1,)), ((), ()))
VMEM = pltpu.VMEM
SMEM = pltpu.SMEM

LANES = 128


def dot(left, right, dims):
    return lax.dot_general(left, right, dims, preferred_element_type=jnp.float32)


def low_matrix(index_row):
    rows = lax.broadcasted_iota(jnp.int32, (LANES, index_row.shape[1]), 0)
    return jnp.where(rows == (index_row & (LANES - 1)), 1.0, 0.0).astype(jnp.bfloat16)


def three_parts(values):
    high = values.astype(jnp.bfloat16).astype(jnp.float32)
    rest = values - high
    middle = rest.astype(jnp.bfloat16).astype(jnp.float32)
    return jnp.concatenate([high, middle, rest - middle], axis=0)


def joined(parts):
    count = parts.shape[0] // 3
    return parts[0:count] + parts[count:2 * count] + parts[2 * count:]


def scattered(values, index_row):
    parts = three_parts(values)
    count = parts.shape[0]
    high = index_row // LANES
    pieces = values.shape[1] // LANES
    left = jnp.concatenate([jnp.where(high == piece, parts, 0.0) for piece in range(pieces)], axis=0)
    moved = dot(left.astype(jnp.bfloat16), low_matrix(index_row), NT)
    return jnp.concatenate(
        [joined(moved[piece * count:(piece + 1) * count]) for piece in range(pieces)], axis=1
    )


def gathered(values, index_row):
    parts = three_parts(values)
    count = parts.shape[0]
    high = index_row // LANES
    pieces = values.shape[1] // LANES
    left = jnp.concatenate(
        [parts[:, piece * LANES:(piece + 1) * LANES] for piece in range(pieces)], axis=0
    )
    moved = dot(left.astype(jnp.bfloat16), low_matrix(index_row), NN)
    total = jnp.zeros((count, index_row.shape[1]), jnp.float32)
    for piece in range(pieces):
        total = jnp.where(high == piece, moved[piece * count:(piece + 1) * count], total)
    return joined(total)


def padded(rows, count):
    missing = count - len(rows)
    if missing:
        rows = rows + [jnp.zeros((missing, rows[0].shape[1]), jnp.float32)]
    return jnp.concatenate(rows, axis=0)


def as_lines(row):
    return jnp.concatenate(
        [row[:, i * LANES:(i + 1) * LANES] for i in range(row.shape[1] // LANES)], axis=0
    )


def peer_lanes(ref, first, members, rows, elem_count):
    width = elem_count // members
    return jnp.concatenate([ref[first + peer, 0:rows, 0:width] for peer in range(members)], axis=1)


def start_copies(sources, targets, sems):
    copies = [
        pltpu.make_async_copy(source, target, sems.at[i])
        for i, (source, target) in enumerate(zip(sources, targets))
    ]
    for copy in copies:
        copy.start()
    return copies


def sort_kernel(members, *refs):
    elem_refs, scalar_refs, weight_refs = refs[:7], refs[7:10], refs[10:14]
    sent_ref, slot_ref, slot_row_ref, near_mask_ref, far_mask_ref = refs[14:19]
    weight_outs, elem_bufs, scalar_bufs, sems = refs[19:23], refs[23:30], refs[30:33], refs[33]
    copies = start_copies(
        [*elem_refs, *scalar_refs, *weight_refs], [*elem_bufs, *scalar_bufs, *weight_outs], sems
    )
    mine = lax.axis_index("leaf")
    elem_count = elem_bufs[0].shape[1]
    peer_rows = elem_count // members
    pieces = elem_count // LANES
    before = lax.broadcasted_iota(jnp.int32, (LANES, LANES), 0)
    after = lax.broadcasted_iota(jnp.int32, (LANES, LANES), 1)
    triangle = jnp.where(before < after, 1.0, 0.0).astype(jnp.bfloat16)
    copies[0].wait()
    local = elem_bufs[0][...] - mine * (members * elem_count)
    target = local // elem_count
    target_row = local - target * elem_count
    peers = lax.broadcasted_iota(jnp.int32, (members, elem_count), 0)
    onehot = jnp.where(peers == target, 1.0, 0.0)
    lines = [onehot[:, i * LANES:(i + 1) * LANES] for i in range(pieces)]
    inside = dot(jnp.concatenate(lines, axis=0).astype(jnp.bfloat16), triangle, NN)
    passed = jnp.zeros((members, 1), jnp.float32)
    ranks = []
    for i, line in enumerate(lines):
        earlier = inside[i * members:(i + 1) * members] + passed
        ranks.append(jnp.sum(earlier * line, axis=0, keepdims=True))
        passed = passed + jnp.sum(line, axis=1, keepdims=True)
    slot = target * peer_rows + jnp.concatenate(ranks, axis=1).astype(jnp.int32)
    slot_ref[...] = slot
    for copy in copies[1:7]:
        copy.wait()
    u, phi, sigma, fric_a, fric_b, dist = (buf[...] for buf in elem_bufs[1:])
    deficit = (PLATE_RATE - jnp.exp(u)).astype(jnp.bfloat16).astype(jnp.float32)
    rows = [u, phi, sigma * fric_a, sigma * fric_b, dist, target_row.astype(jnp.float32), deficit]
    values = scattered(padded(rows, 8), slot)
    slot_row_ref[...] = values[5:6].astype(jnp.int32)
    everyone = jnp.concatenate([as_lines(values[6:7]), as_lines(values[5:6])], axis=0)
    for peer in range(members):
        sent_ref[peer, 0:8, 0:peer_rows] = values[:, peer * peer_rows:(peer + 1) * peer_rows]
        sent_ref[peer, 8:8 + 2 * pieces, :] = everyone

    for copy in copies[7:10]:
        copy.wait()
    near_col, far_col, far_rank = scalar_bufs
    far_slots = far_col.shape[0]
    far_width = far_mask_ref.shape[1] // far_slots
    block = lax.broadcasted_iota(jnp.int32, near_mask_ref.shape[1:], 0)
    for number in range(near_mask_ref.shape[0]):
        near_mask_ref[number] = jnp.where(block == near_col[number], 1.0, 0.0)
    block = lax.broadcasted_iota(jnp.int32, far_mask_ref.shape, 0)
    lane = lax.broadcasted_iota(jnp.int32, far_mask_ref.shape, 1)
    column = jnp.full(far_mask_ref.shape, -1, jnp.int32)
    for number in range(far_slots):
        low = number * far_width
        kept = (lane >= low) & (lane < low + far_rank[number])
        column = jnp.where(kept, far_col[number], column)
    far_mask_ref[...] = jnp.where(block == column, 1.0, 0.0)
    for copy in copies[10:]:
        copy.wait()


def partial_row(deficit, coarse_v_ref):
    wide = jnp.broadcast_to(deficit, (8, deficit.shape[1])).astype(jnp.bfloat16)
    partial = dot(wide, coarse_v_ref[...], NT)[0:1]
    rest = -partial.shape[1] % LANES
    if rest:
        partial = jnp.concatenate([partial, jnp.zeros((1, rest), jnp.float32)], axis=1)
    return partial


def inside_rows(deficits, near_count, near_ref, far_u_ref, far_v_ref, near_mask_ref, far_mask_ref):
    total = jnp.zeros(deficits.shape, jnp.float32)
    for slot in range(near_ref.shape[0]):
        live = jnp.where(slot < near_count[0], 1.0, 0.0)
        source = (deficits * (near_mask_ref[slot] * live)).astype(jnp.bfloat16)
        total = total + dot(source, near_ref[slot], NT)
    project = dot(deficits.astype(jnp.bfloat16), far_v_ref[...], NT) * far_mask_ref[...]
    project = jnp.sum(project, axis=0, keepdims=True)
    project = jnp.broadcast_to(project, (8, project.shape[1])).astype(jnp.bfloat16)
    far = dot(project, far_u_ref[...], NN)
    return jnp.sum(total, axis=0, keepdims=True) + far[0:1]


def coefficients(sums, rank):
    groups, width = len(sums), sums[0].shape[1]
    mine = lax.axis_index("leaf")
    table = padded(sums, -(-groups // 8) * 8)
    lane = lax.broadcasted_iota(jnp.int32, table.shape, 1) // rank
    row = lax.broadcasted_iota(jnp.int32, table.shape, 0)
    table = jnp.where(lane == mine, table, 0.0).astype(jnp.bfloat16)
    across = lax.broadcasted_iota(jnp.int32, (width, width), 0) % rank
    down = lax.broadcasted_iota(jnp.int32, (width, width), 1) % rank
    spread = dot(table, jnp.where(across == down, 1.0, 0.0).astype(jnp.bfloat16), NN)
    weights = jnp.sum(jnp.where(row == mine ^ (lane + 1), spread, 0.0), axis=0, keepdims=True)
    return weights[:, 0:width - rank]


def coarse_all(weights, members, bases_refs):
    row = lax.broadcasted_iota(jnp.int32, (members, weights.shape[1]), 0) ^ lax.axis_index("blk")
    bits = members.bit_length() - 1
    total = jnp.zeros((members, bases_refs[0].shape[1]), jnp.float32)
    for number, ref in enumerate(bases_refs):
        left = []
        for place in range(members // 4):
            source = number
            for bit in range(bits - 2):
                source |= (place >> bit & 1) << (bits - 1 - bit)
            left.append(jnp.where(row == source, weights, 0.0))
        left = jnp.concatenate(left, axis=1).astype(jnp.bfloat16)
        total = total + dot(left, ref[...], NN)
    return total


def pair_kernel(rank, held_ref, came_ref, order_ref, out_ref):
    groups = held_ref.shape[0] // rank
    mine = lax.axis_index("leaf")
    for number, ref in enumerate((held_ref, came_ref)):
        for shift in range(1, groups):
            place = (number * (groups - 1) + shift - 1) * rank
            out_ref[place:place + rank, :] = ref[pl.ds((mine ^ shift) * rank, rank), :]


def stack_kernel(held_ref, came_ref, out_ref):
    count = held_ref.shape[0]
    out_ref[0:count, :] = held_ref[...]
    out_ref[count:2 * count, :] = came_ref[...]


def place_kernel(got_ref, coarse_v_ref, *refs):
    field_refs, state_ref, rows_ref, out_ref, lines_ref = refs[:6], refs[6], refs[7], refs[8], refs[9]
    members = got_ref.shape[0]
    elem_count = state_ref.shape[1]
    pieces = elem_count // LANES
    peer_rows = elem_count // members
    per_line = LANES // peer_rows
    line_block = lax.broadcasted_iota(jnp.int32, (per_line * pieces, LANES), 0) // pieces
    line_piece = lax.broadcasted_iota(jnp.int32, (per_line * pieces, LANES), 0) % pieces
    lane_block = lax.broadcasted_iota(jnp.int32, (per_line * pieces, LANES), 1) // peer_rows
    own_lane = line_block == lane_block
    for line in range(pieces):
        left, right = [], []
        for peer in range(members):
            value = got_ref[peer, 8 + line:9 + line, :]
            row = got_ref[peer, 8 + pieces + line:9 + pieces + line, :].astype(jnp.int32)
            left.append(jnp.where(own_lane & (line_piece == row // LANES), value, 0.0))
            right.append(low_matrix(row))
        left = jnp.concatenate(left, axis=1).astype(jnp.bfloat16)
        count = per_line * pieces
        lines_ref[line * count:(line + 1) * count, :] = dot(left, jnp.concatenate(right, axis=1), NT)
    deficits = jnp.concatenate(
        [lines_ref[pl.ds(piece, members, stride=pieces), :] for piece in range(pieces)], axis=1
    )
    inside = inside_rows(deficits, *field_refs)

    flat = peer_lanes(got_ref, 0, members, 8, elem_count)
    rows = flat[5:6].astype(jnp.int32)
    rows_ref[...] = rows
    state = scattered(flat, rows)
    u, phi, sa, sb, dist = (state[i:i + 1] for i in range(5))
    velocity = jnp.exp(u)
    k1p = (jnp.exp(-phi) - velocity) / dist
    inverse = 1.0 / (sa + DAMPING * velocity)
    u2 = u + TIME_STEP * ((inside - sb * k1p) * inverse)
    factor = TIME_STEP * inverse
    state_ref[...] = jnp.concatenate([u, phi, sa, sb, dist, k1p, u2, factor], axis=0)
    sent = jnp.concatenate([u2, factor, partial_row(state[6:7], coarse_v_ref)], axis=1)
    out_ref[...] = jnp.broadcast_to(sent[None], out_ref.shape)


def second_kernel(groups, state_ref, rows_ref, all_ref, coarse_v_ref, *refs):
    bases_refs, field_refs, sent_ref = refs[:4], refs[4:10], refs[10]
    members, elem_count = refs[8].shape[1], state_ref.shape[1]
    width = coarse_v_ref.shape[0]
    mine, me = lax.axis_index("leaf"), lax.axis_index("blk")
    sums = [
        jnp.sum(
            all_ref[group * members:(group + 1) * members, 0, 2 * elem_count:2 * elem_count + width],
            axis=0, keepdims=True,
        )
        for group in range(groups)
    ]
    weights = coefficients(sums, width // groups)
    own = all_ref[pl.ds(mine * members, members), 0, 0:2 * elem_count]
    coarse = coarse_all(weights, members, bases_refs)
    u2_all = own[:, 0:elem_count] + own[:, elem_count:] * coarse
    deficits = (PLATE_RATE - jnp.exp(u2_all)).astype(jnp.bfloat16).astype(jnp.float32)
    inside = inside_rows(deficits, *field_refs)

    state = state_ref[...]
    u, phi, sa, sb, dist, k1p = (state[i:i + 1] for i in range(6))
    here = lax.broadcasted_iota(jnp.int32, u2_all.shape, 0) == me
    u2 = jnp.sum(jnp.where(here, u2_all, 0.0), axis=0, keepdims=True)
    deficit = jnp.sum(jnp.where(here, deficits, 0.0), axis=0, keepdims=True)
    phi2 = phi + TIME_STEP * k1p
    velocity = jnp.exp(u2)
    k2p = (jnp.exp(-phi2) - velocity) / dist
    inverse = 0.5 * TIME_STEP / (sa + DAMPING * velocity)
    u_next = 0.5 * (u + u2) + (inside - sb * k2p) * inverse
    phi_next = phi + 0.5 * TIME_STEP * (k1p + k2p)
    sent = gathered(padded([u_next, inverse, phi_next], 8), rows_ref[...])
    partial = as_lines(partial_row(deficit, coarse_v_ref))
    peer_rows = elem_count // members
    for device in range(groups * members):
        peer = device % members
        sent_ref[device, 0:3, 0:peer_rows] = sent[0:3, peer * peer_rows:(peer + 1) * peer_rows]
        sent_ref[device, 3:3 + partial.shape[0], :] = partial


def finish_kernel(groups, width, got_ref, slot_ref, slot_row_ref, *refs):
    bases_refs, u_ref, phi_ref = refs[:4], refs[4], refs[5]
    elem_count = slot_ref.shape[1]
    members = got_ref.shape[0] // groups
    sums = []
    for group in range(groups):
        total = jnp.sum(got_ref[group * members:(group + 1) * members], axis=0)
        lines = [total[3 + i:4 + i, :] for i in range(pl.cdiv(width, LANES))]
        sums.append(jnp.concatenate(lines, axis=1)[:, 0:width])
    coarse = coarse_all(coefficients(sums, width // groups), members, bases_refs)
    row = slot_row_ref[...]
    block = lax.broadcasted_iota(jnp.int32, (members, elem_count), 0)
    lane_block = lax.broadcasted_iota(jnp.int32, (members, elem_count), 1) // (elem_count // members)
    rows = gathered(coarse, row)
    found = jnp.sum(jnp.where(block == lane_block, rows, 0.0), axis=0, keepdims=True)
    first = lax.axis_index("leaf") * members
    flat = peer_lanes(got_ref, first, members, 3, elem_count)
    u_next = flat[0:1] + flat[1:2] * found
    out = gathered(padded([u_next, flat[2:3]], 8), slot_ref[...])
    u_ref[...] = out[0:1]
    phi_ref[...] = out[1:2]


def call(kernel, outs, *args, scalars=(), far=(), scratch=(), flops=1000, moved=1000):
    spaces = [SMEM if i in scalars else pl.ANY if i in far else VMEM for i in range(len(args))]
    args = [
        pltpu.with_memory_space_constraint(arg, pltpu.HBM) if i in far else arg
        for i, arg in enumerate(args)
    ]
    return pl.pallas_call(
        kernel,
        out_shape=outs,
        in_specs=[pl.BlockSpec(memory_space=space) for space in spaces],
        out_specs=jax.tree.map(lambda _: pl.BlockSpec(memory_space=VMEM), outs),
        scratch_shapes=list(scratch),
        cost_estimate=pl.CostEstimate(flops=flops, bytes_accessed=moved, transcendentals=0),
        compiler_params=pltpu.CompilerParams(vmem_limit_bytes=32 * 1024 * 1024),
    )(*args)


def shape(*dims, dtype=jnp.float32):
    return jax.ShapeDtypeStruct(dims, dtype)


def body(
    ln_rate,
    log_state,
    sigma,
    fric_a,
    fric_b,
    slip_dist,
    leaf_of_elem,
    near_blocks,
    near_col,
    near_count,
    far_u,
    far_v,
    far_col,
    far_rank,
    coarse_u,
    coarse_v,
):
    members = lax.axis_size("blk")
    elems = ln_rate.shape[0]
    leaf_size = near_blocks.shape[1]
    groups, rank = coarse_v.shape[0], coarse_v.shape[1]
    devices = groups * members
    width = groups * rank
    lines = pl.cdiv(width, LANES)
    sent_rows = 1 << (2 + lines).bit_length()
    integer = jnp.int32

    def swap(value, axes):
        return lax.all_to_all(value, axes, split_axis=0, concat_axis=0, tiled=True)

    def partner(value, bit):
        return lax.ppermute(value, "blk", [(i, i ^ (1 << bit)) for i in range(members)])

    elem_args = [
        value.reshape(1, elems)
        for value in (leaf_of_elem, ln_rate, log_state, sigma, fric_a, fric_b, slip_dist)
    ]
    scalar_args = [near_col, far_col, far_rank]
    weights = [
        near_blocks, far_u.reshape(-1, leaf_size), far_v.reshape(-1, leaf_size),
        coarse_v.reshape(width, elems),
    ]
    far_rows = weights[1].shape[0]
    sent, slot, slot_row, near_mask, far_mask, near, far_u, far_v, coarse_v = call(
        functools.partial(sort_kernel, members),
        (
            shape(members, 8 + 2 * (elems // LANES), LANES),
            shape(1, elems, dtype=integer),
            shape(1, elems, dtype=integer),
            shape(near_blocks.shape[0], members, leaf_size),
            shape(members, far_rows),
            *[shape(*value.shape, dtype=jnp.bfloat16) for value in weights],
        ),
        *elem_args, *scalar_args, *weights, far=range(14),
        scratch=[VMEM(value.shape, value.dtype) for value in elem_args]
        + [SMEM(value.shape, value.dtype) for value in scalar_args]
        + [pltpu.SemaphoreType.DMA((14,))],
    )
    bases = coarse_u.reshape(width, elems)
    top = members.bit_length() - 2
    kept = width - rank
    bases = call(
        functools.partial(pair_kernel, rank), shape(2 * kept, elems, dtype=jnp.bfloat16),
        bases, partner(bases, top), slot, flops=1 << 26, moved=1 << 22,
    )
    for bit in range(top - 1, 1, -1):
        stacked = shape(2 * bases.shape[0], elems, dtype=jnp.bfloat16)
        bases = call(stack_kernel, stacked, bases, partner(bases, bit))
    across = partner(bases, 0)
    bases = bases, across, partner(bases, 1), partner(across, 1)
    fields = near_count, near, far_u, far_v, near_mask, far_mask
    state, rows, out = call(
        place_kernel,
        (
            shape(8, elems),
            shape(1, elems, dtype=integer),
            shape(devices, 1, 2 * elems + lines * LANES),
        ),
        swap(sent, "blk"), coarse_v, *fields, scalars=(2,),
        scratch=[VMEM((members * (elems // LANES), LANES), jnp.float32)],
    )
    sent = call(
        functools.partial(second_kernel, groups), shape(devices, sent_rows, LANES),
        state, rows, swap(out, ("leaf", "blk")), coarse_v, *bases, *fields, scalars=(8,),
    )
    u, phi = call(
        functools.partial(finish_kernel, groups, width), (shape(1, elems), shape(1, elems)),
        swap(sent, ("leaf", "blk")), slot, slot_row, *bases,
    )
    return u.reshape(elems), phi.reshape(elems)


def solution(mesh):
    each = P(("leaf", "blk"))
    blocks = P(("leaf", "blk"), None, None)
    last = P(None, None, ("leaf", "blk"))
    in_specs = (each,) * 7 + (blocks, each, each, blocks, blocks, each, each, last, last)
    return jax.shard_map(body, mesh=mesh, in_specs=in_specs, out_specs=(each, each), check_vma=False)
```

```python
import functools

import jax
import jax.numpy as jnp
from jax import lax
from jax.experimental import pallas as pl
from jax.experimental.pallas import tpu as pltpu
from jax.sharding import PartitionSpec as P

DAMPING = 0.5
PLATE_RATE = 1.0
TIME_STEP = 0.2

NN = (((1,), (0,)), ((), ()))
NT = (((1,), (1,)), ((), ()))
VMEM = pltpu.VMEM
SMEM = pltpu.SMEM

LANES = 128


def dot(left, right, dims):
    return lax.dot_general(left, right, dims, preferred_element_type=jnp.float32)


def low_matrix(index_row):
    rows = lax.broadcasted_iota(jnp.int32, (LANES, index_row.shape[1]), 0)
    return jnp.where(rows == (index_row & (LANES - 1)), 1.0, 0.0).astype(jnp.bfloat16)


def three_parts(values):
    high = values.astype(jnp.bfloat16).astype(jnp.float32)
    rest = values - high
    middle = rest.astype(jnp.bfloat16).astype(jnp.float32)
    return jnp.concatenate([high, middle, rest - middle], axis=0)


def joined(parts):
    count = parts.shape[0] // 3
    return parts[0:count] + parts[count:2 * count] + parts[2 * count:]


def scattered(values, index_row):
    parts = three_parts(values)
    count = parts.shape[0]
    high = index_row // LANES
    pieces = values.shape[1] // LANES
    left = jnp.concatenate([jnp.where(high == piece, parts, 0.0) for piece in range(pieces)], axis=0)
    moved = dot(left.astype(jnp.bfloat16), low_matrix(index_row), NT)
    return jnp.concatenate(
        [joined(moved[piece * count:(piece + 1) * count]) for piece in range(pieces)], axis=1
    )


def gathered(values, index_row):
    parts = three_parts(values)
    count = parts.shape[0]
    high = index_row // LANES
    pieces = values.shape[1] // LANES
    left = jnp.concatenate(
        [parts[:, piece * LANES:(piece + 1) * LANES] for piece in range(pieces)], axis=0
    )
    moved = dot(left.astype(jnp.bfloat16), low_matrix(index_row), NN)
    total = jnp.zeros((count, index_row.shape[1]), jnp.float32)
    for piece in range(pieces):
        total = jnp.where(high == piece, moved[piece * count:(piece + 1) * count], total)
    return joined(total)


def padded(rows, count):
    missing = count - len(rows)
    if missing:
        rows = rows + [jnp.zeros((missing, rows[0].shape[1]), jnp.float32)]
    return jnp.concatenate(rows, axis=0)


def as_lines(row):
    return jnp.concatenate(
        [row[:, i * LANES:(i + 1) * LANES] for i in range(row.shape[1] // LANES)], axis=0
    )


def peer_lanes(ref, first, members, rows, elem_count):
    width = elem_count // members
    return jnp.concatenate([ref[first + peer, 0:rows, 0:width] for peer in range(members)], axis=1)


def start_copies(sources, targets, sems):
    copies = [
        pltpu.make_async_copy(source, target, sems.at[i])
        for i, (source, target) in enumerate(zip(sources, targets))
    ]
    for copy in copies:
        copy.start()
    return copies


def sort_kernel(members, *refs):
    elem_refs, scalar_refs, weight_refs = refs[:7], refs[7:10], refs[10:14]
    sent_ref, slot_ref, slot_row_ref, near_mask_ref, far_mask_ref = refs[14:19]
    weight_outs, elem_bufs, scalar_bufs, sems = refs[19:23], refs[23:30], refs[30:33], refs[33]
    copies = start_copies(
        [*elem_refs, *scalar_refs, *weight_refs], [*elem_bufs, *scalar_bufs, *weight_outs], sems
    )
    mine = lax.axis_index("leaf")
    elem_count = elem_bufs[0].shape[1]
    peer_rows = elem_count // members
    pieces = elem_count // LANES
    before = lax.broadcasted_iota(jnp.int32, (LANES, LANES), 0)
    after = lax.broadcasted_iota(jnp.int32, (LANES, LANES), 1)
    triangle = jnp.where(before < after, 1.0, 0.0).astype(jnp.bfloat16)
    copies[0].wait()
    local = elem_bufs[0][...] - mine * (members * elem_count)
    target = local // elem_count
    target_row = local - target * elem_count
    peers = lax.broadcasted_iota(jnp.int32, (members, elem_count), 0)
    onehot = jnp.where(peers == target, 1.0, 0.0)
    lines = [onehot[:, i * LANES:(i + 1) * LANES] for i in range(pieces)]
    inside = dot(jnp.concatenate(lines, axis=0).astype(jnp.bfloat16), triangle, NN)
    passed = jnp.zeros((members, 1), jnp.float32)
    ranks = []
    for i, line in enumerate(lines):
        earlier = inside[i * members:(i + 1) * members] + passed
        ranks.append(jnp.sum(earlier * line, axis=0, keepdims=True))
        passed = passed + jnp.sum(line, axis=1, keepdims=True)
    slot = target * peer_rows + jnp.concatenate(ranks, axis=1).astype(jnp.int32)
    slot_ref[...] = slot
    for copy in copies[1:7]:
        copy.wait()
    u, phi, sigma, fric_a, fric_b, dist = (buf[...] for buf in elem_bufs[1:])
    deficit = (PLATE_RATE - jnp.exp(u)).astype(jnp.bfloat16).astype(jnp.float32)
    rows = [u, phi, sigma * fric_a, sigma * fric_b, dist, target_row.astype(jnp.float32), deficit]
    values = scattered(padded(rows, 8), slot)
    slot_row_ref[...] = values[5:6].astype(jnp.int32)
    everyone = jnp.concatenate([as_lines(values[6:7]), as_lines(values[5:6])], axis=0)
    for peer in range(members):
        sent_ref[peer, 0:8, 0:peer_rows] = values[:, peer * peer_rows:(peer + 1) * peer_rows]
        sent_ref[peer, 8:8 + 2 * pieces, :] = everyone

    for copy in copies[7:10]:
        copy.wait()
    near_col, far_col, far_rank = scalar_bufs
    far_slots = far_col.shape[0]
    far_width = far_mask_ref.shape[1] // far_slots
    block = lax.broadcasted_iota(jnp.int32, near_mask_ref.shape[1:], 0)
    for number in range(near_mask_ref.shape[0]):
        near_mask_ref[number] = jnp.where(block == near_col[number], 1.0, 0.0)
    block = lax.broadcasted_iota(jnp.int32, far_mask_ref.shape, 0)
    lane = lax.broadcasted_iota(jnp.int32, far_mask_ref.shape, 1)
    column = jnp.full(far_mask_ref.shape, -1, jnp.int32)
    for number in range(far_slots):
        low = number * far_width
        kept = (lane >= low) & (lane < low + far_rank[number])
        column = jnp.where(kept, far_col[number], column)
    far_mask_ref[...] = jnp.where(block == column, 1.0, 0.0)
    for copy in copies[10:]:
        copy.wait()


def partial_row(deficit, coarse_v_ref):
    wide = jnp.broadcast_to(deficit, (8, deficit.shape[1])).astype(jnp.bfloat16)
    partial = dot(wide, coarse_v_ref[...], NT)[0:1]
    rest = -partial.shape[1] % LANES
    if rest:
        partial = jnp.concatenate([partial, jnp.zeros((1, rest), jnp.float32)], axis=1)
    return partial


def inside_rows(deficits, near_count, near_ref, far_u_ref, far_v_ref, near_mask_ref, far_mask_ref):
    total = jnp.zeros(deficits.shape, jnp.float32)
    for slot in range(near_ref.shape[0]):
        live = jnp.where(slot < near_count[0], 1.0, 0.0)
        source = (deficits * (near_mask_ref[slot] * live)).astype(jnp.bfloat16)
        total = total + dot(source, near_ref[slot], NT)
    project = dot(deficits.astype(jnp.bfloat16), far_v_ref[...], NT) * far_mask_ref[...]
    project = jnp.sum(project, axis=0, keepdims=True)
    project = jnp.broadcast_to(project, (8, project.shape[1])).astype(jnp.bfloat16)
    far = dot(project, far_u_ref[...], NN)
    return jnp.sum(total, axis=0, keepdims=True) + far[0:1]


def coefficients(sums, rank):
    groups, width = len(sums), sums[0].shape[1]
    mine = lax.axis_index("leaf")
    table = padded(sums, -(-groups // 8) * 8)
    lane = lax.broadcasted_iota(jnp.int32, table.shape, 1) // rank
    row = lax.broadcasted_iota(jnp.int32, table.shape, 0)
    table = jnp.where(lane == mine, table, 0.0).astype(jnp.bfloat16)
    across = lax.broadcasted_iota(jnp.int32, (width, width), 0) % rank
    down = lax.broadcasted_iota(jnp.int32, (width, width), 1) % rank
    spread = dot(table, jnp.where(across == down, 1.0, 0.0).astype(jnp.bfloat16), NN)
    weights = jnp.sum(jnp.where(row == mine ^ (lane + 1), spread, 0.0), axis=0, keepdims=True)
    return weights[:, 0:width - rank]


def coarse_all(weights, members, bases_refs):
    row = lax.broadcasted_iota(jnp.int32, (members, weights.shape[1]), 0) ^ lax.axis_index("blk")
    bits = members.bit_length() - 1
    total = jnp.zeros((members, bases_refs[0].shape[1]), jnp.float32)
    for number, ref in enumerate(bases_refs):
        left = []
        for place in range(members // 4):
            source = number
            for bit in range(bits - 2):
                source |= (place >> bit & 1) << (bits - 1 - bit)
            left.append(jnp.where(row == source, weights, 0.0))
        left = jnp.concatenate(left, axis=1).astype(jnp.bfloat16)
        total = total + dot(left, ref[...], NN)
    return total


def pair_kernel(rank, held_ref, came_ref, order_ref, out_ref):
    groups = held_ref.shape[0] // rank
    mine = lax.axis_index("leaf")
    for number, ref in enumerate((held_ref, came_ref)):
        for shift in range(1, groups):
            place = (number * (groups - 1) + shift - 1) * rank
            out_ref[place:place + rank, :] = ref[pl.ds((mine ^ shift) * rank, rank), :]


def stack_kernel(held_ref, came_ref, out_ref):
    count = held_ref.shape[0]
    out_ref[0:count, :] = held_ref[...]
    out_ref[count:2 * count, :] = came_ref[...]


def place_kernel(got_ref, coarse_v_ref, early_ref, *refs):
    field_refs, state_ref, rows_ref, out_ref, lines_ref = refs[:6], refs[6], refs[7], refs[8], refs[9]
    members = got_ref.shape[0]
    elem_count = state_ref.shape[1]
    pieces = elem_count // LANES
    peer_rows = elem_count // members
    per_line = LANES // peer_rows
    line_block = lax.broadcasted_iota(jnp.int32, (per_line * pieces, LANES), 0) // pieces
    line_piece = lax.broadcasted_iota(jnp.int32, (per_line * pieces, LANES), 0) % pieces
    lane_block = lax.broadcasted_iota(jnp.int32, (per_line * pieces, LANES), 1) // peer_rows
    own_lane = line_block == lane_block
    for line in range(pieces):
        left, right = [], []
        for peer in range(members):
            value = got_ref[peer, 8 + line:9 + line, :]
            row = got_ref[peer, 8 + pieces + line:9 + pieces + line, :].astype(jnp.int32)
            left.append(jnp.where(own_lane & (line_piece == row // LANES), value, 0.0))
            right.append(low_matrix(row))
        left = jnp.concatenate(left, axis=1).astype(jnp.bfloat16)
        count = per_line * pieces
        lines_ref[line * count:(line + 1) * count, :] = dot(left, jnp.concatenate(right, axis=1), NT)
    deficits = jnp.concatenate(
        [lines_ref[pl.ds(piece, members, stride=pieces), :] for piece in range(pieces)], axis=1
    )
    inside = inside_rows(deficits, *field_refs)

    flat = peer_lanes(got_ref, 0, members, 8, elem_count)
    rows = flat[5:6].astype(jnp.int32)
    rows_ref[...] = rows
    state = scattered(flat, rows)
    u, phi, sa, sb, dist = (state[i:i + 1] for i in range(5))
    velocity = jnp.exp(u)
    k1p = (jnp.exp(-phi) - velocity) / dist
    inverse = 1.0 / (sa + DAMPING * velocity)
    u2 = u + TIME_STEP * ((inside - sb * k1p) * inverse)
    factor = TIME_STEP * inverse
    state_ref[...] = jnp.concatenate([u, phi, sa, sb, dist, k1p, u2, factor], axis=0)
    sent = jnp.concatenate([u2, factor, partial_row(state[6:7], coarse_v_ref)], axis=1)
    out_ref[...] = jnp.broadcast_to(sent[None], out_ref.shape)


def second_kernel(groups, state_ref, rows_ref, all_ref, coarse_v_ref, *refs):
    bases_refs, field_refs, sent_ref = refs[:4], refs[4:10], refs[10]
    members, elem_count = refs[8].shape[1], state_ref.shape[1]
    width = coarse_v_ref.shape[0]
    mine, me = lax.axis_index("leaf"), lax.axis_index("blk")
    sums = [
        jnp.sum(
            all_ref[group * members:(group + 1) * members, 0, 2 * elem_count:2 * elem_count + width],
            axis=0, keepdims=True,
        )
        for group in range(groups)
    ]
    weights = coefficients(sums, width // groups)
    own = all_ref[pl.ds(mine * members, members), 0, 0:2 * elem_count]
    coarse = coarse_all(weights, members, bases_refs)
    u2_all = own[:, 0:elem_count] + own[:, elem_count:] * coarse
    deficits = (PLATE_RATE - jnp.exp(u2_all)).astype(jnp.bfloat16).astype(jnp.float32)
    inside = inside_rows(deficits, *field_refs)

    state = state_ref[...]
    u, phi, sa, sb, dist, k1p = (state[i:i + 1] for i in range(6))
    here = lax.broadcasted_iota(jnp.int32, u2_all.shape, 0) == me
    u2 = jnp.sum(jnp.where(here, u2_all, 0.0), axis=0, keepdims=True)
    deficit = jnp.sum(jnp.where(here, deficits, 0.0), axis=0, keepdims=True)
    phi2 = phi + TIME_STEP * k1p
    velocity = jnp.exp(u2)
    k2p = (jnp.exp(-phi2) - velocity) / dist
    inverse = 0.5 * TIME_STEP / (sa + DAMPING * velocity)
    u_next = 0.5 * (u + u2) + (inside - sb * k2p) * inverse
    phi_next = phi + 0.5 * TIME_STEP * (k1p + k2p)
    sent = gathered(padded([u_next, inverse, phi_next], 8), rows_ref[...])
    partial = as_lines(partial_row(deficit, coarse_v_ref))
    peer_rows = elem_count // members
    for device in range(groups * members):
        peer = device % members
        sent_ref[device, 0:3, 0:peer_rows] = sent[0:3, peer * peer_rows:(peer + 1) * peer_rows]
        sent_ref[device, 3:3 + partial.shape[0], :] = partial


def finish_kernel(groups, width, got_ref, slot_ref, slot_row_ref, *refs):
    bases_refs, u_ref, phi_ref = refs[:4], refs[4], refs[5]
    elem_count = slot_ref.shape[1]
    members = got_ref.shape[0] // groups
    sums = []
    for group in range(groups):
        total = jnp.sum(got_ref[group * members:(group + 1) * members], axis=0)
        lines = [total[3 + i:4 + i, :] for i in range(pl.cdiv(width, LANES))]
        sums.append(jnp.concatenate(lines, axis=1)[:, 0:width])
    coarse = coarse_all(coefficients(sums, width // groups), members, bases_refs)
    row = slot_row_ref[...]
    block = lax.broadcasted_iota(jnp.int32, (members, elem_count), 0)
    lane_block = lax.broadcasted_iota(jnp.int32, (members, elem_count), 1) // (elem_count // members)
    rows = gathered(coarse, row)
    found = jnp.sum(jnp.where(block == lane_block, rows, 0.0), axis=0, keepdims=True)
    first = lax.axis_index("leaf") * members
    flat = peer_lanes(got_ref, first, members, 3, elem_count)
    u_next = flat[0:1] + flat[1:2] * found
    out = gathered(padded([u_next, flat[2:3]], 8), slot_ref[...])
    u_ref[...] = out[0:1]
    phi_ref[...] = out[1:2]


def call(kernel, outs, *args, scalars=(), far=(), scratch=(), flops=1000, moved=1000):
    spaces = [SMEM if i in scalars else pl.ANY if i in far else VMEM for i in range(len(args))]
    args = [
        pltpu.with_memory_space_constraint(arg, pltpu.HBM) if i in far else arg
        for i, arg in enumerate(args)
    ]
    return pl.pallas_call(
        kernel,
        out_shape=outs,
        in_specs=[pl.BlockSpec(memory_space=space) for space in spaces],
        out_specs=jax.tree.map(lambda _: pl.BlockSpec(memory_space=VMEM), outs),
        scratch_shapes=list(scratch),
        cost_estimate=pl.CostEstimate(flops=flops, bytes_accessed=moved, transcendentals=0),
        compiler_params=pltpu.CompilerParams(vmem_limit_bytes=32 * 1024 * 1024),
    )(*args)


def shape(*dims, dtype=jnp.float32):
    return jax.ShapeDtypeStruct(dims, dtype)


def body(
    ln_rate,
    log_state,
    sigma,
    fric_a,
    fric_b,
    slip_dist,
    leaf_of_elem,
    near_blocks,
    near_col,
    near_count,
    far_u,
    far_v,
    far_col,
    far_rank,
    coarse_u,
    coarse_v,
):
    members = lax.axis_size("blk")
    elems = ln_rate.shape[0]
    leaf_size = near_blocks.shape[1]
    groups, rank = coarse_v.shape[0], coarse_v.shape[1]
    devices = groups * members
    width = groups * rank
    lines = pl.cdiv(width, LANES)
    sent_rows = 1 << (2 + lines).bit_length()
    integer = jnp.int32

    def swap(value, axes):
        return lax.all_to_all(value, axes, split_axis=0, concat_axis=0, tiled=True)

    def partner(value, bit):
        return lax.ppermute(value, "blk", [(i, i ^ (1 << bit)) for i in range(members)])

    elem_args = [
        value.reshape(1, elems)
        for value in (leaf_of_elem, ln_rate, log_state, sigma, fric_a, fric_b, slip_dist)
    ]
    scalar_args = [near_col, far_col, far_rank]
    weights = [
        near_blocks, far_u.reshape(-1, leaf_size), far_v.reshape(-1, leaf_size),
        coarse_v.reshape(width, elems),
    ]
    far_rows = weights[1].shape[0]
    sent, slot, slot_row, near_mask, far_mask, near, far_u, far_v, coarse_v = call(
        functools.partial(sort_kernel, members),
        (
            shape(members, 8 + 2 * (elems // LANES), LANES),
            shape(1, elems, dtype=integer),
            shape(1, elems, dtype=integer),
            shape(near_blocks.shape[0], members, leaf_size),
            shape(members, far_rows),
            *[shape(*value.shape, dtype=jnp.bfloat16) for value in weights],
        ),
        *elem_args, *scalar_args, *weights, far=range(14),
        scratch=[VMEM(value.shape, value.dtype) for value in elem_args]
        + [SMEM(value.shape, value.dtype) for value in scalar_args]
        + [pltpu.SemaphoreType.DMA((14,))],
    )
    bases = coarse_u.reshape(width, elems)
    top = members.bit_length() - 2
    kept = width - rank
    early = bases = call(
        functools.partial(pair_kernel, rank), shape(2 * kept, elems, dtype=jnp.bfloat16),
        bases, partner(bases, top), slot, flops=1 << 26, moved=1 << 22,
    )
    for bit in range(top - 1, 1, -1):
        stacked = shape(2 * bases.shape[0], elems, dtype=jnp.bfloat16)
        bases = call(stack_kernel, stacked, bases, partner(bases, bit))
    across = partner(bases, 0)
    bases = bases, across, partner(bases, 1), partner(across, 1)
    fields = near_count, near, far_u, far_v, near_mask, far_mask
    state, rows, out = call(
        place_kernel,
        (
            shape(8, elems),
            shape(1, elems, dtype=integer),
            shape(devices, 1, 2 * elems + lines * LANES),
        ),
        swap(sent, "blk"), coarse_v, early, *fields, scalars=(3,),
        scratch=[VMEM((members * (elems // LANES), LANES), jnp.float32)],
    )
    sent = call(
        functools.partial(second_kernel, groups), shape(devices, sent_rows, LANES),
        state, rows, swap(out, ("leaf", "blk")), coarse_v, *bases, *fields, scalars=(8,),
    )
    u, phi = call(
        functools.partial(finish_kernel, groups, width), (shape(1, elems), shape(1, elems)),
        swap(sent, ("leaf", "blk")), slot, slot_row, *bases,
    )
    return u.reshape(elems), phi.reshape(elems)


def solution(mesh):
    each = P(("leaf", "blk"))
    blocks = P(("leaf", "blk"), None, None)
    last = P(None, None, ("leaf", "blk"))
    in_specs = (each,) * 7 + (blocks, each, each, blocks, blocks, each, each, last, last)
    return jax.shard_map(body, mesh=mesh, in_specs=in_specs, out_specs=(each, each), check_vma=False)
```

```python
import functools

import jax
import jax.numpy as jnp
from jax import lax
from jax.experimental import pallas as pl
from jax.experimental.pallas import tpu as pltpu
from jax.sharding import PartitionSpec as P

DAMPING = 0.5
PLATE_RATE = 1.0
TIME_STEP = 0.2

NN = (((1,), (0,)), ((), ()))
NT = (((1,), (1,)), ((), ()))
VMEM = pltpu.VMEM
SMEM = pltpu.SMEM

LANES = 128


def dot(left, right, dims):
    return lax.dot_general(left, right, dims, preferred_element_type=jnp.float32)


def low_matrix(index_row):
    rows = lax.broadcasted_iota(jnp.int32, (LANES, index_row.shape[1]), 0)
    return jnp.where(rows == (index_row & (LANES - 1)), 1.0, 0.0).astype(jnp.bfloat16)


def three_parts(values):
    high = values.astype(jnp.bfloat16).astype(jnp.float32)
    rest = values - high
    middle = rest.astype(jnp.bfloat16).astype(jnp.float32)
    return jnp.concatenate([high, middle, rest - middle], axis=0)


def joined(parts):
    count = parts.shape[0] // 3
    return parts[0:count] + parts[count:2 * count] + parts[2 * count:]


def scattered(values, index_row):
    parts = three_parts(values)
    count = parts.shape[0]
    high = index_row // LANES
    pieces = values.shape[1] // LANES
    left = jnp.concatenate([jnp.where(high == piece, parts, 0.0) for piece in range(pieces)], axis=0)
    moved = dot(left.astype(jnp.bfloat16), low_matrix(index_row), NT)
    return jnp.concatenate(
        [joined(moved[piece * count:(piece + 1) * count]) for piece in range(pieces)], axis=1
    )


def gathered(values, index_row):
    parts = three_parts(values)
    count = parts.shape[0]
    high = index_row // LANES
    pieces = values.shape[1] // LANES
    left = jnp.concatenate(
        [parts[:, piece * LANES:(piece + 1) * LANES] for piece in range(pieces)], axis=0
    )
    moved = dot(left.astype(jnp.bfloat16), low_matrix(index_row), NN)
    total = jnp.zeros((count, index_row.shape[1]), jnp.float32)
    for piece in range(pieces):
        total = jnp.where(high == piece, moved[piece * count:(piece + 1) * count], total)
    return joined(total)


def padded(rows, count):
    missing = count - len(rows)
    if missing:
        rows = rows + [jnp.zeros((missing, rows[0].shape[1]), jnp.float32)]
    return jnp.concatenate(rows, axis=0)


def as_lines(row):
    return jnp.concatenate(
        [row[:, i * LANES:(i + 1) * LANES] for i in range(row.shape[1] // LANES)], axis=0
    )


def peer_lanes(ref, first, members, rows, elem_count):
    width = elem_count // members
    return jnp.concatenate([ref[first + peer, 0:rows, 0:width] for peer in range(members)], axis=1)


def start_copies(sources, targets, sems):
    copies = [
        pltpu.make_async_copy(source, target, sems.at[i])
        for i, (source, target) in enumerate(zip(sources, targets))
    ]
    for copy in copies:
        copy.start()
    return copies


def sort_kernel(members, *refs):
    elem_refs, scalar_refs, weight_refs = refs[:7], refs[7:10], refs[10:14]
    sent_ref, slot_ref, slot_row_ref, near_mask_ref, far_mask_ref = refs[14:19]
    weight_outs, elem_bufs, scalar_bufs, sems = refs[19:23], refs[23:30], refs[30:33], refs[33]
    copies = start_copies(
        [*elem_refs, *scalar_refs, *weight_refs], [*elem_bufs, *scalar_bufs, *weight_outs], sems
    )
    mine = lax.axis_index("leaf")
    elem_count = elem_bufs[0].shape[1]
    peer_rows = elem_count // members
    pieces = elem_count // LANES
    before = lax.broadcasted_iota(jnp.int32, (LANES, LANES), 0)
    after = lax.broadcasted_iota(jnp.int32, (LANES, LANES), 1)
    triangle = jnp.where(before < after, 1.0, 0.0).astype(jnp.bfloat16)
    copies[0].wait()
    local = elem_bufs[0][...] - mine * (members * elem_count)
    target = local // elem_count
    target_row = local - target * elem_count
    peers = lax.broadcasted_iota(jnp.int32, (members, elem_count), 0)
    onehot = jnp.where(peers == target, 1.0, 0.0)
    lines = [onehot[:, i * LANES:(i + 1) * LANES] for i in range(pieces)]
    inside = dot(jnp.concatenate(lines, axis=0).astype(jnp.bfloat16), triangle, NN)
    passed = jnp.zeros((members, 1), jnp.float32)
    ranks = []
    for i, line in enumerate(lines):
        earlier = inside[i * members:(i + 1) * members] + passed
        ranks.append(jnp.sum(earlier * line, axis=0, keepdims=True))
        passed = passed + jnp.sum(line, axis=1, keepdims=True)
    slot = target * peer_rows + jnp.concatenate(ranks, axis=1).astype(jnp.int32)
    slot_ref[...] = slot
    for copy in copies[1:7]:
        copy.wait()
    u, phi, sigma, fric_a, fric_b, dist = (buf[...] for buf in elem_bufs[1:])
    deficit = (PLATE_RATE - jnp.exp(u)).astype(jnp.bfloat16).astype(jnp.float32)
    rows = [u, phi, sigma * fric_a, sigma * fric_b, dist, target_row.astype(jnp.float32), deficit]
    values = scattered(padded(rows, 8), slot)
    slot_row_ref[...] = values[5:6].astype(jnp.int32)
    everyone = jnp.concatenate([as_lines(values[6:7]), as_lines(values[5:6])], axis=0)
    for peer in range(members):
        sent_ref[peer, 0:8, 0:peer_rows] = values[:, peer * peer_rows:(peer + 1) * peer_rows]
        sent_ref[peer, 8:8 + 2 * pieces, :] = everyone

    for copy in copies[7:10]:
        copy.wait()
    near_col, far_col, far_rank = scalar_bufs
    far_slots = far_col.shape[0]
    far_width = far_mask_ref.shape[1] // far_slots
    block = lax.broadcasted_iota(jnp.int32, near_mask_ref.shape[1:], 0)
    for number in range(near_mask_ref.shape[0]):
        near_mask_ref[number] = jnp.where(block == near_col[number], 1.0, 0.0)
    block = lax.broadcasted_iota(jnp.int32, far_mask_ref.shape, 0)
    lane = lax.broadcasted_iota(jnp.int32, far_mask_ref.shape, 1)
    column = jnp.full(far_mask_ref.shape, -1, jnp.int32)
    for number in range(far_slots):
        low = number * far_width
        kept = (lane >= low) & (lane < low + far_rank[number])
        column = jnp.where(kept, far_col[number], column)
    far_mask_ref[...] = jnp.where(block == column, 1.0, 0.0)
    for copy in copies[10:]:
        copy.wait()


def partial_row(deficit, coarse_v_ref):
    wide = jnp.broadcast_to(deficit, (8, deficit.shape[1])).astype(jnp.bfloat16)
    partial = dot(wide, coarse_v_ref[...], NT)[0:1]
    rest = -partial.shape[1] % LANES
    if rest:
        partial = jnp.concatenate([partial, jnp.zeros((1, rest), jnp.float32)], axis=1)
    return partial


def inside_rows(deficits, near_count, near_ref, far_u_ref, far_v_ref, near_mask_ref, far_mask_ref):
    total = jnp.zeros(deficits.shape, jnp.float32)
    for slot in range(near_ref.shape[0]):
        live = jnp.where(slot < near_count[0], 1.0, 0.0)
        source = (deficits * (near_mask_ref[slot] * live)).astype(jnp.bfloat16)
        total = total + dot(source, near_ref[slot], NT)
    project = dot(deficits.astype(jnp.bfloat16), far_v_ref[...], NT) * far_mask_ref[...]
    project = jnp.sum(project, axis=0, keepdims=True)
    project = jnp.broadcast_to(project, (8, project.shape[1])).astype(jnp.bfloat16)
    far = dot(project, far_u_ref[...], NN)
    return jnp.sum(total, axis=0, keepdims=True) + far[0:1]


def coefficients(sums, rank):
    groups, width = len(sums), sums[0].shape[1]
    mine = lax.axis_index("leaf")
    table = padded(sums, -(-groups // 8) * 8)
    lane = lax.broadcasted_iota(jnp.int32, table.shape, 1) // rank
    row = lax.broadcasted_iota(jnp.int32, table.shape, 0)
    table = jnp.where(lane == mine, table, 0.0).astype(jnp.bfloat16)
    across = lax.broadcasted_iota(jnp.int32, (width, width), 0) % rank
    down = lax.broadcasted_iota(jnp.int32, (width, width), 1) % rank
    spread = dot(table, jnp.where(across == down, 1.0, 0.0).astype(jnp.bfloat16), NN)
    weights = jnp.sum(jnp.where(row == mine ^ (lane + 1), spread, 0.0), axis=0, keepdims=True)
    return weights[:, 0:width - rank]


def coarse_all(weights, members, bases_refs):
    row = lax.broadcasted_iota(jnp.int32, (members, weights.shape[1]), 0) ^ lax.axis_index("blk")
    bits = members.bit_length() - 1
    total = jnp.zeros((members, bases_refs[0].shape[1]), jnp.float32)
    for number, ref in enumerate(bases_refs):
        left = []
        for place in range(members // 2):
            source = number
            for bit in range(bits - 1):
                source |= (place >> bit & 1) << (bits - 1 - bit)
            left.append(jnp.where(row == source, weights, 0.0))
        left = jnp.concatenate(left, axis=1).astype(jnp.bfloat16)
        total = total + dot(left, ref[...], NN)
    return total


def pair_kernel(rank, held_ref, came_ref, order_ref, out_ref):
    groups = held_ref.shape[0] // rank
    mine = lax.axis_index("leaf")
    for number, ref in enumerate((held_ref, came_ref)):
        for shift in range(1, groups):
            place = (number * (groups - 1) + shift - 1) * rank
            out_ref[place:place + rank, :] = ref[pl.ds((mine ^ shift) * rank, rank), :]


def stack_kernel(held_ref, came_ref, out_ref):
    count = held_ref.shape[0]
    out_ref[0:count, :] = held_ref[...]
    out_ref[count:2 * count, :] = came_ref[...]


def place_kernel(got_ref, coarse_v_ref, *refs):
    field_refs, state_ref, rows_ref, out_ref, lines_ref = refs[:6], refs[6], refs[7], refs[8], refs[9]
    members = got_ref.shape[0]
    elem_count = state_ref.shape[1]
    pieces = elem_count // LANES
    peer_rows = elem_count // members
    per_line = LANES // peer_rows
    line_block = lax.broadcasted_iota(jnp.int32, (per_line * pieces, LANES), 0) // pieces
    line_piece = lax.broadcasted_iota(jnp.int32, (per_line * pieces, LANES), 0) % pieces
    lane_block = lax.broadcasted_iota(jnp.int32, (per_line * pieces, LANES), 1) // peer_rows
    own_lane = line_block == lane_block
    for line in range(pieces):
        left, right = [], []
        for peer in range(members):
            value = got_ref[peer, 8 + line:9 + line, :]
            row = got_ref[peer, 8 + pieces + line:9 + pieces + line, :].astype(jnp.int32)
            left.append(jnp.where(own_lane & (line_piece == row // LANES), value, 0.0))
            right.append(low_matrix(row))
        left = jnp.concatenate(left, axis=1).astype(jnp.bfloat16)
        count = per_line * pieces
        lines_ref[line * count:(line + 1) * count, :] = dot(left, jnp.concatenate(right, axis=1), NT)
    deficits = jnp.concatenate(
        [lines_ref[pl.ds(piece, members, stride=pieces), :] for piece in range(pieces)], axis=1
    )
    inside = inside_rows(deficits, *field_refs)

    flat = peer_lanes(got_ref, 0, members, 8, elem_count)
    rows = flat[5:6].astype(jnp.int32)
    rows_ref[...] = rows
    state = scattered(flat, rows)
    u, phi, sa, sb, dist = (state[i:i + 1] for i in range(5))
    velocity = jnp.exp(u)
    k1p = (jnp.exp(-phi) - velocity) / dist
    inverse = 1.0 / (sa + DAMPING * velocity)
    u2 = u + TIME_STEP * ((inside - sb * k1p) * inverse)
    factor = TIME_STEP * inverse
    state_ref[...] = jnp.concatenate([u, phi, sa, sb, dist, k1p, u2, factor], axis=0)
    sent = jnp.concatenate([u2, factor, partial_row(state[6:7], coarse_v_ref)], axis=1)
    out_ref[...] = jnp.broadcast_to(sent[None], out_ref.shape)


def second_kernel(groups, state_ref, rows_ref, all_ref, coarse_v_ref, *refs):
    bases_refs, field_refs, sent_ref = refs[:2], refs[2:8], refs[8]
    members, elem_count = refs[6].shape[1], state_ref.shape[1]
    width = coarse_v_ref.shape[0]
    mine, me = lax.axis_index("leaf"), lax.axis_index("blk")
    sums = [
        jnp.sum(
            all_ref[group * members:(group + 1) * members, 0, 2 * elem_count:2 * elem_count + width],
            axis=0, keepdims=True,
        )
        for group in range(groups)
    ]
    weights = coefficients(sums, width // groups)
    own = all_ref[pl.ds(mine * members, members), 0, 0:2 * elem_count]
    coarse = coarse_all(weights, members, bases_refs)
    u2_all = own[:, 0:elem_count] + own[:, elem_count:] * coarse
    deficits = (PLATE_RATE - jnp.exp(u2_all)).astype(jnp.bfloat16).astype(jnp.float32)
    inside = inside_rows(deficits, *field_refs)

    state = state_ref[...]
    u, phi, sa, sb, dist, k1p = (state[i:i + 1] for i in range(6))
    here = lax.broadcasted_iota(jnp.int32, u2_all.shape, 0) == me
    u2 = jnp.sum(jnp.where(here, u2_all, 0.0), axis=0, keepdims=True)
    deficit = jnp.sum(jnp.where(here, deficits, 0.0), axis=0, keepdims=True)
    phi2 = phi + TIME_STEP * k1p
    velocity = jnp.exp(u2)
    k2p = (jnp.exp(-phi2) - velocity) / dist
    inverse = 0.5 * TIME_STEP / (sa + DAMPING * velocity)
    u_next = 0.5 * (u + u2) + (inside - sb * k2p) * inverse
    phi_next = phi + 0.5 * TIME_STEP * (k1p + k2p)
    sent = gathered(padded([u_next, inverse, phi_next], 8), rows_ref[...])
    partial = as_lines(partial_row(deficit, coarse_v_ref))
    peer_rows = elem_count // members
    for device in range(groups * members):
        peer = device % members
        sent_ref[device, 0:3, 0:peer_rows] = sent[0:3, peer * peer_rows:(peer + 1) * peer_rows]
        sent_ref[device, 3:3 + partial.shape[0], :] = partial


def finish_kernel(groups, width, got_ref, slot_ref, slot_row_ref, *refs):
    bases_refs, u_ref, phi_ref = refs[:2], refs[2], refs[3]
    elem_count = slot_ref.shape[1]
    members = got_ref.shape[0] // groups
    sums = []
    for group in range(groups):
        total = jnp.sum(got_ref[group * members:(group + 1) * members], axis=0)
        lines = [total[3 + i:4 + i, :] for i in range(pl.cdiv(width, LANES))]
        sums.append(jnp.concatenate(lines, axis=1)[:, 0:width])
    coarse = coarse_all(coefficients(sums, width // groups), members, bases_refs)
    row = slot_row_ref[...]
    block = lax.broadcasted_iota(jnp.int32, (members, elem_count), 0)
    lane_block = lax.broadcasted_iota(jnp.int32, (members, elem_count), 1) // (elem_count // members)
    rows = gathered(coarse, row)
    found = jnp.sum(jnp.where(block == lane_block, rows, 0.0), axis=0, keepdims=True)
    first = lax.axis_index("leaf") * members
    flat = peer_lanes(got_ref, first, members, 3, elem_count)
    u_next = flat[0:1] + flat[1:2] * found
    out = gathered(padded([u_next, flat[2:3]], 8), slot_ref[...])
    u_ref[...] = out[0:1]
    phi_ref[...] = out[1:2]


def call(kernel, outs, *args, scalars=(), far=(), scratch=(), flops=1000, moved=1000):
    spaces = [SMEM if i in scalars else pl.ANY if i in far else VMEM for i in range(len(args))]
    args = [
        pltpu.with_memory_space_constraint(arg, pltpu.HBM) if i in far else arg
        for i, arg in enumerate(args)
    ]
    return pl.pallas_call(
        kernel,
        out_shape=outs,
        in_specs=[pl.BlockSpec(memory_space=space) for space in spaces],
        out_specs=jax.tree.map(lambda _: pl.BlockSpec(memory_space=VMEM), outs),
        scratch_shapes=list(scratch),
        cost_estimate=pl.CostEstimate(flops=flops, bytes_accessed=moved, transcendentals=0),
        compiler_params=pltpu.CompilerParams(vmem_limit_bytes=32 * 1024 * 1024),
    )(*args)


def shape(*dims, dtype=jnp.float32):
    return jax.ShapeDtypeStruct(dims, dtype)


def body(
    ln_rate,
    log_state,
    sigma,
    fric_a,
    fric_b,
    slip_dist,
    leaf_of_elem,
    near_blocks,
    near_col,
    near_count,
    far_u,
    far_v,
    far_col,
    far_rank,
    coarse_u,
    coarse_v,
):
    members = lax.axis_size("blk")
    elems = ln_rate.shape[0]
    leaf_size = near_blocks.shape[1]
    groups, rank = coarse_v.shape[0], coarse_v.shape[1]
    devices = groups * members
    width = groups * rank
    lines = pl.cdiv(width, LANES)
    sent_rows = 1 << (2 + lines).bit_length()
    integer = jnp.int32

    def swap(value, axes):
        return lax.all_to_all(value, axes, split_axis=0, concat_axis=0, tiled=True)

    def partner(value, bit):
        return lax.ppermute(value, "blk", [(i, i ^ (1 << bit)) for i in range(members)])

    elem_args = [
        value.reshape(1, elems)
        for value in (leaf_of_elem, ln_rate, log_state, sigma, fric_a, fric_b, slip_dist)
    ]
    scalar_args = [near_col, far_col, far_rank]
    weights = [
        near_blocks, far_u.reshape(-1, leaf_size), far_v.reshape(-1, leaf_size),
        coarse_v.reshape(width, elems),
    ]
    far_rows = weights[1].shape[0]
    sent, slot, slot_row, near_mask, far_mask, near, far_u, far_v, coarse_v = call(
        functools.partial(sort_kernel, members),
        (
            shape(members, 8 + 2 * (elems // LANES), LANES),
            shape(1, elems, dtype=integer),
            shape(1, elems, dtype=integer),
            shape(near_blocks.shape[0], members, leaf_size),
            shape(members, far_rows),
            *[shape(*value.shape, dtype=jnp.bfloat16) for value in weights],
        ),
        *elem_args, *scalar_args, *weights, far=range(14),
        scratch=[VMEM(value.shape, value.dtype) for value in elem_args]
        + [SMEM(value.shape, value.dtype) for value in scalar_args]
        + [pltpu.SemaphoreType.DMA((14,))],
    )
    bases = coarse_u.reshape(width, elems)
    top = members.bit_length() - 2
    kept = width - rank
    bases = call(
        functools.partial(pair_kernel, rank), shape(2 * kept, elems, dtype=jnp.bfloat16),
        bases, partner(bases, top), slot, flops=1 << 26, moved=1 << 22,
    )
    for bit in range(top - 1, 0, -1):
        stacked = shape(2 * bases.shape[0], elems, dtype=jnp.bfloat16)
        bases = call(stack_kernel, stacked, bases, partner(bases, bit))
    bases = bases, partner(bases, 0)
    fields = near_count, near, far_u, far_v, near_mask, far_mask
    state, rows, out = call(
        place_kernel,
        (
            shape(8, elems),
            shape(1, elems, dtype=integer),
            shape(devices, 1, 2 * elems + lines * LANES),
        ),
        swap(sent, "blk"), coarse_v, *fields, scalars=(2,),
        scratch=[VMEM((members * (elems // LANES), LANES), jnp.float32)],
    )
    sent = call(
        functools.partial(second_kernel, groups), shape(devices, sent_rows, LANES),
        state, rows, swap(out, ("leaf", "blk")), coarse_v, *bases, *fields, scalars=(6,),
    )
    u, phi = call(
        functools.partial(finish_kernel, groups, width), (shape(1, elems), shape(1, elems)),
        swap(sent, ("leaf", "blk")), slot, slot_row, *bases,
    )
    return u.reshape(elems), phi.reshape(elems)


def solution(mesh):
    each = P(("leaf", "blk"))
    blocks = P(("leaf", "blk"), None, None)
    last = P(None, None, ("leaf", "blk"))
    in_specs = (each,) * 7 + (blocks, each, each, blocks, blocks, each, each, last, last)
    return jax.shard_map(body, mesh=mesh, in_specs=in_specs, out_specs=(each, each), check_vma=False)
```

```python
import functools

import jax
import jax.numpy as jnp
from jax import lax
from jax.experimental import pallas as pl
from jax.experimental.pallas import tpu as pltpu
from jax.sharding import PartitionSpec as P

DAMPING = 0.5
PLATE_RATE = 1.0
TIME_STEP = 0.2

NN = (((1,), (0,)), ((), ()))
NT = (((1,), (1,)), ((), ()))
VMEM = pltpu.VMEM
SMEM = pltpu.SMEM

LANES = 128


def dot(left, right, dims):
    return lax.dot_general(left, right, dims, preferred_element_type=jnp.float32)


def low_matrix(index_row):
    rows = lax.broadcasted_iota(jnp.int32, (LANES, index_row.shape[1]), 0)
    return jnp.where(rows == (index_row & (LANES - 1)), 1.0, 0.0).astype(jnp.bfloat16)


def three_parts(values):
    high = values.astype(jnp.bfloat16).astype(jnp.float32)
    rest = values - high
    middle = rest.astype(jnp.bfloat16).astype(jnp.float32)
    return jnp.concatenate([high, middle, rest - middle], axis=0)


def joined(parts):
    count = parts.shape[0] // 3
    return parts[0:count] + parts[count:2 * count] + parts[2 * count:]


def scattered(values, index_row):
    parts = three_parts(values)
    count = parts.shape[0]
    high = index_row // LANES
    pieces = values.shape[1] // LANES
    left = jnp.concatenate([jnp.where(high == piece, parts, 0.0) for piece in range(pieces)], axis=0)
    moved = dot(left.astype(jnp.bfloat16), low_matrix(index_row), NT)
    return jnp.concatenate(
        [joined(moved[piece * count:(piece + 1) * count]) for piece in range(pieces)], axis=1
    )


def gathered(values, index_row):
    parts = three_parts(values)
    count = parts.shape[0]
    high = index_row // LANES
    pieces = values.shape[1] // LANES
    left = jnp.concatenate(
        [parts[:, piece * LANES:(piece + 1) * LANES] for piece in range(pieces)], axis=0
    )
    moved = dot(left.astype(jnp.bfloat16), low_matrix(index_row), NN)
    total = jnp.zeros((count, index_row.shape[1]), jnp.float32)
    for piece in range(pieces):
        total = jnp.where(high == piece, moved[piece * count:(piece + 1) * count], total)
    return joined(total)


def padded(rows, count):
    missing = count - len(rows)
    if missing:
        rows = rows + [jnp.zeros((missing, rows[0].shape[1]), jnp.float32)]
    return jnp.concatenate(rows, axis=0)


def as_lines(row):
    return jnp.concatenate(
        [row[:, i * LANES:(i + 1) * LANES] for i in range(row.shape[1] // LANES)], axis=0
    )


def peer_lanes(ref, first, members, rows, elem_count):
    width = elem_count // members
    return jnp.concatenate([ref[first + peer, 0:rows, 0:width] for peer in range(members)], axis=1)


def start_copies(sources, targets, sems):
    copies = [
        pltpu.make_async_copy(source, target, sems.at[i])
        for i, (source, target) in enumerate(zip(sources, targets))
    ]
    for copy in copies:
        copy.start()
    return copies


def sort_kernel(members, *refs):
    elem_refs, scalar_refs, weight_refs = refs[:7], refs[7:10], refs[10:14]
    sent_ref, slot_ref, slot_row_ref, near_mask_ref, far_mask_ref = refs[14:19]
    weight_outs, elem_bufs, scalar_bufs, sems = refs[19:23], refs[23:30], refs[30:33], refs[33]
    copies = start_copies(
        [*elem_refs, *scalar_refs, *weight_refs], [*elem_bufs, *scalar_bufs, *weight_outs], sems
    )
    mine = lax.axis_index("leaf")
    elem_count = elem_bufs[0].shape[1]
    peer_rows = elem_count // members
    pieces = elem_count // LANES
    before = lax.broadcasted_iota(jnp.int32, (LANES, LANES), 0)
    after = lax.broadcasted_iota(jnp.int32, (LANES, LANES), 1)
    triangle = jnp.where(before < after, 1.0, 0.0).astype(jnp.bfloat16)
    copies[0].wait()
    local = elem_bufs[0][...] - mine * (members * elem_count)
    target = local // elem_count
    target_row = local - target * elem_count
    peers = lax.broadcasted_iota(jnp.int32, (members, elem_count), 0)
    onehot = jnp.where(peers == target, 1.0, 0.0)
    lines = [onehot[:, i * LANES:(i + 1) * LANES] for i in range(pieces)]
    inside = dot(jnp.concatenate(lines, axis=0).astype(jnp.bfloat16), triangle, NN)
    passed = jnp.zeros((members, 1), jnp.float32)
    ranks = []
    for i, line in enumerate(lines):
        earlier = inside[i * members:(i + 1) * members] + passed
        ranks.append(jnp.sum(earlier * line, axis=0, keepdims=True))
        passed = passed + jnp.sum(line, axis=1, keepdims=True)
    slot = target * peer_rows + jnp.concatenate(ranks, axis=1).astype(jnp.int32)
    slot_ref[...] = slot
    for copy in copies[1:7]:
        copy.wait()
    u, phi, sigma, fric_a, fric_b, dist = (buf[...] for buf in elem_bufs[1:])
    deficit = (PLATE_RATE - jnp.exp(u)).astype(jnp.bfloat16).astype(jnp.float32)
    rows = [u, phi, sigma * fric_a, sigma * fric_b, dist, target_row.astype(jnp.float32), deficit]
    values = scattered(padded(rows, 8), slot)
    slot_row_ref[...] = values[5:6].astype(jnp.int32)
    everyone = jnp.concatenate([as_lines(values[6:7]), as_lines(values[5:6])], axis=0)
    for peer in range(members):
        sent_ref[peer, 0:8, 0:peer_rows] = values[:, peer * peer_rows:(peer + 1) * peer_rows]
        sent_ref[peer, 8:8 + 2 * pieces, :] = everyone

    for copy in copies[7:10]:
        copy.wait()
    near_col, far_col, far_rank = scalar_bufs
    far_slots = far_col.shape[0]
    far_width = far_mask_ref.shape[1] // far_slots
    block = lax.broadcasted_iota(jnp.int32, near_mask_ref.shape[1:], 0)
    for number in range(near_mask_ref.shape[0]):
        near_mask_ref[number] = jnp.where(block == near_col[number], 1.0, 0.0)
    block = lax.broadcasted_iota(jnp.int32, far_mask_ref.shape, 0)
    lane = lax.broadcasted_iota(jnp.int32, far_mask_ref.shape, 1)
    column = jnp.full(far_mask_ref.shape, -1, jnp.int32)
    for number in range(far_slots):
        low = number * far_width
        kept = (lane >= low) & (lane < low + far_rank[number])
        column = jnp.where(kept, far_col[number], column)
    far_mask_ref[...] = jnp.where(block == column, 1.0, 0.0)
    for copy in copies[10:]:
        copy.wait()


def partial_row(deficit, coarse_v_ref):
    wide = jnp.broadcast_to(deficit, (8, deficit.shape[1])).astype(jnp.bfloat16)
    partial = dot(wide, coarse_v_ref[...], NT)[0:1]
    rest = -partial.shape[1] % LANES
    if rest:
        partial = jnp.concatenate([partial, jnp.zeros((1, rest), jnp.float32)], axis=1)
    return partial


def inside_rows(deficits, near_count, near_ref, far_u_ref, far_v_ref, near_mask_ref, far_mask_ref):
    total = jnp.zeros(deficits.shape, jnp.float32)
    for slot in range(near_ref.shape[0]):
        live = jnp.where(slot < near_count[0], 1.0, 0.0)
        source = (deficits * (near_mask_ref[slot] * live)).astype(jnp.bfloat16)
        total = total + dot(source, near_ref[slot], NT)
    project = dot(deficits.astype(jnp.bfloat16), far_v_ref[...], NT) * far_mask_ref[...]
    project = jnp.sum(project, axis=0, keepdims=True)
    project = jnp.broadcast_to(project, (8, project.shape[1])).astype(jnp.bfloat16)
    far = dot(project, far_u_ref[...], NN)
    return jnp.sum(total, axis=0, keepdims=True) + far[0:1]


def coefficients(sums, rank):
    groups, width = len(sums), sums[0].shape[1]
    mine = lax.axis_index("leaf")
    table = padded(sums, -(-groups // 8) * 8)
    lane = lax.broadcasted_iota(jnp.int32, table.shape, 1) // rank
    row = lax.broadcasted_iota(jnp.int32, table.shape, 0)
    table = jnp.where(lane == mine, table, 0.0).astype(jnp.bfloat16)
    across = lax.broadcasted_iota(jnp.int32, (width, width), 0) % rank
    down = lax.broadcasted_iota(jnp.int32, (width, width), 1) % rank
    spread = dot(table, jnp.where(across == down, 1.0, 0.0).astype(jnp.bfloat16), NN)
    weights = jnp.sum(jnp.where(row == mine ^ (lane + 1), spread, 0.0), axis=0, keepdims=True)
    return weights[:, 0:width - rank]


def coarse_all(weights, members, bases_refs):
    row = lax.broadcasted_iota(jnp.int32, (members, weights.shape[1]), 0) ^ lax.axis_index("blk")
    bits = members.bit_length() - 1
    total = jnp.zeros((members, bases_refs[0].shape[1]), jnp.float32)
    for number, ref in enumerate(bases_refs):
        left = []
        for place in range(members // 2):
            source = number
            for bit in range(bits - 1):
                source |= (place >> bit & 1) << (bits - 1 - bit)
            left.append(jnp.where(row == source, weights, 0.0))
        left = jnp.concatenate(left, axis=1).astype(jnp.bfloat16)
        total = total + dot(left, ref[...], NN)
    return total


def stack_kernel(held_ref, came_ref, *refs):
    out_ref = refs[-1]
    count = held_ref.shape[0]
    out_ref[0:count, :] = held_ref[...]
    out_ref[count:2 * count, :] = came_ref[...]


def stack_foreign_kernel(groups, rank, held_ref, came_ref, *refs):
    out_ref = refs[-1]
    width = groups * rank
    mine = lax.axis_index("leaf")
    place = 0
    for ref in (held_ref, came_ref):
        for low in range(0, ref.shape[0], width):
            for shift in range(1, groups):
                out_ref[place:place + rank, :] = ref[pl.ds(low + (mine ^ shift) * rank, rank), :]
                place += rank


def place_kernel(got_ref, coarse_v_ref, *refs):
    field_refs, state_ref, rows_ref, out_ref, lines_ref = refs[:6], refs[6], refs[7], refs[8], refs[9]
    members = got_ref.shape[0]
    elem_count = state_ref.shape[1]
    pieces = elem_count // LANES
    peer_rows = elem_count // members
    per_line = LANES // peer_rows
    line_block = lax.broadcasted_iota(jnp.int32, (per_line * pieces, LANES), 0) // pieces
    line_piece = lax.broadcasted_iota(jnp.int32, (per_line * pieces, LANES), 0) % pieces
    lane_block = lax.broadcasted_iota(jnp.int32, (per_line * pieces, LANES), 1) // peer_rows
    own_lane = line_block == lane_block
    for line in range(pieces):
        left, right = [], []
        for peer in range(members):
            value = got_ref[peer, 8 + line:9 + line, :]
            row = got_ref[peer, 8 + pieces + line:9 + pieces + line, :].astype(jnp.int32)
            left.append(jnp.where(own_lane & (line_piece == row // LANES), value, 0.0))
            right.append(low_matrix(row))
        left = jnp.concatenate(left, axis=1).astype(jnp.bfloat16)
        count = per_line * pieces
        lines_ref[line * count:(line + 1) * count, :] = dot(left, jnp.concatenate(right, axis=1), NT)
    deficits = jnp.concatenate(
        [lines_ref[pl.ds(piece, members, stride=pieces), :] for piece in range(pieces)], axis=1
    )
    inside = inside_rows(deficits, *field_refs)

    flat = peer_lanes(got_ref, 0, members, 8, elem_count)
    rows = flat[5:6].astype(jnp.int32)
    rows_ref[...] = rows
    state = scattered(flat, rows)
    u, phi, sa, sb, dist = (state[i:i + 1] for i in range(5))
    velocity = jnp.exp(u)
    k1p = (jnp.exp(-phi) - velocity) / dist
    inverse = 1.0 / (sa + DAMPING * velocity)
    u2 = u + TIME_STEP * ((inside - sb * k1p) * inverse)
    factor = TIME_STEP * inverse
    state_ref[...] = jnp.concatenate([u, phi, sa, sb, dist, k1p, u2, factor], axis=0)
    sent = jnp.concatenate([u2, factor, partial_row(state[6:7], coarse_v_ref)], axis=1)
    out_ref[...] = jnp.broadcast_to(sent[None], out_ref.shape)


def second_kernel(groups, state_ref, rows_ref, all_ref, coarse_v_ref, *refs):
    bases_refs, field_refs, sent_ref = refs[:2], refs[2:8], refs[8]
    members, elem_count = refs[6].shape[1], state_ref.shape[1]
    width = coarse_v_ref.shape[0]
    mine, me = lax.axis_index("leaf"), lax.axis_index("blk")
    sums = [
        jnp.sum(
            all_ref[group * members:(group + 1) * members, 0, 2 * elem_count:2 * elem_count + width],
            axis=0, keepdims=True,
        )
        for group in range(groups)
    ]
    weights = coefficients(sums, width // groups)
    own = all_ref[pl.ds(mine * members, members), 0, 0:2 * elem_count]
    coarse = coarse_all(weights, members, bases_refs)
    u2_all = own[:, 0:elem_count] + own[:, elem_count:] * coarse
    deficits = (PLATE_RATE - jnp.exp(u2_all)).astype(jnp.bfloat16).astype(jnp.float32)
    inside = inside_rows(deficits, *field_refs)

    state = state_ref[...]
    u, phi, sa, sb, dist, k1p = (state[i:i + 1] for i in range(6))
    here = lax.broadcasted_iota(jnp.int32, u2_all.shape, 0) == me
    u2 = jnp.sum(jnp.where(here, u2_all, 0.0), axis=0, keepdims=True)
    deficit = jnp.sum(jnp.where(here, deficits, 0.0), axis=0, keepdims=True)
    phi2 = phi + TIME_STEP * k1p
    velocity = jnp.exp(u2)
    k2p = (jnp.exp(-phi2) - velocity) / dist
    inverse = 0.5 * TIME_STEP / (sa + DAMPING * velocity)
    u_next = 0.5 * (u + u2) + (inside - sb * k2p) * inverse
    phi_next = phi + 0.5 * TIME_STEP * (k1p + k2p)
    sent = gathered(padded([u_next, inverse, phi_next], 8), rows_ref[...])
    partial = as_lines(partial_row(deficit, coarse_v_ref))
    peer_rows = elem_count // members
    for device in range(groups * members):
        peer = device % members
        sent_ref[device, 0:3, 0:peer_rows] = sent[0:3, peer * peer_rows:(peer + 1) * peer_rows]
        sent_ref[device, 3:3 + partial.shape[0], :] = partial


def finish_kernel(groups, width, got_ref, slot_ref, slot_row_ref, *refs):
    bases_refs, u_ref, phi_ref = refs[:2], refs[2], refs[3]
    elem_count = slot_ref.shape[1]
    members = got_ref.shape[0] // groups
    sums = []
    for group in range(groups):
        total = jnp.sum(got_ref[group * members:(group + 1) * members], axis=0)
        lines = [total[3 + i:4 + i, :] for i in range(pl.cdiv(width, LANES))]
        sums.append(jnp.concatenate(lines, axis=1)[:, 0:width])
    coarse = coarse_all(coefficients(sums, width // groups), members, bases_refs)
    row = slot_row_ref[...]
    block = lax.broadcasted_iota(jnp.int32, (members, elem_count), 0)
    lane_block = lax.broadcasted_iota(jnp.int32, (members, elem_count), 1) // (elem_count // members)
    rows = gathered(coarse, row)
    found = jnp.sum(jnp.where(block == lane_block, rows, 0.0), axis=0, keepdims=True)
    first = lax.axis_index("leaf") * members
    flat = peer_lanes(got_ref, first, members, 3, elem_count)
    u_next = flat[0:1] + flat[1:2] * found
    out = gathered(padded([u_next, flat[2:3]], 8), slot_ref[...])
    u_ref[...] = out[0:1]
    phi_ref[...] = out[1:2]


def call(kernel, outs, *args, scalars=(), far=(), scratch=(), flops=1000, moved=1000):
    spaces = [SMEM if i in scalars else pl.ANY if i in far else VMEM for i in range(len(args))]
    args = [
        pltpu.with_memory_space_constraint(arg, pltpu.HBM) if i in far else arg
        for i, arg in enumerate(args)
    ]
    return pl.pallas_call(
        kernel,
        out_shape=outs,
        in_specs=[pl.BlockSpec(memory_space=space) for space in spaces],
        out_specs=jax.tree.map(lambda _: pl.BlockSpec(memory_space=VMEM), outs),
        scratch_shapes=list(scratch),
        cost_estimate=pl.CostEstimate(flops=flops, bytes_accessed=moved, transcendentals=0),
        compiler_params=pltpu.CompilerParams(vmem_limit_bytes=32 * 1024 * 1024),
    )(*args)


def shape(*dims, dtype=jnp.float32):
    return jax.ShapeDtypeStruct(dims, dtype)


def body(
    ln_rate,
    log_state,
    sigma,
    fric_a,
    fric_b,
    slip_dist,
    leaf_of_elem,
    near_blocks,
    near_col,
    near_count,
    far_u,
    far_v,
    far_col,
    far_rank,
    coarse_u,
    coarse_v,
):
    members = lax.axis_size("blk")
    elems = ln_rate.shape[0]
    leaf_size = near_blocks.shape[1]
    groups, rank = coarse_v.shape[0], coarse_v.shape[1]
    devices = groups * members
    width = groups * rank
    lines = pl.cdiv(width, LANES)
    sent_rows = 1 << (2 + lines).bit_length()
    integer = jnp.int32

    def swap(value, axes):
        return lax.all_to_all(value, axes, split_axis=0, concat_axis=0, tiled=True)

    def partner(value, bit):
        return lax.ppermute(value, "blk", [(i, i ^ (1 << bit)) for i in range(members)])

    elem_args = [
        value.reshape(1, elems)
        for value in (leaf_of_elem, ln_rate, log_state, sigma, fric_a, fric_b, slip_dist)
    ]
    scalar_args = [near_col, far_col, far_rank]
    weights = [
        near_blocks, far_u.reshape(-1, leaf_size), far_v.reshape(-1, leaf_size),
        coarse_v.reshape(width, elems),
    ]
    far_rows = weights[1].shape[0]
    sent, slot, slot_row, near_mask, far_mask, near, far_u, far_v, coarse_v = call(
        functools.partial(sort_kernel, members),
        (
            shape(members, 8 + 2 * (elems // LANES), LANES),
            shape(1, elems, dtype=integer),
            shape(1, elems, dtype=integer),
            shape(near_blocks.shape[0], members, leaf_size),
            shape(members, far_rows),
            *[shape(*value.shape, dtype=jnp.bfloat16) for value in weights],
        ),
        *elem_args, *scalar_args, *weights, far=range(14),
        scratch=[VMEM(value.shape, value.dtype) for value in elem_args]
        + [SMEM(value.shape, value.dtype) for value in scalar_args]
        + [pltpu.SemaphoreType.DMA((14,))],
    )
    bases = coarse_u.reshape(width, elems)
    for bit in range(members.bit_length() - 2, 0, -1):
        rows_out = 2 * bases.shape[0]
        kernel = stack_kernel
        if bit == 1:
            rows_out = rows_out // groups * (groups - 1)
            kernel = functools.partial(stack_foreign_kernel, groups, rank)
        bases = call(
            kernel, shape(rows_out, elems, dtype=jnp.bfloat16),
            bases, partner(bases, bit), slot, flops=1 << 26, moved=1 << 22,
        )
    bases = bases, partner(bases, 0)
    fields = near_count, near, far_u, far_v, near_mask, far_mask
    state, rows, out = call(
        place_kernel,
        (
            shape(8, elems),
            shape(1, elems, dtype=integer),
            shape(devices, 1, 2 * elems + lines * LANES),
        ),
        swap(sent, "blk"), coarse_v, *fields, scalars=(2,),
        scratch=[VMEM((members * (elems // LANES), LANES), jnp.float32)],
    )
    sent = call(
        functools.partial(second_kernel, groups), shape(devices, sent_rows, LANES),
        state, rows, swap(out, ("leaf", "blk")), coarse_v, *bases, *fields, scalars=(6,),
    )
    u, phi = call(
        functools.partial(finish_kernel, groups, width), (shape(1, elems), shape(1, elems)),
        swap(sent, ("leaf", "blk")), slot, slot_row, *bases,
    )
    return u.reshape(elems), phi.reshape(elems)


def solution(mesh):
    each = P(("leaf", "blk"))
    blocks = P(("leaf", "blk"), None, None)
    last = P(None, None, ("leaf", "blk"))
    in_specs = (each,) * 7 + (blocks, each, each, blocks, blocks, each, each, last, last)
    return jax.shard_map(body, mesh=mesh, in_specs=in_specs, out_specs=(each, each), check_vma=False)
```

```python
import functools

import jax
import jax.numpy as jnp
from jax import lax
from jax.experimental import pallas as pl
from jax.experimental.pallas import tpu as pltpu
from jax.sharding import PartitionSpec as P

DAMPING = 0.5
PLATE_RATE = 1.0
TIME_STEP = 0.2

NN = (((1,), (0,)), ((), ()))
NT = (((1,), (1,)), ((), ()))
VMEM = pltpu.VMEM
SMEM = pltpu.SMEM

LANES = 128


def dot(left, right, dims):
    return lax.dot_general(left, right, dims, preferred_element_type=jnp.float32)


def low_matrix(index_row):
    rows = lax.broadcasted_iota(jnp.int32, (LANES, index_row.shape[1]), 0)
    return jnp.where(rows == (index_row & (LANES - 1)), 1.0, 0.0).astype(jnp.bfloat16)


def three_parts(values):
    high = values.astype(jnp.bfloat16).astype(jnp.float32)
    rest = values - high
    middle = rest.astype(jnp.bfloat16).astype(jnp.float32)
    return jnp.concatenate([high, middle, rest - middle], axis=0)


def joined(parts):
    count = parts.shape[0] // 3
    return parts[0:count] + parts[count:2 * count] + parts[2 * count:]


def scattered(values, index_row):
    parts = three_parts(values)
    count = parts.shape[0]
    high = index_row // LANES
    pieces = values.shape[1] // LANES
    left = jnp.concatenate([jnp.where(high == piece, parts, 0.0) for piece in range(pieces)], axis=0)
    moved = dot(left.astype(jnp.bfloat16), low_matrix(index_row), NT)
    return jnp.concatenate(
        [joined(moved[piece * count:(piece + 1) * count]) for piece in range(pieces)], axis=1
    )


def gathered(values, index_row):
    parts = three_parts(values)
    count = parts.shape[0]
    high = index_row // LANES
    pieces = values.shape[1] // LANES
    left = jnp.concatenate(
        [parts[:, piece * LANES:(piece + 1) * LANES] for piece in range(pieces)], axis=0
    )
    moved = dot(left.astype(jnp.bfloat16), low_matrix(index_row), NN)
    total = jnp.zeros((count, index_row.shape[1]), jnp.float32)
    for piece in range(pieces):
        total = jnp.where(high == piece, moved[piece * count:(piece + 1) * count], total)
    return joined(total)


def padded(rows, count):
    missing = count - len(rows)
    if missing:
        rows = rows + [jnp.zeros((missing, rows[0].shape[1]), jnp.float32)]
    return jnp.concatenate(rows, axis=0)


def as_lines(row):
    return jnp.concatenate(
        [row[:, i * LANES:(i + 1) * LANES] for i in range(row.shape[1] // LANES)], axis=0
    )


def peer_lanes(ref, first, members, rows, elem_count):
    width = elem_count // members
    return jnp.concatenate([ref[first + peer, 0:rows, 0:width] for peer in range(members)], axis=1)


def start_copies(sources, targets, sems):
    copies = [
        pltpu.make_async_copy(source, target, sems.at[i])
        for i, (source, target) in enumerate(zip(sources, targets))
    ]
    for copy in copies:
        copy.start()
    return copies


def sort_kernel(members, *refs):
    elem_refs, scalar_refs, weight_refs = refs[:7], refs[7:10], refs[10:14]
    sent_ref, slot_ref, slot_row_ref, near_mask_ref, far_mask_ref = refs[14:19]
    weight_outs, elem_bufs, scalar_bufs, sems = refs[19:23], refs[23:30], refs[30:33], refs[33]
    copies = start_copies(
        [*elem_refs, *scalar_refs, *weight_refs], [*elem_bufs, *scalar_bufs, *weight_outs], sems
    )
    mine = lax.axis_index("leaf")
    elem_count = elem_bufs[0].shape[1]
    peer_rows = elem_count // members
    pieces = elem_count // LANES
    before = lax.broadcasted_iota(jnp.int32, (LANES, LANES), 0)
    after = lax.broadcasted_iota(jnp.int32, (LANES, LANES), 1)
    triangle = jnp.where(before < after, 1.0, 0.0).astype(jnp.bfloat16)
    copies[0].wait()
    local = elem_bufs[0][...] - mine * (members * elem_count)
    target = local // elem_count
    target_row = local - target * elem_count
    peers = lax.broadcasted_iota(jnp.int32, (members, elem_count), 0)
    onehot = jnp.where(peers == target, 1.0, 0.0)
    lines = [onehot[:, i * LANES:(i + 1) * LANES] for i in range(pieces)]
    inside = dot(jnp.concatenate(lines, axis=0).astype(jnp.bfloat16), triangle, NN)
    passed = jnp.zeros((members, 1), jnp.float32)
    ranks = []
    for i, line in enumerate(lines):
        earlier = inside[i * members:(i + 1) * members] + passed
        ranks.append(jnp.sum(earlier * line, axis=0, keepdims=True))
        passed = passed + jnp.sum(line, axis=1, keepdims=True)
    slot = target * peer_rows + jnp.concatenate(ranks, axis=1).astype(jnp.int32)
    slot_ref[...] = slot
    for copy in copies[1:7]:
        copy.wait()
    u, phi, sigma, fric_a, fric_b, dist = (buf[...] for buf in elem_bufs[1:])
    deficit = (PLATE_RATE - jnp.exp(u)).astype(jnp.bfloat16).astype(jnp.float32)
    rows = [u, phi, sigma * fric_a, sigma * fric_b, dist, target_row.astype(jnp.float32), deficit]
    values = scattered(padded(rows, 8), slot)
    slot_row_ref[...] = values[5:6].astype(jnp.int32)
    everyone = jnp.concatenate([as_lines(values[6:7]), as_lines(values[5:6])], axis=0)
    for peer in range(members):
        sent_ref[peer, 0:8, 0:peer_rows] = values[:, peer * peer_rows:(peer + 1) * peer_rows]
        sent_ref[peer, 8:8 + 2 * pieces, :] = everyone

    for copy in copies[7:10]:
        copy.wait()
    near_col, far_col, far_rank = scalar_bufs
    far_slots = far_col.shape[0]
    far_width = far_mask_ref.shape[1] // far_slots
    block = lax.broadcasted_iota(jnp.int32, near_mask_ref.shape[1:], 0)
    for number in range(near_mask_ref.shape[0]):
        near_mask_ref[number] = jnp.where(block == near_col[number], 1.0, 0.0)
    block = lax.broadcasted_iota(jnp.int32, far_mask_ref.shape, 0)
    lane = lax.broadcasted_iota(jnp.int32, far_mask_ref.shape, 1)
    column = jnp.full(far_mask_ref.shape, -1, jnp.int32)
    for number in range(far_slots):
        low = number * far_width
        kept = (lane >= low) & (lane < low + far_rank[number])
        column = jnp.where(kept, far_col[number], column)
    far_mask_ref[...] = jnp.where(block == column, 1.0, 0.0)
    for copy in copies[10:]:
        copy.wait()


def partial_row(deficit, coarse_v_ref):
    wide = jnp.broadcast_to(deficit, (8, deficit.shape[1])).astype(jnp.bfloat16)
    partial = dot(wide, coarse_v_ref[...], NT)[0:1]
    rest = -partial.shape[1] % LANES
    if rest:
        partial = jnp.concatenate([partial, jnp.zeros((1, rest), jnp.float32)], axis=1)
    return partial


def inside_rows(deficits, near_count, near_ref, far_u_ref, far_v_ref, near_mask_ref, far_mask_ref):
    total = jnp.zeros(deficits.shape, jnp.float32)
    for slot in range(near_ref.shape[0]):
        live = jnp.where(slot < near_count[0], 1.0, 0.0)
        source = (deficits * (near_mask_ref[slot] * live)).astype(jnp.bfloat16)
        total = total + dot(source, near_ref[slot], NT)
    project = dot(deficits.astype(jnp.bfloat16), far_v_ref[...], NT) * far_mask_ref[...]
    project = jnp.sum(project, axis=0, keepdims=True)
    project = jnp.broadcast_to(project, (8, project.shape[1])).astype(jnp.bfloat16)
    far = dot(project, far_u_ref[...], NN)
    return jnp.sum(total, axis=0, keepdims=True) + far[0:1]


def coefficients(sums, rank):
    groups, width = len(sums), sums[0].shape[1]
    mine = lax.axis_index("leaf")
    table = padded(sums, -(-groups // 8) * 8)
    lane = lax.broadcasted_iota(jnp.int32, table.shape, 1) // rank
    row = lax.broadcasted_iota(jnp.int32, table.shape, 0)
    table = jnp.where(lane == mine, table, 0.0).astype(jnp.bfloat16)
    across = lax.broadcasted_iota(jnp.int32, (width, width), 0) % rank
    down = lax.broadcasted_iota(jnp.int32, (width, width), 1) % rank
    spread = dot(table, jnp.where(across == down, 1.0, 0.0).astype(jnp.bfloat16), NN)
    weights = jnp.sum(jnp.where(row == mine ^ (lane + 1), spread, 0.0), axis=0, keepdims=True)
    return weights[:, 0:width - rank]


def coarse_all(weights, members, bases_refs):
    row = lax.broadcasted_iota(jnp.int32, (members, weights.shape[1]), 0) ^ lax.axis_index("blk")
    bits = members.bit_length() - 1
    total = jnp.zeros((members, bases_refs[0].shape[1]), jnp.float32)
    for number, ref in enumerate(bases_refs):
        left = []
        for place in range(members // 2):
            source = number
            for bit in range(bits - 1):
                source |= (place >> bit & 1) << (bits - 1 - bit)
            left.append(jnp.where(row == source, weights, 0.0))
        left = jnp.concatenate(left, axis=1).astype(jnp.bfloat16)
        total = total + dot(left, ref[...], NN)
    return total


def stack_kernel(held_ref, came_ref, *refs):
    out_ref = refs[-1]
    count = held_ref.shape[0]
    out_ref[0:count, :] = held_ref[...]
    out_ref[count:2 * count, :] = came_ref[...]


def stack_foreign_kernel(groups, rank, held_ref, came_ref, *refs):
    out_ref = refs[-1]
    width = groups * rank
    mine = lax.axis_index("leaf")
    place = 0
    for ref in (held_ref, came_ref):
        for low in range(0, ref.shape[0], width):
            for shift in range(1, groups):
                out_ref[place:place + rank, :] = ref[pl.ds(low + (mine ^ shift) * rank, rank), :]
                place += rank


def mark_kernel(came_ref, out_ref):
    out_ref[...] = came_ref[0:16, 0:LANES].astype(jnp.float32)


def place_kernel(got_ref, coarse_v_ref, *refs):
    field_refs, state_ref, rows_ref, out_ref, lines_ref = refs[:6], refs[6], refs[7], refs[8], refs[9]
    members = got_ref.shape[0]
    elem_count = state_ref.shape[1]
    pieces = elem_count // LANES
    peer_rows = elem_count // members
    per_line = LANES // peer_rows
    line_block = lax.broadcasted_iota(jnp.int32, (per_line * pieces, LANES), 0) // pieces
    line_piece = lax.broadcasted_iota(jnp.int32, (per_line * pieces, LANES), 0) % pieces
    lane_block = lax.broadcasted_iota(jnp.int32, (per_line * pieces, LANES), 1) // peer_rows
    own_lane = line_block == lane_block
    for line in range(pieces):
        left, right = [], []
        for peer in range(members):
            value = got_ref[peer, 8 + line:9 + line, :]
            row = got_ref[peer, 8 + pieces + line:9 + pieces + line, :].astype(jnp.int32)
            left.append(jnp.where(own_lane & (line_piece == row // LANES), value, 0.0))
            right.append(low_matrix(row))
        left = jnp.concatenate(left, axis=1).astype(jnp.bfloat16)
        count = per_line * pieces
        lines_ref[line * count:(line + 1) * count, :] = dot(left, jnp.concatenate(right, axis=1), NT)
    deficits = jnp.concatenate(
        [lines_ref[pl.ds(piece, members, stride=pieces), :] for piece in range(pieces)], axis=1
    )
    inside = inside_rows(deficits, *field_refs)

    flat = peer_lanes(got_ref, 0, members, 8, elem_count)
    rows = flat[5:6].astype(jnp.int32)
    rows_ref[...] = rows
    state = scattered(flat, rows)
    u, phi, sa, sb, dist = (state[i:i + 1] for i in range(5))
    velocity = jnp.exp(u)
    k1p = (jnp.exp(-phi) - velocity) / dist
    inverse = 1.0 / (sa + DAMPING * velocity)
    u2 = u + TIME_STEP * ((inside - sb * k1p) * inverse)
    factor = TIME_STEP * inverse
    state_ref[...] = jnp.concatenate([u, phi, sa, sb, dist, k1p, u2, factor], axis=0)
    sent = jnp.concatenate([u2, factor, partial_row(state[6:7], coarse_v_ref)], axis=1)
    out_ref[...] = jnp.broadcast_to(sent[None], out_ref.shape)


def second_kernel(groups, state_ref, rows_ref, all_ref, complete_ref, coarse_v_ref, *refs):
    bases_refs, field_refs, sent_ref = refs[:2], refs[2:8], refs[8]
    members, elem_count = refs[6].shape[1], state_ref.shape[1]
    width = coarse_v_ref.shape[0]
    mine, me = lax.axis_index("leaf"), lax.axis_index("blk")
    sums = [
        jnp.sum(
            all_ref[group * members:(group + 1) * members, 0, 2 * elem_count:2 * elem_count + width],
            axis=0, keepdims=True,
        )
        for group in range(groups)
    ]
    weights = coefficients(sums, width // groups)
    own = all_ref[pl.ds(mine * members, members), 0, 0:2 * elem_count]
    coarse = coarse_all(weights, members, bases_refs)
    u2_all = own[:, 0:elem_count] + own[:, elem_count:] * coarse
    deficits = (PLATE_RATE - jnp.exp(u2_all)).astype(jnp.bfloat16).astype(jnp.float32)
    inside = inside_rows(deficits, *field_refs)

    state = state_ref[...]
    u, phi, sa, sb, dist, k1p = (state[i:i + 1] for i in range(6))
    here = lax.broadcasted_iota(jnp.int32, u2_all.shape, 0) == me
    u2 = jnp.sum(jnp.where(here, u2_all, 0.0), axis=0, keepdims=True)
    deficit = jnp.sum(jnp.where(here, deficits, 0.0), axis=0, keepdims=True)
    phi2 = phi + TIME_STEP * k1p
    velocity = jnp.exp(u2)
    k2p = (jnp.exp(-phi2) - velocity) / dist
    inverse = 0.5 * TIME_STEP / (sa + DAMPING * velocity)
    u_next = 0.5 * (u + u2) + (inside - sb * k2p) * inverse
    phi_next = phi + 0.5 * TIME_STEP * (k1p + k2p)
    sent = gathered(padded([u_next, inverse, phi_next], 8), rows_ref[...])
    partial = as_lines(partial_row(deficit, coarse_v_ref))
    peer_rows = elem_count // members
    for device in range(groups * members):
        peer = device % members
        sent_ref[device, 0:3, 0:peer_rows] = sent[0:3, peer * peer_rows:(peer + 1) * peer_rows]
        sent_ref[device, 3:3 + partial.shape[0], :] = partial


def finish_kernel(groups, width, got_ref, slot_ref, slot_row_ref, *refs):
    bases_refs, u_ref, phi_ref = refs[:2], refs[2], refs[3]
    elem_count = slot_ref.shape[1]
    members = got_ref.shape[0] // groups
    sums = []
    for group in range(groups):
        total = jnp.sum(got_ref[group * members:(group + 1) * members], axis=0)
        lines = [total[3 + i:4 + i, :] for i in range(pl.cdiv(width, LANES))]
        sums.append(jnp.concatenate(lines, axis=1)[:, 0:width])
    coarse = coarse_all(coefficients(sums, width // groups), members, bases_refs)
    row = slot_row_ref[...]
    block = lax.broadcasted_iota(jnp.int32, (members, elem_count), 0)
    lane_block = lax.broadcasted_iota(jnp.int32, (members, elem_count), 1) // (elem_count // members)
    rows = gathered(coarse, row)
    found = jnp.sum(jnp.where(block == lane_block, rows, 0.0), axis=0, keepdims=True)
    first = lax.axis_index("leaf") * members
    flat = peer_lanes(got_ref, first, members, 3, elem_count)
    u_next = flat[0:1] + flat[1:2] * found
    out = gathered(padded([u_next, flat[2:3]], 8), slot_ref[...])
    u_ref[...] = out[0:1]
    phi_ref[...] = out[1:2]


def call(kernel, outs, *args, scalars=(), far=(), scratch=(), flops=1000, moved=1000):
    spaces = [SMEM if i in scalars else pl.ANY if i in far else VMEM for i in range(len(args))]
    args = [
        pltpu.with_memory_space_constraint(arg, pltpu.HBM) if i in far else arg
        for i, arg in enumerate(args)
    ]
    return pl.pallas_call(
        kernel,
        out_shape=outs,
        in_specs=[pl.BlockSpec(memory_space=space) for space in spaces],
        out_specs=jax.tree.map(lambda _: pl.BlockSpec(memory_space=VMEM), outs),
        scratch_shapes=list(scratch),
        cost_estimate=pl.CostEstimate(flops=flops, bytes_accessed=moved, transcendentals=0),
        compiler_params=pltpu.CompilerParams(vmem_limit_bytes=32 * 1024 * 1024),
    )(*args)


def shape(*dims, dtype=jnp.float32):
    return jax.ShapeDtypeStruct(dims, dtype)


def body(
    ln_rate,
    log_state,
    sigma,
    fric_a,
    fric_b,
    slip_dist,
    leaf_of_elem,
    near_blocks,
    near_col,
    near_count,
    far_u,
    far_v,
    far_col,
    far_rank,
    coarse_u,
    coarse_v,
):
    members = lax.axis_size("blk")
    elems = ln_rate.shape[0]
    leaf_size = near_blocks.shape[1]
    groups, rank = coarse_v.shape[0], coarse_v.shape[1]
    devices = groups * members
    width = groups * rank
    lines = pl.cdiv(width, LANES)
    sent_rows = 1 << (2 + lines).bit_length()
    integer = jnp.int32

    def swap(value, axes):
        return lax.all_to_all(value, axes, split_axis=0, concat_axis=0, tiled=True)

    def partner(value, bit):
        return lax.ppermute(value, "blk", [(i, i ^ (1 << bit)) for i in range(members)])

    elem_args = [
        value.reshape(1, elems)
        for value in (leaf_of_elem, ln_rate, log_state, sigma, fric_a, fric_b, slip_dist)
    ]
    scalar_args = [near_col, far_col, far_rank]
    weights = [
        near_blocks, far_u.reshape(-1, leaf_size), far_v.reshape(-1, leaf_size),
        coarse_v.reshape(width, elems),
    ]
    far_rows = weights[1].shape[0]
    sent, slot, slot_row, near_mask, far_mask, near, far_u, far_v, coarse_v = call(
        functools.partial(sort_kernel, members),
        (
            shape(members, 8 + 2 * (elems // LANES), LANES),
            shape(1, elems, dtype=integer),
            shape(1, elems, dtype=integer),
            shape(near_blocks.shape[0], members, leaf_size),
            shape(members, far_rows),
            *[shape(*value.shape, dtype=jnp.bfloat16) for value in weights],
        ),
        *elem_args, *scalar_args, *weights, far=range(14),
        scratch=[VMEM(value.shape, value.dtype) for value in elem_args]
        + [SMEM(value.shape, value.dtype) for value in scalar_args]
        + [pltpu.SemaphoreType.DMA((14,))],
    )
    bases = coarse_u.reshape(width, elems)
    for bit in range(members.bit_length() - 2, 0, -1):
        rows_out = 2 * bases.shape[0]
        kernel = stack_kernel
        if bit == 1:
            rows_out = rows_out // groups * (groups - 1)
            kernel = functools.partial(stack_foreign_kernel, groups, rank)
        bases = call(
            kernel, shape(rows_out, elems, dtype=jnp.bfloat16),
            bases, partner(bases, bit), slot, flops=1 << 26, moved=1 << 22,
        )
    bases = bases, partner(bases, 0)
    complete = call(mark_kernel, shape(16, LANES), bases[1], flops=1 << 34, moved=1 << 26)
    fields = near_count, near, far_u, far_v, near_mask, far_mask
    state, rows, out = call(
        place_kernel,
        (
            shape(8, elems),
            shape(1, elems, dtype=integer),
            shape(devices, 1, 2 * elems + lines * LANES),
        ),
        swap(sent, "blk"), coarse_v, *fields, scalars=(2,),
        scratch=[VMEM((members * (elems // LANES), LANES), jnp.float32)],
    )
    sent = call(
        functools.partial(second_kernel, groups), shape(devices, sent_rows, LANES),
        state, rows, swap(out, ("leaf", "blk")), complete, coarse_v, *bases, *fields, scalars=(7,),
    )
    u, phi = call(
        functools.partial(finish_kernel, groups, width), (shape(1, elems), shape(1, elems)),
        swap(sent, ("leaf", "blk")), slot, slot_row, *bases,
    )
    return u.reshape(elems), phi.reshape(elems)


def solution(mesh):
    each = P(("leaf", "blk"))
    blocks = P(("leaf", "blk"), None, None)
    last = P(None, None, ("leaf", "blk"))
    in_specs = (each,) * 7 + (blocks, each, each, blocks, blocks, each, each, last, last)
    return jax.shard_map(body, mesh=mesh, in_specs=in_specs, out_specs=(each, each), check_vma=False)
```

```python
import functools

import jax
import jax.numpy as jnp
from jax import lax
from jax.experimental import pallas as pl
from jax.experimental.pallas import tpu as pltpu
from jax.sharding import PartitionSpec as P

DAMPING = 0.5
PLATE_RATE = 1.0
TIME_STEP = 0.2

NN = (((1,), (0,)), ((), ()))
NT = (((1,), (1,)), ((), ()))
VMEM = pltpu.VMEM
SMEM = pltpu.SMEM

LANES = 128
HALF = 64


def dot(left, right, dims):
    return lax.dot_general(left, right, dims, preferred_element_type=jnp.float32)


def low_matrix(index_row):
    rows = lax.broadcasted_iota(jnp.int32, (LANES, index_row.shape[1]), 0)
    return jnp.where(rows == (index_row & (LANES - 1)), 1.0, 0.0).astype(jnp.bfloat16)


def three_parts(values):
    high = values.astype(jnp.bfloat16).astype(jnp.float32)
    rest = values - high
    middle = rest.astype(jnp.bfloat16).astype(jnp.float32)
    return jnp.concatenate([high, middle, rest - middle], axis=0)


def joined(parts):
    count = parts.shape[0] // 3
    return parts[0:count] + parts[count:2 * count] + parts[2 * count:]


def scattered(values, index_row):
    parts = three_parts(values)
    count = parts.shape[0]
    high = index_row // LANES
    pieces = values.shape[1] // LANES
    left = jnp.concatenate([jnp.where(high == piece, parts, 0.0) for piece in range(pieces)], axis=0)
    moved = dot(left.astype(jnp.bfloat16), low_matrix(index_row), NT)
    return jnp.concatenate(
        [joined(moved[piece * count:(piece + 1) * count]) for piece in range(pieces)], axis=1
    )


def gathered(values, index_row):
    parts = three_parts(values)
    count = parts.shape[0]
    high = index_row // LANES
    pieces = values.shape[1] // LANES
    left = jnp.concatenate(
        [parts[:, piece * LANES:(piece + 1) * LANES] for piece in range(pieces)], axis=0
    )
    moved = dot(left.astype(jnp.bfloat16), low_matrix(index_row), NN)
    total = jnp.zeros((count, index_row.shape[1]), jnp.float32)
    for piece in range(pieces):
        total = jnp.where(high == piece, moved[piece * count:(piece + 1) * count], total)
    return joined(total)


def padded(rows, count):
    missing = count - len(rows)
    if missing:
        rows = rows + [jnp.zeros((missing, rows[0].shape[1]), jnp.float32)]
    return jnp.concatenate(rows, axis=0)


def as_lines(row):
    return jnp.concatenate(
        [row[:, i * LANES:(i + 1) * LANES] for i in range(row.shape[1] // LANES)], axis=0
    )


def peer_lanes(ref, first, members, rows, elem_count):
    width = elem_count // members
    return jnp.concatenate([ref[first + peer, 0:rows, 0:width] for peer in range(members)], axis=1)


def start_copies(sources, targets, sems):
    copies = [
        pltpu.make_async_copy(source, target, sems.at[i])
        for i, (source, target) in enumerate(zip(sources, targets))
    ]
    for copy in copies:
        copy.start()
    return copies


def sort_kernel(members, *refs):
    elem_refs, scalar_refs, weight_refs = refs[:7], refs[7:10], refs[10:14]
    sent_ref, slot_ref, slot_row_ref, near_mask_ref, far_mask_ref = refs[14:19]
    weight_outs, elem_bufs, scalar_bufs, sems = refs[19:23], refs[23:30], refs[30:33], refs[33]
    copies = start_copies(
        [*elem_refs, *scalar_refs, *weight_refs], [*elem_bufs, *scalar_bufs, *weight_outs], sems
    )
    mine = lax.axis_index("leaf")
    elem_count = elem_bufs[0].shape[1]
    peer_rows = elem_count // members
    pieces = elem_count // LANES
    before = lax.broadcasted_iota(jnp.int32, (LANES, LANES), 0)
    after = lax.broadcasted_iota(jnp.int32, (LANES, LANES), 1)
    triangle = jnp.where(before < after, 1.0, 0.0).astype(jnp.bfloat16)
    copies[0].wait()
    local = elem_bufs[0][...] - mine * (members * elem_count)
    target = local // elem_count
    target_row = local - target * elem_count
    peers = lax.broadcasted_iota(jnp.int32, (members, elem_count), 0)
    onehot = jnp.where(peers == target, 1.0, 0.0)
    lines = [onehot[:, i * LANES:(i + 1) * LANES] for i in range(pieces)]
    inside = dot(jnp.concatenate(lines, axis=0).astype(jnp.bfloat16), triangle, NN)
    passed = jnp.zeros((members, 1), jnp.float32)
    ranks = []
    for i, line in enumerate(lines):
        earlier = inside[i * members:(i + 1) * members] + passed
        ranks.append(jnp.sum(earlier * line, axis=0, keepdims=True))
        passed = passed + jnp.sum(line, axis=1, keepdims=True)
    slot = target * peer_rows + jnp.concatenate(ranks, axis=1).astype(jnp.int32)
    slot_ref[...] = slot
    for copy in copies[1:7]:
        copy.wait()
    u, phi, sigma, fric_a, fric_b, dist = (buf[...] for buf in elem_bufs[1:])
    velocity = jnp.exp(u)
    deficit = (PLATE_RATE - velocity).astype(jnp.bfloat16).astype(jnp.float32)
    sa = sigma * fric_a
    factor = TIME_STEP / (sa + DAMPING * velocity)
    rows = [u, phi, sa, sigma * fric_b, dist, target_row.astype(jnp.float32), deficit, factor]
    values = scattered(padded(rows, 8), slot)
    slot_row_ref[...] = values[5:6].astype(jnp.int32)
    everyone = jnp.concatenate([as_lines(values[i:i + 1]) for i in (6, 5, 7)], axis=0)
    for peer in range(members):
        sent_ref[peer, 0:3 * pieces, :] = everyone
        part = values[0:6, peer * peer_rows:(peer + 1) * peer_rows]
        sent_ref[peer, 3 * pieces:3 * pieces + 4, 0:peer_rows] = part[0:4]
        sent_ref[peer, 3 * pieces:3 * pieces + 2, HALF:HALF + peer_rows] = part[4:6]

    for copy in copies[7:10]:
        copy.wait()
    near_col, far_col, far_rank = scalar_bufs
    far_slots = far_col.shape[0]
    far_width = far_mask_ref.shape[1] // far_slots
    block = lax.broadcasted_iota(jnp.int32, near_mask_ref.shape[1:], 0)
    for number in range(near_mask_ref.shape[0]):
        near_mask_ref[number] = jnp.where(block == near_col[number], 1.0, 0.0)
    block = lax.broadcasted_iota(jnp.int32, far_mask_ref.shape, 0)
    lane = lax.broadcasted_iota(jnp.int32, far_mask_ref.shape, 1)
    column = jnp.full(far_mask_ref.shape, -1, jnp.int32)
    for number in range(far_slots):
        low = number * far_width
        kept = (lane >= low) & (lane < low + far_rank[number])
        column = jnp.where(kept, far_col[number], column)
    far_mask_ref[...] = jnp.where(block == column, 1.0, 0.0)
    for copy in copies[10:]:
        copy.wait()


def partial_row(deficit, coarse_v_ref):
    wide = jnp.broadcast_to(deficit, (8, deficit.shape[1])).astype(jnp.bfloat16)
    partial = dot(wide, coarse_v_ref[...], NT)[0:1]
    rest = -partial.shape[1] % LANES
    if rest:
        partial = jnp.concatenate([partial, jnp.zeros((1, rest), jnp.float32)], axis=1)
    return partial


def inside_rows(deficits, near_count, near_ref, far_u_ref, far_v_ref, near_mask_ref, far_mask_ref):
    total = jnp.zeros(deficits.shape, jnp.float32)
    for slot in range(near_ref.shape[0]):
        live = jnp.where(slot < near_count[0], 1.0, 0.0)
        source = (deficits * (near_mask_ref[slot] * live)).astype(jnp.bfloat16)
        total = total + dot(source, near_ref[slot], NT)
    project = dot(deficits.astype(jnp.bfloat16), far_v_ref[...], NT) * far_mask_ref[...]
    project = jnp.sum(project, axis=0, keepdims=True)
    project = jnp.broadcast_to(project, (8, project.shape[1])).astype(jnp.bfloat16)
    far = dot(project, far_u_ref[...], NN)
    return jnp.sum(total, axis=0, keepdims=True) + far[0:1]


def coefficients(sums, rank):
    groups, width = len(sums), sums[0].shape[1]
    mine = lax.axis_index("leaf")
    table = padded(sums, -(-groups // 8) * 8)
    lane = lax.broadcasted_iota(jnp.int32, table.shape, 1) // rank
    row = lax.broadcasted_iota(jnp.int32, table.shape, 0)
    table = jnp.where(lane == mine, table, 0.0).astype(jnp.bfloat16)
    across = lax.broadcasted_iota(jnp.int32, (width, width), 0) % rank
    down = lax.broadcasted_iota(jnp.int32, (width, width), 1) % rank
    spread = dot(table, jnp.where(across == down, 1.0, 0.0).astype(jnp.bfloat16), NN)
    weights = jnp.sum(jnp.where(row == mine ^ (lane + 1), spread, 0.0), axis=0, keepdims=True)
    return weights[:, 0:width - rank]


def coarse_all(weights, members, bases_refs):
    row = lax.broadcasted_iota(jnp.int32, (members, weights.shape[1]), 0) ^ lax.axis_index("blk")
    bits = members.bit_length() - 1
    total = jnp.zeros((members, bases_refs[0].shape[1]), jnp.float32)
    for number, ref in enumerate(bases_refs):
        left = []
        for place in range(members // 2):
            source = number
            for bit in range(bits - 1):
                source |= (place >> bit & 1) << (bits - 1 - bit)
            left.append(jnp.where(row == source, weights, 0.0))
        left = jnp.concatenate(left, axis=1).astype(jnp.bfloat16)
        total = total + dot(left, ref[...], NN)
    return total


def stack_kernel(held_ref, came_ref, *refs):
    out_ref = refs[-1]
    count = held_ref.shape[0]
    out_ref[0:count, :] = held_ref[...]
    out_ref[count:2 * count, :] = came_ref[...]


def stack_foreign_kernel(groups, rank, held_ref, came_ref, *refs):
    out_ref = refs[-1]
    width = groups * rank
    mine = lax.axis_index("leaf")
    place = 0
    for ref in (held_ref, came_ref):
        for low in range(0, ref.shape[0], width):
            for shift in range(1, groups):
                out_ref[place:place + rank, :] = ref[pl.ds(low + (mine ^ shift) * rank, rank), :]
                place += rank


def mark_kernel(came_ref, out_ref):
    out_ref[...] = came_ref[0:16, 0:LANES].astype(jnp.float32)


def place_kernel(got_ref, coarse_v_ref, *refs):
    field_refs, state_ref, factor_ref, rows_ref, out_ref, lines_ref = refs[:6], *refs[6:]
    members = got_ref.shape[0]
    elem_count = state_ref.shape[1]
    pieces = elem_count // LANES
    peer_rows = elem_count // members
    count = LANES // peer_rows * pieces
    line_row = lax.broadcasted_iota(jnp.int32, (count, LANES), 0)
    lane_block = lax.broadcasted_iota(jnp.int32, (count, LANES), 1) // peer_rows
    own_lane = line_row // pieces == lane_block
    for line in range(pieces):
        rows = got_ref[:, pieces + line, :].astype(jnp.int32)
        parts = [got_ref[:, line, :]]
        split = three_parts(got_ref[:, 2 * pieces + line, :])
        parts += [split[i * members:(i + 1) * members] for i in range(3)]
        left, right = [], []
        for peer in range(members):
            row = rows[peer:peer + 1]
            kept = own_lane & (line_row % pieces == row // LANES)
            left.append(
                jnp.concatenate([jnp.where(kept, part[peer:peer + 1], 0.0) for part in parts], axis=0)
            )
            right.append(low_matrix(row))
        left = jnp.concatenate(left, axis=1).astype(jnp.bfloat16)
        placed = dot(left, jnp.concatenate(right, axis=1), NT)
        lines_ref[0, line * count:(line + 1) * count, :] = placed[0:count]
        lines_ref[1, line * count:(line + 1) * count, :] = joined(placed[count:])

    def blocks(number):
        return jnp.concatenate(
            [lines_ref[number, pl.ds(piece, members, stride=pieces), :] for piece in range(pieces)],
            axis=1,
        )

    factor_ref[...] = blocks(1)
    inside = inside_rows(blocks(0), *field_refs)

    first = 3 * pieces
    flat = jnp.concatenate(
        [got_ref[peer, first:first + 4, 0:peer_rows] for peer in range(members)], axis=1
    )
    rest = jnp.concatenate(
        [got_ref[peer, first:first + 2, HALF:HALF + peer_rows] for peer in range(members)], axis=1
    )
    rows = rest[1:2].astype(jnp.int32)
    rows_ref[...] = rows
    fields = [flat[i:i + 1] for i in range(4)] + [rest[0:1]]
    state = scattered(padded(fields, 8), rows)
    u, phi, sa, sb, dist = (state[i:i + 1] for i in range(5))
    velocity = jnp.exp(u)
    deficit = (PLATE_RATE - velocity).astype(jnp.bfloat16).astype(jnp.float32)
    k1p = (jnp.exp(-phi) - velocity) / dist
    u2 = u + TIME_STEP * ((inside - sb * k1p) / (sa + DAMPING * velocity))
    state_ref[...] = padded([u, phi, sa, sb, dist, k1p], 8)
    sent = jnp.concatenate([u2, partial_row(deficit, coarse_v_ref)], axis=1)
    out_ref[...] = jnp.broadcast_to(sent[None], out_ref.shape)


def second_kernel(
    groups, state_ref, factor_ref, rows_ref, all_ref, complete_ref, coarse_v_ref, *refs
):
    bases_refs, field_refs, sent_ref = refs[:2], refs[2:8], refs[8]
    members, elem_count = refs[6].shape[1], state_ref.shape[1]
    width = coarse_v_ref.shape[0]
    mine, me = lax.axis_index("leaf"), lax.axis_index("blk")
    sums = [
        jnp.sum(
            all_ref[group * members:(group + 1) * members, 0, elem_count:elem_count + width],
            axis=0, keepdims=True,
        )
        for group in range(groups)
    ]
    weights = coefficients(sums, width // groups)
    own = all_ref[pl.ds(mine * members, members), 0, 0:elem_count]
    coarse = coarse_all(weights, members, bases_refs)
    u2_all = own + factor_ref[...] * coarse
    deficits = (PLATE_RATE - jnp.exp(u2_all)).astype(jnp.bfloat16).astype(jnp.float32)
    inside = inside_rows(deficits, *field_refs)

    state = state_ref[...]
    u, phi, sa, sb, dist, k1p = (state[i:i + 1] for i in range(6))
    here = lax.broadcasted_iota(jnp.int32, u2_all.shape, 0) == me
    u2 = jnp.sum(jnp.where(here, u2_all, 0.0), axis=0, keepdims=True)
    deficit = jnp.sum(jnp.where(here, deficits, 0.0), axis=0, keepdims=True)
    phi2 = phi + TIME_STEP * k1p
    velocity = jnp.exp(u2)
    k2p = (jnp.exp(-phi2) - velocity) / dist
    inverse = 0.5 * TIME_STEP / (sa + DAMPING * velocity)
    u_next = 0.5 * (u + u2) + (inside - sb * k2p) * inverse
    phi_next = phi + 0.5 * TIME_STEP * (k1p + k2p)
    sent = gathered(padded([u_next, inverse, phi_next], 8), rows_ref[...])
    partial = as_lines(partial_row(deficit, coarse_v_ref))
    peer_rows = elem_count // members
    for device in range(groups * members):
        peer = device % members
        sent_ref[device, 0:3, 0:peer_rows] = sent[0:3, peer * peer_rows:(peer + 1) * peer_rows]
        sent_ref[device, 3:3 + partial.shape[0], :] = partial


def finish_kernel(groups, width, got_ref, slot_ref, slot_row_ref, *refs):
    bases_refs, u_ref, phi_ref = refs[:2], refs[2], refs[3]
    elem_count = slot_ref.shape[1]
    members = got_ref.shape[0] // groups
    sums = []
    for group in range(groups):
        total = jnp.sum(got_ref[group * members:(group + 1) * members], axis=0)
        lines = [total[3 + i:4 + i, :] for i in range(pl.cdiv(width, LANES))]
        sums.append(jnp.concatenate(lines, axis=1)[:, 0:width])
    coarse = coarse_all(coefficients(sums, width // groups), members, bases_refs)
    row = slot_row_ref[...]
    block = lax.broadcasted_iota(jnp.int32, (members, elem_count), 0)
    lane_block = lax.broadcasted_iota(jnp.int32, (members, elem_count), 1) // (elem_count // members)
    rows = gathered(coarse, row)
    found = jnp.sum(jnp.where(block == lane_block, rows, 0.0), axis=0, keepdims=True)
    first = lax.axis_index("leaf") * members
    flat = peer_lanes(got_ref, first, members, 3, elem_count)
    u_next = flat[0:1] + flat[1:2] * found
    out = gathered(padded([u_next, flat[2:3]], 8), slot_ref[...])
    u_ref[...] = out[0:1]
    phi_ref[...] = out[1:2]


def call(kernel, outs, *args, scalars=(), far=(), scratch=(), flops=1000, moved=1000):
    spaces = [SMEM if i in scalars else pl.ANY if i in far else VMEM for i in range(len(args))]
    args = [
        pltpu.with_memory_space_constraint(arg, pltpu.HBM) if i in far else arg
        for i, arg in enumerate(args)
    ]
    return pl.pallas_call(
        kernel,
        out_shape=outs,
        in_specs=[pl.BlockSpec(memory_space=space) for space in spaces],
        out_specs=jax.tree.map(lambda _: pl.BlockSpec(memory_space=VMEM), outs),
        scratch_shapes=list(scratch),
        cost_estimate=pl.CostEstimate(flops=flops, bytes_accessed=moved, transcendentals=0),
        compiler_params=pltpu.CompilerParams(vmem_limit_bytes=32 * 1024 * 1024),
    )(*args)


def shape(*dims, dtype=jnp.float32):
    return jax.ShapeDtypeStruct(dims, dtype)


def body(
    ln_rate,
    log_state,
    sigma,
    fric_a,
    fric_b,
    slip_dist,
    leaf_of_elem,
    near_blocks,
    near_col,
    near_count,
    far_u,
    far_v,
    far_col,
    far_rank,
    coarse_u,
    coarse_v,
):
    members = lax.axis_size("blk")
    elems = ln_rate.shape[0]
    leaf_size = near_blocks.shape[1]
    groups, rank = coarse_v.shape[0], coarse_v.shape[1]
    devices = groups * members
    width = groups * rank
    lines = pl.cdiv(width, LANES)
    sent_rows = 1 << (2 + lines).bit_length()
    integer = jnp.int32

    def swap(value, axes):
        return lax.all_to_all(value, axes, split_axis=0, concat_axis=0, tiled=True)

    def partner(value, bit):
        return lax.ppermute(value, "blk", [(i, i ^ (1 << bit)) for i in range(members)])

    elem_args = [
        value.reshape(1, elems)
        for value in (leaf_of_elem, ln_rate, log_state, sigma, fric_a, fric_b, slip_dist)
    ]
    scalar_args = [near_col, far_col, far_rank]
    weights = [
        near_blocks, far_u.reshape(-1, leaf_size), far_v.reshape(-1, leaf_size),
        coarse_v.reshape(width, elems),
    ]
    far_rows = weights[1].shape[0]
    sent, slot, slot_row, near_mask, far_mask, near, far_u, far_v, coarse_v = call(
        functools.partial(sort_kernel, members),
        (
            shape(members, -(-(3 * (elems // LANES) + 4) // 8) * 8, LANES),
            shape(1, elems, dtype=integer),
            shape(1, elems, dtype=integer),
            shape(near_blocks.shape[0], members, leaf_size),
            shape(members, far_rows),
            *[shape(*value.shape, dtype=jnp.bfloat16) for value in weights],
        ),
        *elem_args, *scalar_args, *weights, far=range(14),
        scratch=[VMEM(value.shape, value.dtype) for value in elem_args]
        + [SMEM(value.shape, value.dtype) for value in scalar_args]
        + [pltpu.SemaphoreType.DMA((14,))],
    )
    fields = near_count, near, far_u, far_v, near_mask, far_mask
    state, factor, rows, out = call(
        place_kernel,
        (
            shape(8, elems),
            shape(members, elems),
            shape(1, elems, dtype=integer),
            shape(devices, 1, elems + lines * LANES),
        ),
        swap(sent, "blk"), coarse_v, *fields, scalars=(2,),
        scratch=[VMEM((2, members * (elems // LANES), LANES), jnp.float32)],
    )
    bases = coarse_u.reshape(width, elems)
    for bit in range(members.bit_length() - 2, 0, -1):
        rows_out = 2 * bases.shape[0]
        kernel, after = stack_kernel, slot
        if bit == 1:
            rows_out = rows_out // groups * (groups - 1)
            kernel, after = functools.partial(stack_foreign_kernel, groups, rank), rows
        bases = call(
            kernel, shape(rows_out, elems, dtype=jnp.bfloat16),
            bases, partner(bases, bit), after, flops=1 << 26, moved=1 << 22,
        )
    bases = bases, partner(bases, 0)
    complete = call(mark_kernel, shape(16, LANES), bases[1], flops=1 << 34, moved=1 << 26)
    sent = call(
        functools.partial(second_kernel, groups), shape(devices, sent_rows, LANES),
        state, factor, rows, swap(out, ("leaf", "blk")), complete, coarse_v, *bases, *fields, scalars=(8,),
    )
    u, phi = call(
        functools.partial(finish_kernel, groups, width), (shape(1, elems), shape(1, elems)),
        swap(sent, ("leaf", "blk")), slot, slot_row, *bases,
    )
    return u.reshape(elems), phi.reshape(elems)


def solution(mesh):
    each = P(("leaf", "blk"))
    blocks = P(("leaf", "blk"), None, None)
    last = P(None, None, ("leaf", "blk"))
    in_specs = (each,) * 7 + (blocks, each, each, blocks, blocks, each, each, last, last)
    return jax.shard_map(body, mesh=mesh, in_specs=in_specs, out_specs=(each, each), check_vma=False)
```

```python
import functools

import jax
import jax.numpy as jnp
from jax import lax
from jax.experimental import pallas as pl
from jax.experimental.pallas import tpu as pltpu
from jax.sharding import PartitionSpec as P

DAMPING = 0.5
PLATE_RATE = 1.0
TIME_STEP = 0.2

NN = (((1,), (0,)), ((), ()))
NT = (((1,), (1,)), ((), ()))
VMEM = pltpu.VMEM
SMEM = pltpu.SMEM

LANES = 128
HALF = 64


def dot(left, right, dims):
    return lax.dot_general(left, right, dims, preferred_element_type=jnp.float32)


def low_matrix(index_row):
    rows = lax.broadcasted_iota(jnp.int32, (LANES, index_row.shape[1]), 0)
    return jnp.where(rows == (index_row & (LANES - 1)), 1.0, 0.0).astype(jnp.bfloat16)


def three_parts(values):
    high = values.astype(jnp.bfloat16).astype(jnp.float32)
    rest = values - high
    middle = rest.astype(jnp.bfloat16).astype(jnp.float32)
    return jnp.concatenate([high, middle, rest - middle], axis=0)


def joined(parts):
    count = parts.shape[0] // 3
    return parts[0:count] + parts[count:2 * count] + parts[2 * count:]


def scattered(values, index_row):
    parts = three_parts(values)
    count = parts.shape[0]
    high = index_row // LANES
    pieces = values.shape[1] // LANES
    left = jnp.concatenate([jnp.where(high == piece, parts, 0.0) for piece in range(pieces)], axis=0)
    moved = dot(left.astype(jnp.bfloat16), low_matrix(index_row), NT)
    return jnp.concatenate(
        [joined(moved[piece * count:(piece + 1) * count]) for piece in range(pieces)], axis=1
    )


def gathered(values, index_row):
    parts = three_parts(values)
    count = parts.shape[0]
    high = index_row // LANES
    pieces = values.shape[1] // LANES
    left = jnp.concatenate(
        [parts[:, piece * LANES:(piece + 1) * LANES] for piece in range(pieces)], axis=0
    )
    moved = dot(left.astype(jnp.bfloat16), low_matrix(index_row), NN)
    total = jnp.zeros((count, index_row.shape[1]), jnp.float32)
    for piece in range(pieces):
        total = jnp.where(high == piece, moved[piece * count:(piece + 1) * count], total)
    return joined(total)


def padded(rows, count):
    missing = count - len(rows)
    if missing:
        rows = rows + [jnp.zeros((missing, rows[0].shape[1]), jnp.float32)]
    return jnp.concatenate(rows, axis=0)


def as_lines(row):
    return jnp.concatenate(
        [row[:, i * LANES:(i + 1) * LANES] for i in range(row.shape[1] // LANES)], axis=0
    )


def peer_lanes(ref, first, members, rows, elem_count):
    width = elem_count // members
    return jnp.concatenate([ref[first + peer, 0:rows, 0:width] for peer in range(members)], axis=1)


def start_copies(sources, targets, sems):
    copies = [
        pltpu.make_async_copy(source, target, sems.at[i])
        for i, (source, target) in enumerate(zip(sources, targets))
    ]
    for copy in copies:
        copy.start()
    return copies


def sort_kernel(members, *refs):
    elem_refs, scalar_refs, weight_refs = refs[:7], refs[7:10], refs[10:14]
    sent_ref, slot_ref, slot_row_ref, near_mask_ref, far_mask_ref = refs[14:19]
    weight_outs, elem_bufs, scalar_bufs, sems = refs[19:23], refs[23:30], refs[30:33], refs[33]
    copies = start_copies(
        [*elem_refs, *scalar_refs, *weight_refs], [*elem_bufs, *scalar_bufs, *weight_outs], sems
    )
    mine = lax.axis_index("leaf")
    elem_count = elem_bufs[0].shape[1]
    peer_rows = elem_count // members
    pieces = elem_count // LANES
    before = lax.broadcasted_iota(jnp.int32, (LANES, LANES), 0)
    after = lax.broadcasted_iota(jnp.int32, (LANES, LANES), 1)
    triangle = jnp.where(before < after, 1.0, 0.0).astype(jnp.bfloat16)
    copies[0].wait()
    local = elem_bufs[0][...] - mine * (members * elem_count)
    target = local // elem_count
    target_row = local - target * elem_count
    peers = lax.broadcasted_iota(jnp.int32, (members, elem_count), 0)
    onehot = jnp.where(peers == target, 1.0, 0.0)
    lines = [onehot[:, i * LANES:(i + 1) * LANES] for i in range(pieces)]
    inside = dot(jnp.concatenate(lines, axis=0).astype(jnp.bfloat16), triangle, NN)
    passed = jnp.zeros((members, 1), jnp.float32)
    ranks = []
    for i, line in enumerate(lines):
        earlier = inside[i * members:(i + 1) * members] + passed
        ranks.append(jnp.sum(earlier * line, axis=0, keepdims=True))
        passed = passed + jnp.sum(line, axis=1, keepdims=True)
    slot = target * peer_rows + jnp.concatenate(ranks, axis=1).astype(jnp.int32)
    slot_ref[...] = slot
    for copy in copies[1:7]:
        copy.wait()
    u, phi, sigma, fric_a, fric_b, dist = (buf[...] for buf in elem_bufs[1:])
    velocity = jnp.exp(u)
    deficit = (PLATE_RATE - velocity).astype(jnp.bfloat16).astype(jnp.float32)
    sa = sigma * fric_a
    factor = TIME_STEP / (sa + DAMPING * velocity)
    rows = [u, phi, sa, sigma * fric_b, dist, target_row.astype(jnp.float32), deficit, factor]
    values = scattered(padded(rows, 8), slot)
    slot_row_ref[...] = values[5:6].astype(jnp.int32)
    everyone = jnp.concatenate([as_lines(values[i:i + 1]) for i in (6, 5, 7)], axis=0)
    for peer in range(members):
        sent_ref[peer, 0:3 * pieces, :] = everyone
        part = values[0:6, peer * peer_rows:(peer + 1) * peer_rows]
        sent_ref[peer, 3 * pieces:3 * pieces + 4, 0:peer_rows] = part[0:4]
        sent_ref[peer, 3 * pieces:3 * pieces + 2, HALF:HALF + peer_rows] = part[4:6]

    for copy in copies[7:10]:
        copy.wait()
    near_col, far_col, far_rank = scalar_bufs
    far_slots = far_col.shape[0]
    far_width = far_mask_ref.shape[1] // far_slots
    block = lax.broadcasted_iota(jnp.int32, near_mask_ref.shape[1:], 0)
    for number in range(near_mask_ref.shape[0]):
        near_mask_ref[number] = jnp.where(block == near_col[number], 1.0, 0.0)
    block = lax.broadcasted_iota(jnp.int32, far_mask_ref.shape, 0)
    lane = lax.broadcasted_iota(jnp.int32, far_mask_ref.shape, 1)
    column = jnp.full(far_mask_ref.shape, -1, jnp.int32)
    for number in range(far_slots):
        low = number * far_width
        kept = (lane >= low) & (lane < low + far_rank[number])
        column = jnp.where(kept, far_col[number], column)
    far_mask_ref[...] = jnp.where(block == column, 1.0, 0.0)
    for copy in copies[10:]:
        copy.wait()


def partial_row(deficit, coarse_v_ref):
    wide = jnp.broadcast_to(deficit, (8, deficit.shape[1])).astype(jnp.bfloat16)
    partial = dot(wide, coarse_v_ref[...], NT)[0:1]
    rest = -partial.shape[1] % LANES
    if rest:
        partial = jnp.concatenate([partial, jnp.zeros((1, rest), jnp.float32)], axis=1)
    return partial


def inside_rows(deficits, near_count, near_ref, far_u_ref, far_v_ref, near_mask_ref, far_mask_ref):
    total = jnp.zeros(deficits.shape, jnp.float32)
    for slot in range(near_ref.shape[0]):
        live = jnp.where(slot < near_count[0], 1.0, 0.0)
        source = (deficits * (near_mask_ref[slot] * live)).astype(jnp.bfloat16)
        total = total + dot(source, near_ref[slot], NT)
    project = dot(deficits.astype(jnp.bfloat16), far_v_ref[...], NT) * far_mask_ref[...]
    project = jnp.sum(project, axis=0, keepdims=True)
    project = jnp.broadcast_to(project, (8, project.shape[1])).astype(jnp.bfloat16)
    far = dot(project, far_u_ref[...], NN)
    return jnp.sum(total, axis=0, keepdims=True) + far[0:1]


def coefficients(sums, rank):
    groups, width = len(sums), sums[0].shape[1]
    mine = lax.axis_index("leaf")
    table = padded(sums, -(-groups // 8) * 8)
    lane = lax.broadcasted_iota(jnp.int32, table.shape, 1) // rank
    row = lax.broadcasted_iota(jnp.int32, table.shape, 0)
    table = jnp.where(lane == mine, table, 0.0).astype(jnp.bfloat16)
    across = lax.broadcasted_iota(jnp.int32, (width, width), 0) % rank
    down = lax.broadcasted_iota(jnp.int32, (width, width), 1) % rank
    spread = dot(table, jnp.where(across == down, 1.0, 0.0).astype(jnp.bfloat16), NN)
    weights = jnp.sum(jnp.where(row == mine ^ (lane + 1), spread, 0.0), axis=0, keepdims=True)
    return weights[:, 0:width - rank]


def coarse_all(weights, members, bases_refs):
    row = lax.broadcasted_iota(jnp.int32, (members, weights.shape[1]), 0) ^ lax.axis_index("blk")
    bits = members.bit_length() - 1
    total = jnp.zeros((members, bases_refs[0].shape[1]), jnp.float32)
    for number, ref in enumerate(bases_refs):
        left = []
        for place in range(members // 2):
            source = number
            for bit in range(bits - 1):
                source |= (place >> bit & 1) << (bits - 1 - bit)
            left.append(jnp.where(row == source, weights, 0.0))
        left = jnp.concatenate(left, axis=1).astype(jnp.bfloat16)
        total = total + dot(left, ref[...], NN)
    return total


def stack_kernel(held_ref, came_ref, *refs):
    out_ref = refs[-1]
    count = held_ref.shape[0]
    out_ref[0:count, :] = held_ref[...]
    out_ref[count:2 * count, :] = came_ref[...]


def stack_foreign_kernel(groups, rank, held_ref, came_ref, *refs):
    out_ref = refs[-1]
    width = groups * rank
    mine = lax.axis_index("leaf")
    place = 0
    for ref in (held_ref, came_ref):
        for low in range(0, ref.shape[0], width):
            for shift in range(1, groups):
                out_ref[place:place + rank, :] = ref[pl.ds(low + (mine ^ shift) * rank, rank), :]
                place += rank


def mark_kernel(came_ref, out_ref):
    out_ref[...] = came_ref[0:16, 0:LANES].astype(jnp.float32)


def place_kernel(got_ref, coarse_v_ref, *refs):
    field_refs, state_ref, factor_ref, rows_ref, out_ref, lines_ref = refs[:6], *refs[6:]
    members = got_ref.shape[0]
    elem_count = state_ref.shape[1]
    pieces = elem_count // LANES
    peer_rows = elem_count // members
    count = LANES // peer_rows * pieces
    line_row = lax.broadcasted_iota(jnp.int32, (count, LANES), 0)
    lane_block = lax.broadcasted_iota(jnp.int32, (count, LANES), 1) // peer_rows
    own_lane = line_row // pieces == lane_block
    for line in range(pieces):
        rows = got_ref[:, pieces + line, :].astype(jnp.int32)
        parts = [got_ref[:, line, :]]
        split = three_parts(got_ref[:, 2 * pieces + line, :])
        parts += [split[i * members:(i + 1) * members] for i in range(3)]
        left, right = [], []
        for peer in range(members):
            row = rows[peer:peer + 1]
            kept = own_lane & (line_row % pieces == row // LANES)
            left.append(
                jnp.concatenate([jnp.where(kept, part[peer:peer + 1], 0.0) for part in parts], axis=0)
            )
            right.append(low_matrix(row))
        left = jnp.concatenate(left, axis=1).astype(jnp.bfloat16)
        placed = dot(left, jnp.concatenate(right, axis=1), NT)
        lines_ref[0, line * count:(line + 1) * count, :] = placed[0:count]
        lines_ref[1, line * count:(line + 1) * count, :] = joined(placed[count:])

    def blocks(number):
        return jnp.concatenate(
            [lines_ref[number, pl.ds(piece, members, stride=pieces), :] for piece in range(pieces)],
            axis=1,
        )

    factor_ref[...] = blocks(1)
    inside = inside_rows(blocks(0), *field_refs)

    first = 3 * pieces
    flat = jnp.concatenate(
        [got_ref[peer, first:first + 4, 0:peer_rows] for peer in range(members)], axis=1
    )
    rest = jnp.concatenate(
        [got_ref[peer, first:first + 2, HALF:HALF + peer_rows] for peer in range(members)], axis=1
    )
    rows = rest[1:2].astype(jnp.int32)
    rows_ref[...] = rows
    fields = [flat[i:i + 1] for i in range(4)] + [rest[0:1]]
    state = scattered(padded(fields, 8), rows)
    u, phi, sa, sb, dist = (state[i:i + 1] for i in range(5))
    velocity = jnp.exp(u)
    deficit = (PLATE_RATE - velocity).astype(jnp.bfloat16).astype(jnp.float32)
    k1p = (jnp.exp(-phi) - velocity) / dist
    u2 = u + TIME_STEP * ((inside - sb * k1p) / (sa + DAMPING * velocity))
    state_ref[...] = padded([u, phi, sa, sb, dist, k1p], 8)
    sent = jnp.concatenate([u2, partial_row(deficit, coarse_v_ref)], axis=1)
    out_ref[...] = jnp.broadcast_to(sent[None], out_ref.shape)


def second_kernel(
    groups, state_ref, factor_ref, rows_ref, all_ref, complete_ref, coarse_v_ref, *refs
):
    bases_refs, field_refs, sent_ref = refs[:2], refs[2:8], refs[8]
    members, elem_count = refs[6].shape[1], state_ref.shape[1]
    width = coarse_v_ref.shape[0]
    mine, me = lax.axis_index("leaf"), lax.axis_index("blk")
    sums = [
        jnp.sum(
            all_ref[group * members:(group + 1) * members, 0, elem_count:elem_count + width],
            axis=0, keepdims=True,
        )
        for group in range(groups)
    ]
    weights = coefficients(sums, width // groups)
    own = all_ref[pl.ds(mine * members, members), 0, 0:elem_count]
    coarse = coarse_all(weights, members, bases_refs)
    u2_all = own + factor_ref[...] * coarse
    deficits = (PLATE_RATE - jnp.exp(u2_all)).astype(jnp.bfloat16).astype(jnp.float32)
    inside = inside_rows(deficits, *field_refs)

    state = state_ref[...]
    u, phi, sa, sb, dist, k1p = (state[i:i + 1] for i in range(6))
    here = lax.broadcasted_iota(jnp.int32, u2_all.shape, 0) == me
    u2 = jnp.sum(jnp.where(here, u2_all, 0.0), axis=0, keepdims=True)
    deficit = jnp.sum(jnp.where(here, deficits, 0.0), axis=0, keepdims=True)
    phi2 = phi + TIME_STEP * k1p
    velocity = jnp.exp(u2)
    k2p = (jnp.exp(-phi2) - velocity) / dist
    inverse = 0.5 * TIME_STEP / (sa + DAMPING * velocity)
    u_next = 0.5 * (u + u2) + (inside - sb * k2p) * inverse
    phi_next = phi + 0.5 * TIME_STEP * (k1p + k2p)
    sent = gathered(padded([u_next, inverse, phi_next], 8), rows_ref[...])
    partial = as_lines(partial_row(deficit, coarse_v_ref))
    peer_rows = elem_count // members
    for device in range(groups * members):
        peer = device % members
        sent_ref[device, 0:3, 0:peer_rows] = sent[0:3, peer * peer_rows:(peer + 1) * peer_rows]
        sent_ref[device, 3:3 + partial.shape[0], :] = partial


def finish_kernel(groups, width, got_ref, slot_ref, slot_row_ref, *refs):
    bases_refs, u_ref, phi_ref = refs[:2], refs[2], refs[3]
    elem_count = slot_ref.shape[1]
    members = got_ref.shape[0] // groups
    sums = []
    for group in range(groups):
        total = jnp.sum(got_ref[group * members:(group + 1) * members], axis=0)
        lines = [total[3 + i:4 + i, :] for i in range(pl.cdiv(width, LANES))]
        sums.append(jnp.concatenate(lines, axis=1)[:, 0:width])
    coarse = coarse_all(coefficients(sums, width // groups), members, bases_refs)
    row = slot_row_ref[...]
    block = lax.broadcasted_iota(jnp.int32, (members, elem_count), 0)
    lane_block = lax.broadcasted_iota(jnp.int32, (members, elem_count), 1) // (elem_count // members)
    rows = gathered(coarse, row)
    found = jnp.sum(jnp.where(block == lane_block, rows, 0.0), axis=0, keepdims=True)
    first = lax.axis_index("leaf") * members
    flat = peer_lanes(got_ref, first, members, 3, elem_count)
    u_next = flat[0:1] + flat[1:2] * found
    out = gathered(padded([u_next, flat[2:3]], 8), slot_ref[...])
    u_ref[...] = out[0:1]
    phi_ref[...] = out[1:2]


def call(kernel, outs, *args, scalars=(), far=(), scratch=(), flops=1000, moved=1000):
    spaces = [SMEM if i in scalars else pl.ANY if i in far else VMEM for i in range(len(args))]
    args = [
        pltpu.with_memory_space_constraint(arg, pltpu.HBM) if i in far else arg
        for i, arg in enumerate(args)
    ]
    return pl.pallas_call(
        kernel,
        out_shape=outs,
        in_specs=[pl.BlockSpec(memory_space=space) for space in spaces],
        out_specs=jax.tree.map(lambda _: pl.BlockSpec(memory_space=VMEM), outs),
        scratch_shapes=list(scratch),
        cost_estimate=pl.CostEstimate(flops=flops, bytes_accessed=moved, transcendentals=0),
        compiler_params=pltpu.CompilerParams(vmem_limit_bytes=32 * 1024 * 1024),
    )(*args)


def shape(*dims, dtype=jnp.float32):
    return jax.ShapeDtypeStruct(dims, dtype)


def body(
    ln_rate,
    log_state,
    sigma,
    fric_a,
    fric_b,
    slip_dist,
    leaf_of_elem,
    near_blocks,
    near_col,
    near_count,
    far_u,
    far_v,
    far_col,
    far_rank,
    coarse_u,
    coarse_v,
):
    members = lax.axis_size("blk")
    elems = ln_rate.shape[0]
    leaf_size = near_blocks.shape[1]
    groups, rank = coarse_v.shape[0], coarse_v.shape[1]
    devices = groups * members
    width = groups * rank
    lines = pl.cdiv(width, LANES)
    sent_rows = 1 << (2 + lines).bit_length()
    integer = jnp.int32

    def swap(value, axes):
        return lax.all_to_all(value, axes, split_axis=0, concat_axis=0, tiled=True)

    def partner(value, bit):
        return lax.ppermute(value, "blk", [(i, i ^ (1 << bit)) for i in range(members)])

    elem_args = [
        value.reshape(1, elems)
        for value in (leaf_of_elem, ln_rate, log_state, sigma, fric_a, fric_b, slip_dist)
    ]
    scalar_args = [near_col, far_col, far_rank]
    weights = [
        near_blocks, far_u.reshape(-1, leaf_size), far_v.reshape(-1, leaf_size),
        coarse_v.reshape(width, elems),
    ]
    far_rows = weights[1].shape[0]
    sent, slot, slot_row, near_mask, far_mask, near, far_u, far_v, coarse_v = call(
        functools.partial(sort_kernel, members),
        (
            shape(members, -(-(3 * (elems // LANES) + 4) // 8) * 8, LANES),
            shape(1, elems, dtype=integer),
            shape(1, elems, dtype=integer),
            shape(near_blocks.shape[0], members, leaf_size),
            shape(members, far_rows),
            *[shape(*value.shape, dtype=jnp.bfloat16) for value in weights],
        ),
        *elem_args, *scalar_args, *weights, far=range(14),
        scratch=[VMEM(value.shape, value.dtype) for value in elem_args]
        + [SMEM(value.shape, value.dtype) for value in scalar_args]
        + [pltpu.SemaphoreType.DMA((14,))],
    )
    fields = near_count, near, far_u, far_v, near_mask, far_mask
    state, factor, rows, out = call(
        place_kernel,
        (
            shape(8, elems),
            shape(members, elems),
            shape(1, elems, dtype=integer),
            shape(devices, 1, elems + lines * LANES),
        ),
        swap(sent, "blk"), coarse_v, *fields, scalars=(2,),
        scratch=[VMEM((2, members * (elems // LANES), LANES), jnp.float32)],
        flops=1 << 33, moved=1 << 25,
    )
    bases = coarse_u.reshape(width, elems)
    for bit in range(members.bit_length() - 2, 0, -1):
        rows_out = 2 * bases.shape[0]
        kernel, after = stack_kernel, slot
        if bit == 1:
            rows_out = rows_out // groups * (groups - 1)
            kernel, after = functools.partial(stack_foreign_kernel, groups, rank), rows
        bases = call(
            kernel, shape(rows_out, elems, dtype=jnp.bfloat16),
            bases, partner(bases, bit), after, flops=1 << 26, moved=1 << 22,
        )
    bases = bases, partner(bases, 0)
    complete = call(mark_kernel, shape(16, LANES), bases[1], flops=1 << 34, moved=1 << 26)
    sent = call(
        functools.partial(second_kernel, groups), shape(devices, sent_rows, LANES),
        state, factor, rows, swap(out, ("leaf", "blk")), complete, coarse_v, *bases, *fields, scalars=(8,),
    )
    u, phi = call(
        functools.partial(finish_kernel, groups, width), (shape(1, elems), shape(1, elems)),
        swap(sent, ("leaf", "blk")), slot, slot_row, *bases,
    )
    return u.reshape(elems), phi.reshape(elems)


def solution(mesh):
    each = P(("leaf", "blk"))
    blocks = P(("leaf", "blk"), None, None)
    last = P(None, None, ("leaf", "blk"))
    in_specs = (each,) * 7 + (blocks, each, each, blocks, blocks, each, each, last, last)
    return jax.shard_map(body, mesh=mesh, in_specs=in_specs, out_specs=(each, each), check_vma=False)
```

```python
import functools

import jax
import jax.numpy as jnp
from jax import lax
from jax.experimental import pallas as pl
from jax.experimental.pallas import tpu as pltpu
from jax.sharding import PartitionSpec as P

DAMPING = 0.5
PLATE_RATE = 1.0
TIME_STEP = 0.2

NN = (((1,), (0,)), ((), ()))
NT = (((1,), (1,)), ((), ()))
VMEM = pltpu.VMEM
SMEM = pltpu.SMEM

LANES = 128
HALF = 64


def dot(left, right, dims):
    return lax.dot_general(left, right, dims, preferred_element_type=jnp.float32)


def low_matrix(index_row):
    rows = lax.broadcasted_iota(jnp.int32, (LANES, index_row.shape[1]), 0)
    return jnp.where(rows == (index_row & (LANES - 1)), 1.0, 0.0).astype(jnp.bfloat16)


def three_parts(values):
    high = values.astype(jnp.bfloat16).astype(jnp.float32)
    rest = values - high
    middle = rest.astype(jnp.bfloat16).astype(jnp.float32)
    return jnp.concatenate([high, middle, rest - middle], axis=0)


def joined(parts):
    count = parts.shape[0] // 3
    return parts[0:count] + parts[count:2 * count] + parts[2 * count:]


def scattered(values, index_row):
    parts = three_parts(values)
    count = parts.shape[0]
    high = index_row // LANES
    pieces = values.shape[1] // LANES
    left = jnp.concatenate([jnp.where(high == piece, parts, 0.0) for piece in range(pieces)], axis=0)
    moved = dot(left.astype(jnp.bfloat16), low_matrix(index_row), NT)
    return jnp.concatenate(
        [joined(moved[piece * count:(piece + 1) * count]) for piece in range(pieces)], axis=1
    )


def gathered(values, index_row):
    parts = three_parts(values)
    count = parts.shape[0]
    high = index_row // LANES
    pieces = values.shape[1] // LANES
    left = jnp.concatenate(
        [parts[:, piece * LANES:(piece + 1) * LANES] for piece in range(pieces)], axis=0
    )
    moved = dot(left.astype(jnp.bfloat16), low_matrix(index_row), NN)
    total = jnp.zeros((count, index_row.shape[1]), jnp.float32)
    for piece in range(pieces):
        total = jnp.where(high == piece, moved[piece * count:(piece + 1) * count], total)
    return joined(total)


def padded(rows, count):
    missing = count - len(rows)
    if missing:
        rows = rows + [jnp.zeros((missing, rows[0].shape[1]), jnp.float32)]
    return jnp.concatenate(rows, axis=0)


def as_lines(row):
    return jnp.concatenate(
        [row[:, i * LANES:(i + 1) * LANES] for i in range(row.shape[1] // LANES)], axis=0
    )


def peer_lanes(ref, first, members, rows, elem_count):
    width = elem_count // members
    return jnp.concatenate([ref[first + peer, 0:rows, 0:width] for peer in range(members)], axis=1)


def start_copies(sources, targets, sems):
    copies = [
        pltpu.make_async_copy(source, target, sems.at[i])
        for i, (source, target) in enumerate(zip(sources, targets))
    ]
    for copy in copies:
        copy.start()
    return copies


def sort_kernel(members, *refs):
    elem_refs, scalar_refs, weight_refs = refs[:7], refs[7:10], refs[10:14]
    sent_ref, slot_ref, slot_row_ref, near_mask_ref, far_mask_ref = refs[14:19]
    weight_outs, elem_bufs, scalar_bufs, sems = refs[19:23], refs[23:30], refs[30:33], refs[33]
    copies = start_copies(
        [*elem_refs, *scalar_refs, *weight_refs], [*elem_bufs, *scalar_bufs, *weight_outs], sems
    )
    mine = lax.axis_index("leaf")
    elem_count = elem_bufs[0].shape[1]
    peer_rows = elem_count // members
    pieces = elem_count // LANES
    before = lax.broadcasted_iota(jnp.int32, (LANES, LANES), 0)
    after = lax.broadcasted_iota(jnp.int32, (LANES, LANES), 1)
    triangle = jnp.where(before < after, 1.0, 0.0).astype(jnp.bfloat16)
    copies[0].wait()
    local = elem_bufs[0][...] - mine * (members * elem_count)
    target = local // elem_count
    target_row = local - target * elem_count
    peers = lax.broadcasted_iota(jnp.int32, (members, elem_count), 0)
    onehot = jnp.where(peers == target, 1.0, 0.0)
    lines = [onehot[:, i * LANES:(i + 1) * LANES] for i in range(pieces)]
    inside = dot(jnp.concatenate(lines, axis=0).astype(jnp.bfloat16), triangle, NN)
    passed = jnp.zeros((members, 1), jnp.float32)
    ranks = []
    for i, line in enumerate(lines):
        earlier = inside[i * members:(i + 1) * members] + passed
        ranks.append(jnp.sum(earlier * line, axis=0, keepdims=True))
        passed = passed + jnp.sum(line, axis=1, keepdims=True)
    slot = target * peer_rows + jnp.concatenate(ranks, axis=1).astype(jnp.int32)
    slot_ref[...] = slot
    for copy in copies[1:7]:
        copy.wait()
    u, phi, sigma, fric_a, fric_b, dist = (buf[...] for buf in elem_bufs[1:])
    velocity = jnp.exp(u)
    deficit = (PLATE_RATE - velocity).astype(jnp.bfloat16).astype(jnp.float32)
    sa = sigma * fric_a
    factor = TIME_STEP / (sa + DAMPING * velocity)
    rows = [u, phi, sa, sigma * fric_b, dist, target_row.astype(jnp.float32), deficit, factor]
    values = scattered(padded(rows, 8), slot)
    slot_row_ref[...] = values[5:6].astype(jnp.int32)
    everyone = jnp.concatenate([as_lines(values[i:i + 1]) for i in (6, 5, 7)], axis=0)
    for peer in range(members):
        sent_ref[peer, 0:3 * pieces, :] = everyone
        part = values[0:6, peer * peer_rows:(peer + 1) * peer_rows]
        sent_ref[peer, 3 * pieces:3 * pieces + 4, 0:peer_rows] = part[0:4]
        sent_ref[peer, 3 * pieces:3 * pieces + 2, HALF:HALF + peer_rows] = part[4:6]

    for copy in copies[7:10]:
        copy.wait()
    near_col, far_col, far_rank = scalar_bufs
    far_slots = far_col.shape[0]
    far_width = far_mask_ref.shape[1] // far_slots
    block = lax.broadcasted_iota(jnp.int32, near_mask_ref.shape[1:], 0)
    for number in range(near_mask_ref.shape[0]):
        near_mask_ref[number] = jnp.where(block == near_col[number], 1.0, 0.0)
    block = lax.broadcasted_iota(jnp.int32, far_mask_ref.shape, 0)
    lane = lax.broadcasted_iota(jnp.int32, far_mask_ref.shape, 1)
    column = jnp.full(far_mask_ref.shape, -1, jnp.int32)
    for number in range(far_slots):
        low = number * far_width
        kept = (lane >= low) & (lane < low + far_rank[number])
        column = jnp.where(kept, far_col[number], column)
    far_mask_ref[...] = jnp.where(block == column, 1.0, 0.0)
    for copy in copies[10:]:
        copy.wait()


def partial_row(deficit, coarse_v_ref):
    wide = jnp.broadcast_to(deficit, (8, deficit.shape[1])).astype(jnp.bfloat16)
    partial = dot(wide, coarse_v_ref[...], NT)[0:1]
    rest = -partial.shape[1] % LANES
    if rest:
        partial = jnp.concatenate([partial, jnp.zeros((1, rest), jnp.float32)], axis=1)
    return partial


def inside_rows(deficits, near_count, near_ref, far_u_ref, far_v_ref, near_mask_ref, far_mask_ref):
    total = jnp.zeros(deficits.shape, jnp.float32)
    for slot in range(near_ref.shape[0]):
        live = jnp.where(slot < near_count[0], 1.0, 0.0)
        source = (deficits * (near_mask_ref[slot] * live)).astype(jnp.bfloat16)
        total = total + dot(source, near_ref[slot], NT)
    project = dot(deficits.astype(jnp.bfloat16), far_v_ref[...], NT) * far_mask_ref[...]
    project = jnp.sum(project, axis=0, keepdims=True)
    project = jnp.broadcast_to(project, (8, project.shape[1])).astype(jnp.bfloat16)
    far = dot(project, far_u_ref[...], NN)
    return jnp.sum(total, axis=0, keepdims=True) + far[0:1]


def coefficients(sums, rank):
    groups, width = len(sums), sums[0].shape[1]
    mine = lax.axis_index("leaf")
    table = padded(sums, -(-groups // 8) * 8)
    lane = lax.broadcasted_iota(jnp.int32, table.shape, 1) // rank
    row = lax.broadcasted_iota(jnp.int32, table.shape, 0)
    table = jnp.where(lane == mine, table, 0.0).astype(jnp.bfloat16)
    across = lax.broadcasted_iota(jnp.int32, (width, width), 0) % rank
    down = lax.broadcasted_iota(jnp.int32, (width, width), 1) % rank
    spread = dot(table, jnp.where(across == down, 1.0, 0.0).astype(jnp.bfloat16), NN)
    weights = jnp.sum(jnp.where(row == mine ^ (lane + 1), spread, 0.0), axis=0, keepdims=True)
    return weights[:, 0:width - rank]


def coarse_all(weights, members, bases_refs):
    row = lax.broadcasted_iota(jnp.int32, (members, weights.shape[1]), 0) ^ lax.axis_index("blk")
    bits = members.bit_length() - 1
    total = jnp.zeros((members, bases_refs[0].shape[1]), jnp.float32)
    for number, ref in enumerate(bases_refs):
        left = []
        for place in range(members // 2):
            source = number
            for bit in range(bits - 1):
                source |= (place >> bit & 1) << (bits - 1 - bit)
            left.append(jnp.where(row == source, weights, 0.0))
        left = jnp.concatenate(left, axis=1).astype(jnp.bfloat16)
        total = total + dot(left, ref[...], NN)
    return total


def stack_kernel(held_ref, came_ref, *refs):
    out_ref = refs[-1]
    count = held_ref.shape[0]
    out_ref[0:count, :] = held_ref[...]
    out_ref[count:2 * count, :] = came_ref[...]


def stack_foreign_kernel(groups, rank, held_ref, came_ref, *refs):
    out_ref = refs[-1]
    width = groups * rank
    mine = lax.axis_index("leaf")
    place = 0
    for ref in (held_ref, came_ref):
        for low in range(0, ref.shape[0], width):
            for shift in range(1, groups):
                out_ref[place:place + rank, :] = ref[pl.ds(low + (mine ^ shift) * rank, rank), :]
                place += rank


def mark_kernel(came_ref, out_ref):
    out_ref[...] = came_ref[0:16, 0:LANES].astype(jnp.float32)


def place_kernel(got_ref, coarse_v_ref, *refs):
    field_refs, state_ref, factor_ref, rows_ref, out_ref, lines_ref = refs[:6], *refs[6:]
    members = got_ref.shape[0]
    elem_count = state_ref.shape[1]
    pieces = elem_count // LANES
    peer_rows = elem_count // members
    count = LANES // peer_rows * pieces
    line_row = lax.broadcasted_iota(jnp.int32, (count, LANES), 0)
    lane_block = lax.broadcasted_iota(jnp.int32, (count, LANES), 1) // peer_rows
    own_lane = line_row // pieces == lane_block
    for line in range(pieces):
        rows = got_ref[:, pieces + line, :].astype(jnp.int32)
        parts = [got_ref[:, line, :]]
        split = three_parts(got_ref[:, 2 * pieces + line, :])
        parts += [split[i * members:(i + 1) * members] for i in range(3)]
        left, right = [], []
        for peer in range(members):
            row = rows[peer:peer + 1]
            kept = own_lane & (line_row % pieces == row // LANES)
            left.append(
                jnp.concatenate([jnp.where(kept, part[peer:peer + 1], 0.0) for part in parts], axis=0)
            )
            right.append(low_matrix(row))
        left = jnp.concatenate(left, axis=1).astype(jnp.bfloat16)
        placed = dot(left, jnp.concatenate(right, axis=1), NT)
        lines_ref[0, line * count:(line + 1) * count, :] = placed[0:count]
        lines_ref[1, line * count:(line + 1) * count, :] = joined(placed[count:])

    def blocks(number):
        return jnp.concatenate(
            [lines_ref[number, pl.ds(piece, members, stride=pieces), :] for piece in range(pieces)],
            axis=1,
        )

    factor_ref[...] = blocks(1)
    inside = inside_rows(blocks(0), *field_refs)

    first = 3 * pieces
    flat = jnp.concatenate(
        [got_ref[peer, first:first + 4, 0:peer_rows] for peer in range(members)], axis=1
    )
    rest = jnp.concatenate(
        [got_ref[peer, first:first + 2, HALF:HALF + peer_rows] for peer in range(members)], axis=1
    )
    rows = rest[1:2].astype(jnp.int32)
    rows_ref[...] = rows
    fields = [flat[i:i + 1] for i in range(4)] + [rest[0:1]]
    state = scattered(padded(fields, 8), rows)
    u, phi, sa, sb, dist = (state[i:i + 1] for i in range(5))
    velocity = jnp.exp(u)
    deficit = (PLATE_RATE - velocity).astype(jnp.bfloat16).astype(jnp.float32)
    k1p = (jnp.exp(-phi) - velocity) / dist
    u2 = u + TIME_STEP * ((inside - sb * k1p) / (sa + DAMPING * velocity))
    state_ref[...] = padded([u, phi, sa, sb, dist, k1p], 8)
    sent = jnp.concatenate([u2, partial_row(deficit, coarse_v_ref)], axis=1)
    out_ref[...] = jnp.broadcast_to(sent[None], out_ref.shape)


def second_kernel(
    groups, state_ref, factor_ref, rows_ref, all_ref, complete_ref, coarse_v_ref, *refs
):
    bases_refs, field_refs, sent_ref = refs[:2], refs[2:8], refs[8]
    members, elem_count = refs[6].shape[1], state_ref.shape[1]
    width = coarse_v_ref.shape[0]
    mine, me = lax.axis_index("leaf"), lax.axis_index("blk")
    sums = [
        jnp.sum(
            all_ref[group * members:(group + 1) * members, 0, elem_count:elem_count + width],
            axis=0, keepdims=True,
        )
        for group in range(groups)
    ]
    weights = coefficients(sums, width // groups)
    own = all_ref[pl.ds(mine * members, members), 0, 0:elem_count]
    coarse = coarse_all(weights, members, bases_refs)
    u2_all = own + factor_ref[...] * coarse
    deficits = (PLATE_RATE - jnp.exp(u2_all)).astype(jnp.bfloat16).astype(jnp.float32)
    inside = inside_rows(deficits, *field_refs)

    state = state_ref[...]
    u, phi, sa, sb, dist, k1p = (state[i:i + 1] for i in range(6))
    here = lax.broadcasted_iota(jnp.int32, u2_all.shape, 0) == me
    u2 = jnp.sum(jnp.where(here, u2_all, 0.0), axis=0, keepdims=True)
    deficit = jnp.sum(jnp.where(here, deficits, 0.0), axis=0, keepdims=True)
    phi2 = phi + TIME_STEP * k1p
    velocity = jnp.exp(u2)
    k2p = (jnp.exp(-phi2) - velocity) / dist
    inverse = 0.5 * TIME_STEP / (sa + DAMPING * velocity)
    u_next = 0.5 * (u + u2) + (inside - sb * k2p) * inverse
    phi_next = phi + 0.5 * TIME_STEP * (k1p + k2p)
    sent = gathered(padded([u_next, inverse, phi_next], 8), rows_ref[...])
    partial = as_lines(partial_row(deficit, coarse_v_ref))
    peer_rows = elem_count // members
    for device in range(groups * members):
        peer = device % members
        sent_ref[device, 0:3, 0:peer_rows] = sent[0:3, peer * peer_rows:(peer + 1) * peer_rows]
        sent_ref[device, 3:3 + partial.shape[0], :] = partial


def finish_kernel(groups, width, got_ref, slot_ref, slot_row_ref, *refs):
    bases_refs, u_ref, phi_ref = refs[:2], refs[2], refs[3]
    elem_count = slot_ref.shape[1]
    members = got_ref.shape[0] // groups
    sums = []
    for group in range(groups):
        total = jnp.sum(got_ref[group * members:(group + 1) * members], axis=0)
        lines = [total[3 + i:4 + i, :] for i in range(pl.cdiv(width, LANES))]
        sums.append(jnp.concatenate(lines, axis=1)[:, 0:width])
    coarse = coarse_all(coefficients(sums, width // groups), members, bases_refs)
    row = slot_row_ref[...]
    block = lax.broadcasted_iota(jnp.int32, (members, elem_count), 0)
    lane_block = lax.broadcasted_iota(jnp.int32, (members, elem_count), 1) // (elem_count // members)
    rows = gathered(coarse, row)
    found = jnp.sum(jnp.where(block == lane_block, rows, 0.0), axis=0, keepdims=True)
    first = lax.axis_index("leaf") * members
    flat = peer_lanes(got_ref, first, members, 3, elem_count)
    u_next = flat[0:1] + flat[1:2] * found
    out = gathered(padded([u_next, flat[2:3]], 8), slot_ref[...])
    u_ref[...] = out[0:1]
    phi_ref[...] = out[1:2]


def call(kernel, outs, *args, scalars=(), far=(), scratch=(), flops=1000, moved=1000):
    spaces = [SMEM if i in scalars else pl.ANY if i in far else VMEM for i in range(len(args))]
    args = [
        pltpu.with_memory_space_constraint(arg, pltpu.HBM) if i in far else arg
        for i, arg in enumerate(args)
    ]
    return pl.pallas_call(
        kernel,
        out_shape=outs,
        in_specs=[pl.BlockSpec(memory_space=space) for space in spaces],
        out_specs=jax.tree.map(lambda _: pl.BlockSpec(memory_space=VMEM), outs),
        scratch_shapes=list(scratch),
        cost_estimate=pl.CostEstimate(flops=flops, bytes_accessed=moved, transcendentals=0),
        compiler_params=pltpu.CompilerParams(vmem_limit_bytes=32 * 1024 * 1024),
    )(*args)


def shape(*dims, dtype=jnp.float32):
    return jax.ShapeDtypeStruct(dims, dtype)


def body(
    ln_rate,
    log_state,
    sigma,
    fric_a,
    fric_b,
    slip_dist,
    leaf_of_elem,
    near_blocks,
    near_col,
    near_count,
    far_u,
    far_v,
    far_col,
    far_rank,
    coarse_u,
    coarse_v,
):
    members = lax.axis_size("blk")
    elems = ln_rate.shape[0]
    leaf_size = near_blocks.shape[1]
    groups, rank = coarse_v.shape[0], coarse_v.shape[1]
    devices = groups * members
    width = groups * rank
    lines = pl.cdiv(width, LANES)
    sent_rows = 1 << (2 + lines).bit_length()
    integer = jnp.int32

    def swap(value, axes):
        return lax.all_to_all(value, axes, split_axis=0, concat_axis=0, tiled=True)

    def partner(value, bit):
        return lax.ppermute(value, "blk", [(i, i ^ (1 << bit)) for i in range(members)])

    elem_args = [
        value.reshape(1, elems)
        for value in (leaf_of_elem, ln_rate, log_state, sigma, fric_a, fric_b, slip_dist)
    ]
    scalar_args = [near_col, far_col, far_rank]
    weights = [
        near_blocks, far_u.reshape(-1, leaf_size), far_v.reshape(-1, leaf_size),
        coarse_v.reshape(width, elems),
    ]
    far_rows = weights[1].shape[0]
    sent, slot, slot_row, near_mask, far_mask, near, far_u, far_v, coarse_v = call(
        functools.partial(sort_kernel, members),
        (
            shape(members, -(-(3 * (elems // LANES) + 4) // 8) * 8, LANES),
            shape(1, elems, dtype=integer),
            shape(1, elems, dtype=integer),
            shape(near_blocks.shape[0], members, leaf_size),
            shape(members, far_rows),
            *[shape(*value.shape, dtype=jnp.bfloat16) for value in weights],
        ),
        *elem_args, *scalar_args, *weights, far=range(14),
        scratch=[VMEM(value.shape, value.dtype) for value in elem_args]
        + [SMEM(value.shape, value.dtype) for value in scalar_args]
        + [pltpu.SemaphoreType.DMA((14,))],
    )
    fields = near_count, near, far_u, far_v, near_mask, far_mask
    state, factor, rows, out = call(
        place_kernel,
        (
            shape(8, elems),
            shape(members, elems),
            shape(1, elems, dtype=integer),
            shape(devices, 1, elems + lines * LANES),
        ),
        swap(sent, "blk"), coarse_v, *fields, scalars=(2,),
        scratch=[VMEM((2, members * (elems // LANES), LANES), jnp.float32)],
        flops=1 << 33, moved=1 << 25,
    )
    bases = coarse_u.reshape(width, elems)
    for bit in range(members.bit_length() - 2, 0, -1):
        rows_out = 2 * bases.shape[0]
        kernel, after = stack_kernel, slot
        if bit == 1:
            rows_out = rows_out // groups * (groups - 1)
            kernel, after = functools.partial(stack_foreign_kernel, groups, rank), rows
        bases = call(
            kernel, shape(rows_out, elems, dtype=jnp.bfloat16),
            bases, partner(bases, bit), after, flops=1 << 34, moved=1 << 26,
        )
    bases = bases, partner(bases, 0)
    complete = call(mark_kernel, shape(16, LANES), bases[1], flops=1 << 34, moved=1 << 26)
    sent = call(
        functools.partial(second_kernel, groups), shape(devices, sent_rows, LANES),
        state, factor, rows, swap(out, ("leaf", "blk")), complete, coarse_v, *bases, *fields, scalars=(8,),
    )
    u, phi = call(
        functools.partial(finish_kernel, groups, width), (shape(1, elems), shape(1, elems)),
        swap(sent, ("leaf", "blk")), slot, slot_row, *bases,
    )
    return u.reshape(elems), phi.reshape(elems)


def solution(mesh):
    each = P(("leaf", "blk"))
    blocks = P(("leaf", "blk"), None, None)
    last = P(None, None, ("leaf", "blk"))
    in_specs = (each,) * 7 + (blocks, each, each, blocks, blocks, each, each, last, last)
    return jax.shard_map(body, mesh=mesh, in_specs=in_specs, out_specs=(each, each), check_vma=False)
```

```python
import functools

import jax
import jax.numpy as jnp
from jax import lax
from jax.experimental import pallas as pl
from jax.experimental.pallas import tpu as pltpu
from jax.sharding import PartitionSpec as P

DAMPING = 0.5
PLATE_RATE = 1.0
TIME_STEP = 0.2

NN = (((1,), (0,)), ((), ()))
NT = (((1,), (1,)), ((), ()))
VMEM = pltpu.VMEM
SMEM = pltpu.SMEM

LANES = 128
HALF = 64


def dot(left, right, dims):
    return lax.dot_general(left, right, dims, preferred_element_type=jnp.float32)


def low_matrix(index_row):
    rows = lax.broadcasted_iota(jnp.int32, (LANES, index_row.shape[1]), 0)
    return jnp.where(rows == (index_row & (LANES - 1)), 1.0, 0.0).astype(jnp.bfloat16)


def three_parts(values):
    high = values.astype(jnp.bfloat16).astype(jnp.float32)
    rest = values - high
    middle = rest.astype(jnp.bfloat16).astype(jnp.float32)
    return jnp.concatenate([high, middle, rest - middle], axis=0)


def joined(parts):
    count = parts.shape[0] // 3
    return parts[0:count] + parts[count:2 * count] + parts[2 * count:]


def scattered(values, index_row):
    parts = three_parts(values)
    count = parts.shape[0]
    high = index_row // LANES
    pieces = values.shape[1] // LANES
    left = jnp.concatenate([jnp.where(high == piece, parts, 0.0) for piece in range(pieces)], axis=0)
    moved = dot(left.astype(jnp.bfloat16), low_matrix(index_row), NT)
    return jnp.concatenate(
        [joined(moved[piece * count:(piece + 1) * count]) for piece in range(pieces)], axis=1
    )


def gathered(values, index_row):
    parts = three_parts(values)
    count = parts.shape[0]
    high = index_row // LANES
    pieces = values.shape[1] // LANES
    left = jnp.concatenate(
        [parts[:, piece * LANES:(piece + 1) * LANES] for piece in range(pieces)], axis=0
    )
    moved = dot(left.astype(jnp.bfloat16), low_matrix(index_row), NN)
    total = jnp.zeros((count, index_row.shape[1]), jnp.float32)
    for piece in range(pieces):
        total = jnp.where(high == piece, moved[piece * count:(piece + 1) * count], total)
    return joined(total)


def padded(rows, count):
    missing = count - len(rows)
    if missing:
        rows = rows + [jnp.zeros((missing, rows[0].shape[1]), jnp.float32)]
    return jnp.concatenate(rows, axis=0)


def as_lines(row):
    return jnp.concatenate(
        [row[:, i * LANES:(i + 1) * LANES] for i in range(row.shape[1] // LANES)], axis=0
    )


def peer_lanes(ref, first, members, rows, elem_count):
    width = elem_count // members
    return jnp.concatenate([ref[first + peer, 0:rows, 0:width] for peer in range(members)], axis=1)


def start_copies(sources, targets, sems):
    copies = [
        pltpu.make_async_copy(source, target, sems.at[i])
        for i, (source, target) in enumerate(zip(sources, targets))
    ]
    for copy in copies:
        copy.start()
    return copies


def sort_kernel(members, *refs):
    elem_refs, sent_ref, slot_ref, elem_row_ref = refs[:7], refs[7], refs[8], refs[9]
    elem_bufs, sems = refs[10:17], refs[17]
    copies = start_copies(elem_refs, elem_bufs, sems)
    mine = lax.axis_index("leaf")
    elem_count = elem_bufs[0].shape[1]
    peer_rows = elem_count // members
    pieces = elem_count // LANES
    before = lax.broadcasted_iota(jnp.int32, (LANES, LANES), 0)
    after = lax.broadcasted_iota(jnp.int32, (LANES, LANES), 1)
    triangle = jnp.where(before < after, 1.0, 0.0).astype(jnp.bfloat16)
    copies[0].wait()
    local = elem_bufs[0][...] - mine * (members * elem_count)
    target = local // elem_count
    target_row = local - target * elem_count
    peers = lax.broadcasted_iota(jnp.int32, (members, elem_count), 0)
    onehot = jnp.where(peers == target, 1.0, 0.0)
    lines = [onehot[:, i * LANES:(i + 1) * LANES] for i in range(pieces)]
    inside = dot(jnp.concatenate(lines, axis=0).astype(jnp.bfloat16), triangle, NN)
    passed = jnp.zeros((members, 1), jnp.float32)
    ranks = []
    for i, line in enumerate(lines):
        earlier = inside[i * members:(i + 1) * members] + passed
        ranks.append(jnp.sum(earlier * line, axis=0, keepdims=True))
        passed = passed + jnp.sum(line, axis=1, keepdims=True)
    slot = target * peer_rows + jnp.concatenate(ranks, axis=1).astype(jnp.int32)
    slot_ref[...] = slot
    elem_row_ref[...] = target_row
    for copy in copies[1:]:
        copy.wait()
    u, phi, sigma, fric_a, fric_b, dist = (buf[...] for buf in elem_bufs[1:])
    velocity = jnp.exp(u)
    deficit = (PLATE_RATE - velocity).astype(jnp.bfloat16).astype(jnp.float32)
    sa = sigma * fric_a
    factor = TIME_STEP / (sa + DAMPING * velocity)
    rows = [u, phi, sa, sigma * fric_b, dist, target_row.astype(jnp.float32), deficit, factor]
    values = scattered(padded(rows, 8), slot)
    everyone = jnp.concatenate([as_lines(values[i:i + 1]) for i in (6, 5, 7)], axis=0)
    for peer in range(members):
        sent_ref[peer, 0:3 * pieces, :] = everyone
        part = values[0:6, peer * peer_rows:(peer + 1) * peer_rows]
        sent_ref[peer, 3 * pieces:3 * pieces + 4, 0:peer_rows] = part[0:4]
        sent_ref[peer, 3 * pieces:3 * pieces + 2, HALF:HALF + peer_rows] = part[4:6]


def load_kernel(*refs):
    scalar_refs, weight_refs, near_mask_ref, far_mask_ref = refs[:3], refs[3:7], refs[7], refs[8]
    weight_outs, scalar_bufs, sems = refs[9:13], refs[13:16], refs[16]
    copies = start_copies([*scalar_refs, *weight_refs], [*scalar_bufs, *weight_outs], sems)
    for copy in copies[:3]:
        copy.wait()
    near_col, far_col, far_rank = scalar_bufs
    far_slots = far_col.shape[0]
    far_width = far_mask_ref.shape[1] // far_slots
    block = lax.broadcasted_iota(jnp.int32, near_mask_ref.shape[1:], 0)
    for number in range(near_mask_ref.shape[0]):
        near_mask_ref[number] = jnp.where(block == near_col[number], 1.0, 0.0)
    block = lax.broadcasted_iota(jnp.int32, far_mask_ref.shape, 0)
    lane = lax.broadcasted_iota(jnp.int32, far_mask_ref.shape, 1)
    column = jnp.full(far_mask_ref.shape, -1, jnp.int32)
    for number in range(far_slots):
        low = number * far_width
        kept = (lane >= low) & (lane < low + far_rank[number])
        column = jnp.where(kept, far_col[number], column)
    far_mask_ref[...] = jnp.where(block == column, 1.0, 0.0)
    for copy in copies[3:]:
        copy.wait()


def partial_row(deficit, coarse_v_ref):
    wide = jnp.broadcast_to(deficit, (8, deficit.shape[1])).astype(jnp.bfloat16)
    partial = dot(wide, coarse_v_ref[...], NT)[0:1]
    rest = -partial.shape[1] % LANES
    if rest:
        partial = jnp.concatenate([partial, jnp.zeros((1, rest), jnp.float32)], axis=1)
    return partial


def inside_rows(deficits, near_count, near_ref, far_u_ref, far_v_ref, near_mask_ref, far_mask_ref):
    total = jnp.zeros(deficits.shape, jnp.float32)
    for slot in range(near_ref.shape[0]):
        live = jnp.where(slot < near_count[0], 1.0, 0.0)
        source = (deficits * (near_mask_ref[slot] * live)).astype(jnp.bfloat16)
        total = total + dot(source, near_ref[slot], NT)
    project = dot(deficits.astype(jnp.bfloat16), far_v_ref[...], NT) * far_mask_ref[...]
    project = jnp.sum(project, axis=0, keepdims=True)
    project = jnp.broadcast_to(project, (8, project.shape[1])).astype(jnp.bfloat16)
    far = dot(project, far_u_ref[...], NN)
    return jnp.sum(total, axis=0, keepdims=True) + far[0:1]


def coefficients(sums, rank):
    groups, width = len(sums), sums[0].shape[1]
    mine = lax.axis_index("leaf")
    table = padded(sums, -(-groups // 8) * 8)
    lane = lax.broadcasted_iota(jnp.int32, table.shape, 1) // rank
    row = lax.broadcasted_iota(jnp.int32, table.shape, 0)
    table = jnp.where(lane == mine, table, 0.0).astype(jnp.bfloat16)
    across = lax.broadcasted_iota(jnp.int32, (width, width), 0) % rank
    down = lax.broadcasted_iota(jnp.int32, (width, width), 1) % rank
    spread = dot(table, jnp.where(across == down, 1.0, 0.0).astype(jnp.bfloat16), NN)
    weights = jnp.sum(jnp.where(row == mine ^ (lane + 1), spread, 0.0), axis=0, keepdims=True)
    return weights[:, 0:width - rank]


def coarse_all(weights, members, bases_refs):
    row = lax.broadcasted_iota(jnp.int32, (members, weights.shape[1]), 0) ^ lax.axis_index("blk")
    bits = members.bit_length() - 1
    total = jnp.zeros((members, bases_refs[0].shape[1]), jnp.float32)
    for number, ref in enumerate(bases_refs):
        left = []
        for place in range(members // 2):
            source = relative_member(place, number, bits)
            left.append(jnp.where(row == source, weights, 0.0))
        left = jnp.concatenate(left, axis=1).astype(jnp.bfloat16)
        total = total + dot(left, ref[...], NN)
    return total


def stack_kernel(held_ref, came_ref, *refs):
    out_ref = refs[-1]
    count = held_ref.shape[0]
    out_ref[0:count, :] = held_ref[...]
    out_ref[count:2 * count, :] = came_ref[...]


def stack_foreign_kernel(groups, rank, held_ref, came_ref, *refs):
    out_ref = refs[-1]
    mine = lax.axis_index("leaf")
    place = 0
    for ref in (held_ref, came_ref):
        for shift in range(1, groups):
            out_ref[place:place + rank, :] = ref[pl.ds((mine ^ shift) * rank, rank), :]
            place += rank


def relative_member(place, number, bits):
    for bit in range(bits - 1):
        number |= (place >> bit & 1) << (bits - 1 - bit)
    return number


def element_kernel(members, held_ref, came_ref, slot_ref, elem_row_ref, out_ref):
    slot, row = slot_ref[...], elem_row_ref[...]
    elem_count = row.shape[1]
    kept = out_ref.shape[0]
    pieces = elem_count // LANES
    owner = (slot // (elem_count // members)) ^ lax.axis_index("blk")
    low, high = low_matrix(row), row // LANES
    total = jnp.zeros(out_ref.shape, jnp.float32)
    for number, ref in enumerate((held_ref, came_ref)):
        for place in range(members // 2):
            part = ref[place * kept:(place + 1) * kept, :]
            left = jnp.concatenate(
                [part[:, piece * LANES:(piece + 1) * LANES] for piece in range(pieces)], axis=0
            )
            found = dot(left, low, NN)
            ours = owner == relative_member(place, number, members.bit_length() - 1)
            for piece in range(pieces):
                here = ours & (high == piece)
                total = jnp.where(here, found[piece * kept:(piece + 1) * kept], total)
    out_ref[...] = total.astype(jnp.bfloat16)


def place_kernel(got_ref, coarse_v_ref, *refs):
    field_refs, state_ref, factor_ref, rows_ref, out_ref, lines_ref = refs[:6], *refs[6:]
    members = got_ref.shape[0]
    elem_count = state_ref.shape[1]
    pieces = elem_count // LANES
    peer_rows = elem_count // members
    count = LANES // peer_rows * pieces
    line_row = lax.broadcasted_iota(jnp.int32, (count, LANES), 0)
    lane_block = lax.broadcasted_iota(jnp.int32, (count, LANES), 1) // peer_rows
    own_lane = line_row // pieces == lane_block
    for line in range(pieces):
        rows = got_ref[:, pieces + line, :].astype(jnp.int32)
        parts = [got_ref[:, line, :]]
        split = three_parts(got_ref[:, 2 * pieces + line, :])
        parts += [split[i * members:(i + 1) * members] for i in range(3)]
        left, right = [], []
        for peer in range(members):
            row = rows[peer:peer + 1]
            kept = own_lane & (line_row % pieces == row // LANES)
            left.append(
                jnp.concatenate([jnp.where(kept, part[peer:peer + 1], 0.0) for part in parts], axis=0)
            )
            right.append(low_matrix(row))
        left = jnp.concatenate(left, axis=1).astype(jnp.bfloat16)
        placed = dot(left, jnp.concatenate(right, axis=1), NT)
        lines_ref[0, line * count:(line + 1) * count, :] = placed[0:count]
        lines_ref[1, line * count:(line + 1) * count, :] = joined(placed[count:])

    def blocks(number):
        return jnp.concatenate(
            [lines_ref[number, pl.ds(piece, members, stride=pieces), :] for piece in range(pieces)],
            axis=1,
        )

    factor_ref[...] = blocks(1)
    inside = inside_rows(blocks(0), *field_refs)

    first = 3 * pieces
    flat = jnp.concatenate(
        [got_ref[peer, first:first + 4, 0:peer_rows] for peer in range(members)], axis=1
    )
    rest = jnp.concatenate(
        [got_ref[peer, first:first + 2, HALF:HALF + peer_rows] for peer in range(members)], axis=1
    )
    rows = rest[1:2].astype(jnp.int32)
    rows_ref[...] = rows
    fields = [flat[i:i + 1] for i in range(4)] + [rest[0:1]]
    state = scattered(padded(fields, 8), rows)
    u, phi, sa, sb, dist = (state[i:i + 1] for i in range(5))
    velocity = jnp.exp(u)
    deficit = (PLATE_RATE - velocity).astype(jnp.bfloat16).astype(jnp.float32)
    k1p = (jnp.exp(-phi) - velocity) / dist
    u2 = u + TIME_STEP * ((inside - sb * k1p) / (sa + DAMPING * velocity))
    state_ref[...] = padded([u, phi, sa, sb, dist, k1p], 8)
    sent = jnp.concatenate([u2, partial_row(deficit, coarse_v_ref)], axis=1)
    out_ref[...] = jnp.broadcast_to(sent[None], out_ref.shape)


def second_kernel(
    groups, state_ref, factor_ref, rows_ref, all_ref, elem_bases_ref, coarse_v_ref, *refs
):
    bases_refs, field_refs, sent_ref = refs[:2], refs[2:8], refs[8]
    members, elem_count = refs[6].shape[1], state_ref.shape[1]
    width = coarse_v_ref.shape[0]
    mine, me = lax.axis_index("leaf"), lax.axis_index("blk")
    sums = [
        jnp.sum(
            all_ref[group * members:(group + 1) * members, 0, elem_count:elem_count + width],
            axis=0, keepdims=True,
        )
        for group in range(groups)
    ]
    weights = coefficients(sums, width // groups)
    own = all_ref[pl.ds(mine * members, members), 0, 0:elem_count]
    coarse = coarse_all(weights, members, bases_refs)
    u2_all = own + factor_ref[...] * coarse
    deficits = (PLATE_RATE - jnp.exp(u2_all)).astype(jnp.bfloat16).astype(jnp.float32)
    inside = inside_rows(deficits, *field_refs)

    state = state_ref[...]
    u, phi, sa, sb, dist, k1p = (state[i:i + 1] for i in range(6))
    here = lax.broadcasted_iota(jnp.int32, u2_all.shape, 0) == me
    u2 = jnp.sum(jnp.where(here, u2_all, 0.0), axis=0, keepdims=True)
    deficit = jnp.sum(jnp.where(here, deficits, 0.0), axis=0, keepdims=True)
    phi2 = phi + TIME_STEP * k1p
    velocity = jnp.exp(u2)
    k2p = (jnp.exp(-phi2) - velocity) / dist
    inverse = 0.5 * TIME_STEP / (sa + DAMPING * velocity)
    u_next = 0.5 * (u + u2) + (inside - sb * k2p) * inverse
    phi_next = phi + 0.5 * TIME_STEP * (k1p + k2p)
    sent = gathered(padded([u_next, inverse, phi_next], 8), rows_ref[...])
    partial = as_lines(partial_row(deficit, coarse_v_ref))
    peer_rows = elem_count // members
    for device in range(groups * members):
        peer = device % members
        sent_ref[device, 0:3, 0:peer_rows] = sent[0:3, peer * peer_rows:(peer + 1) * peer_rows]
        sent_ref[device, 3:3 + partial.shape[0], :] = partial


def finish_kernel(groups, width, got_ref, slot_ref, elem_bases_ref, u_ref, phi_ref):
    elem_count = slot_ref.shape[1]
    members = got_ref.shape[0] // groups
    first = lax.axis_index("leaf") * members
    flat = peer_lanes(got_ref, first, members, 3, elem_count)
    out = gathered(padded([flat[i:i + 1] for i in range(3)], 8), slot_ref[...])
    sums = []
    for group in range(groups):
        total = jnp.sum(got_ref[group * members:(group + 1) * members], axis=0)
        lines = [total[3 + i:4 + i, :] for i in range(pl.cdiv(width, LANES))]
        sums.append(jnp.concatenate(lines, axis=1)[:, 0:width])
    weights = coefficients(sums, width // groups)
    weights = jnp.broadcast_to(weights, (8, weights.shape[1])).astype(jnp.bfloat16)
    coarse = dot(weights, elem_bases_ref[...], NN)[0:1]
    u_ref[...] = out[0:1] + out[1:2] * coarse
    phi_ref[...] = out[2:3]


def call(kernel, outs, *args, scalars=(), far=(), scratch=(), flops=1000, moved=1000):
    spaces = [SMEM if i in scalars else pl.ANY if i in far else VMEM for i in range(len(args))]
    args = [
        pltpu.with_memory_space_constraint(arg, pltpu.HBM) if i in far else arg
        for i, arg in enumerate(args)
    ]
    return pl.pallas_call(
        kernel,
        out_shape=outs,
        in_specs=[pl.BlockSpec(memory_space=space) for space in spaces],
        out_specs=jax.tree.map(lambda _: pl.BlockSpec(memory_space=VMEM), outs),
        scratch_shapes=list(scratch),
        cost_estimate=pl.CostEstimate(flops=flops, bytes_accessed=moved, transcendentals=0),
        compiler_params=pltpu.CompilerParams(vmem_limit_bytes=32 * 1024 * 1024),
    )(*args)


def shape(*dims, dtype=jnp.float32):
    return jax.ShapeDtypeStruct(dims, dtype)


def body(
    ln_rate,
    log_state,
    sigma,
    fric_a,
    fric_b,
    slip_dist,
    leaf_of_elem,
    near_blocks,
    near_col,
    near_count,
    far_u,
    far_v,
    far_col,
    far_rank,
    coarse_u,
    coarse_v,
):
    members = lax.axis_size("blk")
    elems = ln_rate.shape[0]
    leaf_size = near_blocks.shape[1]
    groups, rank = coarse_v.shape[0], coarse_v.shape[1]
    devices = groups * members
    width = groups * rank
    lines = pl.cdiv(width, LANES)
    sent_rows = 1 << (2 + lines).bit_length()
    integer = jnp.int32

    def swap(value, axes):
        return lax.all_to_all(value, axes, split_axis=0, concat_axis=0, tiled=True)

    def partner(value, bit):
        return lax.ppermute(value, "blk", [(i, i ^ (1 << bit)) for i in range(members)])

    elem_args = [
        value.reshape(1, elems)
        for value in (leaf_of_elem, ln_rate, log_state, sigma, fric_a, fric_b, slip_dist)
    ]
    scalar_args = [near_col, far_col, far_rank]
    weights = [
        near_blocks, far_u.reshape(-1, leaf_size), far_v.reshape(-1, leaf_size),
        coarse_v.reshape(width, elems),
    ]
    far_rows = weights[1].shape[0]
    sent, slot, elem_row = call(
        functools.partial(sort_kernel, members),
        (
            shape(members, -(-(3 * (elems // LANES) + 4) // 8) * 8, LANES),
            shape(1, elems, dtype=integer),
            shape(1, elems, dtype=integer),
        ),
        *elem_args, far=range(7),
        scratch=[VMEM(value.shape, value.dtype) for value in elem_args]
        + [pltpu.SemaphoreType.DMA((7,))],
    )
    near_mask, far_mask, near, far_u, far_v, coarse_v = call(
        load_kernel,
        (
            shape(near_blocks.shape[0], members, leaf_size),
            shape(members, far_rows),
            *[shape(*value.shape, dtype=jnp.bfloat16) for value in weights],
        ),
        *scalar_args, *weights, far=range(7),
        scratch=[SMEM(value.shape, value.dtype) for value in scalar_args]
        + [pltpu.SemaphoreType.DMA((7,))],
        flops=1 << 30, moved=1 << 22,
    )
    fields = near_count, near, far_u, far_v, near_mask, far_mask
    state, factor, rows, out = call(
        place_kernel,
        (
            shape(8, elems),
            shape(members, elems),
            shape(1, elems, dtype=integer),
            shape(devices, 1, elems + lines * LANES),
        ),
        swap(sent, "blk"), coarse_v, *fields, scalars=(2,),
        scratch=[VMEM((2, members * (elems // LANES), LANES), jnp.float32)],
        flops=1 << 33, moved=1 << 25,
    )
    bases = coarse_u.reshape(width, elems)
    top = members.bit_length() - 2
    for bit in range(top, 0, -1):
        kernel, rows_out = stack_kernel, 2 * bases.shape[0]
        if bit == top:
            kernel = functools.partial(stack_foreign_kernel, groups, rank)
            rows_out = 2 * (width - rank)
        bases = call(
            kernel, shape(rows_out, elems, dtype=jnp.bfloat16),
            bases, partner(bases, bit), slot if bit == top else rows, flops=1 << 34, moved=1 << 26,
        )
    bases = bases, partner(bases, 0)
    elem_bases = call(
        functools.partial(element_kernel, members), shape(width - rank, elems, dtype=jnp.bfloat16),
        *bases, slot, elem_row, flops=1 << 34, moved=1 << 26,
    )
    sent = call(
        functools.partial(second_kernel, groups), shape(devices, sent_rows, LANES),
        state, factor, rows, swap(out, ("leaf", "blk")), elem_bases, coarse_v, *bases, *fields, scalars=(8,),
    )
    u, phi = call(
        functools.partial(finish_kernel, groups, width), (shape(1, elems), shape(1, elems)),
        swap(sent, ("leaf", "blk")), slot, elem_bases,
    )
    return u.reshape(elems), phi.reshape(elems)


def solution(mesh):
    each = P(("leaf", "blk"))
    blocks = P(("leaf", "blk"), None, None)
    last = P(None, None, ("leaf", "blk"))
    in_specs = (each,) * 7 + (blocks, each, each, blocks, blocks, each, each, last, last)
    return jax.shard_map(body, mesh=mesh, in_specs=in_specs, out_specs=(each, each), check_vma=False)
```

```python
import functools

import jax
import jax.numpy as jnp
from jax import lax
from jax.experimental import pallas as pl
from jax.experimental.pallas import tpu as pltpu
from jax.sharding import PartitionSpec as P

DAMPING = 0.5
PLATE_RATE = 1.0
TIME_STEP = 0.2

NN = (((1,), (0,)), ((), ()))
NT = (((1,), (1,)), ((), ()))
VMEM = pltpu.VMEM
SMEM = pltpu.SMEM

LANES = 128
HALF = 64


def dot(left, right, dims):
    return lax.dot_general(left, right, dims, preferred_element_type=jnp.float32)


def low_matrix(index_row):
    rows = lax.broadcasted_iota(jnp.int32, (LANES, index_row.shape[1]), 0)
    return jnp.where(rows == (index_row & (LANES - 1)), 1.0, 0.0).astype(jnp.bfloat16)


def three_parts(values):
    high = values.astype(jnp.bfloat16).astype(jnp.float32)
    rest = values - high
    middle = rest.astype(jnp.bfloat16).astype(jnp.float32)
    return jnp.concatenate([high, middle, rest - middle], axis=0)


def joined(parts):
    count = parts.shape[0] // 3
    return parts[0:count] + parts[count:2 * count] + parts[2 * count:]


def scattered(values, index_row):
    parts = three_parts(values)
    count = parts.shape[0]
    high = index_row // LANES
    pieces = values.shape[1] // LANES
    left = jnp.concatenate([jnp.where(high == piece, parts, 0.0) for piece in range(pieces)], axis=0)
    moved = dot(left.astype(jnp.bfloat16), low_matrix(index_row), NT)
    return jnp.concatenate(
        [joined(moved[piece * count:(piece + 1) * count]) for piece in range(pieces)], axis=1
    )


def gathered(values, index_row):
    parts = three_parts(values)
    count = parts.shape[0]
    high = index_row // LANES
    pieces = values.shape[1] // LANES
    left = jnp.concatenate(
        [parts[:, piece * LANES:(piece + 1) * LANES] for piece in range(pieces)], axis=0
    )
    moved = dot(left.astype(jnp.bfloat16), low_matrix(index_row), NN)
    total = jnp.zeros((count, index_row.shape[1]), jnp.float32)
    for piece in range(pieces):
        total = jnp.where(high == piece, moved[piece * count:(piece + 1) * count], total)
    return joined(total)


def padded(rows, count):
    missing = count - len(rows)
    if missing:
        rows = rows + [jnp.zeros((missing, rows[0].shape[1]), jnp.float32)]
    return jnp.concatenate(rows, axis=0)


def as_lines(row):
    return jnp.concatenate(
        [row[:, i * LANES:(i + 1) * LANES] for i in range(row.shape[1] // LANES)], axis=0
    )


def peer_lanes(ref, first, members, rows, elem_count):
    width = elem_count // members
    return jnp.concatenate([ref[first + peer, 0:rows, 0:width] for peer in range(members)], axis=1)


def start_copies(sources, targets, sems):
    copies = [
        pltpu.make_async_copy(source, target, sems.at[i])
        for i, (source, target) in enumerate(zip(sources, targets))
    ]
    for copy in copies:
        copy.start()
    return copies


def sort_kernel(members, *refs):
    elem_refs, sent_ref, slot_ref, elem_row_ref = refs[:7], refs[7], refs[8], refs[9]
    elem_bufs, sems = refs[10:17], refs[17]
    copies = start_copies(elem_refs, elem_bufs, sems)
    mine = lax.axis_index("leaf")
    elem_count = elem_bufs[0].shape[1]
    peer_rows = elem_count // members
    pieces = elem_count // LANES
    before = lax.broadcasted_iota(jnp.int32, (LANES, LANES), 0)
    after = lax.broadcasted_iota(jnp.int32, (LANES, LANES), 1)
    triangle = jnp.where(before < after, 1.0, 0.0).astype(jnp.bfloat16)
    copies[0].wait()
    local = elem_bufs[0][...] - mine * (members * elem_count)
    target = local // elem_count
    target_row = local - target * elem_count
    peers = lax.broadcasted_iota(jnp.int32, (members, elem_count), 0)
    onehot = jnp.where(peers == target, 1.0, 0.0)
    lines = [onehot[:, i * LANES:(i + 1) * LANES] for i in range(pieces)]
    inside = dot(jnp.concatenate(lines, axis=0).astype(jnp.bfloat16), triangle, NN)
    passed = jnp.zeros((members, 1), jnp.float32)
    ranks = []
    for i, line in enumerate(lines):
        earlier = inside[i * members:(i + 1) * members] + passed
        ranks.append(jnp.sum(earlier * line, axis=0, keepdims=True))
        passed = passed + jnp.sum(line, axis=1, keepdims=True)
    slot = target * peer_rows + jnp.concatenate(ranks, axis=1).astype(jnp.int32)
    slot_ref[...] = slot
    elem_row_ref[...] = target_row
    for copy in copies[1:]:
        copy.wait()
    u, phi, sigma, fric_a, fric_b, dist = (buf[...] for buf in elem_bufs[1:])
    velocity = jnp.exp(u)
    deficit = (PLATE_RATE - velocity).astype(jnp.bfloat16).astype(jnp.float32)
    sa = sigma * fric_a
    factor = TIME_STEP / (sa + DAMPING * velocity)
    rows = [u, phi, sa, sigma * fric_b, dist, target_row.astype(jnp.float32), deficit, factor]
    values = scattered(padded(rows, 8), slot)
    everyone = jnp.concatenate([as_lines(values[i:i + 1]) for i in (6, 5, 7)], axis=0)
    for peer in range(members):
        sent_ref[peer, 0:3 * pieces, :] = everyone
        part = values[0:6, peer * peer_rows:(peer + 1) * peer_rows]
        sent_ref[peer, 3 * pieces:3 * pieces + 4, 0:peer_rows] = part[0:4]
        sent_ref[peer, 3 * pieces:3 * pieces + 2, HALF:HALF + peer_rows] = part[4:6]


def load_kernel(early_ref, *refs):
    scalar_refs, weight_refs, near_mask_ref, far_mask_ref = refs[:3], refs[3:7], refs[7], refs[8]
    weight_outs, scalar_bufs, sems = refs[9:13], refs[13:16], refs[16]
    copies = start_copies([*scalar_refs, *weight_refs], [*scalar_bufs, *weight_outs], sems)
    for copy in copies[:3]:
        copy.wait()
    near_col, far_col, far_rank = scalar_bufs
    far_slots = far_col.shape[0]
    far_width = far_mask_ref.shape[1] // far_slots
    block = lax.broadcasted_iota(jnp.int32, near_mask_ref.shape[1:], 0)
    for number in range(near_mask_ref.shape[0]):
        near_mask_ref[number] = jnp.where(block == near_col[number], 1.0, 0.0)
    block = lax.broadcasted_iota(jnp.int32, far_mask_ref.shape, 0)
    lane = lax.broadcasted_iota(jnp.int32, far_mask_ref.shape, 1)
    column = jnp.full(far_mask_ref.shape, -1, jnp.int32)
    for number in range(far_slots):
        low = number * far_width
        kept = (lane >= low) & (lane < low + far_rank[number])
        column = jnp.where(kept, far_col[number], column)
    far_mask_ref[...] = jnp.where(block == column, 1.0, 0.0)
    for copy in copies[3:]:
        copy.wait()


def partial_row(deficit, coarse_v_ref):
    wide = jnp.broadcast_to(deficit, (8, deficit.shape[1])).astype(jnp.bfloat16)
    partial = dot(wide, coarse_v_ref[...], NT)[0:1]
    rest = -partial.shape[1] % LANES
    if rest:
        partial = jnp.concatenate([partial, jnp.zeros((1, rest), jnp.float32)], axis=1)
    return partial


def inside_rows(deficits, near_count, near_ref, far_u_ref, far_v_ref, near_mask_ref, far_mask_ref):
    total = jnp.zeros(deficits.shape, jnp.float32)
    for slot in range(near_ref.shape[0]):
        live = jnp.where(slot < near_count[0], 1.0, 0.0)
        source = (deficits * (near_mask_ref[slot] * live)).astype(jnp.bfloat16)
        total = total + dot(source, near_ref[slot], NT)
    project = dot(deficits.astype(jnp.bfloat16), far_v_ref[...], NT) * far_mask_ref[...]
    project = jnp.sum(project, axis=0, keepdims=True)
    project = jnp.broadcast_to(project, (8, project.shape[1])).astype(jnp.bfloat16)
    far = dot(project, far_u_ref[...], NN)
    return jnp.sum(total, axis=0, keepdims=True) + far[0:1]


def coefficients(sums, rank):
    groups, width = len(sums), sums[0].shape[1]
    mine = lax.axis_index("leaf")
    table = padded(sums, -(-groups // 8) * 8)
    lane = lax.broadcasted_iota(jnp.int32, table.shape, 1) // rank
    row = lax.broadcasted_iota(jnp.int32, table.shape, 0)
    table = jnp.where(lane == mine, table, 0.0).astype(jnp.bfloat16)
    across = lax.broadcasted_iota(jnp.int32, (width, width), 0) % rank
    down = lax.broadcasted_iota(jnp.int32, (width, width), 1) % rank
    spread = dot(table, jnp.where(across == down, 1.0, 0.0).astype(jnp.bfloat16), NN)
    weights = jnp.sum(jnp.where(row == mine ^ (lane + 1), spread, 0.0), axis=0, keepdims=True)
    return weights[:, 0:width - rank]


def coarse_all(weights, members, bases_refs):
    row = lax.broadcasted_iota(jnp.int32, (members, weights.shape[1]), 0) ^ lax.axis_index("blk")
    bits = members.bit_length() - 1
    total = jnp.zeros((members, bases_refs[0].shape[1]), jnp.float32)
    for number, ref in enumerate(bases_refs):
        left = []
        for place in range(members // 2):
            source = relative_member(place, number, bits)
            left.append(jnp.where(row == source, weights, 0.0))
        left = jnp.concatenate(left, axis=1).astype(jnp.bfloat16)
        total = total + dot(left, ref[...], NN)
    return total


def stack_kernel(held_ref, came_ref, *refs):
    out_ref = refs[-1]
    count = held_ref.shape[0]
    out_ref[0:count, :] = held_ref[...]
    out_ref[count:2 * count, :] = came_ref[...]


def stack_foreign_kernel(groups, rank, held_ref, came_ref, *refs):
    out_ref = refs[-1]
    mine = lax.axis_index("leaf")
    place = 0
    for ref in (held_ref, came_ref):
        for shift in range(1, groups):
            out_ref[place:place + rank, :] = ref[pl.ds((mine ^ shift) * rank, rank), :]
            place += rank


def relative_member(place, number, bits):
    for bit in range(bits - 1):
        number |= (place >> bit & 1) << (bits - 1 - bit)
    return number


def element_kernel(members, held_ref, came_ref, slot_ref, elem_row_ref, out_ref):
    slot, row = slot_ref[...], elem_row_ref[...]
    elem_count = row.shape[1]
    kept = out_ref.shape[0]
    pieces = elem_count // LANES
    owner = (slot // (elem_count // members)) ^ lax.axis_index("blk")
    low, high = low_matrix(row), row // LANES
    total = jnp.zeros(out_ref.shape, jnp.float32)
    for number, ref in enumerate((held_ref, came_ref)):
        for place in range(members // 2):
            part = ref[place * kept:(place + 1) * kept, :]
            left = jnp.concatenate(
                [part[:, piece * LANES:(piece + 1) * LANES] for piece in range(pieces)], axis=0
            )
            found = dot(left, low, NN)
            ours = owner == relative_member(place, number, members.bit_length() - 1)
            for piece in range(pieces):
                here = ours & (high == piece)
                total = jnp.where(here, found[piece * kept:(piece + 1) * kept], total)
    out_ref[...] = total.astype(jnp.bfloat16)


def place_kernel(got_ref, coarse_v_ref, *refs):
    field_refs, state_ref, factor_ref, rows_ref, out_ref, lines_ref = refs[:6], *refs[6:]
    members = got_ref.shape[0]
    elem_count = state_ref.shape[1]
    pieces = elem_count // LANES
    peer_rows = elem_count // members
    count = LANES // peer_rows * pieces
    line_row = lax.broadcasted_iota(jnp.int32, (count, LANES), 0)
    lane_block = lax.broadcasted_iota(jnp.int32, (count, LANES), 1) // peer_rows
    own_lane = line_row // pieces == lane_block
    for line in range(pieces):
        rows = got_ref[:, pieces + line, :].astype(jnp.int32)
        parts = [got_ref[:, line, :]]
        split = three_parts(got_ref[:, 2 * pieces + line, :])
        parts += [split[i * members:(i + 1) * members] for i in range(3)]
        left, right = [], []
        for peer in range(members):
            row = rows[peer:peer + 1]
            kept = own_lane & (line_row % pieces == row // LANES)
            left.append(
                jnp.concatenate([jnp.where(kept, part[peer:peer + 1], 0.0) for part in parts], axis=0)
            )
            right.append(low_matrix(row))
        left = jnp.concatenate(left, axis=1).astype(jnp.bfloat16)
        placed = dot(left, jnp.concatenate(right, axis=1), NT)
        lines_ref[0, line * count:(line + 1) * count, :] = placed[0:count]
        lines_ref[1, line * count:(line + 1) * count, :] = joined(placed[count:])

    def blocks(number):
        return jnp.concatenate(
            [lines_ref[number, pl.ds(piece, members, stride=pieces), :] for piece in range(pieces)],
            axis=1,
        )

    factor_ref[...] = blocks(1)
    inside = inside_rows(blocks(0), *field_refs)

    first = 3 * pieces
    flat = jnp.concatenate(
        [got_ref[peer, first:first + 4, 0:peer_rows] for peer in range(members)], axis=1
    )
    rest = jnp.concatenate(
        [got_ref[peer, first:first + 2, HALF:HALF + peer_rows] for peer in range(members)], axis=1
    )
    rows = rest[1:2].astype(jnp.int32)
    rows_ref[...] = rows
    fields = [flat[i:i + 1] for i in range(4)] + [rest[0:1]]
    state = scattered(padded(fields, 8), rows)
    u, phi, sa, sb, dist = (state[i:i + 1] for i in range(5))
    velocity = jnp.exp(u)
    deficit = (PLATE_RATE - velocity).astype(jnp.bfloat16).astype(jnp.float32)
    k1p = (jnp.exp(-phi) - velocity) / dist
    u2 = u + TIME_STEP * ((inside - sb * k1p) / (sa + DAMPING * velocity))
    state_ref[...] = padded([u, phi, sa, sb, dist, k1p], 8)
    sent = jnp.concatenate([u2, partial_row(deficit, coarse_v_ref)], axis=1)
    out_ref[...] = jnp.broadcast_to(sent[None], out_ref.shape)


def second_kernel(
    groups, state_ref, factor_ref, rows_ref, all_ref, elem_bases_ref, coarse_v_ref, *refs
):
    bases_refs, field_refs, sent_ref = refs[:2], refs[2:8], refs[8]
    members, elem_count = refs[6].shape[1], state_ref.shape[1]
    width = coarse_v_ref.shape[0]
    mine, me = lax.axis_index("leaf"), lax.axis_index("blk")
    sums = [
        jnp.sum(
            all_ref[group * members:(group + 1) * members, 0, elem_count:elem_count + width],
            axis=0, keepdims=True,
        )
        for group in range(groups)
    ]
    weights = coefficients(sums, width // groups)
    own = all_ref[pl.ds(mine * members, members), 0, 0:elem_count]
    coarse = coarse_all(weights, members, bases_refs)
    u2_all = own + factor_ref[...] * coarse
    deficits = (PLATE_RATE - jnp.exp(u2_all)).astype(jnp.bfloat16).astype(jnp.float32)
    inside = inside_rows(deficits, *field_refs)

    state = state_ref[...]
    u, phi, sa, sb, dist, k1p = (state[i:i + 1] for i in range(6))
    here = lax.broadcasted_iota(jnp.int32, u2_all.shape, 0) == me
    u2 = jnp.sum(jnp.where(here, u2_all, 0.0), axis=0, keepdims=True)
    deficit = jnp.sum(jnp.where(here, deficits, 0.0), axis=0, keepdims=True)
    phi2 = phi + TIME_STEP * k1p
    velocity = jnp.exp(u2)
    k2p = (jnp.exp(-phi2) - velocity) / dist
    inverse = 0.5 * TIME_STEP / (sa + DAMPING * velocity)
    u_next = 0.5 * (u + u2) + (inside - sb * k2p) * inverse
    phi_next = phi + 0.5 * TIME_STEP * (k1p + k2p)
    sent = gathered(padded([u_next, inverse, phi_next], 8), rows_ref[...])
    partial = as_lines(partial_row(deficit, coarse_v_ref))
    peer_rows = elem_count // members
    for device in range(groups * members):
        peer = device % members
        sent_ref[device, 0:3, 0:peer_rows] = sent[0:3, peer * peer_rows:(peer + 1) * peer_rows]
        sent_ref[device, 3:3 + partial.shape[0], :] = partial


def finish_kernel(groups, width, got_ref, slot_ref, elem_bases_ref, u_ref, phi_ref):
    elem_count = slot_ref.shape[1]
    members = got_ref.shape[0] // groups
    first = lax.axis_index("leaf") * members
    flat = peer_lanes(got_ref, first, members, 3, elem_count)
    out = gathered(padded([flat[i:i + 1] for i in range(3)], 8), slot_ref[...])
    sums = []
    for group in range(groups):
        total = jnp.sum(got_ref[group * members:(group + 1) * members], axis=0)
        lines = [total[3 + i:4 + i, :] for i in range(pl.cdiv(width, LANES))]
        sums.append(jnp.concatenate(lines, axis=1)[:, 0:width])
    weights = coefficients(sums, width // groups)
    weights = jnp.broadcast_to(weights, (8, weights.shape[1])).astype(jnp.bfloat16)
    coarse = dot(weights, elem_bases_ref[...], NN)[0:1]
    u_ref[...] = out[0:1] + out[1:2] * coarse
    phi_ref[...] = out[2:3]


def call(kernel, outs, *args, scalars=(), far=(), scratch=(), flops=1000, moved=1000):
    spaces = [SMEM if i in scalars else pl.ANY if i in far else VMEM for i in range(len(args))]
    args = [
        pltpu.with_memory_space_constraint(arg, pltpu.HBM) if i in far else arg
        for i, arg in enumerate(args)
    ]
    return pl.pallas_call(
        kernel,
        out_shape=outs,
        in_specs=[pl.BlockSpec(memory_space=space) for space in spaces],
        out_specs=jax.tree.map(lambda _: pl.BlockSpec(memory_space=VMEM), outs),
        scratch_shapes=list(scratch),
        cost_estimate=pl.CostEstimate(flops=flops, bytes_accessed=moved, transcendentals=0),
        compiler_params=pltpu.CompilerParams(vmem_limit_bytes=32 * 1024 * 1024),
    )(*args)


def shape(*dims, dtype=jnp.float32):
    return jax.ShapeDtypeStruct(dims, dtype)


def body(
    ln_rate,
    log_state,
    sigma,
    fric_a,
    fric_b,
    slip_dist,
    leaf_of_elem,
    near_blocks,
    near_col,
    near_count,
    far_u,
    far_v,
    far_col,
    far_rank,
    coarse_u,
    coarse_v,
):
    members = lax.axis_size("blk")
    elems = ln_rate.shape[0]
    leaf_size = near_blocks.shape[1]
    groups, rank = coarse_v.shape[0], coarse_v.shape[1]
    devices = groups * members
    width = groups * rank
    lines = pl.cdiv(width, LANES)
    sent_rows = 1 << (2 + lines).bit_length()
    integer = jnp.int32

    def swap(value, axes):
        return lax.all_to_all(value, axes, split_axis=0, concat_axis=0, tiled=True)

    def partner(value, bit):
        return lax.ppermute(value, "blk", [(i, i ^ (1 << bit)) for i in range(members)])

    elem_args = [
        value.reshape(1, elems)
        for value in (leaf_of_elem, ln_rate, log_state, sigma, fric_a, fric_b, slip_dist)
    ]
    scalar_args = [near_col, far_col, far_rank]
    weights = [
        near_blocks, far_u.reshape(-1, leaf_size), far_v.reshape(-1, leaf_size),
        coarse_v.reshape(width, elems),
    ]
    far_rows = weights[1].shape[0]
    sent, slot, elem_row = call(
        functools.partial(sort_kernel, members),
        (
            shape(members, -(-(3 * (elems // LANES) + 4) // 8) * 8, LANES),
            shape(1, elems, dtype=integer),
            shape(1, elems, dtype=integer),
        ),
        *elem_args, far=range(7),
        scratch=[VMEM(value.shape, value.dtype) for value in elem_args]
        + [pltpu.SemaphoreType.DMA((7,))],
    )
    bases = coarse_u.reshape(width, elems)
    top = members.bit_length() - 2
    early = bases = call(
        functools.partial(stack_foreign_kernel, groups, rank),
        shape(2 * (width - rank), elems, dtype=jnp.bfloat16),
        bases, partner(bases, top), slot, flops=1 << 34, moved=1 << 26,
    )
    near_mask, far_mask, near, far_u, far_v, coarse_v = call(
        load_kernel,
        (
            shape(near_blocks.shape[0], members, leaf_size),
            shape(members, far_rows),
            *[shape(*value.shape, dtype=jnp.bfloat16) for value in weights],
        ),
        early, *scalar_args, *weights, far=range(1, 8),
        scratch=[SMEM(value.shape, value.dtype) for value in scalar_args]
        + [pltpu.SemaphoreType.DMA((7,))],
        flops=1 << 30, moved=1 << 22,
    )
    fields = near_count, near, far_u, far_v, near_mask, far_mask
    state, factor, rows, out = call(
        place_kernel,
        (
            shape(8, elems),
            shape(members, elems),
            shape(1, elems, dtype=integer),
            shape(devices, 1, elems + lines * LANES),
        ),
        swap(sent, "blk"), coarse_v, *fields, scalars=(2,),
        scratch=[VMEM((2, members * (elems // LANES), LANES), jnp.float32)],
        flops=1 << 33, moved=1 << 25,
    )
    for bit in range(top - 1, 0, -1):
        bases = call(
            stack_kernel, shape(2 * bases.shape[0], elems, dtype=jnp.bfloat16),
            bases, partner(bases, bit), rows, flops=1 << 34, moved=1 << 26,
        )
    bases = bases, partner(bases, 0)
    elem_bases = call(
        functools.partial(element_kernel, members), shape(width - rank, elems, dtype=jnp.bfloat16),
        *bases, slot, elem_row, flops=1 << 34, moved=1 << 26,
    )
    sent = call(
        functools.partial(second_kernel, groups), shape(devices, sent_rows, LANES),
        state, factor, rows, swap(out, ("leaf", "blk")), elem_bases, coarse_v, *bases, *fields, scalars=(8,),
    )
    u, phi = call(
        functools.partial(finish_kernel, groups, width), (shape(1, elems), shape(1, elems)),
        swap(sent, ("leaf", "blk")), slot, elem_bases,
    )
    return u.reshape(elems), phi.reshape(elems)


def solution(mesh):
    each = P(("leaf", "blk"))
    blocks = P(("leaf", "blk"), None, None)
    last = P(None, None, ("leaf", "blk"))
    in_specs = (each,) * 7 + (blocks, each, each, blocks, blocks, each, each, last, last)
    return jax.shard_map(body, mesh=mesh, in_specs=in_specs, out_specs=(each, each), check_vma=False)
```

```python
import functools

import jax
import jax.numpy as jnp
from jax import lax
from jax.experimental import pallas as pl
from jax.experimental.pallas import tpu as pltpu
from jax.sharding import PartitionSpec as P

DAMPING = 0.5
PLATE_RATE = 1.0
TIME_STEP = 0.2

NN = (((1,), (0,)), ((), ()))
NT = (((1,), (1,)), ((), ()))
VMEM = pltpu.VMEM
SMEM = pltpu.SMEM

LANES = 128
HALF = 64


def dot(left, right, dims):
    return lax.dot_general(left, right, dims, preferred_element_type=jnp.float32)


def low_matrix(index_row):
    rows = lax.broadcasted_iota(jnp.int32, (LANES, index_row.shape[1]), 0)
    rows = rows.astype(jnp.float32).astype(jnp.bfloat16)
    low = (index_row & (LANES - 1)).astype(jnp.float32).astype(jnp.bfloat16)
    one = jnp.ones((), jnp.bfloat16)
    return jnp.where(rows == low, one, jnp.zeros_like(one))


def three_parts(values):
    high = values.astype(jnp.bfloat16).astype(jnp.float32)
    rest = values - high
    middle = rest.astype(jnp.bfloat16).astype(jnp.float32)
    return jnp.concatenate([high, middle, rest - middle], axis=0)


def joined(parts):
    count = parts.shape[0] // 3
    return parts[0:count] + parts[count:2 * count] + parts[2 * count:]


def scattered(values, index_row):
    parts = three_parts(values)
    count = parts.shape[0]
    high = index_row // LANES
    pieces = values.shape[1] // LANES
    left = jnp.concatenate([jnp.where(high == piece, parts, 0.0) for piece in range(pieces)], axis=0)
    moved = dot(left.astype(jnp.bfloat16), low_matrix(index_row), NT)
    return jnp.concatenate(
        [joined(moved[piece * count:(piece + 1) * count]) for piece in range(pieces)], axis=1
    )


def gathered(values, index_row):
    parts = three_parts(values)
    count = parts.shape[0]
    high = index_row // LANES
    pieces = values.shape[1] // LANES
    left = jnp.concatenate(
        [parts[:, piece * LANES:(piece + 1) * LANES] for piece in range(pieces)], axis=0
    )
    moved = dot(left.astype(jnp.bfloat16), low_matrix(index_row), NN)
    total = jnp.zeros((count, index_row.shape[1]), jnp.float32)
    for piece in range(pieces):
        total = jnp.where(high == piece, moved[piece * count:(piece + 1) * count], total)
    return joined(total)


def padded(rows, count):
    missing = count - len(rows)
    if missing:
        rows = rows + [jnp.zeros((missing, rows[0].shape[1]), jnp.float32)]
    return jnp.concatenate(rows, axis=0)


def as_lines(row):
    return jnp.concatenate(
        [row[:, i * LANES:(i + 1) * LANES] for i in range(row.shape[1] // LANES)], axis=0
    )


def peer_lanes(ref, first, members, rows, elem_count):
    width = elem_count // members
    return jnp.concatenate([ref[first + peer, 0:rows, 0:width] for peer in range(members)], axis=1)


def start_copies(sources, targets, sems):
    copies = [
        pltpu.make_async_copy(source, target, sems.at[i])
        for i, (source, target) in enumerate(zip(sources, targets))
    ]
    for copy in copies:
        copy.start()
    return copies


def sort_kernel(members, *refs):
    elem_refs, bases_ref, sent_ref, slot_ref, elem_row_ref, bases_out = refs[:7], *refs[7:12]
    elem_bufs, sems = refs[12:19], refs[19]
    copies = start_copies([*elem_refs, bases_ref], [*elem_bufs, bases_out], sems)
    mine = lax.axis_index("leaf")
    elem_count = elem_bufs[0].shape[1]
    peer_rows = elem_count // members
    pieces = elem_count // LANES
    before = lax.broadcasted_iota(jnp.int32, (LANES, LANES), 0)
    after = lax.broadcasted_iota(jnp.int32, (LANES, LANES), 1)
    triangle = jnp.where(before < after, 1.0, 0.0).astype(jnp.bfloat16)
    copies[0].wait()
    local = elem_bufs[0][...] - mine * (members * elem_count)
    target = local // elem_count
    target_row = local - target * elem_count
    peers = lax.broadcasted_iota(jnp.int32, (members, elem_count), 0)
    onehot = jnp.where(peers == target, 1.0, 0.0)
    lines = [onehot[:, i * LANES:(i + 1) * LANES] for i in range(pieces)]
    inside = dot(jnp.concatenate(lines, axis=0).astype(jnp.bfloat16), triangle, NN)
    passed = jnp.zeros((members, 1), jnp.float32)
    ranks = []
    for i, line in enumerate(lines):
        earlier = inside[i * members:(i + 1) * members] + passed
        ranks.append(jnp.sum(earlier * line, axis=0, keepdims=True))
        passed = passed + jnp.sum(line, axis=1, keepdims=True)
    slot = target * peer_rows + jnp.concatenate(ranks, axis=1).astype(jnp.int32)
    slot_ref[...] = slot
    elem_row_ref[...] = target_row
    for copy in copies[1:7]:
        copy.wait()
    u, phi, sigma, fric_a, fric_b, dist = (buf[...] for buf in elem_bufs[1:])
    velocity = jnp.exp(u)
    deficit = (PLATE_RATE - velocity).astype(jnp.bfloat16).astype(jnp.float32)
    sa = sigma * fric_a
    factor = TIME_STEP / (sa + DAMPING * velocity)
    rows = [u, phi, sa, sigma * fric_b, dist, target_row.astype(jnp.float32), deficit, factor]
    values = scattered(padded(rows, 8), slot)
    everyone = jnp.concatenate([as_lines(values[i:i + 1]) for i in (6, 5, 7)], axis=0)
    for peer in range(members):
        sent_ref[peer, 0:3 * pieces, :] = everyone
        part = values[0:6, peer * peer_rows:(peer + 1) * peer_rows]
        sent_ref[peer, 3 * pieces:3 * pieces + 4, 0:peer_rows] = part[0:4]
        sent_ref[peer, 3 * pieces:3 * pieces + 2, HALF:HALF + peer_rows] = part[4:6]
    copies[7].wait()


def load_kernel(early_ref, *refs):
    scalar_refs, weight_refs, near_mask_ref, far_mask_ref = refs[:3], refs[3:7], refs[7], refs[8]
    weight_outs, scalar_bufs, sems = refs[9:13], refs[13:16], refs[16]
    copies = start_copies([*scalar_refs, *weight_refs], [*scalar_bufs, *weight_outs], sems)
    for copy in copies[:3]:
        copy.wait()
    near_col, far_col, far_rank = scalar_bufs
    far_slots = far_col.shape[0]
    far_width = far_mask_ref.shape[1] // far_slots
    block = lax.broadcasted_iota(jnp.int32, near_mask_ref.shape[1:], 0)
    for number in range(near_mask_ref.shape[0]):
        near_mask_ref[number] = jnp.where(block == near_col[number], 1.0, 0.0)
    block = lax.broadcasted_iota(jnp.int32, far_mask_ref.shape, 0)
    lane = lax.broadcasted_iota(jnp.int32, far_mask_ref.shape, 1)
    column = jnp.full(far_mask_ref.shape, -1, jnp.int32)
    for number in range(far_slots):
        low = number * far_width
        kept = (lane >= low) & (lane < low + far_rank[number])
        column = jnp.where(kept, far_col[number], column)
    far_mask_ref[...] = jnp.where(block == column, 1.0, 0.0)
    for copy in copies[3:]:
        copy.wait()


def partial_row(deficit, coarse_v_ref):
    wide = jnp.broadcast_to(deficit, (8, deficit.shape[1])).astype(jnp.bfloat16)
    partial = dot(wide, coarse_v_ref[...], NT)[0:1]
    rest = -partial.shape[1] % LANES
    if rest:
        partial = jnp.concatenate([partial, jnp.zeros((1, rest), jnp.float32)], axis=1)
    return partial


def inside_rows(deficits, near_count, near_ref, far_u_ref, far_v_ref, near_mask_ref, far_mask_ref):
    total = jnp.zeros(deficits.shape, jnp.float32)
    for slot in range(near_ref.shape[0]):
        live = jnp.where(slot < near_count[0], 1.0, 0.0)
        source = (deficits * (near_mask_ref[slot] * live)).astype(jnp.bfloat16)
        total = total + dot(source, near_ref[slot], NT)
    project = dot(deficits.astype(jnp.bfloat16), far_v_ref[...], NT) * far_mask_ref[...]
    project = jnp.sum(project, axis=0, keepdims=True)
    project = jnp.broadcast_to(project, (8, project.shape[1])).astype(jnp.bfloat16)
    far = dot(project, far_u_ref[...], NN)
    return jnp.sum(total, axis=0, keepdims=True) + far[0:1]


def coefficients(sums, rank):
    groups, width = len(sums), sums[0].shape[1]
    mine = lax.axis_index("leaf")
    table = padded(sums, -(-groups // 8) * 8)
    lane = lax.broadcasted_iota(jnp.int32, table.shape, 1) // rank
    row = lax.broadcasted_iota(jnp.int32, table.shape, 0)
    table = jnp.where(lane == mine, table, 0.0).astype(jnp.bfloat16)
    across = lax.broadcasted_iota(jnp.int32, (width, width), 0) % rank
    down = lax.broadcasted_iota(jnp.int32, (width, width), 1) % rank
    spread = dot(table, jnp.where(across == down, 1.0, 0.0).astype(jnp.bfloat16), NN)
    weights = jnp.sum(jnp.where(row == mine ^ (lane + 1), spread, 0.0), axis=0, keepdims=True)
    return weights[:, 0:width - rank]


def coarse_all(weights, members, bases_refs):
    row = lax.broadcasted_iota(jnp.int32, (members, weights.shape[1]), 0) ^ lax.axis_index("blk")
    bits = members.bit_length() - 1
    total = jnp.zeros((members, bases_refs[0].shape[1]), jnp.float32)
    for number, ref in enumerate(bases_refs):
        left = []
        for place in range(members // 2):
            source = relative_member(place, number, bits)
            left.append(jnp.where(row == source, weights, 0.0))
        left = jnp.concatenate(left, axis=1).astype(jnp.bfloat16)
        total = total + dot(left, ref[...], NN)
    return total


def stack_kernel(held_ref, came_ref, *refs):
    out_ref = refs[-1]
    count = held_ref.shape[0]
    out_ref[0:count, :] = held_ref[...]
    out_ref[count:2 * count, :] = came_ref[...]


def stack_foreign_kernel(groups, rank, held_ref, came_ref, *refs):
    out_ref = refs[-1]
    mine = lax.axis_index("leaf")
    place = 0
    for ref in (held_ref, came_ref):
        for shift in range(1, groups):
            out_ref[place:place + rank, :] = ref[pl.ds((mine ^ shift) * rank, rank), :]
            place += rank


def relative_member(place, number, bits):
    for bit in range(bits - 1):
        number |= (place >> bit & 1) << (bits - 1 - bit)
    return number


def element_kernel(members, held_ref, came_ref, slot_ref, elem_row_ref, out_ref):
    slot, row = slot_ref[...], elem_row_ref[...]
    elem_count = row.shape[1]
    kept = out_ref.shape[0]
    pieces = elem_count // LANES
    owner = (slot // (elem_count // members)) ^ lax.axis_index("blk")
    low, high = low_matrix(row), row // LANES
    total = jnp.zeros(out_ref.shape, jnp.float32)
    for number, ref in enumerate((held_ref, came_ref)):
        for place in range(members // 2):
            part = ref[place * kept:(place + 1) * kept, :]
            left = jnp.concatenate(
                [part[:, piece * LANES:(piece + 1) * LANES] for piece in range(pieces)], axis=0
            )
            found = dot(left, low, NN)
            ours = owner == relative_member(place, number, members.bit_length() - 1)
            for piece in range(pieces):
                here = ours & (high == piece)
                total = jnp.where(here, found[piece * kept:(piece + 1) * kept], total)
    out_ref[...] = total.astype(jnp.bfloat16)


def place_kernel(got_ref, coarse_v_ref, *refs):
    field_refs, state_ref, factor_ref, rows_ref, out_ref, lines_ref = refs[:6], *refs[6:]
    members = got_ref.shape[0]
    elem_count = state_ref.shape[1]
    pieces = elem_count // LANES
    peer_rows = elem_count // members
    count = LANES // peer_rows * pieces
    line_row = lax.broadcasted_iota(jnp.int32, (count, LANES), 0)
    lane_block = lax.broadcasted_iota(jnp.int32, (count, LANES), 1) // peer_rows
    own_lane = line_row // pieces == lane_block
    for line in range(pieces):
        rows = got_ref[:, pieces + line, :].astype(jnp.int32)
        parts = [got_ref[:, line, :]]
        split = three_parts(got_ref[:, 2 * pieces + line, :])
        parts += [split[i * members:(i + 1) * members] for i in range(3)]
        left, right = [], []
        for peer in range(members):
            row = rows[peer:peer + 1]
            kept = own_lane & (line_row % pieces == row // LANES)
            left.append(
                jnp.concatenate([jnp.where(kept, part[peer:peer + 1], 0.0) for part in parts], axis=0)
            )
            right.append(low_matrix(row))
        left = jnp.concatenate(left, axis=1).astype(jnp.bfloat16)
        placed = dot(left, jnp.concatenate(right, axis=1), NT)
        lines_ref[0, line * count:(line + 1) * count, :] = placed[0:count]
        lines_ref[1, line * count:(line + 1) * count, :] = joined(placed[count:])

    def blocks(number):
        return jnp.concatenate(
            [lines_ref[number, pl.ds(piece, members, stride=pieces), :] for piece in range(pieces)],
            axis=1,
        )

    factor_ref[...] = blocks(1)
    inside = inside_rows(blocks(0), *field_refs)

    first = 3 * pieces
    flat = jnp.concatenate(
        [got_ref[peer, first:first + 4, 0:peer_rows] for peer in range(members)], axis=1
    )
    rest = jnp.concatenate(
        [got_ref[peer, first:first + 2, HALF:HALF + peer_rows] for peer in range(members)], axis=1
    )
    rows = rest[1:2].astype(jnp.int32)
    rows_ref[...] = rows
    fields = [flat[i:i + 1] for i in range(4)] + [rest[0:1]]
    state = scattered(padded(fields, 8), rows)
    u, phi, sa, sb, dist = (state[i:i + 1] for i in range(5))
    velocity = jnp.exp(u)
    deficit = (PLATE_RATE - velocity).astype(jnp.bfloat16).astype(jnp.float32)
    k1p = (jnp.exp(-phi) - velocity) / dist
    u2 = u + TIME_STEP * ((inside - sb * k1p) / (sa + DAMPING * velocity))
    state_ref[...] = padded([u, phi, sa, sb, dist, k1p], 8)
    sent = jnp.concatenate([u2, partial_row(deficit, coarse_v_ref)], axis=1)
    out_ref[...] = jnp.broadcast_to(sent[None], out_ref.shape)


def second_kernel(
    groups, state_ref, factor_ref, rows_ref, all_ref, elem_bases_ref, coarse_v_ref, *refs
):
    bases_refs, field_refs, sent_ref = refs[:2], refs[2:8], refs[8]
    members, elem_count = refs[6].shape[1], state_ref.shape[1]
    width = coarse_v_ref.shape[0]
    mine, me = lax.axis_index("leaf"), lax.axis_index("blk")
    sums = [
        jnp.sum(
            all_ref[group * members:(group + 1) * members, 0, elem_count:elem_count + width],
            axis=0, keepdims=True,
        )
        for group in range(groups)
    ]
    weights = coefficients(sums, width // groups)
    own = all_ref[pl.ds(mine * members, members), 0, 0:elem_count]
    coarse = coarse_all(weights, members, bases_refs)
    u2_all = own + factor_ref[...] * coarse
    deficits = (PLATE_RATE - jnp.exp(u2_all)).astype(jnp.bfloat16).astype(jnp.float32)
    inside = inside_rows(deficits, *field_refs)

    state = state_ref[...]
    u, phi, sa, sb, dist, k1p = (state[i:i + 1] for i in range(6))
    here = lax.broadcasted_iota(jnp.int32, u2_all.shape, 0) == me
    u2 = jnp.sum(jnp.where(here, u2_all, 0.0), axis=0, keepdims=True)
    deficit = jnp.sum(jnp.where(here, deficits, 0.0), axis=0, keepdims=True)
    phi2 = phi + TIME_STEP * k1p
    velocity = jnp.exp(u2)
    k2p = (jnp.exp(-phi2) - velocity) / dist
    inverse = 0.5 * TIME_STEP / (sa + DAMPING * velocity)
    u_next = 0.5 * (u + u2) + (inside - sb * k2p) * inverse
    phi_next = phi + 0.5 * TIME_STEP * (k1p + k2p)
    sent = gathered(padded([u_next, inverse, phi_next], 8), rows_ref[...])
    partial = as_lines(partial_row(deficit, coarse_v_ref))
    peer_rows = elem_count // members
    for device in range(groups * members):
        peer = device % members
        sent_ref[device, 0:3, 0:peer_rows] = sent[0:3, peer * peer_rows:(peer + 1) * peer_rows]
        sent_ref[device, 3:3 + partial.shape[0], :] = partial


def finish_kernel(groups, width, got_ref, slot_ref, elem_bases_ref, u_ref, phi_ref):
    elem_count = slot_ref.shape[1]
    members = got_ref.shape[0] // groups
    first = lax.axis_index("leaf") * members
    flat = peer_lanes(got_ref, first, members, 3, elem_count)
    out = gathered(padded([flat[i:i + 1] for i in range(3)], 8), slot_ref[...])
    sums = []
    for group in range(groups):
        total = jnp.sum(got_ref[group * members:(group + 1) * members], axis=0)
        lines = [total[3 + i:4 + i, :] for i in range(pl.cdiv(width, LANES))]
        sums.append(jnp.concatenate(lines, axis=1)[:, 0:width])
    weights = coefficients(sums, width // groups)
    weights = jnp.broadcast_to(weights, (8, weights.shape[1])).astype(jnp.bfloat16)
    coarse = dot(weights, elem_bases_ref[...], NN)[0:1]
    u_ref[...] = out[0:1] + out[1:2] * coarse
    phi_ref[...] = out[2:3]


def call(kernel, outs, *args, scalars=(), far=(), scratch=(), flops=1000, moved=1000):
    spaces = [SMEM if i in scalars else pl.ANY if i in far else VMEM for i in range(len(args))]
    args = [
        pltpu.with_memory_space_constraint(arg, pltpu.HBM) if i in far else arg
        for i, arg in enumerate(args)
    ]
    return pl.pallas_call(
        kernel,
        out_shape=outs,
        in_specs=[pl.BlockSpec(memory_space=space) for space in spaces],
        out_specs=jax.tree.map(lambda _: pl.BlockSpec(memory_space=VMEM), outs),
        scratch_shapes=list(scratch),
        cost_estimate=pl.CostEstimate(flops=flops, bytes_accessed=moved, transcendentals=0),
        compiler_params=pltpu.CompilerParams(vmem_limit_bytes=32 * 1024 * 1024),
    )(*args)


def shape(*dims, dtype=jnp.float32):
    return jax.ShapeDtypeStruct(dims, dtype)


def body(
    ln_rate,
    log_state,
    sigma,
    fric_a,
    fric_b,
    slip_dist,
    leaf_of_elem,
    near_blocks,
    near_col,
    near_count,
    far_u,
    far_v,
    far_col,
    far_rank,
    coarse_u,
    coarse_v,
):
    members = lax.axis_size("blk")
    elems = ln_rate.shape[0]
    leaf_size = near_blocks.shape[1]
    groups, rank = coarse_v.shape[0], coarse_v.shape[1]
    devices = groups * members
    width = groups * rank
    lines = pl.cdiv(width, LANES)
    sent_rows = 1 << (2 + lines).bit_length()
    integer = jnp.int32

    def swap(value, axes):
        return lax.all_to_all(value, axes, split_axis=0, concat_axis=0, tiled=True)

    def partner(value, bit):
        return lax.ppermute(value, "blk", [(i, i ^ (1 << bit)) for i in range(members)])

    elem_args = [
        value.reshape(1, elems)
        for value in (leaf_of_elem, ln_rate, log_state, sigma, fric_a, fric_b, slip_dist)
    ]
    scalar_args = [near_col, far_col, far_rank]
    weights = [
        near_blocks, far_u.reshape(-1, leaf_size), far_v.reshape(-1, leaf_size),
        coarse_v.reshape(width, elems),
    ]
    far_rows = weights[1].shape[0]
    bases = coarse_u.reshape(width, elems)
    sent, slot, elem_row, held = call(
        functools.partial(sort_kernel, members),
        (
            shape(members, -(-(3 * (elems // LANES) + 4) // 8) * 8, LANES),
            shape(1, elems, dtype=integer),
            shape(1, elems, dtype=integer),
            shape(width, elems, dtype=jnp.bfloat16),
        ),
        *elem_args, bases, far=range(8),
        scratch=[VMEM(value.shape, value.dtype) for value in elem_args]
        + [pltpu.SemaphoreType.DMA((8,))],
    )
    top = members.bit_length() - 2
    early = bases = call(
        functools.partial(stack_foreign_kernel, groups, rank),
        shape(2 * (width - rank), elems, dtype=jnp.bfloat16),
        held, partner(bases, top), slot, flops=1 << 34, moved=1 << 26,
    )
    near_mask, far_mask, near, far_u, far_v, coarse_v = call(
        load_kernel,
        (
            shape(near_blocks.shape[0], members, leaf_size),
            shape(members, far_rows),
            *[shape(*value.shape, dtype=jnp.bfloat16) for value in weights],
        ),
        early, *scalar_args, *weights, far=range(1, 8),
        scratch=[SMEM(value.shape, value.dtype) for value in scalar_args]
        + [pltpu.SemaphoreType.DMA((7,))],
        flops=1 << 30, moved=1 << 22,
    )
    fields = near_count, near, far_u, far_v, near_mask, far_mask
    state, factor, rows, out = call(
        place_kernel,
        (
            shape(8, elems),
            shape(members, elems),
            shape(1, elems, dtype=integer),
            shape(devices, 1, elems + lines * LANES),
        ),
        swap(sent, "blk"), coarse_v, *fields, scalars=(2,),
        scratch=[VMEM((2, members * (elems // LANES), LANES), jnp.float32)],
        flops=1 << 33, moved=1 << 25,
    )
    for bit in range(top - 1, 0, -1):
        bases = call(
            stack_kernel, shape(2 * bases.shape[0], elems, dtype=jnp.bfloat16),
            bases, partner(bases, bit), rows, flops=1 << 34, moved=1 << 26,
        )
    bases = bases, partner(bases, 0)
    elem_bases = call(
        functools.partial(element_kernel, members), shape(width - rank, elems, dtype=jnp.bfloat16),
        *bases, slot, elem_row, flops=1 << 34, moved=1 << 26,
    )
    sent = call(
        functools.partial(second_kernel, groups), shape(devices, sent_rows, LANES),
        state, factor, rows, swap(out, ("leaf", "blk")), elem_bases, coarse_v, *bases, *fields, scalars=(8,),
    )
    u, phi = call(
        functools.partial(finish_kernel, groups, width), (shape(1, elems), shape(1, elems)),
        swap(sent, ("leaf", "blk")), slot, elem_bases,
    )
    return u.reshape(elems), phi.reshape(elems)


def solution(mesh):
    each = P(("leaf", "blk"))
    blocks = P(("leaf", "blk"), None, None)
    last = P(None, None, ("leaf", "blk"))
    in_specs = (each,) * 7 + (blocks, each, each, blocks, blocks, each, each, last, last)
    return jax.shard_map(body, mesh=mesh, in_specs=in_specs, out_specs=(each, each), check_vma=False)
```

```python
import functools

import jax
import jax.numpy as jnp
from jax import lax
from jax.experimental import pallas as pl
from jax.experimental.pallas import tpu as pltpu
from jax.sharding import PartitionSpec as P

DAMPING = 0.5
PLATE_RATE = 1.0
TIME_STEP = 0.2

NN = (((1,), (0,)), ((), ()))
NT = (((1,), (1,)), ((), ()))
VMEM = pltpu.VMEM
SMEM = pltpu.SMEM

LANES = 128
HALF = 64


def dot(left, right, dims):
    return lax.dot_general(left, right, dims, preferred_element_type=jnp.float32)


def low_matrix(index_row):
    rows = lax.broadcasted_iota(jnp.int32, (LANES, index_row.shape[1]), 0)
    rows = rows.astype(jnp.float32).astype(jnp.bfloat16)
    low = (index_row & (LANES - 1)).astype(jnp.float32).astype(jnp.bfloat16)
    one = jnp.ones((), jnp.bfloat16)
    return jnp.where(rows == low, one, jnp.zeros_like(one))


def three_parts(values):
    high = values.astype(jnp.bfloat16).astype(jnp.float32)
    rest = values - high
    middle = rest.astype(jnp.bfloat16).astype(jnp.float32)
    return jnp.concatenate([high, middle, rest - middle], axis=0)


def joined(parts):
    count = parts.shape[0] // 3
    return parts[0:count] + parts[count:2 * count] + parts[2 * count:]


def scattered(values, index_row):
    parts = three_parts(values)
    count = parts.shape[0]
    high = index_row // LANES
    pieces = values.shape[1] // LANES
    left = jnp.concatenate([jnp.where(high == piece, parts, 0.0) for piece in range(pieces)], axis=0)
    moved = dot(left.astype(jnp.bfloat16), low_matrix(index_row), NT)
    return jnp.concatenate(
        [joined(moved[piece * count:(piece + 1) * count]) for piece in range(pieces)], axis=1
    )


def gathered(values, index_row):
    parts = three_parts(values)
    count = parts.shape[0]
    high = index_row // LANES
    pieces = values.shape[1] // LANES
    left = jnp.concatenate(
        [parts[:, piece * LANES:(piece + 1) * LANES] for piece in range(pieces)], axis=0
    )
    moved = dot(left.astype(jnp.bfloat16), low_matrix(index_row), NN)
    total = jnp.zeros((count, index_row.shape[1]), jnp.float32)
    for piece in range(pieces):
        total = jnp.where(high == piece, moved[piece * count:(piece + 1) * count], total)
    return joined(total)


def padded(rows, count):
    missing = count - len(rows)
    if missing:
        rows = rows + [jnp.zeros((missing, rows[0].shape[1]), jnp.float32)]
    return jnp.concatenate(rows, axis=0)


def as_lines(row):
    return jnp.concatenate(
        [row[:, i * LANES:(i + 1) * LANES] for i in range(row.shape[1] // LANES)], axis=0
    )


def peer_lanes(ref, first, members, rows, elem_count):
    width = elem_count // members
    return jnp.concatenate([ref[first + peer, 0:rows, 0:width] for peer in range(members)], axis=1)


def start_copies(sources, targets, sems):
    copies = [
        pltpu.make_async_copy(source, target, sems.at[i])
        for i, (source, target) in enumerate(zip(sources, targets))
    ]
    for copy in copies:
        copy.start()
    return copies


def sort_kernel(members, *refs):
    elem_refs, bases_ref, sent_ref, slot_ref, elem_row_ref, bases_out = refs[:7], *refs[7:12]
    elem_bufs, sems = refs[12:19], refs[19]
    copies = start_copies([*elem_refs, bases_ref], [*elem_bufs, bases_out], sems)
    mine = lax.axis_index("leaf")
    elem_count = elem_bufs[0].shape[1]
    peer_rows = elem_count // members
    pieces = elem_count // LANES
    before = lax.broadcasted_iota(jnp.int32, (LANES, LANES), 0)
    after = lax.broadcasted_iota(jnp.int32, (LANES, LANES), 1)
    triangle = jnp.where(before < after, 1.0, 0.0).astype(jnp.bfloat16)
    copies[0].wait()
    local = elem_bufs[0][...] - mine * (members * elem_count)
    target = local // elem_count
    target_row = local - target * elem_count
    peers = lax.broadcasted_iota(jnp.int32, (members, elem_count), 0)
    onehot = jnp.where(peers == target, 1.0, 0.0)
    lines = [onehot[:, i * LANES:(i + 1) * LANES] for i in range(pieces)]
    inside = dot(jnp.concatenate(lines, axis=0).astype(jnp.bfloat16), triangle, NN)
    passed = jnp.zeros((members, 1), jnp.float32)
    ranks = []
    for i, line in enumerate(lines):
        earlier = inside[i * members:(i + 1) * members] + passed
        ranks.append(jnp.sum(earlier * line, axis=0, keepdims=True))
        passed = passed + jnp.sum(line, axis=1, keepdims=True)
    slot = target * peer_rows + jnp.concatenate(ranks, axis=1).astype(jnp.int32)
    slot_ref[...] = slot
    elem_row_ref[...] = target_row
    for copy in copies[1:7]:
        copy.wait()
    u, phi, sigma, fric_a, fric_b, dist = (buf[...] for buf in elem_bufs[1:])
    velocity = jnp.exp(u)
    deficit = (PLATE_RATE - velocity).astype(jnp.bfloat16).astype(jnp.float32)
    sa = sigma * fric_a
    factor = TIME_STEP / (sa + DAMPING * velocity)
    rows = [u, phi, sa, sigma * fric_b, dist, target_row.astype(jnp.float32), deficit, factor]
    values = scattered(padded(rows, 8), slot)
    everyone = jnp.concatenate([as_lines(values[i:i + 1]) for i in (6, 5, 7)], axis=0)
    for peer in range(members):
        sent_ref[peer, 0:3 * pieces, :] = everyone
        part = values[0:6, peer * peer_rows:(peer + 1) * peer_rows]
        sent_ref[peer, 3 * pieces:3 * pieces + 4, 0:peer_rows] = part[0:4]
        sent_ref[peer, 3 * pieces:3 * pieces + 2, HALF:HALF + peer_rows] = part[4:6]
    copies[7].wait()


def load_kernel(early_ref, *refs):
    scalar_refs, weight_refs, near_mask_ref, far_mask_ref = refs[:3], refs[3:7], refs[7], refs[8]
    weight_outs, scalar_bufs, sems = refs[9:13], refs[13:16], refs[16]
    copies = start_copies([*scalar_refs, *weight_refs], [*scalar_bufs, *weight_outs], sems)
    for copy in copies[:3]:
        copy.wait()
    near_col, far_col, far_rank = scalar_bufs
    far_slots = far_col.shape[0]
    far_width = far_mask_ref.shape[1] // far_slots
    block = lax.broadcasted_iota(jnp.int32, near_mask_ref.shape[1:], 0)
    for number in range(near_mask_ref.shape[0]):
        near_mask_ref[number] = jnp.where(block == near_col[number], 1.0, 0.0)
    block = lax.broadcasted_iota(jnp.int32, far_mask_ref.shape, 0)
    lane = lax.broadcasted_iota(jnp.int32, far_mask_ref.shape, 1)
    column = jnp.full(far_mask_ref.shape, -1, jnp.int32)
    for number in range(far_slots):
        low = number * far_width
        kept = (lane >= low) & (lane < low + far_rank[number])
        column = jnp.where(kept, far_col[number], column)
    far_mask_ref[...] = jnp.where(block == column, 1.0, 0.0)
    for copy in copies[3:]:
        copy.wait()


def partial_row(deficit, coarse_v_ref):
    wide = jnp.broadcast_to(deficit, (8, deficit.shape[1])).astype(jnp.bfloat16)
    partial = dot(wide, coarse_v_ref[...], NT)[0:1]
    rest = -partial.shape[1] % LANES
    if rest:
        partial = jnp.concatenate([partial, jnp.zeros((1, rest), jnp.float32)], axis=1)
    return partial


def inside_rows(deficits, near_count, near_ref, far_u_ref, far_v_ref, near_mask_ref, far_mask_ref):
    total = jnp.zeros((near_ref.shape[1], deficits.shape[0]), jnp.float32)
    for slot in range(near_ref.shape[0]):
        live = jnp.where(slot < near_count[0], 1.0, 0.0)
        source = (deficits * (near_mask_ref[slot] * live)).astype(jnp.bfloat16)
        total = total + dot(near_ref[slot], source, NT)
    near = jnp.sum(total.T, axis=0, keepdims=True)
    project = dot(deficits.astype(jnp.bfloat16), far_v_ref[...], NT) * far_mask_ref[...]
    project = jnp.sum(project, axis=0, keepdims=True)
    project = jnp.broadcast_to(project, (8, project.shape[1])).astype(jnp.bfloat16)
    far = dot(project, far_u_ref[...], NN)
    return near + far[0:1]


def coefficients(sums, rank):
    groups, width = len(sums), sums[0].shape[1]
    mine = lax.axis_index("leaf")
    table = padded(sums, -(-groups // 8) * 8)
    lane = lax.broadcasted_iota(jnp.int32, table.shape, 1) // rank
    row = lax.broadcasted_iota(jnp.int32, table.shape, 0)
    table = jnp.where(lane == mine, table, 0.0).astype(jnp.bfloat16)
    across = lax.broadcasted_iota(jnp.int32, (width, width), 0) % rank
    down = lax.broadcasted_iota(jnp.int32, (width, width), 1) % rank
    spread = dot(table, jnp.where(across == down, 1.0, 0.0).astype(jnp.bfloat16), NN)
    weights = jnp.sum(jnp.where(row == mine ^ (lane + 1), spread, 0.0), axis=0, keepdims=True)
    return weights[:, 0:width - rank]


def coarse_all(weights, members, bases_refs):
    row = lax.broadcasted_iota(jnp.int32, (members, weights.shape[1]), 0) ^ lax.axis_index("blk")
    total = jnp.zeros((members, bases_refs[0].shape[1]), jnp.float32)
    for number, ref in enumerate(bases_refs):
        left = []
        for place in range(members // 2):
            source = relative_member(place, number, members)
            left.append(jnp.where(row == source, weights, 0.0))
        left = jnp.concatenate(left, axis=1).astype(jnp.bfloat16)
        total = total + dot(left, ref[...], NN)
    return total


def stack_kernel(held_ref, came_ref, *refs):
    out_ref = refs[-1]
    count = held_ref.shape[0]
    out_ref[0:count, :] = held_ref[...]
    out_ref[count:2 * count, :] = came_ref[...]


def stack_foreign_kernel(groups, rank, held_ref, came_ref, *refs):
    out_ref = refs[-1]
    mine = lax.axis_index("leaf")
    place = 0
    for ref in (held_ref, came_ref):
        for shift in range(1, groups):
            out_ref[place:place + rank, :] = ref[pl.ds((mine ^ shift) * rank, rank), :]
            place += rank


def step_bits(members):
    bits = list(range(members.bit_length() - 2, -1, -1))
    return bits[:-2] + [bits[-1], bits[-2]]


def relative_member(place, number, members):
    order = step_bits(members)
    found = number << order[-1]
    for step, bit in enumerate(order[:-1]):
        found |= (place >> step & 1) << bit
    return found


def element_kernel(members, held_ref, came_ref, slot_ref, elem_row_ref, out_ref):
    slot, row = slot_ref[...], elem_row_ref[...]
    elem_count = row.shape[1]
    kept = out_ref.shape[0]
    pieces = elem_count // LANES
    owner = (slot // (elem_count // members)) ^ lax.axis_index("blk")
    low, high = low_matrix(row), row // LANES
    total = jnp.zeros(out_ref.shape, jnp.float32)
    for number, ref in enumerate((held_ref, came_ref)):
        for place in range(members // 2):
            part = ref[place * kept:(place + 1) * kept, :]
            left = jnp.concatenate(
                [part[:, piece * LANES:(piece + 1) * LANES] for piece in range(pieces)], axis=0
            )
            found = dot(left, low, NN)
            ours = owner == relative_member(place, number, members)
            for piece in range(pieces):
                here = ours & (high == piece)
                total = jnp.where(here, found[piece * kept:(piece + 1) * kept], total)
    out_ref[...] = total.astype(jnp.bfloat16)


def place_kernel(got_ref, coarse_v_ref, *refs):
    field_refs, state_ref, factor_ref, rows_ref, out_ref, lines_ref = refs[:6], *refs[6:]
    members = got_ref.shape[0]
    elem_count = state_ref.shape[1]
    pieces = elem_count // LANES
    peer_rows = elem_count // members
    count = LANES // peer_rows * pieces
    line_row = lax.broadcasted_iota(jnp.int32, (count, LANES), 0)
    lane_block = lax.broadcasted_iota(jnp.int32, (count, LANES), 1) // peer_rows
    own_lane = line_row // pieces == lane_block
    for line in range(pieces):
        rows = got_ref[:, pieces + line, :].astype(jnp.int32)
        parts = [got_ref[:, line, :]]
        split = three_parts(got_ref[:, 2 * pieces + line, :])
        parts += [split[i * members:(i + 1) * members] for i in range(3)]
        left, right = [], []
        for peer in range(members):
            row = rows[peer:peer + 1]
            kept = own_lane & (line_row % pieces == row // LANES)
            left.append(
                jnp.concatenate([jnp.where(kept, part[peer:peer + 1], 0.0) for part in parts], axis=0)
            )
            right.append(low_matrix(row))
        left = jnp.concatenate(left, axis=1).astype(jnp.bfloat16)
        placed = dot(left, jnp.concatenate(right, axis=1), NT)
        lines_ref[0, line * count:(line + 1) * count, :] = placed[0:count]
        lines_ref[1, line * count:(line + 1) * count, :] = joined(placed[count:])

    def blocks(number):
        return jnp.concatenate(
            [lines_ref[number, pl.ds(piece, members, stride=pieces), :] for piece in range(pieces)],
            axis=1,
        )

    factor_ref[...] = blocks(1)
    inside = inside_rows(blocks(0), *field_refs)

    first = 3 * pieces
    flat = jnp.concatenate(
        [got_ref[peer, first:first + 4, 0:peer_rows] for peer in range(members)], axis=1
    )
    rest = jnp.concatenate(
        [got_ref[peer, first:first + 2, HALF:HALF + peer_rows] for peer in range(members)], axis=1
    )
    rows = rest[1:2].astype(jnp.int32)
    rows_ref[...] = rows
    fields = [flat[i:i + 1] for i in range(4)] + [rest[0:1]]
    state = scattered(padded(fields, 8), rows)
    u, phi, sa, sb, dist = (state[i:i + 1] for i in range(5))
    velocity = jnp.exp(u)
    deficit = (PLATE_RATE - velocity).astype(jnp.bfloat16).astype(jnp.float32)
    k1p = (jnp.exp(-phi) - velocity) / dist
    u2 = u + TIME_STEP * ((inside - sb * k1p) / (sa + DAMPING * velocity))
    state_ref[...] = padded([u, phi, sa, sb, dist, k1p], 8)
    sent = jnp.concatenate([u2, partial_row(deficit, coarse_v_ref)], axis=1)
    out_ref[...] = jnp.broadcast_to(sent[None], out_ref.shape)


def second_kernel(
    groups, state_ref, factor_ref, rows_ref, all_ref, elem_bases_ref, coarse_v_ref, *refs
):
    bases_refs, field_refs, sent_ref = refs[:2], refs[2:8], refs[8]
    members, elem_count = refs[6].shape[1], state_ref.shape[1]
    width = coarse_v_ref.shape[0]
    mine, me = lax.axis_index("leaf"), lax.axis_index("blk")
    sums = [
        jnp.sum(
            all_ref[group * members:(group + 1) * members, 0, elem_count:elem_count + width],
            axis=0, keepdims=True,
        )
        for group in range(groups)
    ]
    weights = coefficients(sums, width // groups)
    own = all_ref[pl.ds(mine * members, members), 0, 0:elem_count]
    coarse = coarse_all(weights, members, bases_refs)
    u2_all = own + factor_ref[...] * coarse
    deficits = (PLATE_RATE - jnp.exp(u2_all)).astype(jnp.bfloat16).astype(jnp.float32)
    inside = inside_rows(deficits, *field_refs)

    state = state_ref[...]
    u, phi, sa, sb, dist, k1p = (state[i:i + 1] for i in range(6))
    here = lax.broadcasted_iota(jnp.int32, u2_all.shape, 0) == me
    u2 = jnp.sum(jnp.where(here, u2_all, 0.0), axis=0, keepdims=True)
    deficit = jnp.sum(jnp.where(here, deficits, 0.0), axis=0, keepdims=True)
    phi2 = phi + TIME_STEP * k1p
    velocity = jnp.exp(u2)
    k2p = (jnp.exp(-phi2) - velocity) / dist
    inverse = 0.5 * TIME_STEP / (sa + DAMPING * velocity)
    u_next = 0.5 * (u + u2) + (inside - sb * k2p) * inverse
    phi_next = phi + 0.5 * TIME_STEP * (k1p + k2p)
    sent = gathered(padded([u_next, inverse, phi_next], 8), rows_ref[...])
    partial = as_lines(partial_row(deficit, coarse_v_ref))
    peer_rows = elem_count // members
    for device in range(groups * members):
        peer = device % members
        sent_ref[device, 0:3, 0:peer_rows] = sent[0:3, peer * peer_rows:(peer + 1) * peer_rows]
        sent_ref[device, 3:3 + partial.shape[0], :] = partial


def finish_kernel(groups, width, got_ref, slot_ref, elem_bases_ref, u_ref, phi_ref):
    elem_count = slot_ref.shape[1]
    members = got_ref.shape[0] // groups
    first = lax.axis_index("leaf") * members
    flat = peer_lanes(got_ref, first, members, 3, elem_count)
    out = gathered(padded([flat[i:i + 1] for i in range(3)], 8), slot_ref[...])
    sums = []
    for group in range(groups):
        total = jnp.sum(got_ref[group * members:(group + 1) * members], axis=0)
        lines = [total[3 + i:4 + i, :] for i in range(pl.cdiv(width, LANES))]
        sums.append(jnp.concatenate(lines, axis=1)[:, 0:width])
    weights = coefficients(sums, width // groups)
    weights = jnp.broadcast_to(weights, (8, weights.shape[1])).astype(jnp.bfloat16)
    coarse = dot(weights, elem_bases_ref[...], NN)[0:1]
    u_ref[...] = out[0:1] + out[1:2] * coarse
    phi_ref[...] = out[2:3]


def call(kernel, outs, *args, scalars=(), far=(), scratch=(), flops=1000, moved=1000):
    spaces = [SMEM if i in scalars else pl.ANY if i in far else VMEM for i in range(len(args))]
    args = [
        pltpu.with_memory_space_constraint(arg, pltpu.HBM) if i in far else arg
        for i, arg in enumerate(args)
    ]
    return pl.pallas_call(
        kernel,
        out_shape=outs,
        in_specs=[pl.BlockSpec(memory_space=space) for space in spaces],
        out_specs=jax.tree.map(lambda _: pl.BlockSpec(memory_space=VMEM), outs),
        scratch_shapes=list(scratch),
        cost_estimate=pl.CostEstimate(flops=flops, bytes_accessed=moved, transcendentals=0),
        compiler_params=pltpu.CompilerParams(vmem_limit_bytes=32 * 1024 * 1024),
    )(*args)


def shape(*dims, dtype=jnp.float32):
    return jax.ShapeDtypeStruct(dims, dtype)


def body(
    ln_rate,
    log_state,
    sigma,
    fric_a,
    fric_b,
    slip_dist,
    leaf_of_elem,
    near_blocks,
    near_col,
    near_count,
    far_u,
    far_v,
    far_col,
    far_rank,
    coarse_u,
    coarse_v,
):
    members = lax.axis_size("blk")
    elems = ln_rate.shape[0]
    leaf_size = near_blocks.shape[1]
    groups, rank = coarse_v.shape[0], coarse_v.shape[1]
    devices = groups * members
    width = groups * rank
    lines = pl.cdiv(width, LANES)
    sent_rows = 1 << (2 + lines).bit_length()
    integer = jnp.int32

    def swap(value, axes):
        return lax.all_to_all(value, axes, split_axis=0, concat_axis=0, tiled=True)

    def partner(value, bit):
        return lax.ppermute(value, "blk", [(i, i ^ (1 << bit)) for i in range(members)])

    elem_args = [
        value.reshape(1, elems)
        for value in (leaf_of_elem, ln_rate, log_state, sigma, fric_a, fric_b, slip_dist)
    ]
    scalar_args = [near_col, far_col, far_rank]
    weights = [
        near_blocks, far_u.reshape(-1, leaf_size), far_v.reshape(-1, leaf_size),
        coarse_v.reshape(width, elems),
    ]
    far_rows = weights[1].shape[0]
    bases = coarse_u.reshape(width, elems)
    sent, slot, elem_row, held = call(
        functools.partial(sort_kernel, members),
        (
            shape(members, -(-(3 * (elems // LANES) + 4) // 8) * 8, LANES),
            shape(1, elems, dtype=integer),
            shape(1, elems, dtype=integer),
            shape(width, elems, dtype=jnp.bfloat16),
        ),
        *elem_args, bases, far=range(8),
        scratch=[VMEM(value.shape, value.dtype) for value in elem_args]
        + [pltpu.SemaphoreType.DMA((8,))],
    )
    steps = step_bits(members)
    early = bases = call(
        functools.partial(stack_foreign_kernel, groups, rank),
        shape(2 * (width - rank), elems, dtype=jnp.bfloat16),
        held, partner(bases, steps[0]), slot, flops=1 << 34, moved=1 << 26,
    )
    near_mask, far_mask, near, far_u, far_v, coarse_v = call(
        load_kernel,
        (
            shape(near_blocks.shape[0], members, leaf_size),
            shape(members, far_rows),
            *[shape(*value.shape, dtype=jnp.bfloat16) for value in weights],
        ),
        early, *scalar_args, *weights, far=range(1, 8),
        scratch=[SMEM(value.shape, value.dtype) for value in scalar_args]
        + [pltpu.SemaphoreType.DMA((7,))],
        flops=1 << 30, moved=1 << 22,
    )
    fields = near_count, near, far_u, far_v, near_mask, far_mask
    state, factor, rows, out = call(
        place_kernel,
        (
            shape(8, elems),
            shape(members, elems),
            shape(1, elems, dtype=integer),
            shape(devices, 1, elems + lines * LANES),
        ),
        swap(sent, "blk"), coarse_v, *fields, scalars=(2,),
        scratch=[VMEM((2, members * (elems // LANES), LANES), jnp.float32)],
        flops=1 << 33, moved=1 << 25,
    )
    for bit in steps[1:-1]:
        bases = call(
            stack_kernel, shape(2 * bases.shape[0], elems, dtype=jnp.bfloat16),
            bases, partner(bases, bit), rows, flops=1 << 34, moved=1 << 26,
        )
    bases = bases, partner(bases, steps[-1])
    elem_bases = call(
        functools.partial(element_kernel, members), shape(width - rank, elems, dtype=jnp.bfloat16),
        *bases, slot, elem_row, flops=1 << 34, moved=1 << 26,
    )
    sent = call(
        functools.partial(second_kernel, groups), shape(devices, sent_rows, LANES),
        state, factor, rows, swap(out, ("leaf", "blk")), elem_bases, coarse_v, *bases, *fields, scalars=(8,),
    )
    u, phi = call(
        functools.partial(finish_kernel, groups, width), (shape(1, elems), shape(1, elems)),
        swap(sent, ("leaf", "blk")), slot, elem_bases,
    )
    return u.reshape(elems), phi.reshape(elems)


def solution(mesh):
    each = P(("leaf", "blk"))
    blocks = P(("leaf", "blk"), None, None)
    last = P(None, None, ("leaf", "blk"))
    in_specs = (each,) * 7 + (blocks, each, each, blocks, blocks, each, each, last, last)
    return jax.shard_map(body, mesh=mesh, in_specs=in_specs, out_specs=(each, each), check_vma=False)
```

```python
import functools

import jax
import jax.numpy as jnp
from jax import lax
from jax.experimental import pallas as pl
from jax.experimental.pallas import tpu as pltpu
from jax.sharding import PartitionSpec as P

DAMPING = 0.5
PLATE_RATE = 1.0
TIME_STEP = 0.2

NN = (((1,), (0,)), ((), ()))
NT = (((1,), (1,)), ((), ()))
VMEM = pltpu.VMEM
SMEM = pltpu.SMEM

LANES = 128
HALF = 64


def dot(left, right, dims):
    return lax.dot_general(left, right, dims, preferred_element_type=jnp.float32)


def low_matrix(index_row):
    rows = lax.broadcasted_iota(jnp.int32, (LANES, index_row.shape[1]), 0)
    rows = rows.astype(jnp.float32).astype(jnp.bfloat16)
    low = (index_row & (LANES - 1)).astype(jnp.float32).astype(jnp.bfloat16)
    one = jnp.ones((), jnp.bfloat16)
    return jnp.where(rows == low, one, jnp.zeros_like(one))


def three_parts(values):
    high = values.astype(jnp.bfloat16).astype(jnp.float32)
    rest = values - high
    middle = rest.astype(jnp.bfloat16).astype(jnp.float32)
    return jnp.concatenate([high, middle, rest - middle], axis=0)


def joined(parts):
    count = parts.shape[0] // 3
    return parts[0:count] + parts[count:2 * count] + parts[2 * count:]


def scattered(values, index_row):
    parts = three_parts(values)
    count = parts.shape[0]
    high = index_row // LANES
    pieces = values.shape[1] // LANES
    left = jnp.concatenate([jnp.where(high == piece, parts, 0.0) for piece in range(pieces)], axis=0)
    moved = dot(left.astype(jnp.bfloat16), low_matrix(index_row), NT)
    return jnp.concatenate(
        [joined(moved[piece * count:(piece + 1) * count]) for piece in range(pieces)], axis=1
    )


def gathered(values, index_row):
    parts = three_parts(values)
    count = parts.shape[0]
    high = index_row // LANES
    pieces = values.shape[1] // LANES
    left = jnp.concatenate(
        [parts[:, piece * LANES:(piece + 1) * LANES] for piece in range(pieces)], axis=0
    )
    moved = dot(left.astype(jnp.bfloat16), low_matrix(index_row), NN)
    total = jnp.zeros((count, index_row.shape[1]), jnp.float32)
    for piece in range(pieces):
        total = jnp.where(high == piece, moved[piece * count:(piece + 1) * count], total)
    return joined(total)


def padded(rows, count):
    missing = count - len(rows)
    if missing:
        rows = rows + [jnp.zeros((missing, rows[0].shape[1]), jnp.float32)]
    return jnp.concatenate(rows, axis=0)


def as_lines(row):
    return jnp.concatenate(
        [row[:, i * LANES:(i + 1) * LANES] for i in range(row.shape[1] // LANES)], axis=0
    )


def peer_lanes(ref, first, members, rows, elem_count):
    width = elem_count // members
    return jnp.concatenate([ref[first + peer, 0:rows, 0:width] for peer in range(members)], axis=1)


def start_copies(sources, targets, sems):
    copies = [
        pltpu.make_async_copy(source, target, sems.at[i])
        for i, (source, target) in enumerate(zip(sources, targets))
    ]
    for copy in copies:
        copy.start()
    return copies


def sort_kernel(members, *refs):
    elem_refs, bases_ref, sent_ref, slot_ref, elem_row_ref, bases_out = refs[:7], *refs[7:12]
    elem_bufs, sems = refs[12:19], refs[19]
    copies = start_copies([*elem_refs, bases_ref], [*elem_bufs, bases_out], sems)
    mine = lax.axis_index("leaf")
    elem_count = elem_bufs[0].shape[1]
    peer_rows = elem_count // members
    pieces = elem_count // LANES
    before = lax.broadcasted_iota(jnp.int32, (LANES, LANES), 0)
    after = lax.broadcasted_iota(jnp.int32, (LANES, LANES), 1)
    triangle = jnp.where(before < after, 1.0, 0.0).astype(jnp.bfloat16)
    copies[0].wait()
    local = elem_bufs[0][...] - mine * (members * elem_count)
    target = local // elem_count
    target_row = local - target * elem_count
    peers = lax.broadcasted_iota(jnp.int32, (members, elem_count), 0)
    onehot = jnp.where(peers == target, 1.0, 0.0)
    lines = [onehot[:, i * LANES:(i + 1) * LANES] for i in range(pieces)]
    inside = dot(jnp.concatenate(lines, axis=0).astype(jnp.bfloat16), triangle, NN)
    passed = jnp.zeros((members, 1), jnp.float32)
    ranks = []
    for i, line in enumerate(lines):
        earlier = inside[i * members:(i + 1) * members] + passed
        ranks.append(jnp.sum(earlier * line, axis=0, keepdims=True))
        passed = passed + jnp.sum(line, axis=1, keepdims=True)
    slot = target * peer_rows + jnp.concatenate(ranks, axis=1).astype(jnp.int32)
    slot_ref[...] = slot
    elem_row_ref[...] = target_row
    for copy in copies[1:7]:
        copy.wait()
    u, phi, sigma, fric_a, fric_b, dist = (buf[...] for buf in elem_bufs[1:])
    velocity = jnp.exp(u)
    deficit = (PLATE_RATE - velocity).astype(jnp.bfloat16).astype(jnp.float32)
    sa = sigma * fric_a
    factor = TIME_STEP / (sa + DAMPING * velocity)
    rows = [u, phi, sa, sigma * fric_b, dist, target_row.astype(jnp.float32), deficit, factor]
    values = scattered(padded(rows, 8), slot)
    everyone = jnp.concatenate([as_lines(values[i:i + 1]) for i in (6, 5, 7)], axis=0)
    for peer in range(members):
        sent_ref[peer, 0:3 * pieces, :] = everyone
        part = values[0:6, peer * peer_rows:(peer + 1) * peer_rows]
        sent_ref[peer, 3 * pieces:3 * pieces + 4, 0:peer_rows] = part[0:4]
        sent_ref[peer, 3 * pieces:3 * pieces + 2, HALF:HALF + peer_rows] = part[4:6]
    copies[7].wait()


def load_kernel(early_ref, *refs):
    scalar_refs, weight_refs, near_mask_ref, far_mask_ref = refs[:3], refs[3:7], refs[7], refs[8]
    weight_outs, scalar_bufs, sems = refs[9:13], refs[13:16], refs[16]
    sources, targets = [*scalar_refs, *weight_refs[:3]], [*scalar_bufs, *weight_outs[:3]]
    coarse_v_ref, coarse_v_out = weight_refs[3], weight_outs[3]
    groups, rank = coarse_v_ref.shape[0], coarse_v_ref.shape[1]
    for shift in range(groups):
        place = (shift - 1) % groups * rank
        sources.append(coarse_v_ref.at[lax.axis_index("leaf") ^ shift])
        targets.append(coarse_v_out.at[pl.ds(place, rank), :])
    copies = start_copies(sources, targets, sems)
    for copy in copies[:3]:
        copy.wait()
    near_col, far_col, far_rank = scalar_bufs
    far_slots = far_col.shape[0]
    far_width = far_mask_ref.shape[1] // far_slots
    block = lax.broadcasted_iota(jnp.int32, near_mask_ref.shape[1:], 0)
    for number in range(near_mask_ref.shape[0]):
        near_mask_ref[number] = jnp.where(block == near_col[number], 1.0, 0.0)
    block = lax.broadcasted_iota(jnp.int32, far_mask_ref.shape, 0)
    lane = lax.broadcasted_iota(jnp.int32, far_mask_ref.shape, 1)
    column = jnp.full(far_mask_ref.shape, -1, jnp.int32)
    for number in range(far_slots):
        low = number * far_width
        kept = (lane >= low) & (lane < low + far_rank[number])
        column = jnp.where(kept, far_col[number], column)
    far_mask_ref[...] = jnp.where(block == column, 1.0, 0.0)
    for copy in copies[3:]:
        copy.wait()


def partial_row(deficit, coarse_v_ref):
    wide = jnp.broadcast_to(deficit, (8, deficit.shape[1])).astype(jnp.bfloat16)
    partial = dot(wide, coarse_v_ref[...], NT)[0:1]
    rest = -partial.shape[1] % LANES
    if rest:
        partial = jnp.concatenate([partial, jnp.zeros((1, rest), jnp.float32)], axis=1)
    return partial


def inside_rows(deficits, near_count, near_ref, far_u_ref, far_v_ref, near_mask_ref, far_mask_ref):
    total = jnp.zeros(deficits.shape, jnp.float32)
    for slot in range(near_ref.shape[0]):
        live = jnp.where(slot < near_count[0], 1.0, 0.0)
        source = (deficits * (near_mask_ref[slot] * live)).astype(jnp.bfloat16)
        total = total + dot(source, near_ref[slot], NT)
    project = dot(deficits.astype(jnp.bfloat16), far_v_ref[...], NT) * far_mask_ref[...]
    project = jnp.sum(project, axis=0, keepdims=True)
    project = jnp.broadcast_to(project, (8, project.shape[1])).astype(jnp.bfloat16)
    far = dot(project, far_u_ref[...], NN)
    return jnp.sum(total, axis=0, keepdims=True) + far[0:1]


def coefficients(parts_of, groups, rank):
    mine = lax.axis_index("leaf")
    lane = lax.broadcasted_iota(jnp.int32, (1, groups * rank), 1) // rank
    weights = jnp.zeros(lane.shape, jnp.float32)
    for shift in range(1, groups):
        total = jnp.sum(parts_of(mine ^ shift), axis=0, keepdims=True)
        weights = jnp.where(lane == shift - 1, total, weights)
    return weights[:, 0:(groups - 1) * rank]


def coarse_all(weights, members, bases_refs):
    row = lax.broadcasted_iota(jnp.int32, (members, weights.shape[1]), 0) ^ lax.axis_index("blk")
    total = jnp.zeros((members, bases_refs[0].shape[1]), jnp.float32)
    for number, ref in enumerate(bases_refs):
        left = []
        for place in range(members // 2):
            source = relative_member(place, number, members)
            left.append(jnp.where(row == source, weights, 0.0))
        left = jnp.concatenate(left, axis=1).astype(jnp.bfloat16)
        total = total + dot(left, ref[...], NN)
    return total


def stack_kernel(held_ref, came_ref, *refs):
    out_ref = refs[-1]
    count = held_ref.shape[0]
    out_ref[0:count, :] = held_ref[...]
    out_ref[count:2 * count, :] = came_ref[...]


def stack_foreign_kernel(groups, rank, held_ref, came_ref, *refs):
    out_ref = refs[-1]
    mine = lax.axis_index("leaf")
    place = 0
    for ref in (held_ref, came_ref):
        for shift in range(1, groups):
            out_ref[place:place + rank, :] = ref[pl.ds((mine ^ shift) * rank, rank), :]
            place += rank


def step_bits(members):
    bits = list(range(members.bit_length() - 2, -1, -1))
    return bits[:-2] + [bits[-1], bits[-2]]


def relative_member(place, number, members):
    order = step_bits(members)
    found = number << order[-1]
    for step, bit in enumerate(order[:-1]):
        found |= (place >> step & 1) << bit
    return found


def element_kernel(members, held_ref, came_ref, slot_ref, elem_row_ref, out_ref):
    slot, row = slot_ref[...], elem_row_ref[...]
    elem_count = row.shape[1]
    kept = out_ref.shape[0]
    pieces = elem_count // LANES
    owner = (slot // (elem_count // members)) ^ lax.axis_index("blk")
    low, high = low_matrix(row), row // LANES
    total = jnp.zeros(out_ref.shape, jnp.float32)
    for number, ref in enumerate((held_ref, came_ref)):
        for place in range(members // 2):
            part = ref[place * kept:(place + 1) * kept, :]
            left = jnp.concatenate(
                [part[:, piece * LANES:(piece + 1) * LANES] for piece in range(pieces)], axis=0
            )
            found = dot(left, low, NN)
            ours = owner == relative_member(place, number, members)
            for piece in range(pieces):
                here = ours & (high == piece)
                total = jnp.where(here, found[piece * kept:(piece + 1) * kept], total)
    out_ref[...] = total.astype(jnp.bfloat16)


def place_kernel(got_ref, coarse_v_ref, *refs):
    field_refs, state_ref, factor_ref, rows_ref, out_ref, lines_ref = refs[:6], *refs[6:]
    members = got_ref.shape[0]
    elem_count = state_ref.shape[1]
    pieces = elem_count // LANES
    peer_rows = elem_count // members
    count = LANES // peer_rows * pieces
    line_row = lax.broadcasted_iota(jnp.int32, (count, LANES), 0)
    lane_block = lax.broadcasted_iota(jnp.int32, (count, LANES), 1) // peer_rows
    own_lane = line_row // pieces == lane_block
    for line in range(pieces):
        rows = got_ref[:, pieces + line, :].astype(jnp.int32)
        parts = [got_ref[:, line, :]]
        split = three_parts(got_ref[:, 2 * pieces + line, :])
        parts += [split[i * members:(i + 1) * members] for i in range(3)]
        left, right = [], []
        for peer in range(members):
            row = rows[peer:peer + 1]
            kept = own_lane & (line_row % pieces == row // LANES)
            left.append(
                jnp.concatenate([jnp.where(kept, part[peer:peer + 1], 0.0) for part in parts], axis=0)
            )
            right.append(low_matrix(row))
        left = jnp.concatenate(left, axis=1).astype(jnp.bfloat16)
        placed = dot(left, jnp.concatenate(right, axis=1), NT)
        lines_ref[0, line * count:(line + 1) * count, :] = placed[0:count]
        lines_ref[1, line * count:(line + 1) * count, :] = joined(placed[count:])

    def blocks(number):
        return jnp.concatenate(
            [lines_ref[number, pl.ds(piece, members, stride=pieces), :] for piece in range(pieces)],
            axis=1,
        )

    factor_ref[...] = blocks(1)
    inside = inside_rows(blocks(0), *field_refs)

    first = 3 * pieces
    flat = jnp.concatenate(
        [got_ref[peer, first:first + 4, 0:peer_rows] for peer in range(members)], axis=1
    )
    rest = jnp.concatenate(
        [got_ref[peer, first:first + 2, HALF:HALF + peer_rows] for peer in range(members)], axis=1
    )
    rows = rest[1:2].astype(jnp.int32)
    rows_ref[...] = rows
    fields = [flat[i:i + 1] for i in range(4)] + [rest[0:1]]
    state = scattered(padded(fields, 8), rows)
    u, phi, sa, sb, dist = (state[i:i + 1] for i in range(5))
    velocity = jnp.exp(u)
    deficit = (PLATE_RATE - velocity).astype(jnp.bfloat16).astype(jnp.float32)
    k1p = (jnp.exp(-phi) - velocity) / dist
    u2 = u + TIME_STEP * ((inside - sb * k1p) / (sa + DAMPING * velocity))
    state_ref[...] = padded([u, phi, sa, sb, dist, k1p], 8)
    sent = jnp.concatenate([u2, partial_row(deficit, coarse_v_ref)], axis=1)
    out_ref[...] = jnp.broadcast_to(sent[None], out_ref.shape)


def second_kernel(
    groups, state_ref, factor_ref, rows_ref, all_ref, elem_bases_ref, coarse_v_ref, *refs
):
    bases_refs, field_refs, sent_ref = refs[:2], refs[2:8], refs[8]
    members, elem_count = refs[6].shape[1], state_ref.shape[1]
    width = coarse_v_ref.shape[0]
    mine, me = lax.axis_index("leaf"), lax.axis_index("blk")

    def parts_of(group):
        return all_ref[pl.ds(group * members, members), 0, elem_count:elem_count + width]

    weights = coefficients(parts_of, groups, width // groups)
    own = all_ref[pl.ds(mine * members, members), 0, 0:elem_count]
    coarse = coarse_all(weights, members, bases_refs)
    u2_all = own + factor_ref[...] * coarse
    deficits = (PLATE_RATE - jnp.exp(u2_all)).astype(jnp.bfloat16).astype(jnp.float32)
    inside = inside_rows(deficits, *field_refs)

    state = state_ref[...]
    u, phi, sa, sb, dist, k1p = (state[i:i + 1] for i in range(6))
    here = lax.broadcasted_iota(jnp.int32, u2_all.shape, 0) == me
    u2 = jnp.sum(jnp.where(here, u2_all, 0.0), axis=0, keepdims=True)
    deficit = jnp.sum(jnp.where(here, deficits, 0.0), axis=0, keepdims=True)
    phi2 = phi + TIME_STEP * k1p
    velocity = jnp.exp(u2)
    k2p = (jnp.exp(-phi2) - velocity) / dist
    inverse = 0.5 * TIME_STEP / (sa + DAMPING * velocity)
    u_next = 0.5 * (u + u2) + (inside - sb * k2p) * inverse
    phi_next = phi + 0.5 * TIME_STEP * (k1p + k2p)
    sent = gathered(padded([u_next, inverse, phi_next], 8), rows_ref[...])
    partial = as_lines(partial_row(deficit, coarse_v_ref))
    peer_rows = elem_count // members
    for device in range(groups * members):
        peer = device % members
        sent_ref[device, 0:3, 0:peer_rows] = sent[0:3, peer * peer_rows:(peer + 1) * peer_rows]
        sent_ref[device, 3:3 + partial.shape[0], :] = partial


def finish_kernel(groups, width, got_ref, slot_ref, elem_bases_ref, u_ref, phi_ref):
    elem_count = slot_ref.shape[1]
    members = got_ref.shape[0] // groups
    first = lax.axis_index("leaf") * members
    flat = peer_lanes(got_ref, first, members, 3, elem_count)
    out = gathered(padded([flat[i:i + 1] for i in range(3)], 8), slot_ref[...])

    def parts_of(group):
        sent = pl.ds(group * members, members)
        lines = [got_ref[sent, 3 + i, :] for i in range(pl.cdiv(width, LANES))]
        return jnp.concatenate(lines, axis=1)[:, 0:width]

    weights = coefficients(parts_of, groups, width // groups)
    weights = jnp.broadcast_to(weights, (8, weights.shape[1])).astype(jnp.bfloat16)
    coarse = dot(weights, elem_bases_ref[...], NN)[0:1]
    u_ref[...] = out[0:1] + out[1:2] * coarse
    phi_ref[...] = out[2:3]


def call(kernel, outs, *args, scalars=(), far=(), scratch=(), flops=1000, moved=1000):
    spaces = [SMEM if i in scalars else pl.ANY if i in far else VMEM for i in range(len(args))]
    args = [
        pltpu.with_memory_space_constraint(arg, pltpu.HBM) if i in far else arg
        for i, arg in enumerate(args)
    ]
    return pl.pallas_call(
        kernel,
        out_shape=outs,
        in_specs=[pl.BlockSpec(memory_space=space) for space in spaces],
        out_specs=jax.tree.map(lambda _: pl.BlockSpec(memory_space=VMEM), outs),
        scratch_shapes=list(scratch),
        cost_estimate=pl.CostEstimate(flops=flops, bytes_accessed=moved, transcendentals=0),
        compiler_params=pltpu.CompilerParams(vmem_limit_bytes=32 * 1024 * 1024),
    )(*args)


def shape(*dims, dtype=jnp.float32):
    return jax.ShapeDtypeStruct(dims, dtype)


def body(
    ln_rate,
    log_state,
    sigma,
    fric_a,
    fric_b,
    slip_dist,
    leaf_of_elem,
    near_blocks,
    near_col,
    near_count,
    far_u,
    far_v,
    far_col,
    far_rank,
    coarse_u,
    coarse_v,
):
    members = lax.axis_size("blk")
    elems = ln_rate.shape[0]
    leaf_size = near_blocks.shape[1]
    groups, rank = coarse_v.shape[0], coarse_v.shape[1]
    devices = groups * members
    width = groups * rank
    lines = pl.cdiv(width, LANES)
    sent_rows = 1 << (2 + lines).bit_length()
    integer = jnp.int32

    def swap(value, axes):
        return lax.all_to_all(value, axes, split_axis=0, concat_axis=0, tiled=True)

    def partner(value, bit):
        return lax.ppermute(value, "blk", [(i, i ^ (1 << bit)) for i in range(members)])

    elem_args = [
        value.reshape(1, elems)
        for value in (leaf_of_elem, ln_rate, log_state, sigma, fric_a, fric_b, slip_dist)
    ]
    scalar_args = [near_col, far_col, far_rank]
    weights = [
        near_blocks, far_u.reshape(-1, leaf_size), far_v.reshape(-1, leaf_size), coarse_v
    ]
    far_rows = weights[1].shape[0]
    bases = coarse_u.reshape(width, elems)
    sent, slot, elem_row, held = call(
        functools.partial(sort_kernel, members),
        (
            shape(members, -(-(3 * (elems // LANES) + 4) // 8) * 8, LANES),
            shape(1, elems, dtype=integer),
            shape(1, elems, dtype=integer),
            shape(width, elems, dtype=jnp.bfloat16),
        ),
        *elem_args, bases, far=range(8),
        scratch=[VMEM(value.shape, value.dtype) for value in elem_args]
        + [pltpu.SemaphoreType.DMA((8,))],
    )
    steps = step_bits(members)
    early = bases = call(
        functools.partial(stack_foreign_kernel, groups, rank),
        shape(2 * (width - rank), elems, dtype=jnp.bfloat16),
        held, partner(bases, steps[0]), slot, flops=1 << 34, moved=1 << 26,
    )
    near_mask, far_mask, near, far_u, far_v, coarse_v = call(
        load_kernel,
        (
            shape(near_blocks.shape[0], members, leaf_size),
            shape(members, far_rows),
            *[shape(*value.shape, dtype=jnp.bfloat16) for value in weights[:3]],
            shape(width, elems, dtype=jnp.bfloat16),
        ),
        early, *scalar_args, *weights, far=range(1, 8),
        scratch=[SMEM(value.shape, value.dtype) for value in scalar_args]
        + [pltpu.SemaphoreType.DMA((6 + groups,))],
        flops=1 << 30, moved=1 << 22,
    )
    fields = near_count, near, far_u, far_v, near_mask, far_mask
    state, factor, rows, out = call(
        place_kernel,
        (
            shape(8, elems),
            shape(members, elems),
            shape(1, elems, dtype=integer),
            shape(devices, 1, elems + lines * LANES),
        ),
        swap(sent, "blk"), coarse_v, *fields, scalars=(2,),
        scratch=[VMEM((2, members * (elems // LANES), LANES), jnp.float32)],
        flops=1 << 33, moved=1 << 25,
    )
    for bit in steps[1:-1]:
        bases = call(
            stack_kernel, shape(2 * bases.shape[0], elems, dtype=jnp.bfloat16),
            bases, partner(bases, bit), rows, flops=1 << 34, moved=1 << 26,
        )
    bases = bases, partner(bases, steps[-1])
    elem_bases = call(
        functools.partial(element_kernel, members), shape(width - rank, elems, dtype=jnp.bfloat16),
        *bases, slot, elem_row, flops=1 << 34, moved=1 << 26,
    )
    sent = call(
        functools.partial(second_kernel, groups), shape(devices, sent_rows, LANES),
        state, factor, rows, swap(out, ("leaf", "blk")), elem_bases, coarse_v, *bases, *fields, scalars=(8,),
    )
    u, phi = call(
        functools.partial(finish_kernel, groups, width), (shape(1, elems), shape(1, elems)),
        swap(sent, ("leaf", "blk")), slot, elem_bases,
    )
    return u.reshape(elems), phi.reshape(elems)


def solution(mesh):
    each = P(("leaf", "blk"))
    blocks = P(("leaf", "blk"), None, None)
    last = P(None, None, ("leaf", "blk"))
    in_specs = (each,) * 7 + (blocks, each, each, blocks, blocks, each, each, last, last)
    return jax.shard_map(body, mesh=mesh, in_specs=in_specs, out_specs=(each, each), check_vma=False)
```

```python
import functools

import jax
import jax.numpy as jnp
from jax import lax
from jax.experimental import pallas as pl
from jax.experimental.pallas import tpu as pltpu
from jax.sharding import PartitionSpec as P

DAMPING = 0.5
PLATE_RATE = 1.0
TIME_STEP = 0.2

NN = (((1,), (0,)), ((), ()))
NT = (((1,), (1,)), ((), ()))
VMEM = pltpu.VMEM
SMEM = pltpu.SMEM

LANES = 128
HALF = 64


def dot(left, right, dims):
    return lax.dot_general(left, right, dims, preferred_element_type=jnp.float32)


def low_matrix(index_row):
    rows = lax.broadcasted_iota(jnp.int32, (LANES, index_row.shape[1]), 0)
    rows = rows.astype(jnp.float32).astype(jnp.bfloat16)
    low = (index_row & (LANES - 1)).astype(jnp.float32).astype(jnp.bfloat16)
    one = jnp.ones((), jnp.bfloat16)
    return jnp.where(rows == low, one, jnp.zeros_like(one))


def three_parts(values):
    high = values.astype(jnp.bfloat16).astype(jnp.float32)
    rest = values - high
    middle = rest.astype(jnp.bfloat16).astype(jnp.float32)
    return jnp.concatenate([high, middle, rest - middle], axis=0)


def joined(parts):
    count = parts.shape[0] // 3
    return parts[0:count] + parts[count:2 * count] + parts[2 * count:]


def scattered(values, index_row):
    parts = three_parts(values)
    count = parts.shape[0]
    high = index_row // LANES
    pieces = values.shape[1] // LANES
    left = jnp.concatenate([jnp.where(high == piece, parts, 0.0) for piece in range(pieces)], axis=0)
    moved = dot(left.astype(jnp.bfloat16), low_matrix(index_row), NT)
    return jnp.concatenate(
        [joined(moved[piece * count:(piece + 1) * count]) for piece in range(pieces)], axis=1
    )


def gathered(values, index_row):
    parts = three_parts(values)
    count = parts.shape[0]
    high = index_row // LANES
    pieces = values.shape[1] // LANES
    left = jnp.concatenate(
        [parts[:, piece * LANES:(piece + 1) * LANES] for piece in range(pieces)], axis=0
    )
    moved = dot(left.astype(jnp.bfloat16), low_matrix(index_row), NN)
    total = jnp.zeros((count, index_row.shape[1]), jnp.float32)
    for piece in range(pieces):
        total = jnp.where(high == piece, moved[piece * count:(piece + 1) * count], total)
    return joined(total)


def padded(rows, count):
    missing = count - len(rows)
    if missing:
        rows = rows + [jnp.zeros((missing, rows[0].shape[1]), jnp.float32)]
    return jnp.concatenate(rows, axis=0)


def as_lines(row):
    return jnp.concatenate(
        [row[:, i * LANES:(i + 1) * LANES] for i in range(row.shape[1] // LANES)], axis=0
    )


def peer_lanes(ref, first, members, rows, elem_count):
    width = elem_count // members
    return jnp.concatenate([ref[first + peer, 0:rows, 0:width] for peer in range(members)], axis=1)


def start_copies(sources, targets, sems):
    copies = [
        pltpu.make_async_copy(source, target, sems.at[i])
        for i, (source, target) in enumerate(zip(sources, targets))
    ]
    for copy in copies:
        copy.start()
    return copies


def sort_kernel(members, *refs):
    elem_refs, bases_ref, sent_ref, slot_ref, elem_row_ref, bases_out = refs[:7], *refs[7:12]
    elem_bufs, sems = refs[12:19], refs[19]
    copies = start_copies([*elem_refs, bases_ref], [*elem_bufs, bases_out], sems)
    mine = lax.axis_index("leaf")
    elem_count = elem_bufs[0].shape[1]
    peer_rows = elem_count // members
    pieces = elem_count // LANES
    before = lax.broadcasted_iota(jnp.int32, (LANES, LANES), 0)
    after = lax.broadcasted_iota(jnp.int32, (LANES, LANES), 1)
    triangle = jnp.where(before < after, 1.0, 0.0).astype(jnp.bfloat16)
    copies[0].wait()
    local = elem_bufs[0][...] - mine * (members * elem_count)
    target = local // elem_count
    target_row = local - target * elem_count
    peers = lax.broadcasted_iota(jnp.int32, (members, elem_count), 0)
    onehot = jnp.where(peers == target, 1.0, 0.0)
    lines = [onehot[:, i * LANES:(i + 1) * LANES] for i in range(pieces)]
    inside = dot(jnp.concatenate(lines, axis=0).astype(jnp.bfloat16), triangle, NN)
    passed = jnp.zeros((members, 1), jnp.float32)
    ranks = []
    for i, line in enumerate(lines):
        earlier = inside[i * members:(i + 1) * members] + passed
        ranks.append(jnp.sum(earlier * line, axis=0, keepdims=True))
        passed = passed + jnp.sum(line, axis=1, keepdims=True)
    slot = target * peer_rows + jnp.concatenate(ranks, axis=1).astype(jnp.int32)
    slot_ref[...] = slot
    elem_row_ref[...] = target_row
    for copy in copies[1:7]:
        copy.wait()
    u, phi, sigma, fric_a, fric_b, dist = (buf[...] for buf in elem_bufs[1:])
    velocity = jnp.exp(u)
    deficit = (PLATE_RATE - velocity).astype(jnp.bfloat16).astype(jnp.float32)
    sa = sigma * fric_a
    factor = TIME_STEP / (sa + DAMPING * velocity)
    rows = [u, phi, sa, sigma * fric_b, dist, target_row.astype(jnp.float32), deficit, factor]
    values = scattered(padded(rows, 8), slot)
    everyone = jnp.concatenate([as_lines(values[i:i + 1]) for i in (6, 5, 7)], axis=0)
    for peer in range(members):
        sent_ref[peer, 0:3 * pieces, :] = everyone
        part = values[0:6, peer * peer_rows:(peer + 1) * peer_rows]
        sent_ref[peer, 3 * pieces:3 * pieces + 4, 0:peer_rows] = part[0:4]
        sent_ref[peer, 3 * pieces:3 * pieces + 2, HALF:HALF + peer_rows] = part[4:6]
    copies[7].wait()


def load_kernel(early_ref, *refs):
    scalar_refs, weight_refs, near_mask_ref, far_mask_ref = refs[:3], refs[3:7], refs[7], refs[8]
    weight_outs, scalar_bufs, sems = refs[9:13], refs[13:16], refs[16]
    sources, targets = [*scalar_refs, *weight_refs[:3]], [*scalar_bufs, *weight_outs[:3]]
    coarse_v_ref, coarse_v_out = weight_refs[3], weight_outs[3]
    groups, rank = coarse_v_ref.shape[0], coarse_v_ref.shape[1]
    for shift in range(groups):
        place = (shift - 1) % groups * rank
        sources.append(coarse_v_ref.at[lax.axis_index("leaf") ^ shift])
        targets.append(coarse_v_out.at[pl.ds(place, rank), :])
    copies = start_copies(sources, targets, sems)
    for copy in copies[:3]:
        copy.wait()
    near_col, far_col, far_rank = scalar_bufs
    far_slots = far_col.shape[0]
    far_width = far_mask_ref.shape[1] // far_slots
    block = lax.broadcasted_iota(jnp.int32, near_mask_ref.shape[1:], 0)
    for number in range(near_mask_ref.shape[0]):
        near_mask_ref[number] = jnp.where(block == near_col[number], 1.0, 0.0)
    block = lax.broadcasted_iota(jnp.int32, far_mask_ref.shape, 0)
    lane = lax.broadcasted_iota(jnp.int32, far_mask_ref.shape, 1)
    column = jnp.full(far_mask_ref.shape, -1, jnp.int32)
    for number in range(far_slots):
        low = number * far_width
        kept = (lane >= low) & (lane < low + far_rank[number])
        column = jnp.where(kept, far_col[number], column)
    far_mask_ref[...] = jnp.where(block == column, 1.0, 0.0)
    for copy in copies[3:]:
        copy.wait()


def partial_row(deficit, coarse_v_ref):
    wide = jnp.broadcast_to(deficit, (8, deficit.shape[1])).astype(jnp.bfloat16)
    partial = dot(wide, coarse_v_ref[...], NT)[0:1]
    rest = -partial.shape[1] % LANES
    if rest:
        partial = jnp.concatenate([partial, jnp.zeros((1, rest), jnp.float32)], axis=1)
    return partial


def inside_rows(deficits, near_count, near_ref, far_u_ref, far_v_ref, near_mask_ref, far_mask_ref):
    total = jnp.zeros(deficits.shape, jnp.float32)
    for slot in range(near_ref.shape[0]):
        live = jnp.where(slot < near_count[0], 1.0, 0.0)
        source = (deficits * (near_mask_ref[slot] * live)).astype(jnp.bfloat16)
        total = total + dot(source, near_ref[slot], NT)
    project = dot(deficits.astype(jnp.bfloat16), far_v_ref[...], NT) * far_mask_ref[...]
    project = jnp.sum(project, axis=0, keepdims=True)
    project = jnp.broadcast_to(project, (8, project.shape[1])).astype(jnp.bfloat16)
    far = dot(project, far_u_ref[...], NN)
    return jnp.sum(total, axis=0, keepdims=True) + far[0:1]


def coefficients(parts_of, groups, rank):
    mine = lax.axis_index("leaf")
    lane = lax.broadcasted_iota(jnp.int32, (1, groups * rank), 1) // rank
    weights = jnp.zeros(lane.shape, jnp.float32)
    for shift in range(1, groups):
        total = jnp.sum(parts_of(mine ^ shift), axis=0, keepdims=True)
        weights = jnp.where(lane == shift - 1, total, weights)
    return weights[:, 0:(groups - 1) * rank]


def coarse_all(weights, members, bases_refs):
    row = lax.broadcasted_iota(jnp.int32, (members, weights.shape[1]), 0) ^ lax.axis_index("blk")
    total = jnp.zeros((members, bases_refs[0].shape[1]), jnp.float32)
    for number, ref in enumerate(bases_refs):
        left = []
        for place in range(members // 2):
            source = relative_member(place, number, members)
            left.append(jnp.where(row == source, weights, 0.0))
        left = jnp.concatenate(left, axis=1).astype(jnp.bfloat16)
        total = total + dot(left, ref[...], NN)
    return total


def stack_kernel(held_ref, came_ref, *refs):
    out_ref = refs[-1]
    count = held_ref.shape[0]
    out_ref[0:count, :] = held_ref[...]
    out_ref[count:2 * count, :] = came_ref[...]


def stack_foreign_kernel(groups, rank, held_ref, came_ref, *refs):
    out_ref = refs[-1]
    mine = lax.axis_index("leaf")
    place = 0
    for ref in (held_ref, came_ref):
        for shift in range(1, groups):
            out_ref[place:place + rank, :] = ref[pl.ds((mine ^ shift) * rank, rank), :]
            place += rank


def step_bits(members):
    bits = list(range(members.bit_length() - 2, -1, -1))
    return bits[:-2] + [bits[-1], bits[-2]]


def relative_member(place, number, members):
    order = step_bits(members)
    found = number << order[-1]
    for step, bit in enumerate(order[:-1]):
        found |= (place >> step & 1) << bit
    return found


def element_kernel(members, held_ref, came_ref, slot_ref, elem_row_ref, out_ref):
    slot, row = slot_ref[...], elem_row_ref[...]
    elem_count = row.shape[1]
    kept = out_ref.shape[0]
    pieces = elem_count // LANES
    owner = (slot // (elem_count // members)) ^ lax.axis_index("blk")
    low, high = low_matrix(row), row // LANES
    total = jnp.zeros(out_ref.shape, jnp.float32)
    for number, ref in enumerate((held_ref, came_ref)):
        for place in range(members // 2):
            part = ref[place * kept:(place + 1) * kept, :]
            left = jnp.concatenate(
                [part[:, piece * LANES:(piece + 1) * LANES] for piece in range(pieces)], axis=0
            )
            found = dot(left, low, NN)
            ours = owner == relative_member(place, number, members)
            for piece in range(pieces):
                here = ours & (high == piece)
                total = jnp.where(here, found[piece * kept:(piece + 1) * kept], total)
    out_ref[...] = total.astype(jnp.bfloat16)


def place_kernel(got_ref, coarse_v_ref, *refs):
    field_refs, state_ref, factor_ref, rows_ref, out_ref, lines_ref = refs[:6], *refs[6:]
    members = got_ref.shape[0]
    elem_count = state_ref.shape[1]
    pieces = elem_count // LANES
    peer_rows = elem_count // members
    count = LANES // peer_rows * pieces
    line_row = lax.broadcasted_iota(jnp.int32, (count, LANES), 0)
    lane_block = lax.broadcasted_iota(jnp.int32, (count, LANES), 1) // peer_rows
    own_lane = line_row // pieces == lane_block
    for line in range(pieces):
        rows = got_ref[:, pieces + line, :].astype(jnp.int32)
        parts = [got_ref[:, line, :]]
        split = three_parts(got_ref[:, 2 * pieces + line, :])
        parts += [split[i * members:(i + 1) * members] for i in range(3)]
        left, right = [], []
        for peer in range(members):
            row = rows[peer:peer + 1]
            kept = own_lane & (line_row % pieces == row // LANES)
            left.append(
                jnp.concatenate([jnp.where(kept, part[peer:peer + 1], 0.0) for part in parts], axis=0)
            )
            right.append(low_matrix(row))
        left = jnp.concatenate(left, axis=1).astype(jnp.bfloat16)
        placed = dot(left, jnp.concatenate(right, axis=1), NT)
        lines_ref[0, line * count:(line + 1) * count, :] = placed[0:count]
        lines_ref[1, line * count:(line + 1) * count, :] = joined(placed[count:])

    def blocks(number):
        return jnp.concatenate(
            [lines_ref[number, pl.ds(piece, members, stride=pieces), :] for piece in range(pieces)],
            axis=1,
        )

    factor_ref[...] = blocks(1)
    inside = inside_rows(blocks(0), *field_refs)

    first = 3 * pieces
    flat = jnp.concatenate(
        [got_ref[peer, first:first + 4, 0:peer_rows] for peer in range(members)], axis=1
    )
    rest = jnp.concatenate(
        [got_ref[peer, first:first + 2, HALF:HALF + peer_rows] for peer in range(members)], axis=1
    )
    rows = rest[1:2].astype(jnp.int32)
    rows_ref[...] = rows
    fields = [flat[i:i + 1] for i in range(4)] + [rest[0:1]]
    state = scattered(padded(fields, 8), rows)
    u, phi, sa, sb, dist = (state[i:i + 1] for i in range(5))
    velocity = jnp.exp(u)
    deficit = (PLATE_RATE - velocity).astype(jnp.bfloat16).astype(jnp.float32)
    k1p = (jnp.exp(-phi) - velocity) / dist
    u2 = u + TIME_STEP * ((inside - sb * k1p) / (sa + DAMPING * velocity))
    state_ref[...] = padded([u, phi, sa, sb, dist, k1p], 8)
    sent = jnp.concatenate([u2, partial_row(deficit, coarse_v_ref)], axis=1)
    out_ref[...] = jnp.broadcast_to(sent[None], out_ref.shape)


def second_kernel(
    groups, state_ref, factor_ref, rows_ref, all_ref, elem_bases_ref, coarse_v_ref, *refs
):
    bases_refs, field_refs, sent_ref = refs[:2], refs[2:8], refs[8]
    members, elem_count = refs[6].shape[1], state_ref.shape[1]
    width = coarse_v_ref.shape[0]
    mine, me = lax.axis_index("leaf"), lax.axis_index("blk")

    def parts_of(group):
        return all_ref[pl.ds(group * members, members), 0, elem_count:elem_count + width]

    weights = coefficients(parts_of, groups, width // groups)
    own = all_ref[pl.ds(mine * members, members), 0, 0:elem_count]
    coarse = coarse_all(weights, members, bases_refs)
    u2_all = own + factor_ref[...] * coarse
    deficits = (PLATE_RATE - jnp.exp(u2_all)).astype(jnp.bfloat16).astype(jnp.float32)
    inside = inside_rows(deficits, *field_refs)

    state = state_ref[...]
    u, phi, sa, sb, dist, k1p = (state[i:i + 1] for i in range(6))
    here = lax.broadcasted_iota(jnp.int32, u2_all.shape, 0) == me
    u2 = jnp.sum(jnp.where(here, u2_all, 0.0), axis=0, keepdims=True)
    deficit = jnp.sum(jnp.where(here, deficits, 0.0), axis=0, keepdims=True)
    phi2 = phi + TIME_STEP * k1p
    velocity = jnp.exp(u2)
    k2p = (jnp.exp(-phi2) - velocity) / dist
    inverse = 0.5 * TIME_STEP / (sa + DAMPING * velocity)
    u_next = 0.5 * (u + u2) + (inside - sb * k2p) * inverse
    phi_next = phi + 0.5 * TIME_STEP * (k1p + k2p)
    sent = gathered(padded([u_next, inverse, phi_next], 8), rows_ref[...])
    partial = as_lines(partial_row(deficit, coarse_v_ref))
    peer_rows = elem_count // members
    for device in range(groups * members):
        peer = device % members
        sent_ref[device, 0:3, 0:peer_rows] = sent[0:3, peer * peer_rows:(peer + 1) * peer_rows]
        sent_ref[device, 3:3 + partial.shape[0], :] = partial


def finish_kernel(groups, width, got_ref, slot_ref, elem_bases_ref, u_ref, phi_ref):
    elem_count = slot_ref.shape[1]
    members = got_ref.shape[0] // groups
    first = lax.axis_index("leaf") * members
    flat = peer_lanes(got_ref, first, members, 3, elem_count)
    out = gathered(padded([flat[i:i + 1] for i in range(3)], 8), slot_ref[...])

    def parts_of(group):
        sent = pl.ds(group * members, members)
        lines = [got_ref[sent, 3 + i, :] for i in range(pl.cdiv(width, LANES))]
        return jnp.concatenate(lines, axis=1)[:, 0:width]

    weights = coefficients(parts_of, groups, width // groups)
    weights = jnp.broadcast_to(weights, (8, weights.shape[1])).astype(jnp.bfloat16)
    coarse = dot(weights, elem_bases_ref[...], NN)[0:1]
    u_ref[...] = out[0:1] + out[1:2] * coarse
    phi_ref[...] = out[2:3]


def call(kernel, outs, *args, scalars=(), far=(), scratch=(), flops=1000, moved=1000):
    spaces = [SMEM if i in scalars else pl.ANY if i in far else VMEM for i in range(len(args))]
    args = [
        pltpu.with_memory_space_constraint(arg, pltpu.HBM) if i in far else arg
        for i, arg in enumerate(args)
    ]
    return pl.pallas_call(
        kernel,
        out_shape=outs,
        in_specs=[pl.BlockSpec(memory_space=space) for space in spaces],
        out_specs=jax.tree.map(lambda _: pl.BlockSpec(memory_space=VMEM), outs),
        scratch_shapes=list(scratch),
        cost_estimate=pl.CostEstimate(flops=flops, bytes_accessed=moved, transcendentals=0),
        compiler_params=pltpu.CompilerParams(vmem_limit_bytes=32 * 1024 * 1024),
    )(*args)


def shape(*dims, dtype=jnp.float32):
    return jax.ShapeDtypeStruct(dims, dtype)


def body(
    ln_rate,
    log_state,
    sigma,
    fric_a,
    fric_b,
    slip_dist,
    leaf_of_elem,
    near_blocks,
    near_col,
    near_count,
    far_u,
    far_v,
    far_col,
    far_rank,
    coarse_u,
    coarse_v,
):
    members = lax.axis_size("blk")
    elems = ln_rate.shape[0]
    leaf_size = near_blocks.shape[1]
    groups, rank = coarse_v.shape[0], coarse_v.shape[1]
    devices = groups * members
    width = groups * rank
    lines = pl.cdiv(width, LANES)
    sent_rows = 1 << (2 + lines).bit_length()
    integer = jnp.int32

    def swap(value, axes):
        return lax.all_to_all(value, axes, split_axis=0, concat_axis=0, tiled=True)

    def partner(value, bit):
        return lax.ppermute(value, "blk", [(i, i ^ (1 << bit)) for i in range(members)])

    elem_args = [
        value.reshape(1, elems)
        for value in (leaf_of_elem, ln_rate, log_state, sigma, fric_a, fric_b, slip_dist)
    ]
    scalar_args = [near_col, far_col, far_rank]
    weights = [
        near_blocks, far_u.reshape(-1, leaf_size), far_v.reshape(-1, leaf_size), coarse_v
    ]
    far_rows = weights[1].shape[0]
    bases = coarse_u.reshape(width, elems)
    sent, slot, elem_row, held = call(
        functools.partial(sort_kernel, members),
        (
            shape(members, -(-(3 * (elems // LANES) + 4) // 8) * 8, LANES),
            shape(1, elems, dtype=integer),
            shape(1, elems, dtype=integer),
            shape(width, elems, dtype=jnp.bfloat16),
        ),
        *elem_args, bases, far=range(8),
        scratch=[VMEM(value.shape, value.dtype) for value in elem_args]
        + [pltpu.SemaphoreType.DMA((8,))],
    )
    steps = step_bits(members)
    early = bases = call(
        functools.partial(stack_foreign_kernel, groups, rank),
        shape(2 * (width - rank), elems, dtype=jnp.bfloat16),
        held, partner(bases, steps[0]), slot, flops=1 << 34, moved=1 << 26,
    )
    near_mask, far_mask, near, far_u, far_v, coarse_v = call(
        load_kernel,
        (
            shape(near_blocks.shape[0], members, leaf_size),
            shape(members, far_rows),
            *[shape(*value.shape, dtype=jnp.bfloat16) for value in weights[:3]],
            shape(width, elems, dtype=jnp.bfloat16),
        ),
        early, *scalar_args, *weights, far=range(1, 8),
        scratch=[SMEM(value.shape, value.dtype) for value in scalar_args]
        + [pltpu.SemaphoreType.DMA((6 + groups,))],
    )
    fields = near_count, near, far_u, far_v, near_mask, far_mask
    state, factor, rows, out = call(
        place_kernel,
        (
            shape(8, elems),
            shape(members, elems),
            shape(1, elems, dtype=integer),
            shape(devices, 1, elems + lines * LANES),
        ),
        swap(sent, "blk"), coarse_v, *fields, scalars=(2,),
        scratch=[VMEM((2, members * (elems // LANES), LANES), jnp.float32)],
        flops=1 << 20, moved=1 << 22,
    )
    for bit in steps[1:-1]:
        bases = call(
            stack_kernel, shape(2 * bases.shape[0], elems, dtype=jnp.bfloat16),
            bases, partner(bases, bit), rows, flops=1 << 34, moved=1 << 26,
        )
    bases = bases, partner(bases, steps[-1])
    elem_bases = call(
        functools.partial(element_kernel, members), shape(width - rank, elems, dtype=jnp.bfloat16),
        *bases, slot, elem_row, flops=1 << 34, moved=1 << 26,
    )
    sent = call(
        functools.partial(second_kernel, groups), shape(devices, sent_rows, LANES),
        state, factor, rows, swap(out, ("leaf", "blk")), elem_bases, coarse_v, *bases, *fields, scalars=(8,),
    )
    u, phi = call(
        functools.partial(finish_kernel, groups, width), (shape(1, elems), shape(1, elems)),
        swap(sent, ("leaf", "blk")), slot, elem_bases,
    )
    return u.reshape(elems), phi.reshape(elems)


def solution(mesh):
    each = P(("leaf", "blk"))
    blocks = P(("leaf", "blk"), None, None)
    last = P(None, None, ("leaf", "blk"))
    in_specs = (each,) * 7 + (blocks, each, each, blocks, blocks, each, each, last, last)
    return jax.shard_map(body, mesh=mesh, in_specs=in_specs, out_specs=(each, each), check_vma=False)
```

```python
import functools

import jax
import jax.numpy as jnp
from jax import lax
from jax.experimental import pallas as pl
from jax.experimental.pallas import tpu as pltpu
from jax.sharding import PartitionSpec as P

DAMPING = 0.5
PLATE_RATE = 1.0
TIME_STEP = 0.2

NN = (((1,), (0,)), ((), ()))
NT = (((1,), (1,)), ((), ()))
VMEM = pltpu.VMEM
SMEM = pltpu.SMEM

LANES = 128
HALF = 64


def dot(left, right, dims):
    return lax.dot_general(left, right, dims, preferred_element_type=jnp.float32)


def low_matrix(index_row):
    rows = lax.broadcasted_iota(jnp.int32, (LANES, index_row.shape[1]), 0)
    rows = rows.astype(jnp.float32).astype(jnp.bfloat16)
    low = (index_row & (LANES - 1)).astype(jnp.float32).astype(jnp.bfloat16)
    one = jnp.ones((), jnp.bfloat16)
    return jnp.where(rows == low, one, jnp.zeros_like(one))


def three_parts(values):
    high = values.astype(jnp.bfloat16).astype(jnp.float32)
    rest = values - high
    middle = rest.astype(jnp.bfloat16).astype(jnp.float32)
    return jnp.concatenate([high, middle, rest - middle], axis=0)


def joined(parts):
    count = parts.shape[0] // 3
    return parts[0:count] + parts[count:2 * count] + parts[2 * count:]


def scattered(values, index_row):
    parts = three_parts(values)
    count = parts.shape[0]
    high = index_row // LANES
    pieces = values.shape[1] // LANES
    left = jnp.concatenate([jnp.where(high == piece, parts, 0.0) for piece in range(pieces)], axis=0)
    moved = dot(left.astype(jnp.bfloat16), low_matrix(index_row), NT)
    return jnp.concatenate(
        [joined(moved[piece * count:(piece + 1) * count]) for piece in range(pieces)], axis=1
    )


def gathered(values, index_row):
    parts = three_parts(values)
    count = parts.shape[0]
    high = index_row // LANES
    pieces = values.shape[1] // LANES
    left = jnp.concatenate(
        [parts[:, piece * LANES:(piece + 1) * LANES] for piece in range(pieces)], axis=0
    )
    moved = dot(left.astype(jnp.bfloat16), low_matrix(index_row), NN)
    total = jnp.zeros((count, index_row.shape[1]), jnp.float32)
    for piece in range(pieces):
        total = jnp.where(high == piece, moved[piece * count:(piece + 1) * count], total)
    return joined(total)


def padded(rows, count):
    missing = count - len(rows)
    if missing:
        rows = rows + [jnp.zeros((missing, rows[0].shape[1]), jnp.float32)]
    return jnp.concatenate(rows, axis=0)


def as_lines(row):
    return jnp.concatenate(
        [row[:, i * LANES:(i + 1) * LANES] for i in range(row.shape[1] // LANES)], axis=0
    )


def start_copies(sources, targets, sems):
    copies = [
        pltpu.make_async_copy(source, target, sems.at[i])
        for i, (source, target) in enumerate(zip(sources, targets))
    ]
    for copy in copies:
        copy.start()
    return copies


def sort_kernel(members, *refs):
    elem_refs, bases_ref, sent_ref, slot_ref, elem_row_ref, bases_out = refs[:7], *refs[7:12]
    elem_bufs, sems = refs[12:19], refs[19]
    copies = start_copies([*elem_refs, bases_ref], [*elem_bufs, bases_out], sems)
    mine = lax.axis_index("leaf")
    elem_count = elem_bufs[0].shape[1]
    peer_rows = elem_count // members
    pieces = elem_count // LANES
    before = lax.broadcasted_iota(jnp.int32, (LANES, LANES), 0)
    after = lax.broadcasted_iota(jnp.int32, (LANES, LANES), 1)
    triangle = jnp.where(before < after, 1.0, 0.0).astype(jnp.bfloat16)
    copies[0].wait()
    local = elem_bufs[0][...] - mine * (members * elem_count)
    target = local // elem_count
    target_row = local - target * elem_count
    peers = lax.broadcasted_iota(jnp.int32, (members, elem_count), 0)
    onehot = jnp.where(peers == target, 1.0, 0.0)
    lines = [onehot[:, i * LANES:(i + 1) * LANES] for i in range(pieces)]
    inside = dot(jnp.concatenate(lines, axis=0).astype(jnp.bfloat16), triangle, NN)
    passed = jnp.zeros((members, 1), jnp.float32)
    ranks = []
    for i, line in enumerate(lines):
        earlier = inside[i * members:(i + 1) * members] + passed
        ranks.append(jnp.sum(earlier * line, axis=0, keepdims=True))
        passed = passed + jnp.sum(line, axis=1, keepdims=True)
    slot = target * peer_rows + jnp.concatenate(ranks, axis=1).astype(jnp.int32)
    slot_ref[...] = slot
    elem_row_ref[...] = target_row
    for copy in copies[1:7]:
        copy.wait()
    u, phi, sigma, fric_a, fric_b, dist = (buf[...] for buf in elem_bufs[1:])
    velocity = jnp.exp(u)
    deficit = (PLATE_RATE - velocity).astype(jnp.bfloat16).astype(jnp.float32)
    sa = sigma * fric_a
    factor = TIME_STEP / (sa + DAMPING * velocity)
    rows = [u, phi, sa, sigma * fric_b, dist, target_row.astype(jnp.float32), deficit, factor]
    values = scattered(padded(rows, 8), slot)
    everyone = jnp.concatenate([as_lines(values[i:i + 1]) for i in (6, 5, 7)], axis=0)
    for peer in range(members):
        sent_ref[peer, 0:3 * pieces, :] = everyone
        part = values[0:6, peer * peer_rows:(peer + 1) * peer_rows]
        sent_ref[peer, 3 * pieces:3 * pieces + 4, 0:peer_rows] = part[0:4]
        sent_ref[peer, 3 * pieces:3 * pieces + 2, HALF:HALF + peer_rows] = part[4:6]
    copies[7].wait()


def load_kernel(early_ref, *refs):
    scalar_refs, weight_refs, near_mask_ref, far_mask_ref = refs[:3], refs[3:7], refs[7], refs[8]
    weight_outs, scalar_bufs, sems = refs[9:13], refs[13:16], refs[16]
    sources, targets = [*scalar_refs, *weight_refs[:3]], [*scalar_bufs, *weight_outs[:3]]
    coarse_v_ref, coarse_v_out = weight_refs[3], weight_outs[3]
    groups, rank = coarse_v_ref.shape[0], coarse_v_ref.shape[1]
    for shift in range(groups):
        place = (shift - 1) % groups * rank
        sources.append(coarse_v_ref.at[lax.axis_index("leaf") ^ shift])
        targets.append(coarse_v_out.at[pl.ds(place, rank), :])
    copies = start_copies(sources, targets, sems)
    for copy in copies[:3]:
        copy.wait()
    near_col, far_col, far_rank = scalar_bufs
    far_slots = far_col.shape[0]
    far_width = far_mask_ref.shape[1] // far_slots
    block = lax.broadcasted_iota(jnp.int32, near_mask_ref.shape[1:], 0)
    for number in range(near_mask_ref.shape[0]):
        near_mask_ref[number] = jnp.where(block == near_col[number], 1.0, 0.0)
    block = lax.broadcasted_iota(jnp.int32, far_mask_ref.shape, 0)
    lane = lax.broadcasted_iota(jnp.int32, far_mask_ref.shape, 1)
    column = jnp.full(far_mask_ref.shape, -1, jnp.int32)
    for number in range(far_slots):
        low = number * far_width
        kept = (lane >= low) & (lane < low + far_rank[number])
        column = jnp.where(kept, far_col[number], column)
    far_mask_ref[...] = jnp.where(block == column, 1.0, 0.0)
    for copy in copies[3:]:
        copy.wait()


def partial_row(deficit, coarse_v_ref):
    wide = jnp.broadcast_to(deficit, (8, deficit.shape[1])).astype(jnp.bfloat16)
    partial = dot(wide, coarse_v_ref[...], NT)[0:1]
    rest = -partial.shape[1] % LANES
    if rest:
        partial = jnp.concatenate([partial, jnp.zeros((1, rest), jnp.float32)], axis=1)
    return partial


def inside_rows(deficits, near_count, near_ref, far_u_ref, far_v_ref, near_mask_ref, far_mask_ref):
    total = jnp.zeros(deficits.shape, jnp.float32)
    for slot in range(near_ref.shape[0]):
        live = jnp.where(slot < near_count[0], 1.0, 0.0)
        source = (deficits * (near_mask_ref[slot] * live)).astype(jnp.bfloat16)
        total = total + dot(source, near_ref[slot], NT)
    project = dot(deficits.astype(jnp.bfloat16), far_v_ref[...], NT) * far_mask_ref[...]
    project = jnp.sum(project, axis=0, keepdims=True)
    project = jnp.broadcast_to(project, (8, project.shape[1])).astype(jnp.bfloat16)
    far = dot(project, far_u_ref[...], NN)
    return jnp.sum(total, axis=0, keepdims=True) + far[0:1]


def coefficients(parts_of, groups, rank):
    mine = lax.axis_index("leaf")
    lane = lax.broadcasted_iota(jnp.int32, (1, groups * rank), 1) // rank
    weights = jnp.zeros(lane.shape, jnp.float32)
    for shift in range(1, groups):
        total = jnp.sum(parts_of(mine ^ shift), axis=0, keepdims=True)
        weights = jnp.where(lane == shift - 1, total, weights)
    return weights[:, 0:(groups - 1) * rank]


def coarse_all(weights, members, bases_refs):
    row = lax.broadcasted_iota(jnp.int32, (members, weights.shape[1]), 0) ^ lax.axis_index("blk")
    total = jnp.zeros((members, bases_refs[0].shape[1]), jnp.float32)
    for number, ref in enumerate(bases_refs):
        left = []
        for place in range(members // 2):
            source = relative_member(place, number, members)
            left.append(jnp.where(row == source, weights, 0.0))
        left = jnp.concatenate(left, axis=1).astype(jnp.bfloat16)
        total = total + dot(left, ref[...], NN)
    return total


def stack_kernel(held_ref, came_ref, *refs):
    out_ref = refs[-1]
    count = held_ref.shape[0]
    out_ref[0:count, :] = held_ref[...]
    out_ref[count:2 * count, :] = came_ref[...]


def stack_foreign_kernel(groups, rank, held_ref, came_ref, *refs):
    out_ref = refs[-1]
    mine = lax.axis_index("leaf")
    place = 0
    for ref in (held_ref, came_ref):
        for shift in range(1, groups):
            out_ref[place:place + rank, :] = ref[pl.ds((mine ^ shift) * rank, rank), :]
            place += rank


def step_bits(members):
    bits = list(range(members.bit_length() - 2, -1, -1))
    return bits[:-2] + [bits[-1], bits[-2]]


def relative_member(place, number, members):
    order = step_bits(members)
    found = number << order[-1]
    for step, bit in enumerate(order[:-1]):
        found |= (place >> step & 1) << bit
    return found


def element_kernel(members, held_ref, came_ref, slot_ref, elem_row_ref, out_ref):
    slot, row = slot_ref[...], elem_row_ref[...]
    elem_count = row.shape[1]
    kept = out_ref.shape[0]
    pieces = elem_count // LANES
    owner = (slot // (elem_count // members)) ^ lax.axis_index("blk")
    low, high = low_matrix(row), row // LANES
    total = jnp.zeros(out_ref.shape, jnp.float32)
    for number, ref in enumerate((held_ref, came_ref)):
        for place in range(members // 2):
            part = ref[place * kept:(place + 1) * kept, :]
            left = jnp.concatenate(
                [part[:, piece * LANES:(piece + 1) * LANES] for piece in range(pieces)], axis=0
            )
            found = dot(left, low, NN)
            ours = owner == relative_member(place, number, members)
            for piece in range(pieces):
                here = ours & (high == piece)
                total = jnp.where(here, found[piece * kept:(piece + 1) * kept], total)
    out_ref[...] = total.astype(jnp.bfloat16)


def place_kernel(got_ref, coarse_v_ref, *refs):
    field_refs, state_ref, factor_ref, rows_ref, out_ref, lines_ref = refs[:6], *refs[6:]
    members = got_ref.shape[0]
    elem_count = state_ref.shape[1]
    pieces = elem_count // LANES
    peer_rows = elem_count // members
    count = LANES // peer_rows * pieces
    line_row = lax.broadcasted_iota(jnp.int32, (count, LANES), 0)
    lane_block = lax.broadcasted_iota(jnp.int32, (count, LANES), 1) // peer_rows
    own_lane = line_row // pieces == lane_block
    for line in range(pieces):
        rows = got_ref[:, pieces + line, :].astype(jnp.int32)
        parts = [got_ref[:, line, :]]
        split = three_parts(got_ref[:, 2 * pieces + line, :])
        parts += [split[i * members:(i + 1) * members] for i in range(3)]
        left, right = [], []
        for peer in range(members):
            row = rows[peer:peer + 1]
            kept = own_lane & (line_row % pieces == row // LANES)
            left.append(
                jnp.concatenate([jnp.where(kept, part[peer:peer + 1], 0.0) for part in parts], axis=0)
            )
            right.append(low_matrix(row))
        left = jnp.concatenate(left, axis=1).astype(jnp.bfloat16)
        placed = dot(left, jnp.concatenate(right, axis=1), NT)
        lines_ref[0, line * count:(line + 1) * count, :] = placed[0:count]
        lines_ref[1, line * count:(line + 1) * count, :] = joined(placed[count:])

    def blocks(number):
        return jnp.concatenate(
            [lines_ref[number, pl.ds(piece, members, stride=pieces), :] for piece in range(pieces)],
            axis=1,
        )

    factor_ref[...] = blocks(1)
    inside = inside_rows(blocks(0), *field_refs)

    first = 3 * pieces
    flat = jnp.concatenate(
        [got_ref[peer, first:first + 4, 0:peer_rows] for peer in range(members)], axis=1
    )
    rest = jnp.concatenate(
        [got_ref[peer, first:first + 2, HALF:HALF + peer_rows] for peer in range(members)], axis=1
    )
    rows = rest[1:2].astype(jnp.int32)
    rows_ref[...] = rows
    fields = [flat[i:i + 1] for i in range(4)] + [rest[0:1]]
    state = scattered(padded(fields, 8), rows)
    u, phi, sa, sb, dist = (state[i:i + 1] for i in range(5))
    velocity = jnp.exp(u)
    deficit = (PLATE_RATE - velocity).astype(jnp.bfloat16).astype(jnp.float32)
    k1p = (jnp.exp(-phi) - velocity) / dist
    u2 = u + TIME_STEP * ((inside - sb * k1p) / (sa + DAMPING * velocity))
    state_ref[...] = padded([u, phi, sa, sb, dist, k1p], 8)
    sent = jnp.concatenate([u2, partial_row(deficit, coarse_v_ref)], axis=1)
    out_ref[...] = jnp.broadcast_to(sent[None], out_ref.shape)


def second_kernel(
    groups, state_ref, factor_ref, rows_ref, all_ref, elem_bases_ref, coarse_v_ref, *refs
):
    bases_refs, field_refs, sent_ref = refs[:2], refs[2:8], refs[8]
    members, elem_count = refs[6].shape[1], state_ref.shape[1]
    width = coarse_v_ref.shape[0]
    mine, me = lax.axis_index("leaf"), lax.axis_index("blk")

    def parts_of(group):
        return all_ref[pl.ds(group * members, members), 0, elem_count:elem_count + width]

    weights = coefficients(parts_of, groups, width // groups)
    own = all_ref[pl.ds(mine * members, members), 0, 0:elem_count]
    coarse = coarse_all(weights, members, bases_refs)
    u2_all = own + factor_ref[...] * coarse
    deficits = (PLATE_RATE - jnp.exp(u2_all)).astype(jnp.bfloat16).astype(jnp.float32)
    inside = inside_rows(deficits, *field_refs)

    state = state_ref[...]
    u, phi, sa, sb, dist, k1p = (state[i:i + 1] for i in range(6))
    here = lax.broadcasted_iota(jnp.int32, u2_all.shape, 0) == me
    u2 = jnp.sum(jnp.where(here, u2_all, 0.0), axis=0, keepdims=True)
    deficit = jnp.sum(jnp.where(here, deficits, 0.0), axis=0, keepdims=True)
    phi2 = phi + TIME_STEP * k1p
    velocity = jnp.exp(u2)
    k2p = (jnp.exp(-phi2) - velocity) / dist
    inverse = 0.5 * TIME_STEP / (sa + DAMPING * velocity)
    u_next = 0.5 * (u + u2) + (inside - sb * k2p) * inverse
    phi_next = phi + 0.5 * TIME_STEP * (k1p + k2p)
    sent = gathered(padded([u_next, inverse, phi_next], 8), rows_ref[...])
    partial = partial_row(deficit, coarse_v_ref)
    peer_rows = elem_count // members
    for device in range(groups * members):
        span = slice(device % members * peer_rows, (device % members + 1) * peer_rows)
        sent_ref[device, 0:1, 0:peer_rows] = sent[0:1, span]
        sent_ref[device, 0:1, HALF:HALF + peer_rows] = sent[1:2, span]
        sent_ref[device, 1:2, 0:peer_rows] = sent[2:3, span]
        if width <= LANES - HALF:
            sent_ref[device, 1:2, HALF:HALF + width] = partial[:, 0:width]
        else:
            sent_ref[device, 2:2 + partial.shape[1] // LANES, :] = as_lines(partial)


def finish_kernel(groups, width, got_ref, slot_ref, elem_bases_ref, u_ref, phi_ref):
    elem_count = slot_ref.shape[1]
    members = got_ref.shape[0] // groups
    first = lax.axis_index("leaf") * members
    peer_rows = elem_count // members

    def side_by_side(row, low):
        parts = [got_ref[first + peer, row:row + 1, low:low + peer_rows] for peer in range(members)]
        return jnp.concatenate(parts, axis=1)

    rows = [side_by_side(0, 0), side_by_side(0, HALF), side_by_side(1, 0)]
    out = gathered(padded(rows, 8), slot_ref[...])

    def parts_of(group):
        sent = pl.ds(group * members, members)
        if width <= LANES - HALF:
            return got_ref[sent, 1, HALF:HALF + width]
        lines = [got_ref[sent, 2 + i, :] for i in range(pl.cdiv(width, LANES))]
        return jnp.concatenate(lines, axis=1)[:, 0:width]

    weights = coefficients(parts_of, groups, width // groups)
    weights = jnp.broadcast_to(weights, (8, weights.shape[1])).astype(jnp.bfloat16)
    coarse = dot(weights, elem_bases_ref[...], NN)[0:1]
    u_ref[...] = out[0:1] + out[1:2] * coarse
    phi_ref[...] = out[2:3]


def call(kernel, outs, *args, scalars=(), far=(), scratch=(), flops=1000, moved=1000):
    spaces = [SMEM if i in scalars else pl.ANY if i in far else VMEM for i in range(len(args))]
    args = [
        pltpu.with_memory_space_constraint(arg, pltpu.HBM) if i in far else arg
        for i, arg in enumerate(args)
    ]
    return pl.pallas_call(
        kernel,
        out_shape=outs,
        in_specs=[pl.BlockSpec(memory_space=space) for space in spaces],
        out_specs=jax.tree.map(lambda _: pl.BlockSpec(memory_space=VMEM), outs),
        scratch_shapes=list(scratch),
        cost_estimate=pl.CostEstimate(flops=flops, bytes_accessed=moved, transcendentals=0),
        compiler_params=pltpu.CompilerParams(vmem_limit_bytes=32 * 1024 * 1024),
    )(*args)


def shape(*dims, dtype=jnp.float32):
    return jax.ShapeDtypeStruct(dims, dtype)


def body(
    ln_rate,
    log_state,
    sigma,
    fric_a,
    fric_b,
    slip_dist,
    leaf_of_elem,
    near_blocks,
    near_col,
    near_count,
    far_u,
    far_v,
    far_col,
    far_rank,
    coarse_u,
    coarse_v,
):
    members = lax.axis_size("blk")
    elems = ln_rate.shape[0]
    leaf_size = near_blocks.shape[1]
    groups, rank = coarse_v.shape[0], coarse_v.shape[1]
    devices = groups * members
    width = groups * rank
    lines = pl.cdiv(width, LANES)
    sent_rows = 2 if width <= LANES - HALF else 1 << (1 + lines).bit_length()
    integer = jnp.int32

    def swap(value, axes):
        return lax.all_to_all(value, axes, split_axis=0, concat_axis=0, tiled=True)

    def partner(value, bit):
        return lax.ppermute(value, "blk", [(i, i ^ (1 << bit)) for i in range(members)])

    elem_args = [
        value.reshape(1, elems)
        for value in (leaf_of_elem, ln_rate, log_state, sigma, fric_a, fric_b, slip_dist)
    ]
    scalar_args = [near_col, far_col, far_rank]
    weights = [
        near_blocks, far_u.reshape(-1, leaf_size), far_v.reshape(-1, leaf_size), coarse_v
    ]
    far_rows = weights[1].shape[0]
    bases = coarse_u.reshape(width, elems)
    sent, slot, elem_row, held = call(
        functools.partial(sort_kernel, members),
        (
            shape(members, -(-(3 * (elems // LANES) + 4) // 8) * 8, LANES),
            shape(1, elems, dtype=integer),
            shape(1, elems, dtype=integer),
            shape(width, elems, dtype=jnp.bfloat16),
        ),
        *elem_args, bases, far=range(8),
        scratch=[VMEM(value.shape, value.dtype) for value in elem_args]
        + [pltpu.SemaphoreType.DMA((8,))],
    )
    steps = step_bits(members)
    early = bases = call(
        functools.partial(stack_foreign_kernel, groups, rank),
        shape(2 * (width - rank), elems, dtype=jnp.bfloat16),
        held, partner(bases, steps[0]), slot, flops=1 << 34, moved=1 << 26,
    )
    near_mask, far_mask, near, far_u, far_v, coarse_v = call(
        load_kernel,
        (
            shape(near_blocks.shape[0], members, leaf_size),
            shape(members, far_rows),
            *[shape(*value.shape, dtype=jnp.bfloat16) for value in weights[:3]],
            shape(width, elems, dtype=jnp.bfloat16),
        ),
        early, *scalar_args, *weights, far=range(1, 8),
        scratch=[SMEM(value.shape, value.dtype) for value in scalar_args]
        + [pltpu.SemaphoreType.DMA((6 + groups,))],
    )
    fields = near_count, near, far_u, far_v, near_mask, far_mask
    state, factor, rows, out = call(
        place_kernel,
        (
            shape(8, elems),
            shape(members, elems),
            shape(1, elems, dtype=integer),
            shape(devices, 1, elems + lines * LANES),
        ),
        swap(sent, "blk"), coarse_v, *fields, scalars=(2,),
        scratch=[VMEM((2, members * (elems // LANES), LANES), jnp.float32)],
        flops=1 << 20, moved=1 << 22,
    )
    for bit in steps[1:-1]:
        bases = call(
            stack_kernel, shape(2 * bases.shape[0], elems, dtype=jnp.bfloat16),
            bases, partner(bases, bit), rows, flops=1 << 34, moved=1 << 26,
        )
    bases = bases, partner(bases, steps[-1])
    elem_bases = call(
        functools.partial(element_kernel, members), shape(width - rank, elems, dtype=jnp.bfloat16),
        *bases, slot, elem_row, flops=1 << 34, moved=1 << 26,
    )
    sent = call(
        functools.partial(second_kernel, groups), shape(devices, sent_rows, LANES),
        state, factor, rows, swap(out, ("leaf", "blk")), elem_bases, coarse_v, *bases, *fields, scalars=(8,),
    )
    u, phi = call(
        functools.partial(finish_kernel, groups, width), (shape(1, elems), shape(1, elems)),
        swap(sent, ("leaf", "blk")), slot, elem_bases,
    )
    return u.reshape(elems), phi.reshape(elems)


def solution(mesh):
    each = P(("leaf", "blk"))
    blocks = P(("leaf", "blk"), None, None)
    last = P(None, None, ("leaf", "blk"))
    in_specs = (each,) * 7 + (blocks, each, each, blocks, blocks, each, each, last, last)
    return jax.shard_map(body, mesh=mesh, in_specs=in_specs, out_specs=(each, each), check_vma=False)
```

```python
import functools

import jax
import jax.numpy as jnp
from jax import lax
from jax.experimental import pallas as pl
from jax.experimental.pallas import tpu as pltpu
from jax.sharding import PartitionSpec as P

DAMPING = 0.5
PLATE_RATE = 1.0
TIME_STEP = 0.2

NN = (((1,), (0,)), ((), ()))
NT = (((1,), (1,)), ((), ()))
VMEM = pltpu.VMEM
SMEM = pltpu.SMEM

LANES = 128
HALF = 64


def dot(left, right, dims):
    return lax.dot_general(left, right, dims, preferred_element_type=jnp.float32)


def low_matrix(index_row):
    rows = lax.broadcasted_iota(jnp.int32, (LANES, index_row.shape[1]), 0)
    rows = rows.astype(jnp.float32).astype(jnp.bfloat16)
    low = (index_row & (LANES - 1)).astype(jnp.float32).astype(jnp.bfloat16)
    one = jnp.ones((), jnp.bfloat16)
    return jnp.where(rows == low, one, jnp.zeros_like(one))


def three_parts(values):
    high = values.astype(jnp.bfloat16).astype(jnp.float32)
    rest = values - high
    middle = rest.astype(jnp.bfloat16).astype(jnp.float32)
    return jnp.concatenate([high, middle, rest - middle], axis=0)


def joined(parts):
    count = parts.shape[0] // 3
    return parts[0:count] + parts[count:2 * count] + parts[2 * count:]


def scattered(values, index_row):
    parts = three_parts(values)
    count = parts.shape[0]
    high = index_row // LANES
    pieces = values.shape[1] // LANES
    left = jnp.concatenate([jnp.where(high == piece, parts, 0.0) for piece in range(pieces)], axis=0)
    moved = dot(left.astype(jnp.bfloat16), low_matrix(index_row), NT)
    return jnp.concatenate(
        [joined(moved[piece * count:(piece + 1) * count]) for piece in range(pieces)], axis=1
    )


def gathered(values, index_row):
    parts = three_parts(values)
    count = parts.shape[0]
    high = index_row // LANES
    pieces = values.shape[1] // LANES
    left = jnp.concatenate(
        [parts[:, piece * LANES:(piece + 1) * LANES] for piece in range(pieces)], axis=0
    )
    moved = dot(left.astype(jnp.bfloat16), low_matrix(index_row), NN)
    total = jnp.zeros((count, index_row.shape[1]), jnp.float32)
    for piece in range(pieces):
        total = jnp.where(high == piece, moved[piece * count:(piece + 1) * count], total)
    return joined(total)


def padded(rows, count):
    missing = count - len(rows)
    if missing:
        rows = rows + [jnp.zeros((missing, rows[0].shape[1]), jnp.float32)]
    return jnp.concatenate(rows, axis=0)


def as_lines(row):
    return jnp.concatenate(
        [row[:, i * LANES:(i + 1) * LANES] for i in range(row.shape[1] // LANES)], axis=0
    )


def peer_lanes(ref, first, members, rows, elem_count):
    width = elem_count // members
    return jnp.concatenate([ref[first + peer, 0:rows, 0:width] for peer in range(members)], axis=1)


def start_copies(sources, targets, sems):
    copies = [
        pltpu.make_async_copy(source, target, sems.at[i])
        for i, (source, target) in enumerate(zip(sources, targets))
    ]
    for copy in copies:
        copy.start()
    return copies


def sort_kernel(members, *refs):
    elem_refs, weight_refs = refs[:7], refs[7:9]
    sent_ref, slot_ref, elem_row_ref = refs[9:12]
    weight_outs, elem_bufs, sems = refs[12:14], refs[14:21], refs[21]
    copies = start_copies([*elem_refs, *weight_refs], [*elem_bufs, *weight_outs], sems)
    mine = lax.axis_index("leaf")
    elem_count = elem_bufs[0].shape[1]
    peer_rows = elem_count // members
    pieces = elem_count // LANES
    before = lax.broadcasted_iota(jnp.int32, (LANES, LANES), 0)
    after = lax.broadcasted_iota(jnp.int32, (LANES, LANES), 1)
    triangle = jnp.where(before < after, 1.0, 0.0).astype(jnp.bfloat16)
    copies[0].wait()
    local = elem_bufs[0][...] - mine * (members * elem_count)
    target = local // elem_count
    target_row = local - target * elem_count
    peers = lax.broadcasted_iota(jnp.int32, (members, elem_count), 0)
    onehot = jnp.where(peers == target, 1.0, 0.0)
    lines = [onehot[:, i * LANES:(i + 1) * LANES] for i in range(pieces)]
    inside = dot(jnp.concatenate(lines, axis=0).astype(jnp.bfloat16), triangle, NN)
    passed = jnp.zeros((members, 1), jnp.float32)
    ranks = []
    for i, line in enumerate(lines):
        earlier = inside[i * members:(i + 1) * members] + passed
        ranks.append(jnp.sum(earlier * line, axis=0, keepdims=True))
        passed = passed + jnp.sum(line, axis=1, keepdims=True)
    slot = target * peer_rows + jnp.concatenate(ranks, axis=1).astype(jnp.int32)
    slot_ref[...] = slot
    elem_row_ref[...] = target_row
    for copy in copies[1:7]:
        copy.wait()
    u, phi, sigma, fric_a, fric_b, dist = (buf[...] for buf in elem_bufs[1:])
    velocity = jnp.exp(u)
    deficit = (PLATE_RATE - velocity).astype(jnp.bfloat16).astype(jnp.float32)
    sa = sigma * fric_a
    factor = TIME_STEP / (sa + DAMPING * velocity)
    rows = [u, phi, sa, sigma * fric_b, dist, target_row.astype(jnp.float32), deficit, factor]
    values = scattered(padded(rows, 8), slot)
    everyone = jnp.concatenate([as_lines(values[i:i + 1]) for i in (6, 5, 7)], axis=0)
    for peer in range(members):
        sent_ref[peer, 0:3 * pieces, :] = everyone
        part = values[0:6, peer * peer_rows:(peer + 1) * peer_rows]
        sent_ref[peer, 3 * pieces:3 * pieces + 4, 0:peer_rows] = part[0:4]
        sent_ref[peer, 3 * pieces:3 * pieces + 2, HALF:HALF + peer_rows] = part[4:6]
    for copy in copies[7:]:
        copy.wait()


def load_kernel(early_ref, *refs):
    scalar_refs, weight_refs, near_mask_ref, far_mask_ref = refs[:3], refs[3:6], refs[6], refs[7]
    weight_outs, scalar_bufs, sems = refs[8:11], refs[11:14], refs[14]
    sources, targets = [*scalar_refs, *weight_refs[:2]], [*scalar_bufs, *weight_outs[:2]]
    coarse_v_ref, coarse_v_out = weight_refs[2], weight_outs[2]
    groups, rank = coarse_v_ref.shape[0], coarse_v_ref.shape[1]
    for shift in range(groups):
        place = (shift - 1) % groups * rank
        sources.append(coarse_v_ref.at[lax.axis_index("leaf") ^ shift])
        targets.append(coarse_v_out.at[pl.ds(place, rank), :])
    copies = start_copies(sources, targets, sems)
    for copy in copies[:3]:
        copy.wait()
    near_col, far_col, far_rank = scalar_bufs
    far_slots = far_col.shape[0]
    far_width = far_mask_ref.shape[1] // far_slots
    block = lax.broadcasted_iota(jnp.int32, near_mask_ref.shape[1:], 0)
    for number in range(near_mask_ref.shape[0]):
        near_mask_ref[number] = jnp.where(block == near_col[number], 1.0, 0.0)
    block = lax.broadcasted_iota(jnp.int32, far_mask_ref.shape, 0)
    lane = lax.broadcasted_iota(jnp.int32, far_mask_ref.shape, 1)
    column = jnp.full(far_mask_ref.shape, -1, jnp.int32)
    for number in range(far_slots):
        low = number * far_width
        kept = (lane >= low) & (lane < low + far_rank[number])
        column = jnp.where(kept, far_col[number], column)
    far_mask_ref[...] = jnp.where(block == column, 1.0, 0.0)
    for copy in copies[3:]:
        copy.wait()


def partial_row(deficit, coarse_v_ref):
    wide = jnp.broadcast_to(deficit, (8, deficit.shape[1])).astype(jnp.bfloat16)
    partial = dot(wide, coarse_v_ref[...], NT)[0:1]
    rest = -partial.shape[1] % LANES
    if rest:
        partial = jnp.concatenate([partial, jnp.zeros((1, rest), jnp.float32)], axis=1)
    return partial


def inside_rows(deficits, near_count, near_ref, far_u_ref, far_v_ref, near_mask_ref, far_mask_ref):
    total = jnp.zeros(deficits.shape, jnp.float32)
    for slot in range(near_ref.shape[0]):
        live = jnp.where(slot < near_count[0], 1.0, 0.0)
        source = (deficits * (near_mask_ref[slot] * live)).astype(jnp.bfloat16)
        total = total + dot(source, near_ref[slot], NT)
    project = dot(deficits.astype(jnp.bfloat16), far_v_ref[...], NT) * far_mask_ref[...]
    project = jnp.sum(project, axis=0, keepdims=True)
    project = jnp.broadcast_to(project, (8, project.shape[1])).astype(jnp.bfloat16)
    far = dot(project, far_u_ref[...], NN)
    return jnp.sum(total, axis=0, keepdims=True) + far[0:1]


def coefficients(parts_of, groups, rank):
    mine = lax.axis_index("leaf")
    lane = lax.broadcasted_iota(jnp.int32, (1, groups * rank), 1) // rank
    weights = jnp.zeros(lane.shape, jnp.float32)
    for shift in range(1, groups):
        total = jnp.sum(parts_of(mine ^ shift), axis=0, keepdims=True)
        weights = jnp.where(lane == shift - 1, total, weights)
    return weights[:, 0:(groups - 1) * rank]


def coarse_all(weights, members, bases_refs):
    row = lax.broadcasted_iota(jnp.int32, (members, weights.shape[1]), 0) ^ lax.axis_index("blk")
    total = jnp.zeros((members, bases_refs[0].shape[1]), jnp.float32)
    for number, ref in enumerate(bases_refs):
        left = []
        for place in range(members // 2):
            source = relative_member(place, number, members)
            left.append(jnp.where(row == source, weights, 0.0))
        left = jnp.concatenate(left, axis=1).astype(jnp.bfloat16)
        total = total + dot(left, ref[...], NN)
    return total


def stack_kernel(held_ref, came_ref, *refs):
    out_ref = refs[-1]
    count = held_ref.shape[0]
    out_ref[0:count, :] = held_ref[...]
    out_ref[count:2 * count, :] = came_ref[...]


def stack_foreign_kernel(groups, rank, held_ref, came_ref, *refs):
    out_ref = refs[-1]
    mine = lax.axis_index("leaf")
    place = 0
    for ref in (held_ref, came_ref):
        for shift in range(1, groups):
            out_ref[place:place + rank, :] = ref[pl.ds((mine ^ shift) * rank, rank), :]
            place += rank


def step_bits(members):
    bits = list(range(members.bit_length() - 2, -1, -1))
    return bits[:-2] + [bits[-1], bits[-2]]


def relative_member(place, number, members):
    order = step_bits(members)
    found = number << order[-1]
    for step, bit in enumerate(order[:-1]):
        found |= (place >> step & 1) << bit
    return found


def element_kernel(members, held_ref, came_ref, slot_ref, elem_row_ref, out_ref):
    slot, row = slot_ref[...], elem_row_ref[...]
    elem_count = row.shape[1]
    kept = out_ref.shape[0]
    pieces = elem_count // LANES
    owner = (slot // (elem_count // members)) ^ lax.axis_index("blk")
    low, high = low_matrix(row), row // LANES
    total = jnp.zeros(out_ref.shape, jnp.float32)
    for number, ref in enumerate((held_ref, came_ref)):
        for place in range(members // 2):
            part = ref[place * kept:(place + 1) * kept, :]
            left = jnp.concatenate(
                [part[:, piece * LANES:(piece + 1) * LANES] for piece in range(pieces)], axis=0
            )
            found = dot(left, low, NN)
            ours = owner == relative_member(place, number, members)
            for piece in range(pieces):
                here = ours & (high == piece)
                total = jnp.where(here, found[piece * kept:(piece + 1) * kept], total)
    out_ref[...] = total.astype(jnp.bfloat16)


def place_kernel(got_ref, coarse_v_ref, *refs):
    field_refs, state_ref, factor_ref, rows_ref, out_ref, lines_ref = refs[:6], *refs[6:]
    members = got_ref.shape[0]
    elem_count = state_ref.shape[1]
    pieces = elem_count // LANES
    peer_rows = elem_count // members
    count = LANES // peer_rows * pieces
    line_row = lax.broadcasted_iota(jnp.int32, (count, LANES), 0)
    lane_block = lax.broadcasted_iota(jnp.int32, (count, LANES), 1) // peer_rows
    own_lane = line_row // pieces == lane_block
    for line in range(pieces):
        rows = got_ref[:, pieces + line, :].astype(jnp.int32)
        parts = [got_ref[:, line, :]]
        split = three_parts(got_ref[:, 2 * pieces + line, :])
        parts += [split[i * members:(i + 1) * members] for i in range(3)]
        left, right = [], []
        for peer in range(members):
            row = rows[peer:peer + 1]
            kept = own_lane & (line_row % pieces == row // LANES)
            left.append(
                jnp.concatenate([jnp.where(kept, part[peer:peer + 1], 0.0) for part in parts], axis=0)
            )
            right.append(low_matrix(row))
        left = jnp.concatenate(left, axis=1).astype(jnp.bfloat16)
        placed = dot(left, jnp.concatenate(right, axis=1), NT)
        lines_ref[0, line * count:(line + 1) * count, :] = placed[0:count]
        lines_ref[1, line * count:(line + 1) * count, :] = joined(placed[count:])

    def blocks(number):
        return jnp.concatenate(
            [lines_ref[number, pl.ds(piece, members, stride=pieces), :] for piece in range(pieces)],
            axis=1,
        )

    factor_ref[...] = blocks(1)
    inside = inside_rows(blocks(0), *field_refs)

    first = 3 * pieces
    flat = jnp.concatenate(
        [got_ref[peer, first:first + 4, 0:peer_rows] for peer in range(members)], axis=1
    )
    rest = jnp.concatenate(
        [got_ref[peer, first:first + 2, HALF:HALF + peer_rows] for peer in range(members)], axis=1
    )
    rows = rest[1:2].astype(jnp.int32)
    rows_ref[...] = rows
    fields = [flat[i:i + 1] for i in range(4)] + [rest[0:1]]
    state = scattered(padded(fields, 8), rows)
    u, phi, sa, sb, dist = (state[i:i + 1] for i in range(5))
    velocity = jnp.exp(u)
    deficit = (PLATE_RATE - velocity).astype(jnp.bfloat16).astype(jnp.float32)
    k1p = (jnp.exp(-phi) - velocity) / dist
    u2 = u + TIME_STEP * ((inside - sb * k1p) / (sa + DAMPING * velocity))
    state_ref[...] = padded([u, phi, sa, sb, dist, k1p], 8)
    sent = jnp.concatenate([u2, partial_row(deficit, coarse_v_ref)], axis=1)
    out_ref[...] = jnp.broadcast_to(sent[None], out_ref.shape)


def second_kernel(
    groups, state_ref, factor_ref, rows_ref, all_ref, elem_bases_ref, coarse_v_ref, *refs
):
    bases_refs, field_refs, sent_ref = refs[:2], refs[2:8], refs[8]
    members, elem_count = refs[6].shape[1], state_ref.shape[1]
    width = coarse_v_ref.shape[0]
    mine, me = lax.axis_index("leaf"), lax.axis_index("blk")

    def parts_of(group):
        return all_ref[pl.ds(group * members, members), 0, elem_count:elem_count + width]

    weights = coefficients(parts_of, groups, width // groups)
    own = all_ref[pl.ds(mine * members, members), 0, 0:elem_count]
    coarse = coarse_all(weights, members, bases_refs)
    u2_all = own + factor_ref[...] * coarse
    deficits = (PLATE_RATE - jnp.exp(u2_all)).astype(jnp.bfloat16).astype(jnp.float32)
    inside = inside_rows(deficits, *field_refs)

    state = state_ref[...]
    u, phi, sa, sb, dist, k1p = (state[i:i + 1] for i in range(6))
    here = lax.broadcasted_iota(jnp.int32, u2_all.shape, 0) == me
    u2 = jnp.sum(jnp.where(here, u2_all, 0.0), axis=0, keepdims=True)
    deficit = jnp.sum(jnp.where(here, deficits, 0.0), axis=0, keepdims=True)
    phi2 = phi + TIME_STEP * k1p
    velocity = jnp.exp(u2)
    k2p = (jnp.exp(-phi2) - velocity) / dist
    inverse = 0.5 * TIME_STEP / (sa + DAMPING * velocity)
    u_next = 0.5 * (u + u2) + (inside - sb * k2p) * inverse
    phi_next = phi + 0.5 * TIME_STEP * (k1p + k2p)
    sent = gathered(padded([u_next, inverse, phi_next], 8), rows_ref[...])
    partial = as_lines(partial_row(deficit, coarse_v_ref))
    peer_rows = elem_count // members
    for device in range(groups * members):
        peer = device % members
        sent_ref[device, 0:3, 0:peer_rows] = sent[0:3, peer * peer_rows:(peer + 1) * peer_rows]
        sent_ref[device, 3:3 + partial.shape[0], :] = partial


def finish_kernel(groups, width, got_ref, slot_ref, elem_bases_ref, u_ref, phi_ref):
    elem_count = slot_ref.shape[1]
    members = got_ref.shape[0] // groups
    first = lax.axis_index("leaf") * members
    flat = peer_lanes(got_ref, first, members, 3, elem_count)
    out = gathered(padded([flat[i:i + 1] for i in range(3)], 8), slot_ref[...])

    def parts_of(group):
        sent = pl.ds(group * members, members)
        lines = [got_ref[sent, 3 + i, :] for i in range(pl.cdiv(width, LANES))]
        return jnp.concatenate(lines, axis=1)[:, 0:width]

    weights = coefficients(parts_of, groups, width // groups)
    weights = jnp.broadcast_to(weights, (8, weights.shape[1])).astype(jnp.bfloat16)
    coarse = dot(weights, elem_bases_ref[...], NN)[0:1]
    u_ref[...] = out[0:1] + out[1:2] * coarse
    phi_ref[...] = out[2:3]


def call(kernel, outs, *args, scalars=(), far=(), scratch=(), flops=1000, moved=1000):
    spaces = [SMEM if i in scalars else pl.ANY if i in far else VMEM for i in range(len(args))]
    args = [
        pltpu.with_memory_space_constraint(arg, pltpu.HBM) if i in far else arg
        for i, arg in enumerate(args)
    ]
    return pl.pallas_call(
        kernel,
        out_shape=outs,
        in_specs=[pl.BlockSpec(memory_space=space) for space in spaces],
        out_specs=jax.tree.map(lambda _: pl.BlockSpec(memory_space=VMEM), outs),
        scratch_shapes=list(scratch),
        cost_estimate=pl.CostEstimate(flops=flops, bytes_accessed=moved, transcendentals=0),
        compiler_params=pltpu.CompilerParams(vmem_limit_bytes=32 * 1024 * 1024),
    )(*args)


def shape(*dims, dtype=jnp.float32):
    return jax.ShapeDtypeStruct(dims, dtype)


def body(
    ln_rate,
    log_state,
    sigma,
    fric_a,
    fric_b,
    slip_dist,
    leaf_of_elem,
    near_blocks,
    near_col,
    near_count,
    far_u,
    far_v,
    far_col,
    far_rank,
    coarse_u,
    coarse_v,
):
    members = lax.axis_size("blk")
    elems = ln_rate.shape[0]
    leaf_size = near_blocks.shape[1]
    groups, rank = coarse_v.shape[0], coarse_v.shape[1]
    devices = groups * members
    width = groups * rank
    lines = pl.cdiv(width, LANES)
    sent_rows = 1 << (2 + lines).bit_length()
    integer = jnp.int32

    def swap(value, axes):
        return lax.all_to_all(value, axes, split_axis=0, concat_axis=0, tiled=True)

    def partner(value, bit):
        return lax.ppermute(value, "blk", [(i, i ^ (1 << bit)) for i in range(members)])

    elem_args = [
        value.reshape(1, elems)
        for value in (leaf_of_elem, ln_rate, log_state, sigma, fric_a, fric_b, slip_dist)
    ]
    scalar_args = [near_col, far_col, far_rank]
    weights = [
        far_u.reshape(-1, leaf_size), far_v.reshape(-1, leaf_size), coarse_v
    ]
    far_rows = weights[0].shape[0]
    bases = coarse_u.reshape(width, elems)
    sent, slot, elem_row, held, near = call(
        functools.partial(sort_kernel, members),
        (
            shape(members, -(-(3 * (elems // LANES) + 4) // 8) * 8, LANES),
            shape(1, elems, dtype=integer),
            shape(1, elems, dtype=integer),
            shape(width, elems, dtype=jnp.bfloat16),
            shape(*near_blocks.shape, dtype=jnp.bfloat16),
        ),
        *elem_args, bases, near_blocks, far=range(9),
        scratch=[VMEM(value.shape, value.dtype) for value in elem_args]
        + [pltpu.SemaphoreType.DMA((9,))],
    )
    steps = step_bits(members)
    early = bases = call(
        functools.partial(stack_foreign_kernel, groups, rank),
        shape(2 * (width - rank), elems, dtype=jnp.bfloat16),
        held, partner(bases, steps[0]), slot, flops=1 << 34, moved=1 << 26,
    )
    near_mask, far_mask, far_u, far_v, coarse_v = call(
        load_kernel,
        (
            shape(near_blocks.shape[0], members, leaf_size),
            shape(members, far_rows),
            *[shape(*value.shape, dtype=jnp.bfloat16) for value in weights[:2]],
            shape(width, elems, dtype=jnp.bfloat16),
        ),
        early, *scalar_args, *weights, far=range(1, 7),
        scratch=[SMEM(value.shape, value.dtype) for value in scalar_args]
        + [pltpu.SemaphoreType.DMA((5 + groups,))],
    )
    fields = near_count, near, far_u, far_v, near_mask, far_mask
    state, factor, rows, out = call(
        place_kernel,
        (
            shape(8, elems),
            shape(members, elems),
            shape(1, elems, dtype=integer),
            shape(devices, 1, elems + lines * LANES),
        ),
        swap(sent, "blk"), coarse_v, *fields, scalars=(2,),
        scratch=[VMEM((2, members * (elems // LANES), LANES), jnp.float32)],
        flops=1 << 20, moved=1 << 22,
    )
    for bit in steps[1:-1]:
        bases = call(
            stack_kernel, shape(2 * bases.shape[0], elems, dtype=jnp.bfloat16),
            bases, partner(bases, bit), rows, flops=1 << 34, moved=1 << 26,
        )
    bases = bases, partner(bases, steps[-1])
    elem_bases = call(
        functools.partial(element_kernel, members), shape(width - rank, elems, dtype=jnp.bfloat16),
        *bases, slot, elem_row, flops=1 << 34, moved=1 << 26,
    )
    sent = call(
        functools.partial(second_kernel, groups), shape(devices, sent_rows, LANES),
        state, factor, rows, swap(out, ("leaf", "blk")), elem_bases, coarse_v, *bases, *fields, scalars=(8,),
    )
    u, phi = call(
        functools.partial(finish_kernel, groups, width), (shape(1, elems), shape(1, elems)),
        swap(sent, ("leaf", "blk")), slot, elem_bases,
    )
    return u.reshape(elems), phi.reshape(elems)


def solution(mesh):
    each = P(("leaf", "blk"))
    blocks = P(("leaf", "blk"), None, None)
    last = P(None, None, ("leaf", "blk"))
    in_specs = (each,) * 7 + (blocks, each, each, blocks, blocks, each, each, last, last)
    return jax.shard_map(body, mesh=mesh, in_specs=in_specs, out_specs=(each, each), check_vma=False)
```

```python
import functools

import jax
import jax.numpy as jnp
from jax import lax
from jax.experimental import pallas as pl
from jax.experimental.pallas import tpu as pltpu
from jax.sharding import PartitionSpec as P

DAMPING = 0.5
PLATE_RATE = 1.0
TIME_STEP = 0.2

NN = (((1,), (0,)), ((), ()))
NT = (((1,), (1,)), ((), ()))
VMEM = pltpu.VMEM
SMEM = pltpu.SMEM

LANES = 128
HALF = 64


def dot(left, right, dims):
    return lax.dot_general(left, right, dims, preferred_element_type=jnp.float32)


def low_matrix(index_row):
    rows = lax.broadcasted_iota(jnp.int32, (LANES, index_row.shape[1]), 0)
    rows = rows.astype(jnp.float32).astype(jnp.bfloat16)
    low = (index_row & (LANES - 1)).astype(jnp.float32).astype(jnp.bfloat16)
    one = jnp.ones((), jnp.bfloat16)
    return jnp.where(rows == low, one, jnp.zeros_like(one))


def three_parts(values):
    high = values.astype(jnp.bfloat16).astype(jnp.float32)
    rest = values - high
    middle = rest.astype(jnp.bfloat16).astype(jnp.float32)
    return jnp.concatenate([high, middle, rest - middle], axis=0)


def joined(parts):
    count = parts.shape[0] // 3
    return parts[0:count] + parts[count:2 * count] + parts[2 * count:]


def scattered(values, index_row):
    parts = three_parts(values)
    count = parts.shape[0]
    high = index_row // LANES
    pieces = values.shape[1] // LANES
    left = jnp.concatenate([jnp.where(high == piece, parts, 0.0) for piece in range(pieces)], axis=0)
    moved = dot(left.astype(jnp.bfloat16), low_matrix(index_row), NT)
    return jnp.concatenate(
        [joined(moved[piece * count:(piece + 1) * count]) for piece in range(pieces)], axis=1
    )


def gathered(values, index_row):
    parts = three_parts(values)
    count = parts.shape[0]
    high = index_row // LANES
    pieces = values.shape[1] // LANES
    left = jnp.concatenate(
        [parts[:, piece * LANES:(piece + 1) * LANES] for piece in range(pieces)], axis=0
    )
    moved = dot(left.astype(jnp.bfloat16), low_matrix(index_row), NN)
    total = jnp.zeros((count, index_row.shape[1]), jnp.float32)
    for piece in range(pieces):
        total = jnp.where(high == piece, moved[piece * count:(piece + 1) * count], total)
    return joined(total)


def padded(rows, count):
    missing = count - len(rows)
    if missing:
        rows = rows + [jnp.zeros((missing, rows[0].shape[1]), jnp.float32)]
    return jnp.concatenate(rows, axis=0)


def as_lines(row):
    return jnp.concatenate(
        [row[:, i * LANES:(i + 1) * LANES] for i in range(row.shape[1] // LANES)], axis=0
    )


def peer_lanes(ref, first, members, rows, elem_count):
    width = elem_count // members
    return jnp.concatenate([ref[first + peer, 0:rows, 0:width] for peer in range(members)], axis=1)


def start_copies(sources, targets, sems):
    copies = [
        pltpu.make_async_copy(source, target, sems.at[i])
        for i, (source, target) in enumerate(zip(sources, targets))
    ]
    for copy in copies:
        copy.start()
    return copies


def sort_kernel(members, *refs):
    elem_refs, bases_ref, sent_ref, slot_ref, elem_row_ref, bases_out = refs[:7], *refs[7:12]
    elem_bufs, sems = refs[12:19], refs[19]
    copies = start_copies([*elem_refs, bases_ref], [*elem_bufs, bases_out], sems)
    mine = lax.axis_index("leaf")
    elem_count = elem_bufs[0].shape[1]
    peer_rows = elem_count // members
    pieces = elem_count // LANES
    before = lax.broadcasted_iota(jnp.int32, (LANES, LANES), 0)
    after = lax.broadcasted_iota(jnp.int32, (LANES, LANES), 1)
    triangle = jnp.where(before < after, 1.0, 0.0).astype(jnp.bfloat16)
    copies[0].wait()
    local = elem_bufs[0][...] - mine * (members * elem_count)
    target = local // elem_count
    target_row = local - target * elem_count
    peers = lax.broadcasted_iota(jnp.int32, (members, elem_count), 0)
    onehot = jnp.where(peers == target, 1.0, 0.0)
    lines = [onehot[:, i * LANES:(i + 1) * LANES] for i in range(pieces)]
    inside = dot(jnp.concatenate(lines, axis=0).astype(jnp.bfloat16), triangle, NN)
    passed = jnp.zeros((members, 1), jnp.float32)
    ranks = []
    for i, line in enumerate(lines):
        earlier = inside[i * members:(i + 1) * members] + passed
        ranks.append(jnp.sum(earlier * line, axis=0, keepdims=True))
        passed = passed + jnp.sum(line, axis=1, keepdims=True)
    slot = target * peer_rows + jnp.concatenate(ranks, axis=1).astype(jnp.int32)
    slot_ref[...] = slot
    elem_row_ref[...] = target_row
    for copy in copies[1:7]:
        copy.wait()
    u, phi, sigma, fric_a, fric_b, dist = (buf[...] for buf in elem_bufs[1:])
    velocity = jnp.exp(u)
    deficit = (PLATE_RATE - velocity).astype(jnp.bfloat16).astype(jnp.float32)
    sa = sigma * fric_a
    factor = TIME_STEP / (sa + DAMPING * velocity)
    rows = [u, phi, sa, sigma * fric_b, dist, target_row.astype(jnp.float32), deficit, factor]
    values = scattered(padded(rows, 8), slot)
    everyone = jnp.concatenate([as_lines(values[i:i + 1]) for i in (6, 5, 7)], axis=0)
    for peer in range(members):
        sent_ref[peer, 0:3 * pieces, :] = everyone
        part = values[0:6, peer * peer_rows:(peer + 1) * peer_rows]
        sent_ref[peer, 3 * pieces:3 * pieces + 4, 0:peer_rows] = part[0:4]
        sent_ref[peer, 3 * pieces:3 * pieces + 2, HALF:HALF + peer_rows] = part[4:6]
    copies[7].wait()


def load_kernel(early_ref, *refs):
    scalar_refs, weight_refs, near_mask_ref, far_mask_ref = refs[:3], refs[3:7], refs[7], refs[8]
    weight_outs, scalar_bufs, sems = refs[9:13], refs[13:16], refs[16]
    sources, targets = [*scalar_refs, *weight_refs[:3]], [*scalar_bufs, *weight_outs[:3]]
    coarse_v_ref, coarse_v_out = weight_refs[3], weight_outs[3]
    groups, rank = coarse_v_ref.shape[0], coarse_v_ref.shape[1]
    for shift in range(groups):
        place = (shift - 1) % groups * rank
        sources.append(coarse_v_ref.at[lax.axis_index("leaf") ^ shift])
        targets.append(coarse_v_out.at[pl.ds(place, rank), :])
    copies = start_copies(sources, targets, sems)
    for copy in copies[:3]:
        copy.wait()
    near_col, far_col, far_rank = scalar_bufs
    far_slots = far_col.shape[0]
    far_width = far_mask_ref.shape[1] // far_slots
    block = lax.broadcasted_iota(jnp.int32, near_mask_ref.shape[1:], 0)
    for number in range(near_mask_ref.shape[0]):
        near_mask_ref[number] = jnp.where(block == near_col[number], 1.0, 0.0)
    block = lax.broadcasted_iota(jnp.int32, far_mask_ref.shape, 0)
    lane = lax.broadcasted_iota(jnp.int32, far_mask_ref.shape, 1)
    column = jnp.full(far_mask_ref.shape, -1, jnp.int32)
    for number in range(far_slots):
        low = number * far_width
        kept = (lane >= low) & (lane < low + far_rank[number])
        column = jnp.where(kept, far_col[number], column)
    far_mask_ref[...] = jnp.where(block == column, 1.0, 0.0)
    for copy in copies[3:]:
        copy.wait()


def partial_row(deficit, coarse_v_ref):
    wide = jnp.broadcast_to(deficit, (8, deficit.shape[1])).astype(jnp.bfloat16)
    partial = dot(wide, coarse_v_ref[...], NT)[0:1]
    rest = -partial.shape[1] % LANES
    if rest:
        partial = jnp.concatenate([partial, jnp.zeros((1, rest), jnp.float32)], axis=1)
    return partial


def inside_rows(deficits, near_count, near_ref, far_u_ref, far_v_ref, near_mask_ref, far_mask_ref):
    total = jnp.zeros(deficits.shape, jnp.float32)
    for slot in range(near_ref.shape[0]):
        live = jnp.where(slot < near_count[0], 1.0, 0.0)
        source = (deficits * (near_mask_ref[slot] * live)).astype(jnp.bfloat16)
        total = total + dot(source, near_ref[slot], NT)
    project = dot(deficits.astype(jnp.bfloat16), far_v_ref[...], NT) * far_mask_ref[...]
    project = jnp.sum(project, axis=0, keepdims=True)
    project = jnp.broadcast_to(project, (8, project.shape[1])).astype(jnp.bfloat16)
    far = dot(project, far_u_ref[...], NN)
    return jnp.sum(total, axis=0, keepdims=True) + far[0:1]


def coefficients(parts_of, groups, rank):
    mine = lax.axis_index("leaf")
    lane = lax.broadcasted_iota(jnp.int32, (1, groups * rank), 1) // rank
    weights = jnp.zeros(lane.shape, jnp.float32)
    for shift in range(1, groups):
        total = jnp.sum(parts_of(mine ^ shift), axis=0, keepdims=True)
        weights = jnp.where(lane == shift - 1, total, weights)
    return weights[:, 0:(groups - 1) * rank]


def coarse_all(weights, members, bases_refs):
    row = lax.broadcasted_iota(jnp.int32, (members, weights.shape[1]), 0) ^ lax.axis_index("blk")
    total = jnp.zeros((members, bases_refs[0].shape[1]), jnp.float32)
    for number, ref in enumerate(bases_refs):
        left = []
        for place in range(members // 2):
            source = relative_member(place, number, members)
            left.append(jnp.where(row == source, weights, 0.0))
        left = jnp.concatenate(left, axis=1).astype(jnp.bfloat16)
        total = total + dot(left, ref[...], NN)
    return total


def stack_kernel(held_ref, came_ref, *refs):
    out_ref = refs[-1]
    count = held_ref.shape[0]
    out_ref[0:count, :] = held_ref[...]
    out_ref[count:2 * count, :] = came_ref[...]


def stack_foreign_kernel(groups, rank, held_ref, came_ref, *refs):
    out_ref = refs[-1]
    mine = lax.axis_index("leaf")
    place = 0
    for ref in (held_ref, came_ref):
        for shift in range(1, groups):
            out_ref[place:place + rank, :] = ref[pl.ds((mine ^ shift) * rank, rank), :]
            place += rank


def step_bits(members):
    bits = list(range(members.bit_length() - 2, -1, -1))
    return bits[:-2] + [bits[-1], bits[-2]]


def relative_member(place, number, members):
    order = step_bits(members)
    found = number << order[-1]
    for step, bit in enumerate(order[:-1]):
        found |= (place >> step & 1) << bit
    return found


def element_kernel(
    members, held_ref, came_ref, slot_ref, elem_row_ref, got_ref, out_ref, factor_ref, lines_ref
):
    factor_ref[...] = placed_blocks(got_ref, 2 * (slot_ref.shape[1] // LANES), 3, lines_ref)
    slot, row = slot_ref[...], elem_row_ref[...]
    elem_count = row.shape[1]
    kept = out_ref.shape[0]
    pieces = elem_count // LANES
    owner = (slot // (elem_count // members)) ^ lax.axis_index("blk")
    low, high = low_matrix(row), row // LANES
    total = jnp.zeros(out_ref.shape, jnp.float32)
    for number, ref in enumerate((held_ref, came_ref)):
        for place in range(members // 2):
            part = ref[place * kept:(place + 1) * kept, :]
            left = jnp.concatenate(
                [part[:, piece * LANES:(piece + 1) * LANES] for piece in range(pieces)], axis=0
            )
            found = dot(left, low, NN)
            ours = owner == relative_member(place, number, members)
            for piece in range(pieces):
                here = ours & (high == piece)
                total = jnp.where(here, found[piece * kept:(piece + 1) * kept], total)
    out_ref[...] = total.astype(jnp.bfloat16)


def placed_blocks(got_ref, first, count, lines_ref):
    members = got_ref.shape[0]
    pieces = lines_ref.shape[0] // members
    peer_rows = pieces * LANES // members
    rows_here = LANES // peer_rows * pieces
    line_row = lax.broadcasted_iota(jnp.int32, (rows_here, LANES), 0)
    lane_block = lax.broadcasted_iota(jnp.int32, (rows_here, LANES), 1) // peer_rows
    own_lane = line_row // pieces == lane_block
    for line in range(pieces):
        rows = got_ref[:, pieces + line, :].astype(jnp.int32)
        value = got_ref[:, first + line, :]
        parts = [value]
        if count == 3:
            split = three_parts(value)
            parts = [split[i * members:(i + 1) * members] for i in range(3)]
        left, right = [], []
        for peer in range(members):
            row = rows[peer:peer + 1]
            kept = own_lane & (line_row % pieces == row // LANES)
            left.append(
                jnp.concatenate([jnp.where(kept, part[peer:peer + 1], 0.0) for part in parts], axis=0)
            )
            right.append(low_matrix(row))
        left = jnp.concatenate(left, axis=1).astype(jnp.bfloat16)
        placed = dot(left, jnp.concatenate(right, axis=1), NT)
        lines_ref[line * rows_here:(line + 1) * rows_here, :] = joined(placed) if count == 3 else placed
    return jnp.concatenate(
        [lines_ref[pl.ds(piece, members, stride=pieces), :] for piece in range(pieces)], axis=1
    )


def place_kernel(got_ref, coarse_v_ref, *refs):
    field_refs, state_ref, rows_ref, out_ref, lines_ref = refs[:6], *refs[6:]
    members = got_ref.shape[0]
    elem_count = state_ref.shape[1]
    pieces = elem_count // LANES
    peer_rows = elem_count // members
    deficits = placed_blocks(got_ref, 0, 1, lines_ref)
    inside = inside_rows(deficits, *field_refs)

    first = 3 * pieces
    flat = jnp.concatenate(
        [got_ref[peer, first:first + 4, 0:peer_rows] for peer in range(members)], axis=1
    )
    rest = jnp.concatenate(
        [got_ref[peer, first:first + 2, HALF:HALF + peer_rows] for peer in range(members)], axis=1
    )
    rows = rest[1:2].astype(jnp.int32)
    rows_ref[...] = rows
    fields = [flat[i:i + 1] for i in range(4)] + [rest[0:1]]
    state = scattered(padded(fields, 8), rows)
    u, phi, sa, sb, dist = (state[i:i + 1] for i in range(5))
    velocity = jnp.exp(u)
    deficit = (PLATE_RATE - velocity).astype(jnp.bfloat16).astype(jnp.float32)
    k1p = (jnp.exp(-phi) - velocity) / dist
    u2 = u + TIME_STEP * ((inside - sb * k1p) / (sa + DAMPING * velocity))
    state_ref[...] = padded([u, phi, sa, sb, dist, k1p], 8)
    sent = jnp.concatenate([u2, partial_row(deficit, coarse_v_ref)], axis=1)
    out_ref[...] = jnp.broadcast_to(sent[None], out_ref.shape)


def second_kernel(
    groups, state_ref, factor_ref, rows_ref, all_ref, elem_bases_ref, coarse_v_ref, *refs
):
    bases_refs, field_refs, sent_ref = refs[:2], refs[2:8], refs[8]
    members, elem_count = refs[6].shape[1], state_ref.shape[1]
    width = coarse_v_ref.shape[0]
    mine, me = lax.axis_index("leaf"), lax.axis_index("blk")

    def parts_of(group):
        return all_ref[pl.ds(group * members, members), 0, elem_count:elem_count + width]

    weights = coefficients(parts_of, groups, width // groups)
    own = all_ref[pl.ds(mine * members, members), 0, 0:elem_count]
    coarse = coarse_all(weights, members, bases_refs)
    u2_all = own + factor_ref[...] * coarse
    deficits = (PLATE_RATE - jnp.exp(u2_all)).astype(jnp.bfloat16).astype(jnp.float32)
    inside = inside_rows(deficits, *field_refs)

    state = state_ref[...]
    u, phi, sa, sb, dist, k1p = (state[i:i + 1] for i in range(6))
    here = lax.broadcasted_iota(jnp.int32, u2_all.shape, 0) == me
    u2 = jnp.sum(jnp.where(here, u2_all, 0.0), axis=0, keepdims=True)
    deficit = jnp.sum(jnp.where(here, deficits, 0.0), axis=0, keepdims=True)
    phi2 = phi + TIME_STEP * k1p
    velocity = jnp.exp(u2)
    k2p = (jnp.exp(-phi2) - velocity) / dist
    inverse = 0.5 * TIME_STEP / (sa + DAMPING * velocity)
    u_next = 0.5 * (u + u2) + (inside - sb * k2p) * inverse
    phi_next = phi + 0.5 * TIME_STEP * (k1p + k2p)
    sent = gathered(padded([u_next, inverse, phi_next], 8), rows_ref[...])
    partial = as_lines(partial_row(deficit, coarse_v_ref))
    peer_rows = elem_count // members
    for device in range(groups * members):
        peer = device % members
        sent_ref[device, 0:3, 0:peer_rows] = sent[0:3, peer * peer_rows:(peer + 1) * peer_rows]
        sent_ref[device, 3:3 + partial.shape[0], :] = partial


def finish_kernel(groups, width, got_ref, slot_ref, elem_bases_ref, u_ref, phi_ref):
    elem_count = slot_ref.shape[1]
    members = got_ref.shape[0] // groups
    first = lax.axis_index("leaf") * members
    flat = peer_lanes(got_ref, first, members, 3, elem_count)
    out = gathered(padded([flat[i:i + 1] for i in range(3)], 8), slot_ref[...])

    def parts_of(group):
        sent = pl.ds(group * members, members)
        lines = [got_ref[sent, 3 + i, :] for i in range(pl.cdiv(width, LANES))]
        return jnp.concatenate(lines, axis=1)[:, 0:width]

    weights = coefficients(parts_of, groups, width // groups)
    weights = jnp.broadcast_to(weights, (8, weights.shape[1])).astype(jnp.bfloat16)
    coarse = dot(weights, elem_bases_ref[...], NN)[0:1]
    u_ref[...] = out[0:1] + out[1:2] * coarse
    phi_ref[...] = out[2:3]


def call(kernel, outs, *args, scalars=(), far=(), scratch=(), flops=1000, moved=1000):
    spaces = [SMEM if i in scalars else pl.ANY if i in far else VMEM for i in range(len(args))]
    args = [
        pltpu.with_memory_space_constraint(arg, pltpu.HBM) if i in far else arg
        for i, arg in enumerate(args)
    ]
    return pl.pallas_call(
        kernel,
        out_shape=outs,
        in_specs=[pl.BlockSpec(memory_space=space) for space in spaces],
        out_specs=jax.tree.map(lambda _: pl.BlockSpec(memory_space=VMEM), outs),
        scratch_shapes=list(scratch),
        cost_estimate=pl.CostEstimate(flops=flops, bytes_accessed=moved, transcendentals=0),
        compiler_params=pltpu.CompilerParams(vmem_limit_bytes=32 * 1024 * 1024),
    )(*args)


def shape(*dims, dtype=jnp.float32):
    return jax.ShapeDtypeStruct(dims, dtype)


def body(
    ln_rate,
    log_state,
    sigma,
    fric_a,
    fric_b,
    slip_dist,
    leaf_of_elem,
    near_blocks,
    near_col,
    near_count,
    far_u,
    far_v,
    far_col,
    far_rank,
    coarse_u,
    coarse_v,
):
    members = lax.axis_size("blk")
    elems = ln_rate.shape[0]
    leaf_size = near_blocks.shape[1]
    groups, rank = coarse_v.shape[0], coarse_v.shape[1]
    devices = groups * members
    width = groups * rank
    lines = pl.cdiv(width, LANES)
    sent_rows = 1 << (2 + lines).bit_length()
    integer = jnp.int32

    def swap(value, axes):
        return lax.all_to_all(value, axes, split_axis=0, concat_axis=0, tiled=True)

    def partner(value, bit):
        return lax.ppermute(value, "blk", [(i, i ^ (1 << bit)) for i in range(members)])

    elem_args = [
        value.reshape(1, elems)
        for value in (leaf_of_elem, ln_rate, log_state, sigma, fric_a, fric_b, slip_dist)
    ]
    scalar_args = [near_col, far_col, far_rank]
    weights = [
        near_blocks, far_u.reshape(-1, leaf_size), far_v.reshape(-1, leaf_size), coarse_v
    ]
    far_rows = weights[1].shape[0]
    bases = coarse_u.reshape(width, elems)
    sent, slot, elem_row, held = call(
        functools.partial(sort_kernel, members),
        (
            shape(members, -(-(3 * (elems // LANES) + 4) // 8) * 8, LANES),
            shape(1, elems, dtype=integer),
            shape(1, elems, dtype=integer),
            shape(width, elems, dtype=jnp.bfloat16),
        ),
        *elem_args, bases, far=range(8),
        scratch=[VMEM(value.shape, value.dtype) for value in elem_args]
        + [pltpu.SemaphoreType.DMA((8,))],
    )
    steps = step_bits(members)
    early = bases = call(
        functools.partial(stack_foreign_kernel, groups, rank),
        shape(2 * (width - rank), elems, dtype=jnp.bfloat16),
        held, partner(bases, steps[0]), slot, flops=1 << 34, moved=1 << 26,
    )
    near_mask, far_mask, near, far_u, far_v, coarse_v = call(
        load_kernel,
        (
            shape(near_blocks.shape[0], members, leaf_size),
            shape(members, far_rows),
            *[shape(*value.shape, dtype=jnp.bfloat16) for value in weights[:3]],
            shape(width, elems, dtype=jnp.bfloat16),
        ),
        early, *scalar_args, *weights, far=range(1, 8),
        scratch=[SMEM(value.shape, value.dtype) for value in scalar_args]
        + [pltpu.SemaphoreType.DMA((6 + groups,))],
    )
    fields = near_count, near, far_u, far_v, near_mask, far_mask
    got = swap(sent, "blk")
    state, rows, out = call(
        place_kernel,
        (
            shape(8, elems),
            shape(1, elems, dtype=integer),
            shape(devices, 1, elems + lines * LANES),
        ),
        got, coarse_v, *fields, scalars=(2,),
        scratch=[VMEM((members * (elems // LANES), LANES), jnp.float32)],
        flops=1 << 20, moved=1 << 22,
    )
    for bit in steps[1:-1]:
        bases = call(
            stack_kernel, shape(2 * bases.shape[0], elems, dtype=jnp.bfloat16),
            bases, partner(bases, bit), rows, flops=1 << 34, moved=1 << 26,
        )
    bases = bases, partner(bases, steps[-1])
    elem_bases, factor = call(
        functools.partial(element_kernel, members),
        (shape(width - rank, elems, dtype=jnp.bfloat16), shape(members, elems)),
        *bases, slot, elem_row, got,
        scratch=[VMEM((members * (elems // LANES), LANES), jnp.float32)],
        flops=1 << 34, moved=1 << 26,
    )
    sent = call(
        functools.partial(second_kernel, groups), shape(devices, sent_rows, LANES),
        state, factor, rows, swap(out, ("leaf", "blk")), elem_bases, coarse_v, *bases, *fields, scalars=(8,),
    )
    u, phi = call(
        functools.partial(finish_kernel, groups, width), (shape(1, elems), shape(1, elems)),
        swap(sent, ("leaf", "blk")), slot, elem_bases,
    )
    return u.reshape(elems), phi.reshape(elems)


def solution(mesh):
    each = P(("leaf", "blk"))
    blocks = P(("leaf", "blk"), None, None)
    last = P(None, None, ("leaf", "blk"))
    in_specs = (each,) * 7 + (blocks, each, each, blocks, blocks, each, each, last, last)
    return jax.shard_map(body, mesh=mesh, in_specs=in_specs, out_specs=(each, each), check_vma=False)
```

```python
import functools

import jax
import jax.numpy as jnp
from jax import lax
from jax.experimental import pallas as pl
from jax.experimental.pallas import tpu as pltpu
from jax.sharding import PartitionSpec as P

DAMPING = 0.5
PLATE_RATE = 1.0
TIME_STEP = 0.2

NN = (((1,), (0,)), ((), ()))
NT = (((1,), (1,)), ((), ()))
VMEM = pltpu.VMEM
SMEM = pltpu.SMEM

LANES = 128
HALF = 64


def dot(left, right, dims):
    return lax.dot_general(left, right, dims, preferred_element_type=jnp.float32)


def low_matrix(index_row):
    rows = lax.broadcasted_iota(jnp.int32, (LANES, index_row.shape[1]), 0)
    rows = rows.astype(jnp.float32).astype(jnp.bfloat16)
    low = (index_row & (LANES - 1)).astype(jnp.float32).astype(jnp.bfloat16)
    one = jnp.ones((), jnp.bfloat16)
    return jnp.where(rows == low, one, jnp.zeros_like(one))


def three_parts(values):
    high = values.astype(jnp.bfloat16).astype(jnp.float32)
    rest = values - high
    middle = rest.astype(jnp.bfloat16).astype(jnp.float32)
    return jnp.concatenate([high, middle, rest - middle], axis=0)


def joined(parts):
    count = parts.shape[0] // 3
    return parts[0:count] + parts[count:2 * count] + parts[2 * count:]


def scattered(values, index_row):
    parts = three_parts(values)
    count = parts.shape[0]
    high = index_row // LANES
    pieces = values.shape[1] // LANES
    left = jnp.concatenate([jnp.where(high == piece, parts, 0.0) for piece in range(pieces)], axis=0)
    moved = dot(left.astype(jnp.bfloat16), low_matrix(index_row), NT)
    return jnp.concatenate(
        [joined(moved[piece * count:(piece + 1) * count]) for piece in range(pieces)], axis=1
    )


def gathered(values, index_row):
    parts = three_parts(values)
    count = parts.shape[0]
    high = index_row // LANES
    pieces = values.shape[1] // LANES
    left = jnp.concatenate(
        [parts[:, piece * LANES:(piece + 1) * LANES] for piece in range(pieces)], axis=0
    )
    moved = dot(left.astype(jnp.bfloat16), low_matrix(index_row), NN)
    total = jnp.zeros((count, index_row.shape[1]), jnp.float32)
    for piece in range(pieces):
        total = jnp.where(high == piece, moved[piece * count:(piece + 1) * count], total)
    return joined(total)


def padded(rows, count):
    missing = count - len(rows)
    if missing:
        rows = rows + [jnp.zeros((missing, rows[0].shape[1]), jnp.float32)]
    return jnp.concatenate(rows, axis=0)


def as_lines(row):
    return jnp.concatenate(
        [row[:, i * LANES:(i + 1) * LANES] for i in range(row.shape[1] // LANES)], axis=0
    )


def peer_lanes(ref, first, members, rows, elem_count):
    width = elem_count // members
    return jnp.concatenate([ref[first + peer, 0:rows, 0:width] for peer in range(members)], axis=1)


def start_copies(sources, targets, sems):
    copies = [
        pltpu.make_async_copy(source, target, sems.at[i])
        for i, (source, target) in enumerate(zip(sources, targets))
    ]
    for copy in copies:
        copy.start()
    return copies


def sort_kernel(members, *refs):
    elem_refs, bases_ref, sent_ref, slot_ref, elem_row_ref, bases_out = refs[:7], *refs[7:12]
    elem_bufs, sems = refs[12:19], refs[19]
    copies = start_copies([*elem_refs, bases_ref], [*elem_bufs, bases_out], sems)
    mine = lax.axis_index("leaf")
    elem_count = elem_bufs[0].shape[1]
    peer_rows = elem_count // members
    pieces = elem_count // LANES
    before = lax.broadcasted_iota(jnp.int32, (LANES, LANES), 0)
    after = lax.broadcasted_iota(jnp.int32, (LANES, LANES), 1)
    triangle = jnp.where(before < after, 1.0, 0.0).astype(jnp.bfloat16)
    copies[0].wait()
    local = elem_bufs[0][...] - mine * (members * elem_count)
    target = local // elem_count
    target_row = local - target * elem_count
    peers = lax.broadcasted_iota(jnp.int32, (members, elem_count), 0)
    onehot = jnp.where(peers == target, 1.0, 0.0)
    lines = [onehot[:, i * LANES:(i + 1) * LANES] for i in range(pieces)]
    inside = dot(jnp.concatenate(lines, axis=0).astype(jnp.bfloat16), triangle, NN)
    passed = jnp.zeros((members, 1), jnp.float32)
    ranks = []
    for i, line in enumerate(lines):
        earlier = inside[i * members:(i + 1) * members] + passed
        ranks.append(jnp.sum(earlier * line, axis=0, keepdims=True))
        passed = passed + jnp.sum(line, axis=1, keepdims=True)
    slot = target * peer_rows + jnp.concatenate(ranks, axis=1).astype(jnp.int32)
    slot_ref[...] = slot
    elem_row_ref[...] = target_row
    for copy in copies[1:7]:
        copy.wait()
    u, phi, sigma, fric_a, fric_b, dist = (buf[...] for buf in elem_bufs[1:])
    velocity = jnp.exp(u)
    deficit = (PLATE_RATE - velocity).astype(jnp.bfloat16).astype(jnp.float32)
    sa = sigma * fric_a
    factor = TIME_STEP / (sa + DAMPING * velocity)
    rows = [u, phi, sa, sigma * fric_b, dist, target_row.astype(jnp.float32), deficit, factor]
    values = scattered(padded(rows, 8), slot)
    everyone = jnp.concatenate([as_lines(values[i:i + 1]) for i in (6, 5, 7)], axis=0)
    for peer in range(members):
        sent_ref[peer, 0:3 * pieces, :] = everyone
        part = values[0:6, peer * peer_rows:(peer + 1) * peer_rows]
        sent_ref[peer, 3 * pieces:3 * pieces + 4, 0:peer_rows] = part[0:4]
        sent_ref[peer, 3 * pieces:3 * pieces + 2, HALF:HALF + peer_rows] = part[4:6]
    copies[7].wait()


def load_kernel(early_ref, *refs):
    scalar_refs, weight_refs, near_mask_ref, far_mask_ref = refs[:3], refs[3:7], refs[7], refs[8]
    weight_outs, scalar_bufs, sems = refs[9:13], refs[13:16], refs[16]
    sources, targets = [*scalar_refs, *weight_refs[:3]], [*scalar_bufs, *weight_outs[:3]]
    coarse_v_ref, coarse_v_out = weight_refs[3], weight_outs[3]
    groups, rank = coarse_v_ref.shape[0], coarse_v_ref.shape[1]
    for shift in range(groups):
        place = (shift - 1) % groups * rank
        sources.append(coarse_v_ref.at[lax.axis_index("leaf") ^ shift])
        targets.append(coarse_v_out.at[pl.ds(place, rank), :])
    copies = start_copies(sources, targets, sems)
    for copy in copies[:3]:
        copy.wait()
    near_col, far_col, far_rank = scalar_bufs
    far_slots = far_col.shape[0]
    far_width = far_mask_ref.shape[1] // far_slots
    block = lax.broadcasted_iota(jnp.int32, near_mask_ref.shape[1:], 0)
    for number in range(near_mask_ref.shape[0]):
        near_mask_ref[number] = jnp.where(block == near_col[number], 1.0, 0.0)
    block = lax.broadcasted_iota(jnp.int32, far_mask_ref.shape, 0)
    lane = lax.broadcasted_iota(jnp.int32, far_mask_ref.shape, 1)
    column = jnp.full(far_mask_ref.shape, -1, jnp.int32)
    for number in range(far_slots):
        low = number * far_width
        kept = (lane >= low) & (lane < low + far_rank[number])
        column = jnp.where(kept, far_col[number], column)
    far_mask_ref[...] = jnp.where(block == column, 1.0, 0.0)
    for copy in copies[3:]:
        copy.wait()


def partial_row(deficit, coarse_v_ref):
    wide = jnp.broadcast_to(deficit, (8, deficit.shape[1])).astype(jnp.bfloat16)
    partial = dot(wide, coarse_v_ref[...], NT)[0:1]
    rest = -partial.shape[1] % LANES
    if rest:
        partial = jnp.concatenate([partial, jnp.zeros((1, rest), jnp.float32)], axis=1)
    return partial


def inside_rows(deficits, near_count, near_ref, far_u_ref, far_v_ref, near_mask_ref, far_mask_ref):
    total = jnp.zeros(deficits.shape, jnp.float32)
    for slot in range(near_ref.shape[0]):
        live = jnp.where(slot < near_count[0], 1.0, 0.0)
        source = (deficits * (near_mask_ref[slot] * live)).astype(jnp.bfloat16)
        total = total + dot(source, near_ref[slot], NT)
    project = dot(deficits.astype(jnp.bfloat16), far_v_ref[...], NT) * far_mask_ref[...]
    project = jnp.sum(project, axis=0, keepdims=True)
    project = jnp.broadcast_to(project, (8, project.shape[1])).astype(jnp.bfloat16)
    far = dot(project, far_u_ref[...], NN)
    return jnp.sum(total, axis=0, keepdims=True) + far[0:1]


def coefficients(parts_of, groups, rank):
    mine = lax.axis_index("leaf")
    lane = lax.broadcasted_iota(jnp.int32, (1, groups * rank), 1) // rank
    weights = jnp.zeros(lane.shape, jnp.float32)
    for shift in range(1, groups):
        total = jnp.sum(parts_of(mine ^ shift), axis=0, keepdims=True)
        weights = jnp.where(lane == shift - 1, total, weights)
    return weights[:, 0:(groups - 1) * rank]


def coarse_all(weights, members, bases_refs):
    row = lax.broadcasted_iota(jnp.int32, (members, weights.shape[1]), 0) ^ lax.axis_index("blk")
    total = jnp.zeros((members, bases_refs[0].shape[1]), jnp.float32)
    for number, ref in enumerate(bases_refs):
        left = []
        for place in range(members // 2):
            source = relative_member(place, number, members)
            left.append(jnp.where(row == source, weights, 0.0))
        left = jnp.concatenate(left, axis=1).astype(jnp.bfloat16)
        total = total + dot(left, ref[...], NN)
    return total


def stack_kernel(held_ref, came_ref, *refs):
    out_ref = refs[-1]
    count = held_ref.shape[0]
    out_ref[0:count, :] = held_ref[...]
    out_ref[count:2 * count, :] = came_ref[...]


def stack_foreign_kernel(groups, rank, held_ref, came_ref, *refs):
    out_ref = refs[-1]
    mine = lax.axis_index("leaf")
    place = 0
    for ref in (held_ref, came_ref):
        for shift in range(1, groups):
            out_ref[place:place + rank, :] = ref[pl.ds((mine ^ shift) * rank, rank), :]
            place += rank


def step_bits(members):
    return list(range(members.bit_length() - 2, -1, -1))


def relative_member(place, number, members):
    order = step_bits(members)
    found = number << order[-1]
    for step, bit in enumerate(order[:-1]):
        found |= (place >> step & 1) << bit
    return found


def element_kernel(
    members, held_ref, came_ref, slot_ref, elem_row_ref, got_ref, out_ref, factor_ref, lines_ref
):
    factor_ref[...] = placed_blocks(got_ref, 2 * (slot_ref.shape[1] // LANES), 3, lines_ref)
    slot, row = slot_ref[...], elem_row_ref[...]
    elem_count = row.shape[1]
    kept = out_ref.shape[0]
    pieces = elem_count // LANES
    owner = (slot // (elem_count // members)) ^ lax.axis_index("blk")
    low, high = low_matrix(row), row // LANES
    total = jnp.zeros(out_ref.shape, jnp.float32)
    for number, ref in enumerate((held_ref, came_ref)):
        for place in range(members // 2):
            part = ref[place * kept:(place + 1) * kept, :]
            left = jnp.concatenate(
                [part[:, piece * LANES:(piece + 1) * LANES] for piece in range(pieces)], axis=0
            )
            found = dot(left, low, NN)
            ours = owner == relative_member(place, number, members)
            for piece in range(pieces):
                here = ours & (high == piece)
                total = jnp.where(here, found[piece * kept:(piece + 1) * kept], total)
    out_ref[...] = total.astype(jnp.bfloat16)


def placed_blocks(got_ref, first, count, lines_ref):
    members = got_ref.shape[0]
    pieces = lines_ref.shape[0] // members
    peer_rows = pieces * LANES // members
    rows_here = LANES // peer_rows * pieces
    line_row = lax.broadcasted_iota(jnp.int32, (rows_here, LANES), 0)
    lane_block = lax.broadcasted_iota(jnp.int32, (rows_here, LANES), 1) // peer_rows
    own_lane = line_row // pieces == lane_block
    for line in range(pieces):
        rows = got_ref[:, pieces + line, :].astype(jnp.int32)
        value = got_ref[:, first + line, :]
        parts = [value]
        if count == 3:
            split = three_parts(value)
            parts = [split[i * members:(i + 1) * members] for i in range(3)]
        left, right = [], []
        for peer in range(members):
            row = rows[peer:peer + 1]
            kept = own_lane & (line_row % pieces == row // LANES)
            left.append(
                jnp.concatenate([jnp.where(kept, part[peer:peer + 1], 0.0) for part in parts], axis=0)
            )
            right.append(low_matrix(row))
        left = jnp.concatenate(left, axis=1).astype(jnp.bfloat16)
        placed = dot(left, jnp.concatenate(right, axis=1), NT)
        lines_ref[line * rows_here:(line + 1) * rows_here, :] = joined(placed) if count == 3 else placed
    return jnp.concatenate(
        [lines_ref[pl.ds(piece, members, stride=pieces), :] for piece in range(pieces)], axis=1
    )


def place_kernel(got_ref, coarse_v_ref, *refs):
    field_refs, state_ref, rows_ref, out_ref, lines_ref = refs[:6], *refs[6:]
    members = got_ref.shape[0]
    elem_count = state_ref.shape[1]
    pieces = elem_count // LANES
    peer_rows = elem_count // members
    deficits = placed_blocks(got_ref, 0, 1, lines_ref)
    inside = inside_rows(deficits, *field_refs)

    first = 3 * pieces
    flat = jnp.concatenate(
        [got_ref[peer, first:first + 4, 0:peer_rows] for peer in range(members)], axis=1
    )
    rest = jnp.concatenate(
        [got_ref[peer, first:first + 2, HALF:HALF + peer_rows] for peer in range(members)], axis=1
    )
    rows = rest[1:2].astype(jnp.int32)
    rows_ref[...] = rows
    fields = [flat[i:i + 1] for i in range(4)] + [rest[0:1]]
    state = scattered(padded(fields, 8), rows)
    u, phi, sa, sb, dist = (state[i:i + 1] for i in range(5))
    velocity = jnp.exp(u)
    deficit = (PLATE_RATE - velocity).astype(jnp.bfloat16).astype(jnp.float32)
    k1p = (jnp.exp(-phi) - velocity) / dist
    u2 = u + TIME_STEP * ((inside - sb * k1p) / (sa + DAMPING * velocity))
    state_ref[...] = padded([u, phi, sa, sb, dist, k1p], 8)
    sent = jnp.concatenate([u2, partial_row(deficit, coarse_v_ref)], axis=1)
    out_ref[...] = jnp.broadcast_to(sent[None], out_ref.shape)


def second_kernel(
    groups, state_ref, factor_ref, rows_ref, all_ref, elem_bases_ref, coarse_v_ref, *refs
):
    bases_refs, field_refs, sent_ref = refs[:2], refs[2:8], refs[8]
    members, elem_count = refs[6].shape[1], state_ref.shape[1]
    width = coarse_v_ref.shape[0]
    mine, me = lax.axis_index("leaf"), lax.axis_index("blk")

    def parts_of(group):
        return all_ref[pl.ds(group * members, members), 0, elem_count:elem_count + width]

    weights = coefficients(parts_of, groups, width // groups)
    own = all_ref[pl.ds(mine * members, members), 0, 0:elem_count]
    coarse = coarse_all(weights, members, bases_refs)
    u2_all = own + factor_ref[...] * coarse
    deficits = (PLATE_RATE - jnp.exp(u2_all)).astype(jnp.bfloat16).astype(jnp.float32)
    inside = inside_rows(deficits, *field_refs)

    state = state_ref[...]
    u, phi, sa, sb, dist, k1p = (state[i:i + 1] for i in range(6))
    here = lax.broadcasted_iota(jnp.int32, u2_all.shape, 0) == me
    u2 = jnp.sum(jnp.where(here, u2_all, 0.0), axis=0, keepdims=True)
    deficit = jnp.sum(jnp.where(here, deficits, 0.0), axis=0, keepdims=True)
    phi2 = phi + TIME_STEP * k1p
    velocity = jnp.exp(u2)
    k2p = (jnp.exp(-phi2) - velocity) / dist
    inverse = 0.5 * TIME_STEP / (sa + DAMPING * velocity)
    u_next = 0.5 * (u + u2) + (inside - sb * k2p) * inverse
    phi_next = phi + 0.5 * TIME_STEP * (k1p + k2p)
    sent = gathered(padded([u_next, inverse, phi_next], 8), rows_ref[...])
    partial = as_lines(partial_row(deficit, coarse_v_ref))
    peer_rows = elem_count // members
    for device in range(groups * members):
        peer = device % members
        sent_ref[device, 0:3, 0:peer_rows] = sent[0:3, peer * peer_rows:(peer + 1) * peer_rows]
        sent_ref[device, 3:3 + partial.shape[0], :] = partial


def finish_kernel(groups, width, got_ref, slot_ref, elem_bases_ref, u_ref, phi_ref):
    elem_count = slot_ref.shape[1]
    members = got_ref.shape[0] // groups
    first = lax.axis_index("leaf") * members
    flat = peer_lanes(got_ref, first, members, 3, elem_count)
    out = gathered(padded([flat[i:i + 1] for i in range(3)], 8), slot_ref[...])

    def parts_of(group):
        sent = pl.ds(group * members, members)
        lines = [got_ref[sent, 3 + i, :] for i in range(pl.cdiv(width, LANES))]
        return jnp.concatenate(lines, axis=1)[:, 0:width]

    weights = coefficients(parts_of, groups, width // groups)
    weights = jnp.broadcast_to(weights, (8, weights.shape[1])).astype(jnp.bfloat16)
    coarse = dot(weights, elem_bases_ref[...], NN)[0:1]
    u_ref[...] = out[0:1] + out[1:2] * coarse
    phi_ref[...] = out[2:3]


def call(kernel, outs, *args, scalars=(), far=(), scratch=(), flops=1000, moved=1000):
    spaces = [SMEM if i in scalars else pl.ANY if i in far else VMEM for i in range(len(args))]
    args = [
        pltpu.with_memory_space_constraint(arg, pltpu.HBM) if i in far else arg
        for i, arg in enumerate(args)
    ]
    return pl.pallas_call(
        kernel,
        out_shape=outs,
        in_specs=[pl.BlockSpec(memory_space=space) for space in spaces],
        out_specs=jax.tree.map(lambda _: pl.BlockSpec(memory_space=VMEM), outs),
        scratch_shapes=list(scratch),
        cost_estimate=pl.CostEstimate(flops=flops, bytes_accessed=moved, transcendentals=0),
        compiler_params=pltpu.CompilerParams(vmem_limit_bytes=32 * 1024 * 1024),
    )(*args)


def shape(*dims, dtype=jnp.float32):
    return jax.ShapeDtypeStruct(dims, dtype)


def body(
    ln_rate,
    log_state,
    sigma,
    fric_a,
    fric_b,
    slip_dist,
    leaf_of_elem,
    near_blocks,
    near_col,
    near_count,
    far_u,
    far_v,
    far_col,
    far_rank,
    coarse_u,
    coarse_v,
):
    members = lax.axis_size("blk")
    elems = ln_rate.shape[0]
    leaf_size = near_blocks.shape[1]
    groups, rank = coarse_v.shape[0], coarse_v.shape[1]
    devices = groups * members
    width = groups * rank
    lines = pl.cdiv(width, LANES)
    sent_rows = 1 << (2 + lines).bit_length()
    integer = jnp.int32

    def swap(value, axes):
        return lax.all_to_all(value, axes, split_axis=0, concat_axis=0, tiled=True)

    def partner(value, bit):
        return lax.ppermute(value, "blk", [(i, i ^ (1 << bit)) for i in range(members)])

    elem_args = [
        value.reshape(1, elems)
        for value in (leaf_of_elem, ln_rate, log_state, sigma, fric_a, fric_b, slip_dist)
    ]
    scalar_args = [near_col, far_col, far_rank]
    weights = [
        near_blocks, far_u.reshape(-1, leaf_size), far_v.reshape(-1, leaf_size), coarse_v
    ]
    far_rows = weights[1].shape[0]
    bases = coarse_u.reshape(width, elems)
    sent, slot, elem_row, held = call(
        functools.partial(sort_kernel, members),
        (
            shape(members, -(-(3 * (elems // LANES) + 4) // 8) * 8, LANES),
            shape(1, elems, dtype=integer),
            shape(1, elems, dtype=integer),
            shape(width, elems, dtype=jnp.bfloat16),
        ),
        *elem_args, bases, far=range(8),
        scratch=[VMEM(value.shape, value.dtype) for value in elem_args]
        + [pltpu.SemaphoreType.DMA((8,))],
    )
    steps = step_bits(members)
    early = bases = call(
        functools.partial(stack_foreign_kernel, groups, rank),
        shape(2 * (width - rank), elems, dtype=jnp.bfloat16),
        held, partner(bases, steps[0]), slot, flops=1 << 34, moved=1 << 26,
    )
    near_mask, far_mask, near, far_u, far_v, coarse_v = call(
        load_kernel,
        (
            shape(near_blocks.shape[0], members, leaf_size),
            shape(members, far_rows),
            *[shape(*value.shape, dtype=jnp.bfloat16) for value in weights[:3]],
            shape(width, elems, dtype=jnp.bfloat16),
        ),
        early, *scalar_args, *weights, far=range(1, 8),
        scratch=[SMEM(value.shape, value.dtype) for value in scalar_args]
        + [pltpu.SemaphoreType.DMA((6 + groups,))],
    )
    fields = near_count, near, far_u, far_v, near_mask, far_mask
    got = swap(sent, "blk")
    state, rows, out = call(
        place_kernel,
        (
            shape(8, elems),
            shape(1, elems, dtype=integer),
            shape(devices, 1, elems + lines * LANES),
        ),
        got, coarse_v, *fields, scalars=(2,),
        scratch=[VMEM((members * (elems // LANES), LANES), jnp.float32)],
        flops=1 << 20, moved=1 << 22,
    )
    for bit in steps[1:-1]:
        bases = call(
            stack_kernel, shape(2 * bases.shape[0], elems, dtype=jnp.bfloat16),
            bases, partner(bases, bit), rows, flops=1 << 34, moved=1 << 26,
        )
    bases = bases, partner(bases, steps[-1])
    elem_bases, factor = call(
        functools.partial(element_kernel, members),
        (shape(width - rank, elems, dtype=jnp.bfloat16), shape(members, elems)),
        *bases, slot, elem_row, got,
        scratch=[VMEM((members * (elems // LANES), LANES), jnp.float32)],
        flops=1 << 34, moved=1 << 26,
    )
    sent = call(
        functools.partial(second_kernel, groups), shape(devices, sent_rows, LANES),
        state, factor, rows, swap(out, ("leaf", "blk")), elem_bases, coarse_v, *bases, *fields, scalars=(8,),
    )
    u, phi = call(
        functools.partial(finish_kernel, groups, width), (shape(1, elems), shape(1, elems)),
        swap(sent, ("leaf", "blk")), slot, elem_bases,
    )
    return u.reshape(elems), phi.reshape(elems)


def solution(mesh):
    each = P(("leaf", "blk"))
    blocks = P(("leaf", "blk"), None, None)
    last = P(None, None, ("leaf", "blk"))
    in_specs = (each,) * 7 + (blocks, each, each, blocks, blocks, each, each, last, last)
    return jax.shard_map(body, mesh=mesh, in_specs=in_specs, out_specs=(each, each), check_vma=False)
```

```python
import functools

import jax
import jax.numpy as jnp
from jax import lax
from jax.experimental import pallas as pl
from jax.experimental.pallas import tpu as pltpu
from jax.sharding import PartitionSpec as P

DAMPING = 0.5
PLATE_RATE = 1.0
TIME_STEP = 0.2

NN = (((1,), (0,)), ((), ()))
NT = (((1,), (1,)), ((), ()))
VMEM = pltpu.VMEM
SMEM = pltpu.SMEM

LANES = 128
HALF = 64


def dot(left, right, dims):
    return lax.dot_general(left, right, dims, preferred_element_type=jnp.float32)


def low_matrix(index_row):
    rows = lax.broadcasted_iota(jnp.int32, (LANES, index_row.shape[1]), 0)
    rows = rows.astype(jnp.float32).astype(jnp.bfloat16)
    low = (index_row & (LANES - 1)).astype(jnp.float32).astype(jnp.bfloat16)
    one = jnp.ones((), jnp.bfloat16)
    return jnp.where(rows == low, one, jnp.zeros_like(one))


def three_parts(values):
    high = values.astype(jnp.bfloat16).astype(jnp.float32)
    rest = values - high
    middle = rest.astype(jnp.bfloat16).astype(jnp.float32)
    return jnp.concatenate([high, middle, rest - middle], axis=0)


def joined(parts):
    count = parts.shape[0] // 3
    return parts[0:count] + parts[count:2 * count] + parts[2 * count:]


def scattered(values, index_row):
    parts = three_parts(values)
    count = parts.shape[0]
    high = index_row // LANES
    pieces = values.shape[1] // LANES
    left = jnp.concatenate([jnp.where(high == piece, parts, 0.0) for piece in range(pieces)], axis=0)
    moved = dot(left.astype(jnp.bfloat16), low_matrix(index_row), NT)
    return jnp.concatenate(
        [joined(moved[piece * count:(piece + 1) * count]) for piece in range(pieces)], axis=1
    )


def gathered(values, index_row, low):
    parts = three_parts(values)
    count = parts.shape[0]
    high = index_row // LANES
    pieces = values.shape[1] // LANES
    left = jnp.concatenate(
        [parts[:, piece * LANES:(piece + 1) * LANES] for piece in range(pieces)], axis=0
    )
    moved = dot(left.astype(jnp.bfloat16), low, NN)
    total = jnp.zeros((count, index_row.shape[1]), jnp.float32)
    for piece in range(pieces):
        total = jnp.where(high == piece, moved[piece * count:(piece + 1) * count], total)
    return joined(total)


def padded(rows, count):
    missing = count - len(rows)
    if missing:
        rows = rows + [jnp.zeros((missing, rows[0].shape[1]), jnp.float32)]
    return jnp.concatenate(rows, axis=0)


def as_lines(row):
    return jnp.concatenate(
        [row[:, i * LANES:(i + 1) * LANES] for i in range(row.shape[1] // LANES)], axis=0
    )


def peer_lanes(ref, first, members, rows, elem_count):
    width = elem_count // members
    return jnp.concatenate([ref[first + peer, 0:rows, 0:width] for peer in range(members)], axis=1)


def start_copies(sources, targets, sems):
    copies = [
        pltpu.make_async_copy(source, target, sems.at[i])
        for i, (source, target) in enumerate(zip(sources, targets))
    ]
    for copy in copies:
        copy.start()
    return copies


def sort_kernel(members, *refs):
    elem_refs, bases_ref, sent_ref, slot_ref, elem_row_ref, bases_out = refs[:7], *refs[7:12]
    elem_bufs, sems = refs[12:19], refs[19]
    copies = start_copies([*elem_refs, bases_ref], [*elem_bufs, bases_out], sems)
    mine = lax.axis_index("leaf")
    elem_count = elem_bufs[0].shape[1]
    peer_rows = elem_count // members
    pieces = elem_count // LANES
    before = lax.broadcasted_iota(jnp.int32, (LANES, LANES), 0)
    after = lax.broadcasted_iota(jnp.int32, (LANES, LANES), 1)
    triangle = jnp.where(before < after, 1.0, 0.0).astype(jnp.bfloat16)
    copies[0].wait()
    local = elem_bufs[0][...] - mine * (members * elem_count)
    target = local // elem_count
    target_row = local - target * elem_count
    peers = lax.broadcasted_iota(jnp.int32, (members, elem_count), 0)
    onehot = jnp.where(peers == target, 1.0, 0.0)
    lines = [onehot[:, i * LANES:(i + 1) * LANES] for i in range(pieces)]
    inside = dot(jnp.concatenate(lines, axis=0).astype(jnp.bfloat16), triangle, NN)
    passed = jnp.zeros((members, 1), jnp.float32)
    ranks = []
    for i, line in enumerate(lines):
        earlier = inside[i * members:(i + 1) * members] + passed
        ranks.append(jnp.sum(earlier * line, axis=0, keepdims=True))
        passed = passed + jnp.sum(line, axis=1, keepdims=True)
    slot = target * peer_rows + jnp.concatenate(ranks, axis=1).astype(jnp.int32)
    slot_ref[...] = slot
    elem_row_ref[...] = target_row
    for copy in copies[1:7]:
        copy.wait()
    u, phi, sigma, fric_a, fric_b, dist = (buf[...] for buf in elem_bufs[1:])
    velocity = jnp.exp(u)
    deficit = (PLATE_RATE - velocity).astype(jnp.bfloat16).astype(jnp.float32)
    sa = sigma * fric_a
    factor = TIME_STEP / (sa + DAMPING * velocity)
    rows = [u, phi, sa, sigma * fric_b, dist, target_row.astype(jnp.float32), deficit, factor]
    values = scattered(padded(rows, 8), slot)
    everyone = jnp.concatenate([as_lines(values[i:i + 1]) for i in (6, 5, 7)], axis=0)
    for peer in range(members):
        sent_ref[peer, 0:3 * pieces, :] = everyone
        part = values[0:6, peer * peer_rows:(peer + 1) * peer_rows]
        sent_ref[peer, 3 * pieces:3 * pieces + 4, 0:peer_rows] = part[0:4]
        sent_ref[peer, 3 * pieces:3 * pieces + 2, HALF:HALF + peer_rows] = part[4:6]
    copies[7].wait()


def load_kernel(early_ref, *refs):
    scalar_refs, weight_refs, near_mask_ref, far_mask_ref = refs[:3], refs[3:7], refs[7], refs[8]
    weight_outs, scalar_bufs, sems = refs[9:13], refs[13:16], refs[16]
    sources, targets = [*scalar_refs, *weight_refs[:3]], [*scalar_bufs, *weight_outs[:3]]
    coarse_v_ref, coarse_v_out = weight_refs[3], weight_outs[3]
    groups, rank = coarse_v_ref.shape[0], coarse_v_ref.shape[1]
    for shift in range(groups):
        place = (shift - 1) % groups * rank
        sources.append(coarse_v_ref.at[lax.axis_index("leaf") ^ shift])
        targets.append(coarse_v_out.at[pl.ds(place, rank), :])
    copies = start_copies(sources, targets, sems)
    for copy in copies[:3]:
        copy.wait()
    near_col, far_col, far_rank = scalar_bufs
    far_slots = far_col.shape[0]
    far_width = far_mask_ref.shape[1] // far_slots
    block = lax.broadcasted_iota(jnp.int32, near_mask_ref.shape[1:], 0)
    for number in range(near_mask_ref.shape[0]):
        near_mask_ref[number] = jnp.where(block == near_col[number], 1.0, 0.0)
    block = lax.broadcasted_iota(jnp.int32, far_mask_ref.shape, 0)
    lane = lax.broadcasted_iota(jnp.int32, far_mask_ref.shape, 1)
    column = jnp.full(far_mask_ref.shape, -1, jnp.int32)
    for number in range(far_slots):
        low = number * far_width
        kept = (lane >= low) & (lane < low + far_rank[number])
        column = jnp.where(kept, far_col[number], column)
    far_mask_ref[...] = jnp.where(block == column, 1.0, 0.0)
    for copy in copies[3:]:
        copy.wait()


def partial_row(deficit, coarse_v_ref):
    wide = jnp.broadcast_to(deficit, (8, deficit.shape[1])).astype(jnp.bfloat16)
    partial = dot(wide, coarse_v_ref[...], NT)[0:1]
    rest = -partial.shape[1] % LANES
    if rest:
        partial = jnp.concatenate([partial, jnp.zeros((1, rest), jnp.float32)], axis=1)
    return partial


def inside_rows(deficits, near_count, near_ref, far_u_ref, far_v_ref, near_mask_ref, far_mask_ref):
    total = jnp.zeros(deficits.shape, jnp.float32)
    for slot in range(near_ref.shape[0]):
        live = jnp.where(slot < near_count[0], 1.0, 0.0)
        source = (deficits * (near_mask_ref[slot] * live)).astype(jnp.bfloat16)
        total = total + dot(source, near_ref[slot], NT)
    project = dot(deficits.astype(jnp.bfloat16), far_v_ref[...], NT) * far_mask_ref[...]
    project = jnp.sum(project, axis=0, keepdims=True)
    project = jnp.broadcast_to(project, (8, project.shape[1])).astype(jnp.bfloat16)
    far = dot(project, far_u_ref[...], NN)
    return jnp.sum(total, axis=0, keepdims=True) + far[0:1]


def coefficients(parts_of, groups, rank):
    mine = lax.axis_index("leaf")
    lane = lax.broadcasted_iota(jnp.int32, (1, groups * rank), 1) // rank
    weights = jnp.zeros(lane.shape, jnp.float32)
    for shift in range(1, groups):
        total = jnp.sum(parts_of(mine ^ shift), axis=0, keepdims=True)
        weights = jnp.where(lane == shift - 1, total, weights)
    return weights[:, 0:(groups - 1) * rank]


def coarse_all(weights, members, bases_refs):
    row = lax.broadcasted_iota(jnp.int32, (members, weights.shape[1]), 0) ^ lax.axis_index("blk")
    total = jnp.zeros((members, bases_refs[0].shape[1]), jnp.float32)
    for number, ref in enumerate(bases_refs):
        left = []
        for place in range(members // 2):
            source = relative_member(place, number, members)
            left.append(jnp.where(row == source, weights, 0.0))
        left = jnp.concatenate(left, axis=1).astype(jnp.bfloat16)
        total = total + dot(left, ref[...], NN)
    return total


def stack_kernel(held_ref, came_ref, *refs):
    out_ref = refs[-1]
    count = held_ref.shape[0]
    out_ref[0:count, :] = held_ref[...]
    out_ref[count:2 * count, :] = came_ref[...]


def stack_foreign_kernel(groups, rank, held_ref, came_ref, *refs):
    out_ref = refs[-1]
    mine = lax.axis_index("leaf")
    place = 0
    for ref in (held_ref, came_ref):
        for shift in range(1, groups):
            out_ref[place:place + rank, :] = ref[pl.ds((mine ^ shift) * rank, rank), :]
            place += rank


def step_bits(members):
    bits = list(range(members.bit_length() - 2, -1, -1))
    return bits[:-2] + [bits[-1], bits[-2]]


def relative_member(place, number, members):
    order = step_bits(members)
    found = number << order[-1]
    for step, bit in enumerate(order[:-1]):
        found |= (place >> step & 1) << bit
    return found


def element_kernel(
    members, held_ref, came_ref, slot_ref, elem_row_ref, got_ref, rows_ref,
    out_ref, factor_ref, rows_low_ref, slot_low_ref, lines_ref
):
    rows_low_ref[...] = low_matrix(rows_ref[...])
    slot_low_ref[...] = low_matrix(slot_ref[...])
    factor_ref[...] = placed_blocks(got_ref, 2 * (slot_ref.shape[1] // LANES), 3, lines_ref)
    slot, row = slot_ref[...], elem_row_ref[...]
    elem_count = row.shape[1]
    kept = out_ref.shape[0]
    pieces = elem_count // LANES
    owner = (slot // (elem_count // members)) ^ lax.axis_index("blk")
    low, high = low_matrix(row), row // LANES
    total = jnp.zeros(out_ref.shape, jnp.float32)
    for number, ref in enumerate((held_ref, came_ref)):
        for place in range(members // 2):
            part = ref[place * kept:(place + 1) * kept, :]
            left = jnp.concatenate(
                [part[:, piece * LANES:(piece + 1) * LANES] for piece in range(pieces)], axis=0
            )
            found = dot(left, low, NN)
            ours = owner == relative_member(place, number, members)
            for piece in range(pieces):
                here = ours & (high == piece)
                total = jnp.where(here, found[piece * kept:(piece + 1) * kept], total)
    out_ref[...] = total.astype(jnp.bfloat16)


def placed_blocks(got_ref, first, count, lines_ref):
    members = got_ref.shape[0]
    pieces = lines_ref.shape[0] // members
    peer_rows = pieces * LANES // members
    rows_here = LANES // peer_rows * pieces
    line_row = lax.broadcasted_iota(jnp.int32, (rows_here, LANES), 0)
    lane_block = lax.broadcasted_iota(jnp.int32, (rows_here, LANES), 1) // peer_rows
    own_lane = line_row // pieces == lane_block
    for line in range(pieces):
        rows = got_ref[:, pieces + line, :].astype(jnp.int32)
        value = got_ref[:, first + line, :]
        parts = [value]
        if count == 3:
            split = three_parts(value)
            parts = [split[i * members:(i + 1) * members] for i in range(3)]
        left, right = [], []
        for peer in range(members):
            row = rows[peer:peer + 1]
            kept = own_lane & (line_row % pieces == row // LANES)
            left.append(
                jnp.concatenate([jnp.where(kept, part[peer:peer + 1], 0.0) for part in parts], axis=0)
            )
            right.append(low_matrix(row))
        left = jnp.concatenate(left, axis=1).astype(jnp.bfloat16)
        placed = dot(left, jnp.concatenate(right, axis=1), NT)
        lines_ref[line * rows_here:(line + 1) * rows_here, :] = joined(placed) if count == 3 else placed
    return jnp.concatenate(
        [lines_ref[pl.ds(piece, members, stride=pieces), :] for piece in range(pieces)], axis=1
    )


def place_kernel(got_ref, coarse_v_ref, *refs):
    field_refs, state_ref, rows_ref, out_ref, lines_ref = refs[:6], *refs[6:]
    members = got_ref.shape[0]
    elem_count = state_ref.shape[1]
    pieces = elem_count // LANES
    peer_rows = elem_count // members
    deficits = placed_blocks(got_ref, 0, 1, lines_ref)
    inside = inside_rows(deficits, *field_refs)

    first = 3 * pieces
    flat = jnp.concatenate(
        [got_ref[peer, first:first + 4, 0:peer_rows] for peer in range(members)], axis=1
    )
    rest = jnp.concatenate(
        [got_ref[peer, first:first + 2, HALF:HALF + peer_rows] for peer in range(members)], axis=1
    )
    rows = rest[1:2].astype(jnp.int32)
    rows_ref[...] = rows
    fields = [flat[i:i + 1] for i in range(4)] + [rest[0:1]]
    state = scattered(padded(fields, 8), rows)
    u, phi, sa, sb, dist = (state[i:i + 1] for i in range(5))
    velocity = jnp.exp(u)
    deficit = (PLATE_RATE - velocity).astype(jnp.bfloat16).astype(jnp.float32)
    k1p = (jnp.exp(-phi) - velocity) / dist
    u2 = u + TIME_STEP * ((inside - sb * k1p) / (sa + DAMPING * velocity))
    state_ref[...] = padded([u, phi, sa, sb, dist, k1p], 8)
    sent = jnp.concatenate([u2, partial_row(deficit, coarse_v_ref)], axis=1)
    out_ref[...] = jnp.broadcast_to(sent[None], out_ref.shape)


def second_kernel(
    groups, state_ref, factor_ref, rows_ref, rows_low_ref, all_ref, elem_bases_ref, coarse_v_ref, *refs
):
    bases_refs, field_refs, sent_ref = refs[:2], refs[2:8], refs[8]
    members, elem_count = refs[6].shape[1], state_ref.shape[1]
    width = coarse_v_ref.shape[0]
    mine, me = lax.axis_index("leaf"), lax.axis_index("blk")

    def parts_of(group):
        return all_ref[pl.ds(group * members, members), 0, elem_count:elem_count + width]

    weights = coefficients(parts_of, groups, width // groups)
    own = all_ref[pl.ds(mine * members, members), 0, 0:elem_count]
    coarse = coarse_all(weights, members, bases_refs)
    u2_all = own + factor_ref[...] * coarse
    deficits = (PLATE_RATE - jnp.exp(u2_all)).astype(jnp.bfloat16).astype(jnp.float32)
    inside = inside_rows(deficits, *field_refs)

    state = state_ref[...]
    u, phi, sa, sb, dist, k1p = (state[i:i + 1] for i in range(6))
    here = lax.broadcasted_iota(jnp.int32, u2_all.shape, 0) == me
    u2 = jnp.sum(jnp.where(here, u2_all, 0.0), axis=0, keepdims=True)
    deficit = jnp.sum(jnp.where(here, deficits, 0.0), axis=0, keepdims=True)
    phi2 = phi + TIME_STEP * k1p
    velocity = jnp.exp(u2)
    k2p = (jnp.exp(-phi2) - velocity) / dist
    inverse = 0.5 * TIME_STEP / (sa + DAMPING * velocity)
    u_next = 0.5 * (u + u2) + (inside - sb * k2p) * inverse
    phi_next = phi + 0.5 * TIME_STEP * (k1p + k2p)
    sent = gathered(padded([u_next, inverse, phi_next], 8), rows_ref[...], rows_low_ref[...])
    partial = as_lines(partial_row(deficit, coarse_v_ref))
    peer_rows = elem_count // members
    for device in range(groups * members):
        peer = device % members
        sent_ref[device, 0:3, 0:peer_rows] = sent[0:3, peer * peer_rows:(peer + 1) * peer_rows]
        sent_ref[device, 3:3 + partial.shape[0], :] = partial


def finish_kernel(groups, width, got_ref, slot_ref, slot_low_ref, elem_bases_ref, u_ref, phi_ref):
    elem_count = slot_ref.shape[1]
    members = got_ref.shape[0] // groups
    first = lax.axis_index("leaf") * members
    flat = peer_lanes(got_ref, first, members, 3, elem_count)
    out = gathered(padded([flat[i:i + 1] for i in range(3)], 8), slot_ref[...], slot_low_ref[...])

    def parts_of(group):
        sent = pl.ds(group * members, members)
        lines = [got_ref[sent, 3 + i, :] for i in range(pl.cdiv(width, LANES))]
        return jnp.concatenate(lines, axis=1)[:, 0:width]

    weights = coefficients(parts_of, groups, width // groups)
    weights = jnp.broadcast_to(weights, (8, weights.shape[1])).astype(jnp.bfloat16)
    coarse = dot(weights, elem_bases_ref[...], NN)[0:1]
    u_ref[...] = out[0:1] + out[1:2] * coarse
    phi_ref[...] = out[2:3]


def call(kernel, outs, *args, scalars=(), far=(), scratch=(), flops=1000, moved=1000):
    spaces = [SMEM if i in scalars else pl.ANY if i in far else VMEM for i in range(len(args))]
    args = [
        pltpu.with_memory_space_constraint(arg, pltpu.HBM) if i in far else arg
        for i, arg in enumerate(args)
    ]
    return pl.pallas_call(
        kernel,
        out_shape=outs,
        in_specs=[pl.BlockSpec(memory_space=space) for space in spaces],
        out_specs=jax.tree.map(lambda _: pl.BlockSpec(memory_space=VMEM), outs),
        scratch_shapes=list(scratch),
        cost_estimate=pl.CostEstimate(flops=flops, bytes_accessed=moved, transcendentals=0),
        compiler_params=pltpu.CompilerParams(vmem_limit_bytes=32 * 1024 * 1024),
    )(*args)


def shape(*dims, dtype=jnp.float32):
    return jax.ShapeDtypeStruct(dims, dtype)


def body(
    ln_rate,
    log_state,
    sigma,
    fric_a,
    fric_b,
    slip_dist,
    leaf_of_elem,
    near_blocks,
    near_col,
    near_count,
    far_u,
    far_v,
    far_col,
    far_rank,
    coarse_u,
    coarse_v,
):
    members = lax.axis_size("blk")
    elems = ln_rate.shape[0]
    leaf_size = near_blocks.shape[1]
    groups, rank = coarse_v.shape[0], coarse_v.shape[1]
    devices = groups * members
    width = groups * rank
    lines = pl.cdiv(width, LANES)
    sent_rows = 1 << (2 + lines).bit_length()
    integer = jnp.int32

    def swap(value, axes):
        return lax.all_to_all(value, axes, split_axis=0, concat_axis=0, tiled=True)

    def partner(value, bit):
        return lax.ppermute(value, "blk", [(i, i ^ (1 << bit)) for i in range(members)])

    elem_args = [
        value.reshape(1, elems)
        for value in (leaf_of_elem, ln_rate, log_state, sigma, fric_a, fric_b, slip_dist)
    ]
    scalar_args = [near_col, far_col, far_rank]
    weights = [
        near_blocks, far_u.reshape(-1, leaf_size), far_v.reshape(-1, leaf_size), coarse_v
    ]
    far_rows = weights[1].shape[0]
    bases = coarse_u.reshape(width, elems)
    sent, slot, elem_row, held = call(
        functools.partial(sort_kernel, members),
        (
            shape(members, -(-(3 * (elems // LANES) + 4) // 8) * 8, LANES),
            shape(1, elems, dtype=integer),
            shape(1, elems, dtype=integer),
            shape(width, elems, dtype=jnp.bfloat16),
        ),
        *elem_args, bases, far=range(8),
        scratch=[VMEM(value.shape, value.dtype) for value in elem_args]
        + [pltpu.SemaphoreType.DMA((8,))],
    )
    steps = step_bits(members)
    early = bases = call(
        functools.partial(stack_foreign_kernel, groups, rank),
        shape(2 * (width - rank), elems, dtype=jnp.bfloat16),
        held, partner(bases, steps[0]), slot, flops=1 << 34, moved=1 << 26,
    )
    near_mask, far_mask, near, far_u, far_v, coarse_v = call(
        load_kernel,
        (
            shape(near_blocks.shape[0], members, leaf_size),
            shape(members, far_rows),
            *[shape(*value.shape, dtype=jnp.bfloat16) for value in weights[:3]],
            shape(width, elems, dtype=jnp.bfloat16),
        ),
        early, *scalar_args, *weights, far=range(1, 8),
        scratch=[SMEM(value.shape, value.dtype) for value in scalar_args]
        + [pltpu.SemaphoreType.DMA((6 + groups,))],
    )
    fields = near_count, near, far_u, far_v, near_mask, far_mask
    got = swap(sent, "blk")
    state, rows, out = call(
        place_kernel,
        (
            shape(8, elems),
            shape(1, elems, dtype=integer),
            shape(devices, 1, elems + lines * LANES),
        ),
        got, coarse_v, *fields, scalars=(2,),
        scratch=[VMEM((members * (elems // LANES), LANES), jnp.float32)],
        flops=1 << 20, moved=1 << 22,
    )
    for bit in steps[1:-1]:
        bases = call(
            stack_kernel, shape(2 * bases.shape[0], elems, dtype=jnp.bfloat16),
            bases, partner(bases, bit), rows, flops=1 << 34, moved=1 << 26,
        )
    bases = bases, partner(bases, steps[-1])
    elem_bases, factor, rows_low, slot_low = call(
        functools.partial(element_kernel, members),
        (
            shape(width - rank, elems, dtype=jnp.bfloat16),
            shape(members, elems),
            shape(LANES, elems, dtype=jnp.bfloat16),
            shape(LANES, elems, dtype=jnp.bfloat16),
        ),
        *bases, slot, elem_row, got, rows,
        scratch=[VMEM((members * (elems // LANES), LANES), jnp.float32)],
        flops=1 << 34, moved=1 << 26,
    )
    sent = call(
        functools.partial(second_kernel, groups), shape(devices, sent_rows, LANES),
        state, factor, rows, rows_low, swap(out, ("leaf", "blk")), elem_bases, coarse_v, *bases, *fields, scalars=(9,),
    )
    u, phi = call(
        functools.partial(finish_kernel, groups, width), (shape(1, elems), shape(1, elems)),
        swap(sent, ("leaf", "blk")), slot, slot_low, elem_bases,
    )
    return u.reshape(elems), phi.reshape(elems)


def solution(mesh):
    each = P(("leaf", "blk"))
    blocks = P(("leaf", "blk"), None, None)
    last = P(None, None, ("leaf", "blk"))
    in_specs = (each,) * 7 + (blocks, each, each, blocks, blocks, each, each, last, last)
    return jax.shard_map(body, mesh=mesh, in_specs=in_specs, out_specs=(each, each), check_vma=False)
```
